32 devices in a mesh: section: 2 (over x), group: 4 (over z), dp: 4 (over y, core).
Axes of the slice: x: 2, y: 2, z: 4, core: 2. Of those that a mesh axis runs over, the one named last changes fastest.
Arguments:
- enc_input: bfloat16 [2, 16, 256, 768], P('section', ('group', 'dp')), may hold values from -6 to 6
- segments: int32 [2, 16, 256], P(None, ('group', 'dp')), may hold values from 0 to 5, as said below
- slots: int32 [2, 16, 256], P(None, ('group', 'dp')), may hold values from 0 to 195, as said below
- params: bfloat16 [2, 7088128], P('section', 'group'), as said below
- cot: bfloat16 [2, 16, 980, 512], P('section', ('group', 'dp')), may hold values from -6 to 6
Outputs:
- dec_out: bfloat16 [2, 16, 980, 512], P('section', ('group', 'dp'))
- in_grad: float32 [2, 16, 256, 768], P('section', ('group', 'dp'))
- param_grad: float32 [2, 7088128], P('section', 'group')
The draws below stay inside these ranges and needn't reach their ends.
Inputs may be any that keep to these rules, and one draw needn't show every extreme that they name: `segments`: each packed row holds 5 images numbered 0 to 4 with exactly 49 positions each, in any order of positions; all other positions carry the number 5. The positions of one image have distinct slots; positions numbered 5 have slot 0. `params`: laid out as the first step says.
All inputs are finite; a program needn't handle non-finite values.
Results may differ from the reference program's by a relative error of at most 0.018.
Values may be sent and summed in bfloat16 or wider, within the bound.
No kernel may reach another device: no remote copies, remote signals or barrier semaphores. Data moves between devices by JAX's collectives and lax.ppermute only.
A program may use at most 384 MiB of HBM per device.

```python
import math
import jax
import jax.numpy as jnp
from jax import lax

WIDTH = 768
HEADS = 12
HIDDEN_SIZE = 3072
DEC_WIDTH = 512
DEC_HEADS = 16
DEC_HIDDEN = 2048
SLOTS = 196
VISIBLE = 49
IMAGES_ROW = 5
ROW = 256
MICRO = 2
ROWS = 16
DEC_ROWS = 980
PARAMS = 7088128


def block_layout_drawn(width, hidden):
    return [('norm1_gain', (width,)), ('norm1_bias', (width,)), ('qkv_weight', (width, 3 * width)), ('query_bias', (width,)), ('value_bias', (width,)), ('proj_weight', (width, width)), ('proj_bias', (width,)), ('norm2_gain', (width,)), ('norm2_bias', (width,)), ('up_weight', (width, hidden)), ('up_bias', (hidden,)), ('down_weight', (hidden, width)), ('down_bias', (width,))]


def decoder_layout_drawn(enc_width, width, hidden, slot_count):
    return [('embed_weight', (enc_width, width)), ('embed_bias', (width,)), ('mask_token', (width,)), ('position', (slot_count, width))] + block_layout_drawn(width, hidden)


gain_names = ('norm1_gain', 'norm2_gain')


bias_names = ('norm1_bias', 'query_bias', 'value_bias', 'proj_bias', 'norm2_bias', 'up_bias', 'down_bias', 'embed_bias')


def layout_spread(layout, attend_fan):
    scales = []
    offsets = []
    used_size = 0
    for entry_name, extent in layout:
        entry_size = math.prod(extent)
        used_size += entry_size
        if entry_name in gain_names:
            scale_value, offset_value = (0.15, 1.0)
        elif entry_name == 'proj_weight':
            scale_value, offset_value = (attend_fan ** (-0.5), 0.0)
        elif entry_name == 'mask_token':
            scale_value, offset_value = (1.0, 0.0)
        elif entry_name == 'position':
            scale_value, offset_value = (0.5, 0.0)
        elif entry_name in bias_names:
            scale_value, offset_value = (0.2, 0.0)
        else:
            scale_value, offset_value = (extent[0] ** (-0.5), 0.0)
        scales.append(jnp.full((entry_size,), scale_value, jnp.float32))
        offsets.append(jnp.full((entry_size,), offset_value, jnp.float32))
    scales.append(jnp.full((PARAMS - used_size,), 0.02, jnp.float32))
    offsets.append(jnp.zeros((PARAMS - used_size,), jnp.float32))
    return (jnp.concatenate(scales), jnp.concatenate(offsets))


def packing_layout(key):
    rows_all = MICRO * ROWS
    order_keys = jax.random.split(jax.random.fold_in(key, 11), rows_all)
    orders = jax.vmap(lambda row_key: jax.random.permutation(row_key, ROW))(order_keys)
    base_index = jnp.arange(ROW, dtype=jnp.int32)
    image_base = jnp.minimum(base_index // VISIBLE, IMAGES_ROW)
    rank_base = base_index % VISIBLE
    slot_keys = jax.random.split(jax.random.fold_in(key, 12), rows_all * IMAGES_ROW)
    chosen = jax.vmap(lambda row_key: jax.random.permutation(row_key, SLOTS)[:VISIBLE])(slot_keys)
    chosen = chosen.reshape(rows_all, IMAGES_ROW, VISIBLE).astype(jnp.int32)
    image_of = image_base[orders]
    rank_of = rank_base[orders]
    row_index = jnp.arange(rows_all, dtype=jnp.int32)[:, None]
    picked = chosen[row_index, jnp.minimum(image_of, IMAGES_ROW - 1), rank_of]
    slot_of = jnp.where(image_of == IMAGES_ROW, 0, picked).astype(jnp.int32)
    return (image_of.astype(jnp.int32).reshape(MICRO, ROWS, ROW), slot_of.reshape(MICRO, ROWS, ROW))


def draw_segments(key, part):
    return packing_layout(key)[0]


def draw_slots(key, part):
    return packing_layout(key)[1]


def draw_params(key, part):
    key = jax.random.fold_in(key, 3)
    enc_scale, enc_offset = layout_spread(block_layout_drawn(WIDTH, HIDDEN_SIZE), max(WIDTH * 4 // VISIBLE, 1))
    dec_scale, dec_offset = layout_spread(decoder_layout_drawn(WIDTH, DEC_WIDTH, DEC_HIDDEN, SLOTS), max(DEC_WIDTH * 4 // SLOTS, 1))
    noise = jax.random.truncated_normal(key, -3.0, 3.0, (2, PARAMS), jnp.float32)
    values = jnp.stack([enc_offset, dec_offset]) + jnp.stack([enc_scale, dec_scale]) * noise
    return values.astype(jnp.bfloat16)


def block_levels(rng, dims, cuts, low, largest):
    def one(dim, shards_of):
        heights = jax.random.uniform(jax.random.fold_in(jax.random.fold_in(rng, 6), dim), (shards_of,), jnp.float32, low / len(cuts), largest / len(cuts))
        return jnp.repeat(jnp.exp(heights), dims[dim] // shards_of).reshape((-1,) + (1,) * (len(dims) - dim - 1))

    loudness = one(*cuts[0])
    for cut in cuts[1:]:
        loudness = loudness * one(*cut)
    return loudness


def centred(own_key, shape, deviation, most, cuts=(), kind=jnp.bfloat16):
    gain = block_levels(own_key, shape, cuts, -0.22, 0.18) if cuts else 1.0
    drawn = jax.random.normal(own_key, shape, jnp.float32) * deviation * gain
    return jnp.minimum(jnp.maximum(drawn, -most), most).astype(kind)


def setup_inputs(seed: int = 0) -> dict:
    seeds = jax.random.split(jax.random.key(seed), 6)
    return {
        "enc_input": centred(seeds[0], (MICRO, ROWS, ROW, WIDTH), 1.0, 6.0, ((0, 2), (1, 16))),
        "segments": draw_segments(jax.random.fold_in(seeds[5], 71), 0),
        "slots": draw_slots(jax.random.fold_in(seeds[5], 71), 0),
        "params": draw_params(jax.random.fold_in(seeds[5], 71), 0),
        "cot": centred(seeds[4], (MICRO, ROWS, DEC_ROWS, DEC_WIDTH), 1.0, 6.0, ((0, 2), (1, 16))),
    }


@jax.custom_vjp
def low(v):
    return lax.optimization_barrier(v.astype(jnp.bfloat16)).astype(jnp.float32)

@jax.custom_vjp
def low_back(v):
    return v

def low_keep(v):
    return (low(v), None)

def low_pass(kept, grad):
    return (grad,)

def back_keep(v):
    return (v, None)

def back_low(kept, grad):
    return (low(grad),)
low.defvjp(low_keep, low_pass)
low_back.defvjp(back_keep, back_low)
norm_eps = 1e-06

def block_layout(width, hidden):
    return [('norm1_gain', (width,)), ('norm1_bias', (width,)), ('qkv_weight', (width, 3 * width)), ('query_bias', (width,)), ('value_bias', (width,)), ('proj_weight', (width, width)), ('proj_bias', (width,)), ('norm2_gain', (width,)), ('norm2_bias', (width,)), ('up_weight', (width, hidden)), ('up_bias', (hidden,)), ('down_weight', (hidden, width)), ('down_bias', (width,))]

def decoder_layout(enc_width, width, hidden, slot_count):
    return [('embed_weight', (enc_width, width)), ('embed_bias', (width,)), ('mask_token', (width,)), ('position', (slot_count, width))] + block_layout(width, hidden)

def unpack(flat_vec, layout):
    result = {}
    offset = 0
    for entry_name, extent in layout:
        entry_size = math.prod(extent)
        result[entry_name] = flat_vec[offset:offset + entry_size].reshape(extent)
        offset += entry_size
    return result

def product(form, left, right):
    return jnp.einsum(form, left, right, precision=lax.Precision.HIGHEST)

def layer_norm(inputs, gain_vec, bias_vec):
    centered = inputs - lax.optimization_barrier(jnp.mean(inputs, axis=-1, keepdims=True))
    inverse = lax.rsqrt(lax.optimization_barrier(jnp.mean(centered * centered, axis=-1, keepdims=True)) + norm_eps)
    return centered * inverse * gain_vec + bias_vec

def block(inputs, weights, heads, allowed):
    batch_n, length, width = inputs.shape
    head_dim = width // heads
    normed1 = low(layer_norm(inputs, weights['norm1_gain'], weights['norm1_bias']))
    bias_all = jnp.concatenate([weights['query_bias'], jnp.zeros((width,), inputs.dtype), weights['value_bias']])
    qkv = low_back(low(product('nlw,wc->nlc', normed1, weights['qkv_weight']) + bias_all))
    heads_split = qkv.reshape(batch_n, length, 3, heads, head_dim)
    queries, keys_all, values_all = (heads_split[:, :, 0], heads_split[:, :, 1], heads_split[:, :, 2])
    scores = product('nqhd,nkhd->nhqk', queries, keys_all) * head_dim ** (-0.5)
    if allowed is not None:
        scores = jnp.where(allowed[:, None], scores, -1000000000.0)
    scores = low_back(scores)
    probs = low(jax.nn.softmax(scores, axis=-1))
    attended = low_back(low(product('nhqk,nkhd->nqhd', probs, values_all).reshape(batch_n, length, width)))
    middle = inputs + low_back(product('nlw,wv->nlv', attended, weights['proj_weight']) + weights['proj_bias'])
    normed2 = low(layer_norm(middle, weights['norm2_gain'], weights['norm2_bias']))
    upward = low_back(product('nlw,wh->nlh', normed2, weights['up_weight']) + weights['up_bias'])
    active = low(jax.nn.gelu(upward, approximate=False))
    return middle + low_back(product('nlh,hw->nlw', active, weights['down_weight']) + weights['down_bias'])

def one_row(flat_pair, enc_row, seg_row, slot_row):
    enc_weights = unpack(flat_pair[0], block_layout(WIDTH, HIDDEN_SIZE))
    dec_weights = unpack(flat_pair[1], decoder_layout(WIDTH, DEC_WIDTH, DEC_HIDDEN, SLOTS))
    allowed = seg_row[:, None] == seg_row[None, :]
    encoded = block(enc_row[None], enc_weights, HEADS, allowed[None])[0]
    sent = low_back(low(encoded))
    embedded = low_back(low(product('tw,wd->td', sent, dec_weights['embed_weight']) + dec_weights['embed_bias']))
    positions = jnp.arange(DEC_ROWS, dtype=jnp.int32)
    image_index = positions // SLOTS
    slot_index = positions % SLOTS
    match = (seg_row[None, :] == image_index[:, None]) & (slot_row[None, :] == slot_index[:, None])
    onehot = match.astype(enc_row.dtype)
    covered = lax.optimization_barrier(jnp.sum(onehot, axis=1, keepdims=True))
    filled = product('st,td->sd', onehot, embedded)
    dec_in = filled + (1.0 - covered) * dec_weights['mask_token'] + jnp.tile(dec_weights['position'], (IMAGES_ROW, 1))
    dec_in = low_back(dec_in)
    decoded = block(dec_in.reshape(IMAGES_ROW, SLOTS, DEC_WIDTH), dec_weights, DEC_HEADS, None)
    return decoded.reshape(DEC_ROWS, DEC_WIDTH)

def reference(enc_input, segments, slots, params, cot):
    rows_all = MICRO * ROWS
    seg_flat = segments.reshape(rows_all, ROW)
    slot_flat = slots.reshape(rows_all, ROW)

    def forward(inputs, flat_pair):

        def per_row(packed):
            enc_row, seg_row, slot_row = packed
            return one_row(flat_pair, enc_row, seg_row, slot_row)
        return lax.map(jax.checkpoint(per_row), (inputs.reshape(rows_all, ROW, WIDTH), seg_flat, slot_flat))
    outputs, pullback = jax.vjp(forward, enc_input.astype(jnp.float32), params.astype(jnp.float32))
    grad_in, grad_params = pullback(cot.astype(jnp.float32).reshape(rows_all, DEC_ROWS, DEC_WIDTH))
    dec_out = outputs.reshape(MICRO, ROWS, DEC_ROWS, DEC_WIDTH).astype(jnp.bfloat16)
    return (dec_out, grad_in, grad_params)
```

```python
from functools import partial
import math

import jax
import jax.numpy as jnp
import numpy as np
from jax import lax
from jax.experimental import pallas as pl
from jax.experimental.pallas import tpu as pltpu
from jax.sharding import PartitionSpec as P

WIDTH = 768
HEADS = 12
HIDDEN_SIZE = 3072
DEC_WIDTH = 512
DEC_HEADS = 16
DEC_HIDDEN = 2048
SLOTS = 196
IMAGES_ROW = 5
ROW = 256
PARAMS = 7088128
LANES = 128
SEC, GRP, DP = "section", "group", "dp"
(
    N1G, N1B, QKV_W, QB, VB, PROJ_W, PB, N2G,
) = range(0, 8)
(
    N2B, UP_W, UB, DOWN_W, DB, EMBED_W, EB, MT,
) = range(8, 16)
(
    POS, QKV_B, VECS, SENT, H1, QKV, PROBS, ATT,
) = range(16, 24)
(
    MID, H2, ACT, SLOPE, OUT, QKV_L, PROJ_L, UP_L,
) = range(24, 32)
(
    EMBED_L, GSENT, GPOS,
) = range(32, 35)
SLOT_PAD = 208
VMEM_BYTES = 60 * 1024 * 1024

norm_eps = 1e-06
masked_score = -1000000000.0
f32 = jnp.float32
bf16 = jnp.bfloat16


def block_layout(width, hidden):
    return [
        (N1G, (width,)),
        (N1B, (width,)),
        (QKV_W, (width, 3 * width)),
        (QB, (width,)),
        (VB, (width,)),
        (PROJ_W, (width, width)),
        (PB, (width,)),
        (N2G, (width,)),
        (N2B, (width,)),
        (UP_W, (width, hidden)),
        (UB, (hidden,)),
        (DOWN_W, (hidden, width)),
        (DB, (width,)),
    ]


def decoder_layout(enc_width, width, hidden, slot_count):
    return [
        (EMBED_W, (enc_width, width)),
        (EB, (width,)),
        (MT, (width,)),
        (POS, (slot_count, width)),
    ] + block_layout(width, hidden)


ENC_LAYOUT = block_layout(WIDTH, HIDDEN_SIZE)
DEC_LAYOUT = decoder_layout(WIDTH, DEC_WIDTH, DEC_HIDDEN, SLOTS)
VEC = {
    N1G: 0,
    N1B: 1,
    QKV_B: 2,
    PB: 3,
    N2G: 4,
    N2B: 5,
    UB: 6,
    DB: 7,
    EB: 8,
    MT: 9,
}
VEC_ROWS = 16


def dot(a, b):
    return lax.dot_general(a, b, (((1,), (0,)), ((), ())), preferred_element_type=f32)


def dot_nt(a, b):
    return lax.dot_general(a, b, (((1,), (1,)), ((), ())), preferred_element_type=f32)


def dot_tn(a, b):
    return lax.dot_general(a, b, (((0,), (0,)), ((), ())), preferred_element_type=f32)


def normalised(values):
    centered = values - jnp.mean(values, axis=-1, keepdims=True)
    inverse = lax.rsqrt(jnp.mean(centered * centered, axis=-1, keepdims=True) + norm_eps)
    return centered * inverse, inverse


def norm_back(grad, hat, inverse, gain):
    scaled = grad * gain
    first = jnp.mean(scaled, axis=-1, keepdims=True)
    second = jnp.mean(scaled * hat, axis=-1, keepdims=True)
    return inverse * (scaled - first - hat * second)


def col_sum(values):
    return jnp.sum(values, axis=0, keepdims=True)


def gelu_parts(upward):
    half = 0.5 + 0.5 * lax.erf(upward * f32(math.sqrt(0.5)))
    slope = half + upward * (jnp.exp(upward * upward * f32(-0.5)) * f32(1.0 / math.sqrt(2.0 * math.pi)))
    return upward * half, slope


def head_mask(head, head_dim):
    lane = lax.broadcasted_iota(jnp.int32, (1, LANES), 1)
    return jnp.where(lane // head_dim == head, 1.0, 0.0).astype(bf16)


def lane_block(group, start=0):
    return pl.ds(pl.multiple_of(start + group * LANES, LANES), LANES)


def flip(values):
    return values.astype(f32).T.astype(bf16)


def attention_forward(qkv_ref, probs_ref, joined_ref, width, heads, keep):
    head_dim = width // heads
    scale = f32(head_dim ** (-0.5))
    per_group = LANES // head_dim

    def one_group(group, carry):
        queries = qkv_ref[:, lane_block(group)]
        keys = qkv_ref[:, lane_block(group, width)]
        values_t = flip(qkv_ref[:, lane_block(group, 2 * width)])
        for sub in range(per_group):
            scores = dot_nt(keys, queries * head_mask(sub, head_dim)) * scale
            scores = keep(scores)
            expo = jnp.exp(scores - jnp.max(scores, axis=0, keepdims=True))
            probs = expo * (1.0 / col_sum(expo))
            probs_ref[group * per_group + sub] = probs
            rows = pl.ds(pl.multiple_of(group * LANES + sub * head_dim, head_dim), head_dim)
            joined_ref[rows, :] = dot(
                values_t[sub * head_dim : (sub + 1) * head_dim], probs.astype(bf16)
            )
        return carry

    lax.fori_loop(0, width // LANES, one_group, 0)


def attention_backward(qkv_ref, probs_ref, grad_ref, low_ref, width, heads):
    head_dim = width // heads
    scale = f32(head_dim ** (-0.5))
    per_group = LANES // head_dim

    def one_group(group, carry):
        queries = qkv_ref[:, lane_block(group)]
        keys = qkv_ref[:, lane_block(group, width)]
        values = qkv_ref[:, lane_block(group, 2 * width)]
        grads = grad_ref[:, lane_block(group)]
        keys_t = flip(keys)
        grad_values = jnp.zeros(values.shape, f32)
        grad_keys = jnp.zeros(values.shape, f32)
        grad_queries = []
        for sub in range(per_group):
            mask = head_mask(sub, head_dim)
            probs = probs_ref[group * per_group + sub]
            own = grads * mask
            grad_values += dot(probs.astype(bf16), own)
            grad_probs = dot_nt(values, own)
            delta = col_sum(probs * grad_probs)
            low = (probs * (grad_probs - delta)).astype(bf16)
            grad_keys += dot(low, queries * mask)
            grad_queries.append(dot(keys_t[sub * head_dim : (sub + 1) * head_dim], low))
        low_ref[:, lane_block(group)] = (jnp.concatenate(grad_queries, axis=0).T * scale).astype(bf16)
        low_ref[:, lane_block(group, width)] = (grad_keys * scale).astype(bf16)
        low_ref[:, lane_block(group, 2 * width)] = grad_values.astype(bf16)
        return carry

    lax.fori_loop(0, width // LANES, one_group, 0)


def encode_kernel(
    x_ref, seg_row_ref, seg_col_ref, qkv_w, proj_w, up_w, down_w, vec,
    sent_ref, normed1_ref, qkv_ref, probs_ref, attended_ref, middle_ref, normed2_ref, active_ref,
    slope_ref, joined_ref,
):
    width, hidden = WIDTH, HIDDEN_SIZE
    inputs = x_ref[...].astype(f32)
    hat, _ = normalised(inputs)
    normed1 = (hat * vec[0:1, :width] + vec[1:2, :width]).astype(bf16)
    normed1_ref[...] = normed1
    qkv_ref[...] = (dot(normed1, qkv_w[...]) + vec[2:3, : 3 * width]).astype(bf16)
    allowed = seg_col_ref[...] == seg_row_ref[...]
    attention_forward(
        qkv_ref, probs_ref, joined_ref, width, HEADS,
        lambda scores: jnp.where(allowed, scores, f32(masked_score)),
    )
    attended = joined_ref[...].T.astype(bf16)
    attended_ref[...] = attended
    middle = inputs + (dot(attended, proj_w[...]) + vec[3:4, :width])
    middle_ref[...] = middle
    hat, _ = normalised(middle)
    normed2_ref[...] = (hat * vec[4:5, :width] + vec[5:6, :width]).astype(bf16)
    joined_ref[...] = jnp.zeros_like(joined_ref)
    total = jnp.zeros((inputs.shape[0], width), f32)
    part = 512
    for start in range(0, hidden, part):
        cols = slice(start, start + part)
        upward = dot(normed2_ref[...], up_w[:, cols]) + vec[6:7, cols]
        active, slope = gelu_parts(upward)
        active_ref[:, cols] = active.astype(bf16)
        slope_ref[:, cols] = slope.astype(slope_ref.dtype)
        total += dot(active_ref[:, cols], down_w[cols, :])
    sent_ref[...] = (middle + (total + vec[7:8, :width])).astype(bf16)


def encode_back_kernel(
    grad_ref, x_ref, qkv_ref, probs_ref, middle_ref, slope_ref, qkv_w, proj_w, up_w, down_w, vec,
    in_grad_ref, qkv_low_ref, proj_low_ref, up_low_ref, vec_grad, grad_att_ref,
):
    width, hidden = WIDTH, HIDDEN_SIZE
    grad_out = grad_ref[...]
    vec_grad[...] = jnp.zeros_like(vec_grad)
    vec_grad[7:8, :width] = col_sum(grad_out.astype(f32))
    grad_normed2 = jnp.zeros((grad_out.shape[0], width), f32)
    part = 512
    for start in range(0, hidden, part):
        cols = slice(start, start + part)
        low = (dot_nt(grad_out, down_w[cols, :]) * slope_ref[:, cols]).astype(bf16)
        up_low_ref[:, cols] = low
        vec_grad[6:7, cols] = col_sum(low.astype(f32))
        grad_normed2 += dot_nt(low, up_w[:, cols])
    hat, inverse = normalised(middle_ref[...])
    vec_grad[4:5, :width] = col_sum(grad_normed2 * hat)
    vec_grad[5:6, :width] = col_sum(grad_normed2)
    grad_middle = grad_out.astype(f32) + norm_back(grad_normed2, hat, inverse, vec[4:5, :width])
    proj_low = grad_middle.astype(bf16)
    proj_low_ref[...] = proj_low
    vec_grad[3:4, :width] = col_sum(proj_low.astype(f32))
    grad_att_ref[...] = dot_nt(proj_low, proj_w[...]).astype(bf16)
    attention_backward(qkv_ref, probs_ref, grad_att_ref, qkv_low_ref, width, HEADS)
    qkv_low = qkv_low_ref[...]
    vec_grad[2:3, : 3 * width] = col_sum(qkv_low.astype(f32))
    grad_normed1 = dot_nt(qkv_low, qkv_w[...])
    hat, inverse = normalised(x_ref[...].astype(f32))
    vec_grad[0:1, :width] = col_sum(grad_normed1 * hat)
    vec_grad[1:2, :width] = col_sum(grad_normed1)
    in_grad_ref[...] = grad_middle + norm_back(grad_normed1, hat, inverse, vec[0:1, :width])


def decode_kernel(
    sent_ref, embed_w, qkv_w, proj_w, up_w, down_w, vec, pos_ref,
    seg_row, slot_row, seg_col, slot_col, cot_ref,
    out_ref, normed1_ref, qkv_low_ref, attended_ref, proj_low_ref, normed2_ref, up_low_ref,
    active_ref, embed_low_ref, grad_sent_ref, vec_grad, pos_grad,
    embedded_ref, embed_sum, qkv_ref, probs_ref, joined_ref, grad_att_ref,
):
    width, hidden = DEC_WIDTH, DEC_HIDDEN
    image = pl.program_id(0)
    length = SLOT_PAD

    @pl.when(image == 0)
    def _():
        embedded_ref[...] = (dot(sent_ref[...], embed_w[...]) + vec[8:9, :width]).astype(bf16)
        vec_grad[...] = jnp.zeros_like(vec_grad)
        pos_grad[...] = jnp.zeros_like(pos_grad)
        embed_sum[...] = jnp.zeros_like(embed_sum)

    def add_vec(row, values):
        vec_grad[row : row + 1, : values.shape[1]] += values

    place = lax.broadcasted_iota(jnp.int32, (length, ROW), 0)
    match = (seg_row[...] == image) & (slot_row[...] == place)
    onehot = jnp.where(match, 1.0, 0.0)
    free = 1.0 - jnp.sum(onehot, axis=1, keepdims=True)
    x = dot(onehot.astype(bf16), embedded_ref[...]) + free * vec[9:10, :width] + pos_ref[...].astype(f32)
    hat1, inverse1 = normalised(x)
    normed1 = (hat1 * vec[0:1, :width] + vec[1:2, :width]).astype(bf16)
    normed1_ref[...] = normed1
    qkv_ref[...] = (dot(normed1, qkv_w[...]) + vec[2:3, : 3 * width]).astype(bf16)
    key_place = lax.broadcasted_iota(jnp.int32, (length, length), 0)
    attention_forward(
        qkv_ref, probs_ref, joined_ref, width, DEC_HEADS,
        lambda scores: jnp.where(key_place < SLOTS, scores, f32(-1e30)),
    )
    attended = joined_ref[...].T.astype(bf16)
    attended_ref[...] = attended
    middle = x + (dot(attended, proj_w[...]) + vec[3:4, :width])
    hat2, inverse2 = normalised(middle)
    normed2 = (hat2 * vec[4:5, :width] + vec[5:6, :width]).astype(bf16)
    normed2_ref[...] = normed2
    cot = cot_ref[...]
    add_vec(7, col_sum(cot.astype(f32)))
    total = jnp.zeros((length, width), f32)
    grad_normed2 = jnp.zeros((length, width), f32)
    part = 512
    for start in range(0, hidden, part):
        cols = slice(start, start + part)
        upward = dot(normed2_ref[...], up_w[:, cols]) + vec[6:7, cols]
        active, slope = gelu_parts(upward)
        active = active.astype(bf16)
        active_ref[:, cols] = active
        total += dot(active, down_w[cols, :])
        low = (dot_nt(cot_ref[...], down_w[cols, :]) * slope).astype(bf16)
        up_low_ref[:, cols] = low
        vec_grad[6:7, cols] += col_sum(low.astype(f32))
        grad_normed2 += dot_nt(low, up_w[:, cols])
    out_ref[...] = (middle + (total + vec[7:8, :width])).astype(bf16)

    add_vec(4, col_sum(grad_normed2 * hat2))
    add_vec(5, col_sum(grad_normed2))
    grad_middle = cot.astype(f32) + norm_back(grad_normed2, hat2, inverse2, vec[4:5, :width])
    proj_low = grad_middle.astype(bf16)
    proj_low_ref[...] = proj_low
    add_vec(3, col_sum(proj_low.astype(f32)))
    grad_att_ref[...] = dot_nt(proj_low, proj_w[...]).astype(bf16)
    attention_backward(qkv_ref, probs_ref, grad_att_ref, qkv_low_ref, width, DEC_HEADS)
    qkv_low = qkv_low_ref[...]
    add_vec(2, col_sum(qkv_low.astype(f32)))
    grad_normed1 = dot_nt(qkv_low, qkv_w[...])
    add_vec(0, col_sum(grad_normed1 * hat1))
    add_vec(1, col_sum(grad_normed1))
    grad_in = grad_middle + norm_back(grad_normed1, hat1, inverse1, vec[0:1, :width])
    low_in = grad_in.astype(bf16)
    wide = low_in.astype(f32)
    add_vec(9, col_sum(free * wide))
    pos_grad[...] += wide
    place_t = lax.broadcasted_iota(jnp.int32, (ROW, length), 1)
    match_t = (seg_col[...] == image) & (slot_col[...] == place_t)
    embed_sum[...] += dot(jnp.where(match_t, 1.0, 0.0).astype(bf16), low_in)

    @pl.when(image == IMAGES_ROW - 1)
    def _():
        embed_low = embed_sum[...].astype(bf16)
        embed_low_ref[...] = embed_low
        add_vec(8, col_sum(embed_low.astype(f32)))
        grad_sent_ref[...] = dot_nt(embed_low, embed_w[...]).astype(bf16)


def params_of(**extra):
    return pltpu.CompilerParams(vmem_limit_bytes=VMEM_BYTES, **extra)


def shape(dims, kind):
    return jax.ShapeDtypeStruct(dims, kind)


def encode(x, seg, weights):
    width, hidden, length = WIDTH, HIDDEN_SIZE, ROW
    names = [QKV_W, PROJ_W, UP_W, DOWN_W, VECS]
    return pl.pallas_call(
        encode_kernel,
        out_shape=[
            shape((length, width), bf16),
            shape((length, width), bf16),
            shape((length, 3 * width), bf16),
            shape((HEADS, length, length), f32),
            shape((length, width), bf16),
            shape((length, width), f32),
            shape((length, width), bf16),
            shape((length, hidden), bf16),
            shape((length, hidden), bf16),
        ],
        scratch_shapes=[pltpu.VMEM((width, length), f32)],
        compiler_params=params_of(),
        name="encode",
    )(x, seg.reshape(1, length), seg.reshape(length, 1), *[weights[n] for n in names])


def encode_back(grad, x, saved, weights):
    width, hidden, length = WIDTH, HIDDEN_SIZE, ROW
    names = [QKV_W, PROJ_W, UP_W, DOWN_W, VECS]
    return pl.pallas_call(
        encode_back_kernel,
        out_shape=[
            shape((length, width), f32),
            shape((length, 3 * width), bf16),
            shape((length, width), bf16),
            shape((length, hidden), bf16),
            shape((VEC_ROWS, hidden), f32),
        ],
        scratch_shapes=[pltpu.VMEM((length, width), bf16)],
        compiler_params=params_of(),
        name="encode_back",
    )(grad, x, saved[QKV], saved[PROBS], saved[MID], saved[SLOPE], *[weights[n] for n in names])


def decode(sent, seg, slot, cot, weights):
    width, hidden, length = DEC_WIDTH, DEC_HIDDEN, SLOT_PAD
    names = [EMBED_W, QKV_W, PROJ_W, UP_W, DOWN_W, VECS, POS]
    held = [sent] + [weights[n] for n in names]
    held += [seg.reshape(1, ROW), slot.reshape(1, ROW), seg.reshape(ROW, 1), slot.reshape(ROW, 1)]

    def whole(array):
        return pl.BlockSpec(array.shape, lambda i: (0,) * array.ndim, pipeline_mode=pl.Buffered(1))

    def image(cols):
        return pl.BlockSpec((length, cols), lambda i: (i, 0))

    rows = IMAGES_ROW * length
    per_image = [width, width, 3 * width, width, width, width, hidden, hidden]
    kept = [
        shape((ROW, width), bf16),
        shape((ROW, WIDTH), bf16),
        shape((VEC_ROWS, hidden), f32),
        shape((length, width), f32),
    ]
    return pl.pallas_call(
        decode_kernel,
        grid=(IMAGES_ROW,),
        in_specs=[whole(a) for a in held] + [image(width)],
        out_specs=[image(c) for c in per_image]
        + [pl.BlockSpec(s.shape, lambda i: (0, 0)) for s in kept],
        out_shape=[shape((rows, c), bf16) for c in per_image] + kept,
        scratch_shapes=[
            pltpu.VMEM((ROW, width), bf16),
            pltpu.VMEM((ROW, width), f32),
            pltpu.VMEM((length, 3 * width), bf16),
            pltpu.VMEM((DEC_HEADS, length, length), f32),
            pltpu.VMEM((width, length), f32),
            pltpu.VMEM((length, width), bf16),
        ],
        compiler_params=params_of(dimension_semantics=("arbitrary",)),
        name="decode",
    )(*held, cot)


def rows_of(extent):
    return math.prod(extent) // LANES


def up_to(value, step):
    return -(-value // step) * step


def flat_starts(layout):
    starts, here = {}, 0
    for name, extent in layout:
        starts[name] = here
        here += rows_of(extent)
    return starts, here


def kept_starts(layout):
    starts, here = {}, 0
    for name, extent in layout:
        starts[name] = here
        here += up_to(rows_of(extent), 16)
    return starts, here


class Plan:
    def __init__(self, mesh_shape):
        self.ns, self.ng, self.nd = (mesh_shape[a] for a in (SEC, GRP, DP))
        self.ny = self.nd // 2
        self.chunk = PARAMS // LANES // self.ng
        self.pieces = self.ns * self.nd
        self.piece = up_to(-(-self.chunk // self.pieces), 64)
        self.half = self.piece // 2
        self.room = self.piece * self.pieces
        self.units = 2 * self.pieces
        self.full = self.ng // 2
        self.dec_rows = flat_starts(DEC_LAYOUT)[1]
        self.rest = self.dec_rows - self.full * self.chunk
        self.rest_room = up_to(self.rest + 80, 16)
        assert 0 < self.rest <= self.chunk and self.rest_room <= self.half + self.chunk
        self.enc_keep, self.enc_kept = kept_starts(ENC_LAYOUT)
        self.dec_keep, self.dec_kept = kept_starts(DEC_LAYOUT)
        self.enc_starts = [self.kept_row(ENC_LAYOUT, z * self.chunk) // 16 * 16 for z in range(self.ng)]
        self.dec_starts = [self.kept_row(DEC_LAYOUT, z * self.chunk) // 16 * 16 for z in range(self.full)]
        self.rest_start = self.kept_row(DEC_LAYOUT, self.full * self.chunk) // 16 * 16
        for z in range(self.ng):
            last = self.kept_row(ENC_LAYOUT, min((z + 1) * self.chunk, flat_starts(ENC_LAYOUT)[1]) - 1)
            assert last < self.enc_starts[z] + self.room
        for z in range(self.full):
            last = self.kept_row(DEC_LAYOUT, (z + 1) * self.chunk - 1)
            assert last < self.dec_starts[z] + self.room
        assert self.dec_kept <= self.rest_start + self.rest_room
        self.enc_table = self.enc_starts[-1] + self.room
        self.dec_table = max(self.dec_starts[-1] + self.room, self.rest_start + self.rest_room)

    def kept_row(self, layout, flat_row):
        flat, _ = flat_starts(layout)
        kept, _ = kept_starts(layout)
        for name, extent in layout:
            if flat_row < flat[name] + rows_of(extent):
                return kept[name] + flat_row - flat[name]
        return kept[name] + rows_of(extent)

    def ranges(self, first, count, cut, chunks):
        found = []
        whole = self.chunk // cut * cut
        while count:
            z, row = divmod(first, self.chunk)
            if z >= chunks:
                here, room = chunks * self.room + row, count
            elif row < whole:
                here, room = z * self.room + row, whole - row
            else:
                here, room = z * self.room + row + cut - (self.chunk - whole), self.chunk - row
            take = min(count, room)
            found.append((here, take))
            first, count = first + take, count - take
        return found

    def segments(self):
        count = len(DEC_LAYOUT) + 1
        table = np.zeros((self.ns, self.ng, count, 3), np.int32)
        for s, layout in enumerate((ENC_LAYOUT, DEC_LAYOUT)):
            flat, used = flat_starts(layout)
            for z in range(self.ng):
                low, high = z * self.chunk, (z + 1) * self.chunk
                if s == 0:
                    base = -self.enc_starts[z]
                elif z < self.full:
                    base = -self.dec_starts[z]
                else:
                    base = self.room - self.rest_start
                for k, (name, extent) in enumerate(layout):
                    first, last = max(flat[name], low), min(flat[name] + rows_of(extent), high)
                    if first < last:
                        table[s, z, k] = (
                            base + self.kept_row(layout, first), first - low, -(-(last - first) // 8),
                        )
                if used < high:
                    table[s, z, count - 1] = (self.room + self.rest_room, max(used - low, 0), 1)
        return table


def widen_block(held, wide, spare, ranges):
    def load(start, count):
        first = start // 16 * 16
        size = up_to(start + count - first, 16)
        return held[first : first + size, :].astype(f32), size, start - first

    if len(ranges) == 1:
        block, size, skip = load(*ranges[0])
        wide[0:size, :] = block
        return skip
    here = 0
    for start, count in ranges:
        block, size, skip = load(start, count)
        spare[0:size, :] = block
        wide[here : here + count, :] = spare[skip : skip + count, :]
        here += count
    return 0


def unpack_kernel(plan, layout, unit, cut, chunks, counts, place_ref, *refs):
    sources = refs[: len(counts)]
    refs = refs[len(counts) :]
    rest = None
    if chunks < plan.ng:
        rest, refs = refs[0], refs[1:]
    matrices = [(n, e) for n, e in layout if len(e) == 2]
    outs, vec = refs[: len(matrices)], refs[len(matrices)]
    held, wide, spare, sems = refs[len(matrices) + 1 :]
    per_chunk = plan.room // unit
    number = 0
    for source, count in zip(sources, counts):
        for k in range(count):
            slot = place_ref[number]
            number += 1
            target = held.at[pl.ds(pl.multiple_of(slot * unit, 16), unit), :]
            pltpu.make_async_copy(source.at[pl.ds(k * unit, unit), :], target, sems.at[slot // per_chunk]).start()
    if rest is not None:
        target = held.at[pl.ds(chunks * plan.room, rest.shape[0]), :]
        pltpu.make_async_copy(rest, target, sems.at[chunks]).start()
    arrived = set()

    def arrive(ranges):
        for start, count in ranges:
            z = min(start // plan.room, chunks)
            if z not in arrived:
                arrived.add(z)
                rows = plan.room if z < chunks else rest.shape[0]
                part = held.at[pl.ds(z * plan.room, rows), :]
                pltpu.make_async_copy(part, part, sems.at[z]).wait()

    vec[...] = jnp.zeros_like(vec)
    flat, _ = flat_starts(layout)
    by_name = dict(zip([n for n, _ in matrices], outs))
    for name, extent in layout:
        if len(extent) == 2:
            depth, lanes = extent[0], extent[1] // LANES
            step = depth if name == POS else max(128, 2048 // lanes // 128 * 128)
            out = by_name[name]
            if name == POS:
                out[...] = jnp.zeros_like(out)
            for first in range(0, depth, step):
                size = min(step, depth - first)
                ranges = plan.ranges(flat[name] + first * lanes, size * lanes, cut, chunks)
                arrive(ranges)
                skip = widen_block(held, wide, spare, ranges)
                for j in range(lanes):
                    block = wide[pl.ds(skip + j, size, stride=lanes), :].astype(bf16)
                    out[first : first + size, j * LANES : (j + 1) * LANES] = block
        else:
            lanes = extent[0] // LANES
            ranges = plan.ranges(flat[name], lanes, cut, chunks)
            arrive(ranges)
            skip = widen_block(held, wide, spare, ranges)
            row, shift = {QB: (2, 0), VB: (2, 2 * extent[0])}.get(name, (VEC.get(name), 0))
            for j in range(lanes):
                vec[row : row + 1, shift + j * LANES : shift + (j + 1) * LANES] = wide[skip + j : skip + j + 1, :]
    for z in range(chunks + (rest is not None)):
        if z not in arrived:
            arrive([(z * plan.room, 1)])


def unpack(plan, layout, unit, cut, chunks, place, sources, rest=None):
    matrices = [(n, e) for n, e in layout if len(e) == 2]
    outs = [
        shape((SLOT_PAD if n == POS else e[0], e[1]), bf16) for n, e in matrices
    ] + [shape((VEC_ROWS, 4 * dict(layout)[PB][0]), f32)]
    operands = list(sources) + ([] if rest is None else [rest])
    rows = chunks * plan.room + (0 if rest is None else rest.shape[0])
    result = pl.pallas_call(
        partial(unpack_kernel, plan, layout, unit, cut, chunks, [s.shape[0] // unit for s in sources]),
        in_specs=[pl.BlockSpec(memory_space=pltpu.SMEM)]
        + [pl.BlockSpec(memory_space=pl.ANY)] * len(operands),
        out_shape=outs,
        scratch_shapes=[
            pltpu.VMEM((rows, LANES), bf16),
            pltpu.VMEM((3200, LANES), f32),
            pltpu.VMEM((3200, LANES), f32),
            pltpu.SemaphoreType.DMA((chunks + 1,)),
        ],
        compiler_params=params_of(),
        name="unpack",
    )(place, *operands)
    return dict(zip([n for n, _ in matrices] + [VECS], result))


def pack_kernel(layout, names, *refs):
    pairs = {}
    for name in names:
        pairs[name], refs = refs[:2], refs[2:]
    vec, refs = refs[0], refs[1:]
    pos = None
    if POS in dict(layout):
        pos, refs = refs[0], refs[1:]
    table, wide, stage, small, sems, small_sem = refs
    kept, _ = kept_starts(layout)
    extents = dict(layout)
    step = 128
    for name in names:
        left, right = pairs[name]
        depth, width = extents[name]
        lanes = width // LANES
        rows = step * lanes

        def copy(index, slot, rows=rows, name=name):
            start = pl.multiple_of(kept[name] + index * rows, 16)
            return pltpu.make_async_copy(
                stage.at[slot, pl.ds(0, rows), :], table.at[pl.ds(start, rows), :], sems.at[slot]
            )

        def one(index, carry, left=left, right=right, width=width, lanes=lanes, rows=rows, copy=copy):
            slot = lax.rem(index, 2)
            columns = flip(left[:, pl.ds(pl.multiple_of(index * step, step), step)])
            part = 256
            for first in range(0, width, part):
                block = dot(columns, right[:, first : first + part])
                for j in range(part // LANES):
                    wide[pl.ds(first // LANES + j, step, stride=lanes), :] = block[:, j * LANES : (j + 1) * LANES]

            @pl.when(index >= 2)
            def _():
                copy(index - 2, slot).wait()

            stage[slot, 0:rows, :] = wide[0:rows, :].astype(bf16)
            copy(index, slot).start()
            return carry

        count = depth // step
        lax.fori_loop(0, count, one, 0)
        for index in range(max(count - 2, 0), count):
            copy(index, index % 2).wait()
    here = 0
    copies = []
    for name, extent in layout:
        if len(extent) == 2 and name != POS:
            continue
        rows = rows_of(extent)
        room = up_to(rows, 16)
        wide[0:room, :] = jnp.zeros((room, LANES), f32)
        if name == POS:
            lanes = extent[1] // LANES
            for j in range(lanes):
                wide[pl.ds(j, extent[0], stride=lanes), :] = pos[0 : extent[0], j * LANES : (j + 1) * LANES]
        else:
            row, shift = {QB: (2, 0), VB: (2, 2 * extent[0])}.get(name, (VEC.get(name), 0))
            for j in range(rows):
                wide[j : j + 1, :] = vec[row : row + 1, shift + j * LANES : shift + (j + 1) * LANES]
        small[here : here + room, :] = wide[0:room, :].astype(bf16)
        copies.append(
            pltpu.make_async_copy(
                small.at[pl.ds(here, room), :], table.at[pl.ds(kept[name], room), :], small_sem.at[0]
            )
        )
        here += room
    for each in copies:
        each.start()
    pltpu.make_async_copy(small, small, small_sem.at[0]).wait()


def pack(layout, table_rows, pairs, vec, pos=None):
    names = list(pairs)
    operands = [a for name in names for a in pairs[name]] + [vec] + ([] if pos is None else [pos])
    small = sum(
        up_to(rows_of(e), 16) for n, e in layout if len(e) == 1 or n == POS
    )
    most = 128 * max(e[1] for n, e in layout if len(e) == 2) // LANES
    return pl.pallas_call(
        partial(pack_kernel, layout, names),
        in_specs=[pl.BlockSpec(memory_space=pltpu.VMEM)] * len(operands),
        out_specs=pl.BlockSpec(memory_space=pl.ANY),
        out_shape=shape((table_rows, LANES), bf16),
        scratch_shapes=[
            pltpu.VMEM((most, LANES), f32),
            pltpu.VMEM((2, most, LANES), bf16),
            pltpu.VMEM((small, LANES), bf16),
            pltpu.SemaphoreType.DMA((2,)),
            pltpu.SemaphoreType.DMA((1,)),
        ],
        compiler_params=params_of(),
        name="pack",
    )(*operands)


def finish_kernel(plan, counts, place_ref, seg_ref, *refs):
    sources, rest, out, held, wide, sem = refs[: len(counts)], *refs[len(counts) :]
    unit = plan.half
    number = 0
    for source, count in zip(sources, counts):
        for k in range(count):
            target = held.at[pl.ds(pl.multiple_of(place_ref[number] * unit, 16), unit), :]
            number += 1
            pltpu.make_async_copy(source.at[pl.ds(k * unit, unit), :], target, sem.at[0]).start()
    pltpu.make_async_copy(rest, held.at[pl.ds(plan.room, plan.rest_room), :], sem.at[0]).start()
    out[...] = jnp.zeros_like(out)
    pltpu.make_async_copy(held, held, sem.at[0]).wait()
    total = plan.room + plan.rest_room
    wide[total : total + 16, :] = jnp.zeros((16, LANES), f32)
    wide[0:total, :] = held[...].astype(f32)

    def one(k, carry):
        source, first, steps = seg_ref[3 * k], seg_ref[3 * k + 1], seg_ref[3 * k + 2]

        def step(i, carry):
            out[pl.ds(first + 8 * i, 8), :] = wide[pl.ds(source + 8 * i, 8), :]
            return carry

        def steps8(i, carry):
            out[pl.ds(first + 64 * i, 64), :] = wide[pl.ds(source + 64 * i, 64), :]
            return carry

        many = steps // 8
        lax.fori_loop(0, many, steps8, 0)
        return lax.fori_loop(many * 8, steps, step, carry)

    lax.fori_loop(0, seg_ref.shape[0] // 3, one, 0)


def finish(plan, place, segments, sources, rest):
    total = plan.room + plan.rest_room
    return pl.pallas_call(
        partial(finish_kernel, plan, [s.shape[0] // plan.half for s in sources]),
        in_specs=[pl.BlockSpec(memory_space=pltpu.SMEM)] * 2
        + [pl.BlockSpec(memory_space=pl.ANY)] * (len(sources) + 1),
        out_shape=shape((up_to(plan.chunk, 8) + 8, LANES), f32),
        scratch_shapes=[
            pltpu.VMEM((total, LANES), bf16),
            pltpu.VMEM((total + 16, LANES), f32),
            pltpu.SemaphoreType.DMA((1,)),
        ],
        compiler_params=params_of(),
        name="finish",
    )(place, segments, *sources, rest)


def per_device(plan, enc_input, segments, slots, params, cot):
    ns, ng, nd, ny = plan.ns, plan.ng, plan.nd, plan.ny
    piece, half, room, chunk = plan.piece, plan.half, plan.room, plan.chunk
    sec = lax.axis_index(SEC)
    grp = lax.axis_index(GRP)
    dp = lax.axis_index(DP)
    yy, core = dp // 2, dp % 2
    first_section = sec == 0

    def over_x(block):
        return lax.ppermute(block, SEC, [(0, 1), (1, 0)])

    def over_core(block):
        return lax.ppermute(block, DP, [(d, d ^ 1) for d in range(nd)])

    def over_y(block):
        return lax.ppermute(block, DP, [(d, (d + 2) % nd) for d in range(nd)])

    def over_z(block):
        return lax.ppermute(block, GRP, [(g, (g + 1) % ng) for g in range(ng)])

    def share(start):
        cut = lax.dynamic_slice(params, (0, start * LANES), (1, half * LANES))
        return cut.astype(f32).reshape(half, LANES).astype(bf16)

    def shares(section):
        number = section * nd + dp
        enc_first = jnp.minimum(number * piece, chunk - piece)
        dec_first = [jnp.minimum((h * plan.pieces + number) * half, chunk - half) for h in range(2)]
        starts = [
            jnp.where(first_section, enc_first, dec_first[0]),
            jnp.where(first_section, enc_first + half, dec_first[1]),
        ]
        return jnp.concatenate([share(s) for s in starts])

    keep = shares(sec)
    got = over_x(shares(1 - sec))
    enc_piece = jnp.where(first_section, keep, got)
    dec_pieces = jnp.where(first_section, got, keep)
    spread = [
        lax.ppermute(dec_pieces[h * half : (h + 1) * half], GRP, [(z, 2 * z + h) for z in range(plan.full)])
        for h in range(2)
    ]
    dec_piece = jnp.where(grp % 2 == 0, spread[0], spread[1])
    holds_rest = jnp.logical_and(sec == 1, grp == plan.full)
    rest_cut = params[:, : plan.rest * LANES].astype(f32).reshape(plan.rest, LANES)
    rest_weights = lax.psum(
        jnp.where(holds_rest, rest_cut, 0.0).astype(bf16), (SEC, GRP)
    )
    rest_weights = jnp.pad(rest_weights, ((0, plan.rest_room - plan.rest), (0, 0)))

    def gather(block):
        size = block.shape[0]
        sources, places = [], []
        here = block
        for step in range(ng):
            own_group = (grp - step) % ng
            number = lambda s, y, c: (own_group * plan.pieces + s * nd + y * 2 + c) * 2
            if ny == 2:
                from_x, from_y = over_x(here), over_y(here)
                corner_0 = over_y(from_x[: size // 2])
                corner_1 = over_x(from_y[size // 2 :])
                all_four = jnp.concatenate([here, from_x, from_y, corner_0, corner_1])
                owners = [(sec, yy), (1 - sec, yy), (sec, 1 - yy), (1 - sec, 1 - yy)]
            else:
                ring = [here]
                for _ in range(ny - 1):
                    ring.append(over_y(ring[-1]))
                column = jnp.concatenate(ring)
                all_four = jnp.concatenate([column, over_x(column)])
                owners = [(s, (yy - k) % ny) for s in (sec, 1 - sec) for k in range(ny)]
            sources += [all_four, over_core(all_four)]
            for c in (core, 1 - core):
                for s, y in owners:
                    places += [number(s, y, c), number(s, y, c) + 1]
            if step < ng - 1:
                here = over_z(here)
        return sources, jnp.stack(places).astype(jnp.int32)

    enc_sources, enc_places = gather(enc_piece)
    dec_sources, dec_places = gather(dec_piece)

    micro_rows = enc_input.reshape(ROW, WIDTH)
    seg = lax.dynamic_index_in_dim(segments, sec, 0, keepdims=False).reshape(ROW)
    slot = lax.dynamic_index_in_dim(slots, sec, 0, keepdims=False).reshape(ROW)
    cot_rows = jnp.pad(
        cot.reshape(IMAGES_ROW, SLOTS, DEC_WIDTH), ((0, 0), (0, SLOT_PAD - SLOTS), (0, 0))
    ).reshape(IMAGES_ROW * SLOT_PAD, DEC_WIDTH)

    enc_weights = unpack(plan, ENC_LAYOUT, half, piece, ng, enc_places, enc_sources)
    saved = dict(
        zip(
            [SENT, H1, QKV, PROBS, ATT, MID, H2, ACT, SLOPE],
            encode(micro_rows, seg, enc_weights),
        )
    )
    dec_weights = unpack(plan, DEC_LAYOUT, half // 2, half, plan.full, dec_places, dec_sources, rest_weights)
    dec = dict(
        zip(
            [OUT, H1, QKV_L, ATT, PROJ_L, H2, UP_L, ACT,
             EMBED_L, GSENT, VECS, GPOS],
            decode(saved[SENT], seg, slot, cot_rows, dec_weights),
        )
    )
    dec_table = pack(
        DEC_LAYOUT,
        plan.dec_table,
        {
            EMBED_W: (saved[SENT], dec[EMBED_L]),
            QKV_W: (dec[H1], dec[QKV_L]),
            PROJ_W: (dec[ATT], dec[PROJ_L]),
            UP_W: (dec[H2], dec[UP_L]),
            DOWN_W: (dec[ACT], cot_rows),
        },
        dec[VECS],
        dec[GPOS],
    )
    in_grad, qkv_low, proj_low, up_low, enc_vec = encode_back(dec[GSENT], micro_rows, saved, enc_weights)
    enc_table = pack(
        ENC_LAYOUT,
        plan.enc_table,
        {
            DOWN_W: (saved[ACT], dec[GSENT]),
            UP_W: (saved[H2], up_low),
            PROJ_W: (saved[ATT], proj_low),
            QKV_W: (saved[H1], qkv_low),
        },
        enc_vec,
    )

    def add(first, *others):
        total = first.astype(f32)
        for other in others:
            total = total + other.astype(f32)
        return total.astype(bf16)

    def reduce(table, starts, length):
        part = length // 2

        def core_half(which):
            return jnp.stack([lax.dynamic_slice(table, (s + which * part, 0), (part, LANES)) for s in starts])

        held = add(core_half(core), over_core(core_half(1 - core)))
        size = part // (2 * ny)

        def owned_by(s, y):
            return lax.dynamic_slice(held, (0, (s * ny + y) * size, 0), (len(starts), size, LANES))

        if ny == 2:
            corner = owned_by(1 - sec, 1 - yy)
            corner_x = over_x(corner[:, : size // 2])
            corner_y = over_y(corner[:, size // 2 :])
            beside_y = owned_by(sec, 1 - yy)
            beside_x = owned_by(1 - sec, yy)
            send_y = jnp.concatenate([add(beside_y[:, : size // 2], corner_x), beside_y[:, size // 2 :]], axis=1)
            send_x = jnp.concatenate([beside_x[:, : size // 2], add(beside_x[:, size // 2 :], corner_y)], axis=1)
            mine = add(owned_by(sec, yy), over_x(send_x), over_y(send_y))
        else:
            column = lambda s: lax.dynamic_slice(held, (0, s * ny * size, 0), (len(starts), ny * size, LANES))
            own = add(column(sec), over_x(column(1 - sec)))
            block = lambda y: lax.dynamic_slice(own, (0, (y % ny) * size, 0), (len(starts), size, LANES))
            mine = block(yy - 1)
            for step in range(ny - 1):
                mine = add(block(yy - 2 - step), over_y(mine))
        one = lambda g: lax.dynamic_index_in_dim(mine, g % ng, 0, keepdims=False)
        total = one(grp - 1)
        for step in range(ng - 1):
            total = add(one(grp - 2 - step), over_z(total))
        return total

    dec_half_starts = [s + h * (room // 2) for s in plan.dec_starts for h in range(2)]
    dec_sum = reduce(dec_table, dec_half_starts, room // 2)
    dec_sums = [
        lax.ppermute(dec_sum, GRP, [(2 * z + h, z) for z in range(plan.full)]) for h in range(2)
    ]
    dec_own = jnp.concatenate(dec_sums)
    rest_sum = lax.psum(
        dec_table[plan.rest_start : plan.rest_start + plan.rest_room], (SEC, GRP, DP)
    )
    enc_own = reduce(enc_table, plan.enc_starts, room)
    own = jnp.where(first_section, enc_own, dec_own)
    other = over_x(jnp.where(first_section, dec_own, enc_own))
    pair = jnp.concatenate([own, other])
    column = [pair]
    for _ in range(ny - 1):
        column.append(over_y(column[-1]))
    sources = column + [over_core(c) for c in column]
    places = []
    for c in (core, 1 - core):
        for k in range(ny):
            for s in (sec, 1 - sec):
                number = (c * 2 + s) * ny + (yy - k) % ny
                places += [
                    jnp.where(first_section, 2 * number, number),
                    jnp.where(first_section, 2 * number + 1, plan.pieces + number),
                ]
    table = jnp.asarray(plan.segments())[sec, grp].reshape(-1)
    flat = finish(plan, jnp.stack(places).astype(jnp.int32), table, sources, rest_sum)
    param_grad = flat.reshape(-1)[: chunk * LANES].reshape(1, chunk * LANES)
    dec_out = dec[OUT].reshape(IMAGES_ROW, SLOT_PAD, DEC_WIDTH)[:, :SLOTS]
    return (
        dec_out.reshape(1, 1, IMAGES_ROW * SLOTS, DEC_WIDTH),
        in_grad.reshape(1, 1, ROW, WIDTH),
        param_grad,
    )


def solution(mesh):
    placed = (
        P(SEC, (GRP, DP), None, None),
        P(None, (GRP, DP), None),
        P(None, (GRP, DP), None),
        P(SEC, GRP),
        P(SEC, (GRP, DP), None, None),
    )
    return jax.shard_map(
        partial(per_device, Plan(dict(mesh.shape))),
        mesh=mesh,
        in_specs=placed,
        out_specs=(
            P(SEC, (GRP, DP), None, None),
            P(SEC, (GRP, DP), None, None),
            P(SEC, GRP),
        ),
        check_vma=False,
    )
```

```python
from functools import partial
import math

import jax
import jax.numpy as jnp
import numpy as np
from jax import lax
from jax.experimental import pallas as pl
from jax.experimental.pallas import tpu as pltpu
from jax.sharding import PartitionSpec as P

WIDTH = 768
HEADS = 12
HIDDEN_SIZE = 3072
DEC_WIDTH = 512
DEC_HEADS = 16
DEC_HIDDEN = 2048
SLOTS = 196
IMAGES_ROW = 5
ROW = 256
PARAMS = 7088128
LANES = 128
SEC, GRP, DP = "section", "group", "dp"
(
    N1G, N1B, QKV_W, QB, VB, PROJ_W, PB, N2G,
) = range(0, 8)
(
    N2B, UP_W, UB, DOWN_W, DB, EMBED_W, EB, MT,
) = range(8, 16)
(
    POS, QKV_B, VECS, SENT, H1, QKV, PROBS, ATT,
) = range(16, 24)
(
    MID, H2, ACT, SLOPE, OUT, QKV_L, PROJ_L, UP_L,
) = range(24, 32)
(
    EMBED_L, GSENT, GPOS,
) = range(32, 35)
SLOT_PAD = 208
VMEM_BYTES = 60 * 1024 * 1024

norm_eps = 1e-06
masked_score = -1000000000.0
f32 = jnp.float32
bf16 = jnp.bfloat16


def block_layout(width, hidden):
    return [
        (N1G, (width,)),
        (N1B, (width,)),
        (QKV_W, (width, 3 * width)),
        (QB, (width,)),
        (VB, (width,)),
        (PROJ_W, (width, width)),
        (PB, (width,)),
        (N2G, (width,)),
        (N2B, (width,)),
        (UP_W, (width, hidden)),
        (UB, (hidden,)),
        (DOWN_W, (hidden, width)),
        (DB, (width,)),
    ]


def decoder_layout(enc_width, width, hidden, slot_count):
    return [
        (EMBED_W, (enc_width, width)),
        (EB, (width,)),
        (MT, (width,)),
        (POS, (slot_count, width)),
    ] + block_layout(width, hidden)


ENC_LAYOUT = block_layout(WIDTH, HIDDEN_SIZE)
DEC_LAYOUT = decoder_layout(WIDTH, DEC_WIDTH, DEC_HIDDEN, SLOTS)
VEC = {
    N1G: 0,
    N1B: 1,
    QKV_B: 2,
    PB: 3,
    N2G: 4,
    N2B: 5,
    UB: 6,
    DB: 7,
    EB: 8,
    MT: 9,
}
VEC_ROWS = 16


def dot(a, b):
    return lax.dot_general(a, b, (((1,), (0,)), ((), ())), preferred_element_type=f32)


def dot_nt(a, b):
    return lax.dot_general(a, b, (((1,), (1,)), ((), ())), preferred_element_type=f32)


def dot_tn(a, b):
    return lax.dot_general(a, b, (((0,), (0,)), ((), ())), preferred_element_type=f32)


def normalised(values):
    centered = values - jnp.mean(values, axis=-1, keepdims=True)
    inverse = lax.rsqrt(jnp.mean(centered * centered, axis=-1, keepdims=True) + norm_eps)
    return centered * inverse, inverse


def norm_back(grad, hat, inverse, gain):
    scaled = grad * gain
    first = jnp.mean(scaled, axis=-1, keepdims=True)
    second = jnp.mean(scaled * hat, axis=-1, keepdims=True)
    return inverse * (scaled - first - hat * second)


def col_sum(values):
    return jnp.sum(values, axis=0, keepdims=True)


def gelu_parts(upward):
    half = 0.5 + 0.5 * lax.erf(upward * f32(math.sqrt(0.5)))
    slope = half + upward * (jnp.exp(upward * upward * f32(-0.5)) * f32(1.0 / math.sqrt(2.0 * math.pi)))
    return upward * half, slope


def head_mask(head, head_dim):
    lane = lax.broadcasted_iota(jnp.int32, (1, LANES), 1)
    return jnp.where(lane // head_dim == head, 1.0, 0.0).astype(bf16)


def lane_block(group, start=0):
    return pl.ds(pl.multiple_of(start + group * LANES, LANES), LANES)


def flip(values):
    return values.astype(f32).T.astype(bf16)


def attention_forward(qkv_ref, probs_ref, joined_ref, width, heads, keep):
    head_dim = width // heads
    scale = f32(head_dim ** (-0.5))
    per_group = LANES // head_dim

    def one_group(group, carry):
        queries = qkv_ref[:, lane_block(group)]
        keys = qkv_ref[:, lane_block(group, width)]
        values_t = flip(qkv_ref[:, lane_block(group, 2 * width)])
        for sub in range(per_group):
            scores = dot_nt(keys, queries * head_mask(sub, head_dim)) * scale
            scores = keep(scores)
            expo = jnp.exp(scores - jnp.max(scores, axis=0, keepdims=True))
            probs = expo * (1.0 / col_sum(expo))
            probs_ref[group * per_group + sub] = probs
            rows = pl.ds(pl.multiple_of(group * LANES + sub * head_dim, head_dim), head_dim)
            joined_ref[rows, :] = dot(
                values_t[sub * head_dim : (sub + 1) * head_dim], probs.astype(bf16)
            )
        return carry

    lax.fori_loop(0, width // LANES, one_group, 0)


def attention_backward(qkv_ref, probs_ref, grad_ref, low_ref, width, heads):
    head_dim = width // heads
    scale = f32(head_dim ** (-0.5))
    per_group = LANES // head_dim

    def one_group(group, carry):
        queries = qkv_ref[:, lane_block(group)]
        keys = qkv_ref[:, lane_block(group, width)]
        values = qkv_ref[:, lane_block(group, 2 * width)]
        grads = grad_ref[:, lane_block(group)]
        keys_t = flip(keys)
        grad_values = jnp.zeros(values.shape, f32)
        grad_keys = jnp.zeros(values.shape, f32)
        grad_queries = []
        for sub in range(per_group):
            mask = head_mask(sub, head_dim)
            probs = probs_ref[group * per_group + sub]
            own = grads * mask
            grad_values += dot(probs.astype(bf16), own)
            grad_probs = dot_nt(values, own)
            delta = col_sum(probs * grad_probs)
            low = (probs * (grad_probs - delta)).astype(bf16)
            grad_keys += dot(low, queries * mask)
            grad_queries.append(dot(keys_t[sub * head_dim : (sub + 1) * head_dim], low))
        low_ref[:, lane_block(group)] = (jnp.concatenate(grad_queries, axis=0).T * scale).astype(bf16)
        low_ref[:, lane_block(group, width)] = (grad_keys * scale).astype(bf16)
        low_ref[:, lane_block(group, 2 * width)] = grad_values.astype(bf16)
        return carry

    lax.fori_loop(0, width // LANES, one_group, 0)


def encode_kernel(
    x_ref, seg_row_ref, seg_col_ref, qkv_w, proj_w, up_w, down_w, vec,
    sent_ref, normed1_ref, qkv_ref, probs_ref, attended_ref, middle_ref, normed2_ref, active_ref,
    slope_ref, joined_ref,
):
    width, hidden = WIDTH, HIDDEN_SIZE
    inputs = x_ref[...].astype(f32)
    hat, _ = normalised(inputs)
    normed1 = (hat * vec[0:1, :width] + vec[1:2, :width]).astype(bf16)
    normed1_ref[...] = normed1
    qkv_ref[...] = (dot(normed1, qkv_w[...]) + vec[2:3, : 3 * width]).astype(bf16)
    allowed = seg_col_ref[...] == seg_row_ref[...]
    attention_forward(
        qkv_ref, probs_ref, joined_ref, width, HEADS,
        lambda scores: jnp.where(allowed, scores, f32(masked_score)),
    )
    attended = joined_ref[...].T.astype(bf16)
    attended_ref[...] = attended
    middle = inputs + (dot(attended, proj_w[...]) + vec[3:4, :width])
    middle_ref[...] = middle
    hat, _ = normalised(middle)
    normed2_ref[...] = (hat * vec[4:5, :width] + vec[5:6, :width]).astype(bf16)
    joined_ref[...] = jnp.zeros_like(joined_ref)
    total = jnp.zeros((inputs.shape[0], width), f32)
    part = 512
    for start in range(0, hidden, part):
        cols = slice(start, start + part)
        upward = dot(normed2_ref[...], up_w[:, cols]) + vec[6:7, cols]
        active, slope = gelu_parts(upward)
        active_ref[:, cols] = active.astype(bf16)
        slope_ref[:, cols] = slope.astype(slope_ref.dtype)
        total += dot(active_ref[:, cols], down_w[cols, :])
    sent_ref[...] = (middle + (total + vec[7:8, :width])).astype(bf16)


def mlp_back_kernel(
    grad_ref, middle_ref, slope_ref, up_w, down_w, vec,
    up_low_ref, proj_low_ref, grad_middle_ref, vec_grad,
):
    width, hidden = WIDTH, HIDDEN_SIZE
    grad_out = grad_ref[...]
    vec_grad[...] = jnp.zeros_like(vec_grad)
    vec_grad[7:8, :width] = col_sum(grad_out.astype(f32))
    grad_normed2 = jnp.zeros((grad_out.shape[0], width), f32)
    part = 512
    for start in range(0, hidden, part):
        cols = slice(start, start + part)
        low = (dot_nt(grad_out, down_w[cols, :]) * slope_ref[:, cols]).astype(bf16)
        up_low_ref[:, cols] = low
        vec_grad[6:7, cols] = col_sum(low.astype(f32))
        grad_normed2 += dot_nt(low, up_w[:, cols])
    hat, inverse = normalised(middle_ref[...])
    vec_grad[4:5, :width] = col_sum(grad_normed2 * hat)
    vec_grad[5:6, :width] = col_sum(grad_normed2)
    grad_middle = grad_out.astype(f32) + norm_back(grad_normed2, hat, inverse, vec[4:5, :width])
    grad_middle_ref[...] = grad_middle
    proj_low = grad_middle.astype(bf16)
    proj_low_ref[...] = proj_low
    vec_grad[3:4, :width] = col_sum(proj_low.astype(f32))


def attention_back_kernel(
    grad_middle_ref, proj_low_ref, x_ref, qkv_ref, probs_ref, qkv_w, proj_w, vec, vec_in,
    in_grad_ref, qkv_low_ref, vec_grad, grad_att_ref,
):
    width = WIDTH
    vec_grad[...] = vec_in[...]
    grad_att_ref[...] = dot_nt(proj_low_ref[...], proj_w[...]).astype(bf16)
    attention_backward(qkv_ref, probs_ref, grad_att_ref, qkv_low_ref, width, HEADS)
    qkv_low = qkv_low_ref[...]
    vec_grad[2:3, : 3 * width] = col_sum(qkv_low.astype(f32))
    grad_normed1 = dot_nt(qkv_low, qkv_w[...])
    hat, inverse = normalised(x_ref[...].astype(f32))
    vec_grad[0:1, :width] = col_sum(grad_normed1 * hat)
    vec_grad[1:2, :width] = col_sum(grad_normed1)
    in_grad_ref[...] = grad_middle_ref[...] + norm_back(grad_normed1, hat, inverse, vec[0:1, :width])


def decode_kernel(
    sent_ref, embed_w, qkv_w, proj_w, up_w, down_w, vec, pos_ref,
    seg_row, slot_row, seg_col, slot_col, cot_ref,
    out_ref, normed1_ref, qkv_low_ref, attended_ref, proj_low_ref, normed2_ref, up_low_ref,
    active_ref, embed_low_ref, grad_sent_ref, vec_grad, pos_grad,
    embedded_ref, embed_sum, qkv_ref, probs_ref, joined_ref, grad_att_ref,
):
    width, hidden = DEC_WIDTH, DEC_HIDDEN
    image = pl.program_id(0)
    length = SLOT_PAD

    @pl.when(image == 0)
    def _():
        embedded_ref[...] = (dot(sent_ref[...], embed_w[...]) + vec[8:9, :width]).astype(bf16)
        vec_grad[...] = jnp.zeros_like(vec_grad)
        pos_grad[...] = jnp.zeros_like(pos_grad)
        embed_sum[...] = jnp.zeros_like(embed_sum)

    def add_vec(row, values):
        vec_grad[row : row + 1, : values.shape[1]] += values

    place = lax.broadcasted_iota(jnp.int32, (length, ROW), 0)
    match = (seg_row[...] == image) & (slot_row[...] == place)
    onehot = jnp.where(match, 1.0, 0.0)
    free = 1.0 - jnp.sum(onehot, axis=1, keepdims=True)
    x = dot(onehot.astype(bf16), embedded_ref[...]) + free * vec[9:10, :width] + pos_ref[...].astype(f32)
    hat1, inverse1 = normalised(x)
    normed1 = (hat1 * vec[0:1, :width] + vec[1:2, :width]).astype(bf16)
    normed1_ref[...] = normed1
    qkv_ref[...] = (dot(normed1, qkv_w[...]) + vec[2:3, : 3 * width]).astype(bf16)
    key_place = lax.broadcasted_iota(jnp.int32, (length, length), 0)
    attention_forward(
        qkv_ref, probs_ref, joined_ref, width, DEC_HEADS,
        lambda scores: jnp.where(key_place < SLOTS, scores, f32(-1e30)),
    )
    attended = joined_ref[...].T.astype(bf16)
    attended_ref[...] = attended
    middle = x + (dot(attended, proj_w[...]) + vec[3:4, :width])
    hat2, inverse2 = normalised(middle)
    normed2 = (hat2 * vec[4:5, :width] + vec[5:6, :width]).astype(bf16)
    normed2_ref[...] = normed2
    cot = cot_ref[...]
    add_vec(7, col_sum(cot.astype(f32)))
    total = jnp.zeros((length, width), f32)
    grad_normed2 = jnp.zeros((length, width), f32)
    part = 512
    for start in range(0, hidden, part):
        cols = slice(start, start + part)
        upward = dot(normed2_ref[...], up_w[:, cols]) + vec[6:7, cols]
        active, slope = gelu_parts(upward)
        active = active.astype(bf16)
        active_ref[:, cols] = active
        total += dot(active, down_w[cols, :])
        low = (dot_nt(cot_ref[...], down_w[cols, :]) * slope).astype(bf16)
        up_low_ref[:, cols] = low
        vec_grad[6:7, cols] += col_sum(low.astype(f32))
        grad_normed2 += dot_nt(low, up_w[:, cols])
    out_ref[...] = (middle + (total + vec[7:8, :width])).astype(bf16)

    add_vec(4, col_sum(grad_normed2 * hat2))
    add_vec(5, col_sum(grad_normed2))
    grad_middle = cot.astype(f32) + norm_back(grad_normed2, hat2, inverse2, vec[4:5, :width])
    proj_low = grad_middle.astype(bf16)
    proj_low_ref[...] = proj_low
    add_vec(3, col_sum(proj_low.astype(f32)))
    grad_att_ref[...] = dot_nt(proj_low, proj_w[...]).astype(bf16)
    attention_backward(qkv_ref, probs_ref, grad_att_ref, qkv_low_ref, width, DEC_HEADS)
    qkv_low = qkv_low_ref[...]
    add_vec(2, col_sum(qkv_low.astype(f32)))
    grad_normed1 = dot_nt(qkv_low, qkv_w[...])
    add_vec(0, col_sum(grad_normed1 * hat1))
    add_vec(1, col_sum(grad_normed1))
    grad_in = grad_middle + norm_back(grad_normed1, hat1, inverse1, vec[0:1, :width])
    low_in = grad_in.astype(bf16)
    wide = low_in.astype(f32)
    add_vec(9, col_sum(free * wide))
    pos_grad[...] += wide
    place_t = lax.broadcasted_iota(jnp.int32, (ROW, length), 1)
    match_t = (seg_col[...] == image) & (slot_col[...] == place_t)
    embed_sum[...] += dot(jnp.where(match_t, 1.0, 0.0).astype(bf16), low_in)

    @pl.when(image == IMAGES_ROW - 1)
    def _():
        embed_low = embed_sum[...].astype(bf16)
        embed_low_ref[...] = embed_low
        add_vec(8, col_sum(embed_low.astype(f32)))
        grad_sent_ref[...] = dot_nt(embed_low, embed_w[...]).astype(bf16)


def cost(microseconds):
    return pl.CostEstimate(flops=int(microseconds * 1e9), bytes_accessed=0, transcendentals=0)


def params_of(**extra):
    return pltpu.CompilerParams(vmem_limit_bytes=VMEM_BYTES, **extra)


def shape(dims, kind):
    return jax.ShapeDtypeStruct(dims, kind)


def encode(x, seg, weights):
    width, hidden, length = WIDTH, HIDDEN_SIZE, ROW
    names = [QKV_W, PROJ_W, UP_W, DOWN_W, VECS]
    return pl.pallas_call(
        encode_kernel,
        out_shape=[
            shape((length, width), bf16),
            shape((length, width), bf16),
            shape((length, 3 * width), bf16),
            shape((HEADS, length, length), f32),
            shape((length, width), bf16),
            shape((length, width), f32),
            shape((length, width), bf16),
            shape((length, hidden), bf16),
            shape((length, hidden), bf16),
        ],
        scratch_shapes=[pltpu.VMEM((width, length), f32)],
        compiler_params=params_of(),
        cost_estimate=cost(18),
        name="encode",
    )(x, seg.reshape(1, length), seg.reshape(length, 1), *[weights[n] for n in names])


def mlp_back(grad, saved, weights):
    width, hidden, length = WIDTH, HIDDEN_SIZE, ROW
    return pl.pallas_call(
        mlp_back_kernel,
        out_shape=[
            shape((length, hidden), bf16),
            shape((length, width), bf16),
            shape((length, width), f32),
            shape((VEC_ROWS, hidden), f32),
        ],
        compiler_params=params_of(),
        cost_estimate=cost(9),
        name="mlp_back",
    )(grad, saved[MID], saved[SLOPE], weights[UP_W], weights[DOWN_W], weights[VECS])


def attention_back(grad_middle, proj_low, x, saved, weights, vec_grad):
    width, hidden, length = WIDTH, HIDDEN_SIZE, ROW
    return pl.pallas_call(
        attention_back_kernel,
        out_shape=[
            shape((length, width), f32),
            shape((length, 3 * width), bf16),
            shape((VEC_ROWS, hidden), f32),
        ],
        scratch_shapes=[pltpu.VMEM((length, width), bf16)],
        compiler_params=params_of(),
        cost_estimate=cost(10),
        name="attention_back",
    )(
        grad_middle, proj_low, x, saved[QKV], saved[PROBS],
        weights[QKV_W], weights[PROJ_W], weights[VECS], vec_grad,
    )


def decode(sent, seg, slot, cot, weights):
    width, hidden, length = DEC_WIDTH, DEC_HIDDEN, SLOT_PAD
    names = [EMBED_W, QKV_W, PROJ_W, UP_W, DOWN_W, VECS, POS]
    held = [sent] + [weights[n] for n in names]
    held += [seg.reshape(1, ROW), slot.reshape(1, ROW), seg.reshape(ROW, 1), slot.reshape(ROW, 1)]

    def whole(array):
        return pl.BlockSpec(array.shape, lambda i: (0,) * array.ndim, pipeline_mode=pl.Buffered(1))

    def image(cols):
        return pl.BlockSpec((length, cols), lambda i: (i, 0))

    rows = IMAGES_ROW * length
    per_image = [width, width, 3 * width, width, width, width, hidden, hidden]
    kept = [
        shape((ROW, width), bf16),
        shape((ROW, WIDTH), bf16),
        shape((VEC_ROWS, hidden), f32),
        shape((length, width), f32),
    ]
    return pl.pallas_call(
        decode_kernel,
        grid=(IMAGES_ROW,),
        in_specs=[whole(a) for a in held] + [image(width)],
        out_specs=[image(c) for c in per_image]
        + [pl.BlockSpec(s.shape, lambda i: (0, 0)) for s in kept],
        out_shape=[shape((rows, c), bf16) for c in per_image] + kept,
        scratch_shapes=[
            pltpu.VMEM((ROW, width), bf16),
            pltpu.VMEM((ROW, width), f32),
            pltpu.VMEM((length, 3 * width), bf16),
            pltpu.VMEM((DEC_HEADS, length, length), f32),
            pltpu.VMEM((width, length), f32),
            pltpu.VMEM((length, width), bf16),
        ],
        compiler_params=params_of(dimension_semantics=("arbitrary",)),
        cost_estimate=cost(85),
        name="decode",
    )(*held, cot)


def rows_of(extent):
    return math.prod(extent) // LANES


def up_to(value, step):
    return -(-value // step) * step


def flat_starts(layout):
    starts, here = {}, 0
    for name, extent in layout:
        starts[name] = here
        here += rows_of(extent)
    return starts, here


def kept_starts(layout):
    starts, here = {}, 0
    for name, extent in layout:
        starts[name] = here
        here += up_to(rows_of(extent), 16)
    return starts, here


class Plan:
    def __init__(self, mesh_shape):
        self.ns, self.ng, self.nd = (mesh_shape[a] for a in (SEC, GRP, DP))
        self.ny = self.nd // 2
        self.chunk = PARAMS // LANES // self.ng
        self.pieces = self.ns * self.nd
        self.piece = up_to(-(-self.chunk // self.pieces), 64)
        self.half = self.piece // 2
        self.room = self.piece * self.pieces
        self.full = self.ng // 2
        self.rest = flat_starts(DEC_LAYOUT)[1] - self.full * self.chunk
        assert 0 < self.rest <= self.chunk
        whole = self.chunk // self.half * self.half
        last_piece_used = whole == self.room - self.half
        free = self.half - (self.chunk - whole) if last_piece_used else self.half
        self.part_in = free // 16 * 16
        self.parts_in = -(-self.rest // self.part_in)
        assert self.parts_in <= self.full
        self.enc_starts = [self.kept_row(ENC_LAYOUT, z * self.chunk) // 16 * 16 for z in range(self.ng)]
        self.enc_ends = [
            up_to(self.kept_row(ENC_LAYOUT, min((z + 1) * self.chunk, flat_starts(ENC_LAYOUT)[1]) - 1) + 1, 16)
            for z in range(self.ng)
        ]
        self.dec_starts = [self.kept_row(DEC_LAYOUT, z * self.chunk) // 16 * 16 for z in range(self.full)]
        self.dec_ends = [
            up_to(self.kept_row(DEC_LAYOUT, (z + 1) * self.chunk - 1) + 1, 16) for z in range(self.full)
        ]
        assert all(e - s <= self.room for s, e in zip(self.enc_starts, self.enc_ends))
        self.rest_start = self.kept_row(DEC_LAYOUT, self.full * self.chunk) // 16 * 16
        self.rest_end = kept_starts(DEC_LAYOUT)[1]
        self.part_out = [self.room - (self.dec_ends[k] - self.dec_starts[k]) for k in range(2)]
        assert max(self.part_out) <= self.room // 2
        assert self.part_out[0] < self.rest_end - self.rest_start <= sum(self.part_out)

    def kept_row(self, layout, flat_row):
        flat, _ = flat_starts(layout)
        kept, _ = kept_starts(layout)
        for name, extent in layout:
            if flat_row < flat[name] + rows_of(extent):
                return kept[name] + flat_row - flat[name]
        return kept[name] + rows_of(extent)

    def ranges(self, first, count, cut, chunks):
        found = []
        whole = self.chunk // cut * cut
        while count:
            z, row = divmod(first, self.chunk)
            if z >= chunks:
                k, row = divmod(row, self.part_in)
                here, room = (k + 1) * self.room - self.half + row, self.part_in - row
            elif row < whole:
                here, room = z * self.room + row, whole - row
            else:
                here, room = z * self.room + row + cut - (self.chunk - whole), self.chunk - row
            take = min(count, room)
            found.append((here, take))
            first, count = first + take, count - take
        return found

    def enc_regions(self, groups):
        return [(self.enc_starts[z], self.enc_ends[z], k, 0) for k, z in enumerate(groups)]

    def dec_regions(self):
        length = self.room // 2
        found = []
        for z in range(self.full):
            low, high = self.dec_starts[z], self.dec_ends[z]
            found += [(low, low + length, 2 * z, 0), (low + length, high, 2 * z + 1, 0)]
        middle = self.rest_start + self.part_out[0]
        found.append((self.rest_start, middle, 1, length - self.part_out[0]))
        found.append((middle, self.rest_end, 3, length - self.part_out[1]))
        return found

    def segments(self):
        count = len(DEC_LAYOUT) + 2
        table = np.zeros((self.ns, self.ng, count, 3), np.int32)
        length = self.room // 2
        for s, layout in enumerate((ENC_LAYOUT, DEC_LAYOUT)):
            flat, used = flat_starts(layout)
            for z in range(self.ng):
                low, high = z * self.chunk, (z + 1) * self.chunk
                found = []
                for name, extent in layout:
                    first, last = max(flat[name], low), min(flat[name] + rows_of(extent), high)
                    while first < last:
                        row, stop = self.kept_row(layout, first), last
                        if s == 0:
                            source = row - self.enc_starts[z]
                        elif z < self.full:
                            source = row - self.dec_starts[z]
                        else:
                            row -= self.rest_start
                            k = int(row >= self.part_out[0])
                            row -= k * self.part_out[0]
                            source = (k + 1) * length - self.part_out[k] + row
                            stop = min(last, first + self.part_out[k] - row)
                        found.append((source, first - low, -(-(stop - first) // 8)))
                        first = stop
                if used < high:
                    found.append((self.room, max(used - low, 0), 1))
                table[s, z, : len(found)] = found
        return table


def widen_block(held, wide, spare, ranges):
    def load(start, count):
        first = start // 16 * 16
        size = up_to(start + count - first, 16)
        return held[first : first + size, :].astype(f32), size, start - first

    if len(ranges) == 1:
        block, size, skip = load(*ranges[0])
        wide[0:size, :] = block
        return skip
    here = 0
    for start, count in ranges:
        block, size, skip = load(start, count)
        spare[0:size, :] = block
        wide[here : here + count, :] = spare[skip : skip + count, :]
        here += count
    return 0


def unpack_kernel(plan, layout, unit, cut, chunks, counts, place_ref, *refs):
    sources = refs[: len(counts)]
    refs = refs[len(counts) :]
    matrices = [(n, e) for n, e in layout if len(e) == 2]
    outs, vec = refs[: len(matrices)], refs[len(matrices)]
    held, wide, spare, sems = refs[len(matrices) + 1 :]
    per_chunk = plan.room // unit
    number = 0
    for source, count in zip(sources, counts):
        for k in range(count):
            slot = place_ref[number]
            number += 1
            target = held.at[pl.ds(pl.multiple_of(slot * unit, 16), unit), :]
            pltpu.make_async_copy(source.at[pl.ds(k * unit, unit), :], target, sems.at[slot // per_chunk]).start()
    arrived = set()

    def arrive(ranges):
        for start, count in ranges:
            z = start // plan.room
            if z not in arrived:
                arrived.add(z)
                part = held.at[pl.ds(z * plan.room, plan.room), :]
                pltpu.make_async_copy(part, part, sems.at[z]).wait()

    vec[...] = jnp.zeros_like(vec)
    flat, _ = flat_starts(layout)
    by_name = dict(zip([n for n, _ in matrices], outs))
    for name, extent in layout:
        if len(extent) == 2:
            depth, lanes = extent[0], extent[1] // LANES
            step = depth if name == POS else max(128, 2048 // lanes // 128 * 128)
            out = by_name[name]
            if name == POS:
                out[...] = jnp.zeros_like(out)
            for first in range(0, depth, step):
                size = min(step, depth - first)
                ranges = plan.ranges(flat[name] + first * lanes, size * lanes, cut, chunks)
                arrive(ranges)
                skip = widen_block(held, wide, spare, ranges)
                for j in range(lanes):
                    block = wide[pl.ds(skip + j, size, stride=lanes), :].astype(bf16)
                    out[first : first + size, j * LANES : (j + 1) * LANES] = block
        else:
            lanes = extent[0] // LANES
            ranges = plan.ranges(flat[name], lanes, cut, chunks)
            arrive(ranges)
            skip = widen_block(held, wide, spare, ranges)
            row, shift = {QB: (2, 0), VB: (2, 2 * extent[0])}.get(name, (VEC.get(name), 0))
            for j in range(lanes):
                vec[row : row + 1, shift + j * LANES : shift + (j + 1) * LANES] = wide[skip + j : skip + j + 1, :]
    for z in range(chunks):
        arrive([(z * plan.room, 1)])


def unpack(plan, layout, unit, cut, chunks, place, sources):
    matrices = [(n, e) for n, e in layout if len(e) == 2]
    outs = [
        shape((SLOT_PAD if n == POS else e[0], e[1]), bf16) for n, e in matrices
    ] + [shape((VEC_ROWS, 4 * dict(layout)[PB][0]), f32)]
    operands = list(sources)
    rows = chunks * plan.room
    result = pl.pallas_call(
        partial(unpack_kernel, plan, layout, unit, cut, chunks, [s.shape[0] // unit for s in sources]),
        in_specs=[pl.BlockSpec(memory_space=pltpu.SMEM)]
        + [pl.BlockSpec(memory_space=pl.ANY)] * len(operands),
        out_shape=outs,
        scratch_shapes=[
            pltpu.VMEM((rows, LANES), bf16),
            pltpu.VMEM((3200, LANES), f32),
            pltpu.VMEM((3200, LANES), f32),
            pltpu.SemaphoreType.DMA((chunks,)),
        ],
        compiler_params=params_of(),
        cost_estimate=cost(12),
        name="unpack",
    )(place, *operands)
    return dict(zip([n for n, _ in matrices] + [VECS], result))


def pack_kernel(plan, layout, names, regions, size, groups, place_ref, *refs):
    pairs = {}
    for name in names:
        pairs[name], refs = refs[:2], refs[2:]
    vec, refs = refs[0], refs[1:]
    pos = None
    if POS in names:
        pos, refs = pairs[POS][0], refs
    mine, theirs, wide, stage, small, sems = refs
    kept, _ = kept_starts(layout)
    extents = dict(layout)
    ny = plan.ny

    def send(source, first, rows, sem):
        moved = 0
        for low, high, index, base in regions:
            start, stop = max(first, low), min(first + rows, high)
            while start < stop:
                number, row = divmod(base + start - low, size)
                count = min(stop - start, size - row)
                c, s, y = number // (2 * ny), number // ny % 2, number % ny
                owner = lax.rem(s - place_ref[0] + 2, 2) * ny + lax.rem(y - place_ref[1] + ny, ny)
                target = pl.ds(pl.multiple_of(owner * (groups * size), 16) + index * size + row, count)
                block = source.at[pl.ds(start - first, count), :]
                for same, table in ((True, mine), (False, theirs)):

                    @pl.when((place_ref[2] == c) == same)
                    def _():
                        pltpu.make_async_copy(block, table.at[target, :], sem).start()

                moved += count
                start += count
        return moved

    def wait(rows, slot):
        if rows:
            block = stage.at[slot, pl.ds(0, rows), :]
            pltpu.make_async_copy(block, block, sems.at[slot]).wait()

    turn = 0
    pending = [0, 0]
    for name in names:
        if name == POS:
            continue
        left, right = pairs[name]
        depth, width = extents[name]
        lanes = width // LANES
        step = max(k for k in (128, 256, 384, 512) if depth % k == 0 and k * lanes <= 3072)
        rows = step * lanes
        for first in range(0, depth, step):
            start = kept[name] + first * lanes
            if all(start >= high or start + rows <= low for low, high, _, _ in regions):
                continue
            slot = turn % 2
            turn += 1
            columns = flip(left[:, first : first + step])
            part = 256
            for start in range(0, width, part):
                block = dot(columns, right[:, start : start + part])
                for j in range(part // LANES):
                    wide[pl.ds(start // LANES + j, step, stride=lanes), :] = block[:, j * LANES : (j + 1) * LANES]
            wait(pending[slot], slot)
            stage[slot, 0:rows, :] = wide[0:rows, :].astype(bf16)
            pending[slot] = send(stage.at[slot], kept[name] + first * lanes, rows, sems.at[slot])
    here = 0
    total = 0
    for name, extent in layout:
        if name not in names and len(extent) == 2 or name not in kept_names(names):
            continue
        if len(extent) == 2 and name != POS:
            continue
        rows = rows_of(extent)
        room = up_to(rows, 16)
        wide[0:room, :] = jnp.zeros((room, LANES), f32)
        if name == POS:
            lanes = extent[1] // LANES
            for j in range(lanes):
                wide[pl.ds(j, extent[0], stride=lanes), :] = pos[0 : extent[0], j * LANES : (j + 1) * LANES]
        else:
            row, shift = {QB: (2, 0), VB: (2, 2 * extent[0])}.get(name, (VEC.get(name), 0))
            for j in range(rows):
                wide[j : j + 1, :] = vec[row : row + 1, shift + j * LANES : shift + (j + 1) * LANES]
        small[here : here + room, :] = wide[0:room, :].astype(bf16)
        total += send(small.at[pl.ds(here, room), :], kept[name], room, sems.at[2])
        here += room
    wait(pending[0], 0)
    wait(pending[1], 1)
    block = small.at[pl.ds(0, total), :]
    pltpu.make_async_copy(block, block, sems.at[2]).wait()


def kept_names(names):
    with_matrix = {
        QKV_W: [N1G, N1B, QB, VB],
        PROJ_W: [PB, N2G, N2B],
        UP_W: [UB],
        DOWN_W: [DB],
        EMBED_W: [EB, MT],
        POS: [POS],
    }
    return [v for n in names for v in with_matrix[n]]


def pack(plan, layout, regions, size, groups, place, pairs, vec):
    names = list(pairs)
    operands = [a for name in names for a in pairs[name]] + [vec]
    extents = dict(layout)
    small = sum(up_to(rows_of(extents[n]), 16) for n in kept_names(names))
    rows = 2 * plan.ny * groups * size
    return pl.pallas_call(
        partial(pack_kernel, plan, layout, names, regions, size, groups),
        in_specs=[pl.BlockSpec(memory_space=pltpu.SMEM)]
        + [pl.BlockSpec(memory_space=pltpu.VMEM)] * len(operands),
        out_specs=[pl.BlockSpec(memory_space=pl.ANY)] * 2,
        out_shape=[shape((rows, LANES), bf16)] * 2,
        scratch_shapes=[
            pltpu.VMEM((3072, LANES), f32),
            pltpu.VMEM((2, 3072 + 64, LANES), bf16),
            pltpu.VMEM((small + 64, LANES), bf16),
            pltpu.SemaphoreType.DMA((3,)),
        ],
        compiler_params=params_of(),
        cost_estimate=cost(25 if EMBED_W in names else 12),
        name="pack",
    )(place, *operands)


def finish_kernel(plan, counts, place_ref, seg_ref, *refs):
    sources, result, held, wide, out, sem = refs[: len(counts)], *refs[len(counts) :]
    unit = plan.half
    number = 0
    for source, count in zip(sources, counts):
        for k in range(count):
            target = held.at[pl.ds(pl.multiple_of(place_ref[number] * unit, 16), unit), :]
            number += 1
            pltpu.make_async_copy(source.at[pl.ds(k * unit, unit), :], target, sem.at[0]).start()
    out[...] = jnp.zeros_like(out)
    pltpu.make_async_copy(held, held, sem.at[0]).wait()
    total = plan.room
    wide[total : total + 16, :] = jnp.zeros((16, LANES), f32)
    wide[0:total, :] = held[...].astype(f32)

    def one(k, carry):
        source, first, steps = seg_ref[3 * k], seg_ref[3 * k + 1], seg_ref[3 * k + 2]

        def step(i, carry):
            out[pl.ds(first + 8 * i, 8), :] = wide[pl.ds(source + 8 * i, 8), :]
            return carry

        def steps8(i, carry):
            out[pl.ds(first + 64 * i, 64), :] = wide[pl.ds(source + 64 * i, 64), :]
            return carry

        many = steps // 8
        lax.fori_loop(0, many, steps8, 0)
        return lax.fori_loop(many * 8, steps, step, carry)

    lax.fori_loop(0, seg_ref.shape[0] // 3, one, 0)
    rows = up_to(plan.chunk, 8)
    lines = out.at[pl.ds(0, rows), :].reshape(rows, 1, LANES)
    copy = pltpu.make_async_copy(lines.at[pl.ds(0, plan.chunk)], result, sem.at[0])
    copy.start()
    copy.wait()


def finish(plan, place, segments, sources):
    total = plan.room
    return pl.pallas_call(
        partial(finish_kernel, plan, [s.shape[0] // plan.half for s in sources]),
        in_specs=[pl.BlockSpec(memory_space=pltpu.SMEM)] * 2
        + [pl.BlockSpec(memory_space=pl.ANY)] * len(sources),
        out_specs=pl.BlockSpec(memory_space=pl.ANY),
        out_shape=shape((plan.chunk, 1, LANES), f32),
        scratch_shapes=[
            pltpu.VMEM((total, LANES), bf16),
            pltpu.VMEM((total + 16, LANES), f32),
            pltpu.VMEM((up_to(plan.chunk, 8) + 8, LANES), f32),
            pltpu.SemaphoreType.DMA((1,)),
        ],
        compiler_params=params_of(),
        cost_estimate=cost(8),
        name="finish",
    )(place, segments, *sources)


def after(values, *before):
    return lax.optimization_barrier((values, before))[0]


def per_device(plan, enc_input, segments, slots, params, cot):
    ns, ng, nd, ny = plan.ns, plan.ng, plan.nd, plan.ny
    piece, half, room, chunk = plan.piece, plan.half, plan.room, plan.chunk
    sec = lax.axis_index(SEC)
    grp = lax.axis_index(GRP)
    dp = lax.axis_index(DP)
    yy, core = dp // 2, dp % 2
    first_section = sec == 0

    def over_x(block):
        return lax.ppermute(block, SEC, [(0, 1), (1, 0)])

    def over_core(block):
        return lax.ppermute(block, DP, [(d, d ^ 1) for d in range(nd)])

    def over_y(block):
        return lax.ppermute(block, DP, [(d, (d + 2) % nd) for d in range(nd)])

    def over_z(block, senders=None):
        senders = range(ng) if senders is None else senders
        return lax.ppermute(block, GRP, [(g, (g + 1) % ng) for g in senders])

    def share(start):
        cut = lax.dynamic_slice(params, (0, start * LANES), (1, half * LANES))
        return cut.astype(f32).reshape(half, LANES).astype(bf16)

    def shares(section):
        number = section * nd + dp
        enc_first = jnp.minimum(number * piece, chunk - piece)
        dec_first = [jnp.minimum((h * plan.pieces + number) * half, chunk - half) for h in range(2)]
        starts = [
            jnp.where(first_section, enc_first, dec_first[0]),
            jnp.where(first_section, enc_first + half, dec_first[1]),
        ]
        return jnp.concatenate([share(s) for s in starts])

    send = shares(1 - sec)
    got = over_x(send)
    keep = shares(sec)
    rest = params[:, : plan.part_in * plan.parts_in * LANES].astype(f32).reshape(-1, LANES).astype(bf16)
    enc_piece = jnp.where(first_section, keep, got)
    dec_pieces = jnp.where(first_section, got, keep)

    def gather(parts, first, wait_for=()):
        here = jnp.concatenate(parts) if len(parts) > 1 else parts[0]
        here = after(here, *wait_for)
        size = here.shape[0]
        if ny == 2:
            from_x, from_y = over_x(here), over_y(here)
            corner_0 = over_y(from_x[: size // 2])
            corner_1 = over_x(from_y[size // 2 :])
            sources = [here, from_x, from_y, corner_0, corner_1]
            owners = [(sec, yy), (1 - sec, yy), (sec, 1 - yy), (1 - sec, 1 - yy)]
            early, late = (from_x, from_y), (corner_0, corner_1)
        else:
            column = [here]
            for _ in range(ny - 1):
                column.append(over_y(column[-1]))
            sources = column + [over_x(block) for block in column]
            owners = [(s, (yy - k) % ny) for s in (sec, 1 - sec) for k in range(ny)]
            early, late = (column[1],), (sources[-1],)
        sources = sources + [over_core(block) for block in sources]
        places = []
        for c in (core, 1 - core):
            for s, y in owners:
                for k in range(len(parts)):
                    number = (grp - first - k) % ng * plan.pieces + s * nd + y * 2 + c
                    places += [2 * number, 2 * number + 1]
        return sources, jnp.stack(places).astype(jnp.int32), early, late

    near = ng // 2
    enc_parts = [enc_piece]
    for _ in range(near - 1):
        enc_parts.append(over_z(enc_parts[-1]))
    sources_0, places_0, early_0, late_0 = gather(enc_parts[:near], 0)
    enc_parts.append(over_z(enc_parts[-1]))
    enc_parts[-1] = after(enc_parts[-1], *early_0)
    for _ in range(ng - near - 1):
        enc_parts.append(over_z(enc_parts[-1]))
    sources_1, places_1, early_1, late_1 = gather(enc_parts[near:], near, late_0)
    enc_sources, enc_places = sources_0 + sources_1, jnp.concatenate([places_0, places_1])

    dec_pieces, rest = after((dec_pieces, rest), enc_parts[-1])
    spread = [
        lax.ppermute(dec_pieces[h * half : (h + 1) * half], GRP, [(z, 2 * z + h) for z in range(plan.full)])
        for h in range(2)
    ]
    dec_piece = jnp.where(grp % 2 == 0, spread[0], spread[1])
    last = jnp.logical_and(sec == ns - 1, dp == nd - 1)
    for k in range(plan.parts_in):
        part = lax.ppermute(
            rest[k * plan.part_in : (k + 1) * plan.part_in], GRP, [(plan.full, 2 * k + 1)]
        )
        filled = lax.dynamic_update_slice(dec_piece, part, (0, 0))
        dec_piece = jnp.where(jnp.logical_and(last, grp == 2 * k + 1), filled, dec_piece)
    dec_parts = [dec_piece]
    for _ in range(ng - 1):
        dec_parts.append(over_z(dec_parts[-1]))
    dec_sources, dec_places, early_2, late_2 = gather(dec_parts, 0, late_1)

    micro_rows = enc_input.reshape(ROW, WIDTH)
    seg = lax.dynamic_index_in_dim(segments, sec, 0, keepdims=False).reshape(ROW)
    slot = lax.dynamic_index_in_dim(slots, sec, 0, keepdims=False).reshape(ROW)
    cot_rows = jnp.pad(
        cot.reshape(IMAGES_ROW, SLOTS, DEC_WIDTH), ((0, 0), (0, SLOT_PAD - SLOTS), (0, 0))
    ).reshape(IMAGES_ROW * SLOT_PAD, DEC_WIDTH)

    enc_weights = unpack(plan, ENC_LAYOUT, half, piece, ng, enc_places, enc_sources)
    micro_rows = after(micro_rows, *early_2)
    saved = dict(
        zip([SENT, H1, QKV, PROBS, ATT, MID, H2, ACT, SLOPE], encode(micro_rows, seg, enc_weights))
    )
    dec_weights = unpack(plan, DEC_LAYOUT, half // 2, half, plan.full, dec_places, dec_sources)
    dec = dict(
        zip(
            [OUT, H1, QKV_L, ATT, PROJ_L, H2, UP_L, ACT, EMBED_L, GSENT, VECS, GPOS],
            decode(saved[SENT], seg, slot, cot_rows, dec_weights),
        )
    )

    def add(first, *others):
        total = first.astype(f32)
        for other in others:
            total = total + other.astype(f32)
        return total.astype(bf16)

    class Reduction:
        def __init__(self, tables, groups, size):
            self.mine, theirs = tables
            self.groups, self.size = groups, size
            self.from_core = over_core(theirs)

        def block(self, k, low=0, high=None):
            rows = len(self.groups) * self.size
            low, high = k * rows + low, k * rows + (rows if high is None else high)
            return add(self.mine[low:high], self.from_core[low:high])

        def corners(self):
            rows = len(self.groups) * self.size
            if ny == 2:
                self.middle = rows // 2
                self.corner_x = over_x(self.block(3, 0, self.middle))
                self.corner_y = over_y(self.block(3, self.middle))
                self.early_y = over_y(self.block(1, self.middle))
                self.early_x = over_x(self.block(2, 0, self.middle))
                return self.corner_x, self.corner_y
            held = [self.block(k) for k in range(2 * ny)]
            self.column = [add(held[k], over_x(held[ny + k])) for k in range(ny)]
            return tuple(self.column)

        def sides(self):
            rows = len(self.groups) * self.size
            if ny == 2:
                m = self.middle
                late_y = over_y(add(self.mine[rows : rows + m], self.from_core[rows : rows + m], self.corner_x))
                low, high = 2 * rows + m, 3 * rows
                late_x = over_x(add(self.mine[low:high], self.from_core[low:high], self.corner_y))
                self.own = jnp.concatenate(
                    [
                        add(self.mine[:m], self.from_core[:m], self.early_x, late_y),
                        add(self.mine[m:rows], self.from_core[m:rows], late_x, self.early_y),
                    ]
                )
            else:
                total = self.column[ny - 1]
                for k in range(ny - 2, -1, -1):
                    total = add(self.column[k], over_y(total))
                self.own = total
            return self.own

        def along(self):
            def one(g):
                index = (g - self.groups[0]) % ng
                index = jnp.minimum(index, len(self.groups) - 1)
                return lax.dynamic_slice(self.own, (index * self.size, 0), (self.size, LANES))

            total = one(grp - 1)
            for step in range(ng - 1):
                senders = [g for g in range(ng) if (g - 1 - step) % ng in self.groups]
                total = add(one(grp - 2 - step), over_z(total, senders))
            return total

    place = jnp.stack([sec, yy, core]).astype(jnp.int32)
    every = list(range(ng))
    dec_red = Reduction(
        pack(
            plan, DEC_LAYOUT, plan.dec_regions(), half, ng, place,
            {
                EMBED_W: (saved[SENT], dec[EMBED_L]),
                QKV_W: (dec[H1], dec[QKV_L]),
                PROJ_W: (dec[ATT], dec[PROJ_L]),
                UP_W: (dec[H2], dec[UP_L]),
                DOWN_W: (dec[ACT], cot_rows),
                POS: (dec[GPOS], dec[GPOS]),
            },
            dec[VECS],
        ),
        every,
        half,
    )
    grad_sent = after(dec[GSENT], dec_red.mine)
    up_low, proj_low, grad_middle, enc_vec = mlp_back(grad_sent, saved, enc_weights)
    up_low = after(up_low, *dec_red.corners())
    upper, lower = every[near:], every[:near]
    enc_up = Reduction(
        pack(
            plan, ENC_LAYOUT, plan.enc_regions(upper), piece, len(upper), place,
            {DOWN_W: (saved[ACT], grad_sent), UP_W: (saved[H2], up_low)},
            enc_vec,
        ),
        upper,
        piece,
    )
    grad_middle = after(grad_middle, enc_up.mine, dec_red.sides())
    in_grad, qkv_low, enc_vec = attention_back(grad_middle, proj_low, micro_rows, saved, enc_weights, enc_vec)
    qkv_low = after(qkv_low, *enc_up.corners())
    enc_low = Reduction(
        pack(
            plan, ENC_LAYOUT, plan.enc_regions(lower), piece, len(lower), place,
            {
                PROJ_W: (saved[ATT], proj_low),
                QKV_W: (saved[H1], qkv_low),
                UP_W: (saved[H2], up_low),
            },
            enc_vec,
        ),
        lower,
        piece,
    )
    dec_sum = dec_red.along()
    spread_back = [[(2 * z + h, z) for z in range(plan.full)] for h in range(2)]
    spread_back[0].append((1, plan.full))
    dec_low, dec_high = (lax.ppermute(dec_sum, GRP, pairs) for pairs in spread_back)
    dec_rest = lax.ppermute(dec_sum, GRP, [(3, plan.full)])
    dec_own = jnp.concatenate([dec_low, jnp.where(grp == plan.full, dec_rest, dec_high)])
    enc_up.sides()
    up_own = enc_up.along()
    enc_low.corners()
    enc_low.sides()
    enc_own = jnp.where(grp >= near, up_own, enc_low.along())

    own = jnp.where(first_section, enc_own, dec_own)
    other = jnp.where(first_section, dec_own, enc_own)
    if ny == 2:
        from_x, from_y = over_x(other), over_y(own)
        sources = [own, from_x, from_y, over_y(from_x)]
        owners = [(sec, yy), (1 - sec, yy), (sec, 1 - yy), (1 - sec, 1 - yy)]
    else:
        column = [jnp.concatenate([own, over_x(other)])]
        for _ in range(ny - 1):
            column.append(over_y(column[-1]))
        sources = column
        owners = [(s, (yy - k) % ny) for k in range(ny) for s in (sec, 1 - sec)]
    sources = sources + [over_core(block) for block in sources]
    places = []
    for c in (core, 1 - core):
        for s, y in owners:
            number = (c * 2 + s) * ny + y
            places += [
                jnp.where(first_section, 2 * number, number),
                jnp.where(first_section, 2 * number + 1, plan.pieces + number),
            ]
    table = jnp.asarray(plan.segments())[sec, grp].reshape(-1)
    flat = finish(plan, jnp.stack(places).astype(jnp.int32), table, sources)
    param_grad = flat.reshape(1, chunk * LANES)
    dec_out = dec[OUT].reshape(IMAGES_ROW, SLOT_PAD, DEC_WIDTH)[:, :SLOTS]
    return (
        dec_out.reshape(1, 1, IMAGES_ROW * SLOTS, DEC_WIDTH),
        in_grad.reshape(1, 1, ROW, WIDTH),
        param_grad,
    )


def solution(mesh):
    placed = (
        P(SEC, (GRP, DP), None, None),
        P(None, (GRP, DP), None),
        P(None, (GRP, DP), None),
        P(SEC, GRP),
        P(SEC, (GRP, DP), None, None),
    )
    return jax.shard_map(
        partial(per_device, Plan(dict(mesh.shape))),
        mesh=mesh,
        in_specs=placed,
        out_specs=(
            P(SEC, (GRP, DP), None, None),
            P(SEC, (GRP, DP), None, None),
            P(SEC, GRP),
        ),
        check_vma=False,
    )
```

```python
from functools import partial
import math

import jax
import jax.numpy as jnp
import numpy as np
from jax import lax
from jax.experimental import pallas as pl
from jax.experimental.pallas import tpu as pltpu
from jax.sharding import PartitionSpec as P

WIDTH = 768
HEADS = 12
HIDDEN_SIZE = 3072
DEC_WIDTH = 512
DEC_HEADS = 16
DEC_HIDDEN = 2048
SLOTS = 196
IMAGES_ROW = 5
ROW = 256
PARAMS = 7088128
LANES = 128
SEC, GRP, DP = "section", "group", "dp"
(
    N1G, N1B, QKV_W, QB, VB, PROJ_W, PB, N2G,
) = range(0, 8)
(
    N2B, UP_W, UB, DOWN_W, DB, EMBED_W, EB, MT,
) = range(8, 16)
(
    POS, QKV_B, VECS, SENT, H1, QKV, PROBS, ATT,
) = range(16, 24)
(
    MID, H2, ACT, SLOPE, OUT, QKV_L, PROJ_L, UP_L,
) = range(24, 32)
(
    EMBED_L, GSENT, GPOS,
) = range(32, 35)
SLOT_PAD = 208
VMEM_BYTES = 60 * 1024 * 1024

norm_eps = 1e-06
masked_score = -1000000000.0
f32 = jnp.float32
bf16 = jnp.bfloat16


def block_layout(width, hidden):
    return [
        (N1G, (width,)),
        (N1B, (width,)),
        (QKV_W, (width, 3 * width)),
        (QB, (width,)),
        (VB, (width,)),
        (PROJ_W, (width, width)),
        (PB, (width,)),
        (N2G, (width,)),
        (N2B, (width,)),
        (UP_W, (width, hidden)),
        (UB, (hidden,)),
        (DOWN_W, (hidden, width)),
        (DB, (width,)),
    ]


def decoder_layout(enc_width, width, hidden, slot_count):
    return [
        (EMBED_W, (enc_width, width)),
        (EB, (width,)),
        (MT, (width,)),
        (POS, (slot_count, width)),
    ] + block_layout(width, hidden)


ENC_LAYOUT = block_layout(WIDTH, HIDDEN_SIZE)
DEC_LAYOUT = decoder_layout(WIDTH, DEC_WIDTH, DEC_HIDDEN, SLOTS)
VEC = {
    N1G: 0,
    N1B: 1,
    QKV_B: 2,
    PB: 3,
    N2G: 4,
    N2B: 5,
    UB: 6,
    DB: 7,
    EB: 8,
    MT: 9,
}
VEC_ROWS = 16


def dot(a, b):
    return lax.dot_general(a, b, (((1,), (0,)), ((), ())), preferred_element_type=f32)


def dot_nt(a, b):
    return lax.dot_general(a, b, (((1,), (1,)), ((), ())), preferred_element_type=f32)


def dot_tn(a, b):
    return lax.dot_general(a, b, (((0,), (0,)), ((), ())), preferred_element_type=f32)


def normalised(values):
    centered = values - jnp.mean(values, axis=-1, keepdims=True)
    inverse = lax.rsqrt(jnp.mean(centered * centered, axis=-1, keepdims=True) + norm_eps)
    return centered * inverse, inverse


def norm_back(grad, hat, inverse, gain):
    scaled = grad * gain
    first = jnp.mean(scaled, axis=-1, keepdims=True)
    second = jnp.mean(scaled * hat, axis=-1, keepdims=True)
    return inverse * (scaled - first - hat * second)


def col_sum(values):
    return jnp.sum(values, axis=0, keepdims=True)


def gelu_parts(upward):
    half = 0.5 + 0.5 * lax.erf(upward * f32(math.sqrt(0.5)))
    slope = half + upward * (jnp.exp(upward * upward * f32(-0.5)) * f32(1.0 / math.sqrt(2.0 * math.pi)))
    return upward * half, slope


def head_mask(head, head_dim):
    lane = lax.broadcasted_iota(jnp.int32, (1, LANES), 1)
    return jnp.where(lane // head_dim == head, 1.0, 0.0).astype(bf16)


def lane_block(group, start=0):
    return slice(start + group * LANES, start + (group + 1) * LANES)


def flip(values):
    return values.astype(f32).T.astype(bf16)


def attention_forward(qkv_ref, probs_ref, joined_ref, width, heads, keep):
    head_dim = width // heads
    scale = f32(head_dim ** (-0.5))
    per_group = LANES // head_dim

    def one_group(group):
        queries = qkv_ref[:, lane_block(group)]
        keys = qkv_ref[:, lane_block(group, width)]
        values_t = flip(qkv_ref[:, lane_block(group, 2 * width)])
        subs = range(per_group)
        scores = [dot_nt(keys, queries * head_mask(sub, head_dim)) for sub in subs]
        scores = [keep(s * scale) for s in scores]
        expo = [jnp.exp(s - jnp.max(s, axis=0, keepdims=True)) for s in scores]
        probs = [e * (1.0 / col_sum(e)) for e in expo]
        for sub in subs:
            probs_ref[group * per_group + sub] = probs[sub]
        outs = [
            dot(values_t[sub * head_dim : (sub + 1) * head_dim], probs[sub].astype(bf16)) for sub in subs
        ]
        joined_ref[group * LANES : (group + 1) * LANES, :] = jnp.concatenate(outs, axis=0)

    for group in range(width // LANES):
        one_group(group)


def attention_backward(qkv_ref, probs_ref, grad_ref, low_ref, width, heads):
    head_dim = width // heads
    scale = f32(head_dim ** (-0.5))
    per_group = LANES // head_dim

    def one_group(group):
        queries = qkv_ref[:, lane_block(group)]
        keys = qkv_ref[:, lane_block(group, width)]
        values = qkv_ref[:, lane_block(group, 2 * width)]
        grads = grad_ref[:, lane_block(group)]
        keys_t = flip(keys)
        subs = range(per_group)
        masks = [head_mask(sub, head_dim) for sub in subs]
        own = [grads * m for m in masks]
        grad_probs = [dot_nt(values, o) for o in own]
        probs = [probs_ref[group * per_group + sub] for sub in subs]
        grad_values = sum(dot(p.astype(bf16), o) for p, o in zip(probs, own))
        low = [
            (p * (g - col_sum(p * g))).astype(bf16) for p, g in zip(probs, grad_probs)
        ]
        grad_keys = sum(dot(l, queries * m) for l, m in zip(low, masks))
        grad_queries = [
            dot(keys_t[sub * head_dim : (sub + 1) * head_dim], low[sub]) for sub in subs
        ]
        low_ref[:, lane_block(group)] = (jnp.concatenate(grad_queries, axis=0).T * scale).astype(bf16)
        low_ref[:, lane_block(group, width)] = (grad_keys * scale).astype(bf16)
        low_ref[:, lane_block(group, 2 * width)] = grad_values.astype(bf16)

    for group in range(width // LANES):
        one_group(group)


def encode_kernel(
    x_ref, seg_row_ref, seg_col_ref, qkv_w, proj_w, up_w, down_w, vec,
    sent_ref, normed1_ref, qkv_ref, probs_ref, attended_ref, middle_ref, normed2_ref, active_ref,
    slope_ref, joined_ref,
):
    width, hidden = WIDTH, HIDDEN_SIZE
    inputs = x_ref[...].astype(f32)
    hat, _ = normalised(inputs)
    normed1 = (hat * vec[0:1, :width] + vec[1:2, :width]).astype(bf16)
    normed1_ref[...] = normed1
    qkv_ref[...] = (dot(normed1, qkv_w[...]) + vec[2:3, : 3 * width]).astype(bf16)
    allowed = seg_col_ref[...] == seg_row_ref[...]
    attention_forward(
        qkv_ref, probs_ref, joined_ref, width, HEADS,
        lambda scores: jnp.where(allowed, scores, f32(masked_score)),
    )
    attended = joined_ref[...].T.astype(bf16)
    attended_ref[...] = attended
    middle = inputs + (dot(attended, proj_w[...]) + vec[3:4, :width])
    middle_ref[...] = middle
    hat, _ = normalised(middle)
    normed2_ref[...] = (hat * vec[4:5, :width] + vec[5:6, :width]).astype(bf16)
    joined_ref[...] = jnp.zeros_like(joined_ref)
    total = jnp.zeros((inputs.shape[0], width), f32)
    part = 1536
    for start in range(0, hidden, part):
        cols = slice(start, start + part)
        upward = dot(normed2_ref[...], up_w[:, cols]) + vec[6:7, cols]
        active, slope = gelu_parts(upward)
        active_ref[:, cols] = active.astype(bf16)
        slope_ref[:, cols] = slope.astype(slope_ref.dtype)
        total += dot(active_ref[:, cols], down_w[cols, :])
    sent_ref[...] = (middle + (total + vec[7:8, :width])).astype(bf16)


def mlp_back_kernel(
    grad_ref, middle_ref, slope_ref, up_w, down_w, vec,
    up_low_ref, proj_low_ref, grad_middle_ref, vec_grad,
):
    width, hidden = WIDTH, HIDDEN_SIZE
    grad_out = grad_ref[...]
    vec_grad[...] = jnp.zeros_like(vec_grad)
    vec_grad[7:8, :width] = col_sum(grad_out.astype(f32))
    grad_normed2 = jnp.zeros((grad_out.shape[0], width), f32)
    part = 3072
    for start in range(0, hidden, part):
        cols = slice(start, start + part)
        low = (dot_nt(grad_out, down_w[cols, :]) * slope_ref[:, cols]).astype(bf16)
        up_low_ref[:, cols] = low
        vec_grad[6:7, cols] = col_sum(low.astype(f32))
        grad_normed2 += dot_nt(low, up_w[:, cols])
    hat, inverse = normalised(middle_ref[...])
    vec_grad[4:5, :width] = col_sum(grad_normed2 * hat)
    vec_grad[5:6, :width] = col_sum(grad_normed2)
    grad_middle = grad_out.astype(f32) + norm_back(grad_normed2, hat, inverse, vec[4:5, :width])
    grad_middle_ref[...] = grad_middle
    proj_low = grad_middle.astype(bf16)
    proj_low_ref[...] = proj_low
    vec_grad[3:4, :width] = col_sum(proj_low.astype(f32))


def attention_back_kernel(
    grad_middle_ref, proj_low_ref, x_ref, qkv_ref, probs_ref, qkv_w, proj_w, vec, vec_in,
    in_grad_ref, qkv_low_ref, vec_grad, grad_att_ref,
):
    width = WIDTH
    vec_grad[...] = vec_in[...]
    grad_att_ref[...] = dot_nt(proj_low_ref[...], proj_w[...]).astype(bf16)
    attention_backward(qkv_ref, probs_ref, grad_att_ref, qkv_low_ref, width, HEADS)
    qkv_low = qkv_low_ref[...]
    vec_grad[2:3, : 3 * width] = col_sum(qkv_low.astype(f32))
    grad_normed1 = dot_nt(qkv_low, qkv_w[...])
    hat, inverse = normalised(x_ref[...].astype(f32))
    vec_grad[0:1, :width] = col_sum(grad_normed1 * hat)
    vec_grad[1:2, :width] = col_sum(grad_normed1)
    in_grad_ref[...] = grad_middle_ref[...] + norm_back(grad_normed1, hat, inverse, vec[0:1, :width])


def decode_kernel(
    sent_ref, embed_w, qkv_w, proj_w, up_w, down_w, vec, pos_ref,
    seg_row, slot_row, seg_col, slot_col, cot_ref,
    out_ref, normed1_ref, qkv_low_ref, attended_ref, proj_low_ref, normed2_ref, up_low_ref,
    active_ref, embed_low_ref, grad_sent_ref, vec_grad, pos_grad,
    embedded_ref, embed_sum, qkv_ref, probs_ref, joined_ref, grad_att_ref,
):
    width, hidden = DEC_WIDTH, DEC_HIDDEN
    image = pl.program_id(0)
    length = SLOT_PAD

    @pl.when(image == 0)
    def _():
        embedded_ref[...] = (dot(sent_ref[...], embed_w[...]) + vec[8:9, :width]).astype(bf16)
        vec_grad[...] = jnp.zeros_like(vec_grad)
        pos_grad[...] = jnp.zeros_like(pos_grad)
        embed_sum[...] = jnp.zeros_like(embed_sum)

    def add_vec(row, values):
        vec_grad[row : row + 1, : values.shape[1]] += values

    place = lax.broadcasted_iota(jnp.int32, (length, ROW), 0)
    match = (seg_row[...] == image) & (slot_row[...] == place)
    onehot = jnp.where(match, 1.0, 0.0)
    free = 1.0 - jnp.sum(onehot, axis=1, keepdims=True)
    x = dot(onehot.astype(bf16), embedded_ref[...]) + free * vec[9:10, :width] + pos_ref[...].astype(f32)
    hat1, inverse1 = normalised(x)
    normed1 = (hat1 * vec[0:1, :width] + vec[1:2, :width]).astype(bf16)
    normed1_ref[...] = normed1
    qkv_ref[...] = (dot(normed1, qkv_w[...]) + vec[2:3, : 3 * width]).astype(bf16)
    key_place = lax.broadcasted_iota(jnp.int32, (length, length), 0)
    attention_forward(
        qkv_ref, probs_ref, joined_ref, width, DEC_HEADS,
        lambda scores: jnp.where(key_place < SLOTS, scores, f32(-1e30)),
    )
    attended = joined_ref[...].T.astype(bf16)
    attended_ref[...] = attended
    middle = x + (dot(attended, proj_w[...]) + vec[3:4, :width])
    hat2, inverse2 = normalised(middle)
    normed2 = (hat2 * vec[4:5, :width] + vec[5:6, :width]).astype(bf16)
    normed2_ref[...] = normed2
    cot = cot_ref[...]
    add_vec(7, col_sum(cot.astype(f32)))
    total = jnp.zeros((length, width), f32)
    grad_normed2 = jnp.zeros((length, width), f32)
    part = 1024
    for start in range(0, hidden, part):
        cols = slice(start, start + part)
        upward = dot(normed2_ref[...], up_w[:, cols]) + vec[6:7, cols]
        active, slope = gelu_parts(upward)
        active = active.astype(bf16)
        active_ref[:, cols] = active
        total += dot(active, down_w[cols, :])
        low = (dot_nt(cot_ref[...], down_w[cols, :]) * slope).astype(bf16)
        up_low_ref[:, cols] = low
        vec_grad[6:7, cols] += col_sum(low.astype(f32))
        grad_normed2 += dot_nt(low, up_w[:, cols])
    out_ref[...] = (middle + (total + vec[7:8, :width])).astype(bf16)

    add_vec(4, col_sum(grad_normed2 * hat2))
    add_vec(5, col_sum(grad_normed2))
    grad_middle = cot.astype(f32) + norm_back(grad_normed2, hat2, inverse2, vec[4:5, :width])
    proj_low = grad_middle.astype(bf16)
    proj_low_ref[...] = proj_low
    add_vec(3, col_sum(proj_low.astype(f32)))
    grad_att_ref[...] = dot_nt(proj_low, proj_w[...]).astype(bf16)
    attention_backward(qkv_ref, probs_ref, grad_att_ref, qkv_low_ref, width, DEC_HEADS)
    qkv_low = qkv_low_ref[...]
    add_vec(2, col_sum(qkv_low.astype(f32)))
    grad_normed1 = dot_nt(qkv_low, qkv_w[...])
    add_vec(0, col_sum(grad_normed1 * hat1))
    add_vec(1, col_sum(grad_normed1))
    grad_in = grad_middle + norm_back(grad_normed1, hat1, inverse1, vec[0:1, :width])
    low_in = grad_in.astype(bf16)
    wide = low_in.astype(f32)
    add_vec(9, col_sum(free * wide))
    pos_grad[...] += wide
    place_t = lax.broadcasted_iota(jnp.int32, (ROW, length), 1)
    match_t = (seg_col[...] == image) & (slot_col[...] == place_t)
    embed_sum[...] += dot(jnp.where(match_t, 1.0, 0.0).astype(bf16), low_in)

    @pl.when(image == IMAGES_ROW - 1)
    def _():
        embed_low = embed_sum[...].astype(bf16)
        embed_low_ref[...] = embed_low
        add_vec(8, col_sum(embed_low.astype(f32)))
        grad_sent_ref[...] = dot_nt(embed_low, embed_w[...]).astype(bf16)


def cost(microseconds):
    return pl.CostEstimate(flops=int(microseconds * 1e11), bytes_accessed=int(microseconds * 3e8), transcendentals=0)


def params_of(**extra):
    return pltpu.CompilerParams(vmem_limit_bytes=VMEM_BYTES, **extra)


def shape(dims, kind):
    return jax.ShapeDtypeStruct(dims, kind)


def encode(x, seg, weights):
    width, hidden, length = WIDTH, HIDDEN_SIZE, ROW
    names = [QKV_W, PROJ_W, UP_W, DOWN_W, VECS]
    return pl.pallas_call(
        encode_kernel,
        out_shape=[
            shape((length, width), bf16),
            shape((length, width), bf16),
            shape((length, 3 * width), bf16),
            shape((HEADS, length, length), f32),
            shape((length, width), bf16),
            shape((length, width), f32),
            shape((length, width), bf16),
            shape((length, hidden), bf16),
            shape((length, hidden), bf16),
        ],
        scratch_shapes=[pltpu.VMEM((width, length), f32)],
        compiler_params=params_of(),
        cost_estimate=cost(18),
        name="encode",
    )(x, seg.reshape(1, length), seg.reshape(length, 1), *[weights[n] for n in names])


def mlp_back(grad, saved, weights):
    width, hidden, length = WIDTH, HIDDEN_SIZE, ROW
    return pl.pallas_call(
        mlp_back_kernel,
        out_shape=[
            shape((length, hidden), bf16),
            shape((length, width), bf16),
            shape((length, width), f32),
            shape((VEC_ROWS, hidden), f32),
        ],
        compiler_params=params_of(),
        cost_estimate=cost(9),
        name="mlp_back",
    )(grad, saved[MID], saved[SLOPE], weights[UP_W], weights[DOWN_W], weights[VECS])


def attention_back(grad_middle, proj_low, x, saved, weights, vec_grad):
    width, hidden, length = WIDTH, HIDDEN_SIZE, ROW
    return pl.pallas_call(
        attention_back_kernel,
        out_shape=[
            shape((length, width), f32),
            shape((length, 3 * width), bf16),
            shape((VEC_ROWS, hidden), f32),
        ],
        scratch_shapes=[pltpu.VMEM((length, width), bf16)],
        compiler_params=params_of(),
        cost_estimate=cost(10),
        name="attention_back",
    )(
        grad_middle, proj_low, x, saved[QKV], saved[PROBS],
        weights[QKV_W], weights[PROJ_W], weights[VECS], vec_grad,
    )


def decode(sent, seg, slot, cot, weights):
    width, hidden, length = DEC_WIDTH, DEC_HIDDEN, SLOT_PAD
    names = [EMBED_W, QKV_W, PROJ_W, UP_W, DOWN_W, VECS, POS]
    held = [sent] + [weights[n] for n in names]
    held += [seg.reshape(1, ROW), slot.reshape(1, ROW), seg.reshape(ROW, 1), slot.reshape(ROW, 1)]

    def whole(array):
        return pl.BlockSpec(array.shape, lambda i: (0,) * array.ndim, pipeline_mode=pl.Buffered(1))

    def image(cols):
        return pl.BlockSpec((length, cols), lambda i: (i, 0))

    rows = IMAGES_ROW * length
    per_image = [width, width, 3 * width, width, width, width, hidden, hidden]
    kept = [
        shape((ROW, width), bf16),
        shape((ROW, WIDTH), bf16),
        shape((VEC_ROWS, hidden), f32),
        shape((length, width), f32),
    ]
    return pl.pallas_call(
        decode_kernel,
        grid=(IMAGES_ROW,),
        in_specs=[whole(a) for a in held] + [image(width)],
        out_specs=[image(c) for c in per_image]
        + [pl.BlockSpec(s.shape, lambda i: (0, 0)) for s in kept],
        out_shape=[shape((rows, c), bf16) for c in per_image] + kept,
        scratch_shapes=[
            pltpu.VMEM((ROW, width), bf16),
            pltpu.VMEM((ROW, width), f32),
            pltpu.VMEM((length, 3 * width), bf16),
            pltpu.VMEM((DEC_HEADS, length, length), f32),
            pltpu.VMEM((width, length), f32),
            pltpu.VMEM((length, width), bf16),
        ],
        compiler_params=params_of(dimension_semantics=("arbitrary",)),
        cost_estimate=cost(85),
        name="decode",
    )(*held, cot)


def rows_of(extent):
    return math.prod(extent) // LANES


def up_to(value, step):
    return -(-value // step) * step


def flat_starts(layout):
    starts, here = {}, 0
    for name, extent in layout:
        starts[name] = here
        here += rows_of(extent)
    return starts, here


def kept_starts(layout):
    starts, here = {}, 0
    for name, extent in layout:
        starts[name] = here
        here += up_to(rows_of(extent), 16)
    return starts, here


class Plan:
    def __init__(self, mesh_shape):
        self.ns, self.ng, self.nd = (mesh_shape[a] for a in (SEC, GRP, DP))
        self.ny = self.nd // 2
        self.chunk = PARAMS // LANES // self.ng
        self.pieces = self.ns * self.nd
        self.piece = up_to(-(-self.chunk // self.pieces), 64)
        self.half = self.piece // 2
        self.room = self.piece * self.pieces
        self.tables = 4 if self.ny == 2 else 2
        self.units = 2 * self.pieces
        self.full = self.ng // 2
        self.rest = flat_starts(DEC_LAYOUT)[1] - self.full * self.chunk
        assert 0 < self.rest <= self.chunk
        self.unit = up_to(-(-self.chunk // (self.units - 1)), 64)
        self.dec_room = self.unit * self.units
        whole = self.chunk // self.unit * self.unit
        self.part_in = self.unit if whole < self.dec_room - self.unit else 0
        self.parts_in = -(-self.rest // self.part_in)
        assert self.parts_in <= self.full
        self.enc_starts = [self.kept_row(ENC_LAYOUT, z * self.chunk) // 16 * 16 for z in range(self.ng)]
        self.enc_ends = [
            up_to(self.kept_row(ENC_LAYOUT, min((z + 1) * self.chunk, flat_starts(ENC_LAYOUT)[1]) - 1) + 1, 16)
            for z in range(self.ng)
        ]
        self.dec_starts = [self.kept_row(DEC_LAYOUT, z * self.chunk) // 16 * 16 for z in range(self.full)]
        self.dec_ends = [
            up_to(self.kept_row(DEC_LAYOUT, (z + 1) * self.chunk - 1) + 1, 16) for z in range(self.full)
        ]
        assert all(e - s <= self.room for s, e in zip(self.enc_starts, self.enc_ends))
        self.rest_start = self.kept_row(DEC_LAYOUT, self.full * self.chunk) // 16 * 16
        self.rest_end = kept_starts(DEC_LAYOUT)[1]
        self.part_out = [self.room - (self.dec_ends[k] - self.dec_starts[k]) for k in range(2)]
        assert max(self.part_out) <= self.room // 2
        assert self.part_out[0] < self.rest_end - self.rest_start <= sum(self.part_out)

    def kept_row(self, layout, flat_row):
        flat, _ = flat_starts(layout)
        kept, _ = kept_starts(layout)
        for name, extent in layout:
            if flat_row < flat[name] + rows_of(extent):
                return kept[name] + flat_row - flat[name]
        return kept[name] + rows_of(extent)

    def ranges(self, first, count, cut, chunks, chunk_room):
        found = []
        whole = self.chunk // cut * cut
        while count:
            z, row = divmod(first, self.chunk)
            if z >= chunks:
                k, row = divmod(row, self.part_in)
                here, room = (k + 1) * chunk_room - cut + row, self.part_in - row
            elif row < whole:
                here, room = z * chunk_room + row, whole - row
            else:
                here, room = z * chunk_room + row + cut - (self.chunk - whole), self.chunk - row
            take = min(count, room)
            found.append((here, take))
            first, count = first + take, count - take
        return found

    def packed_row(self, size, groups, group_first, index, row, away_x, away_y):
        owner = away_x * self.ny + away_y
        turned = away_y * 2 + away_x
        if self.ny != 2:
            first = index * (2 * self.ny) + owner if group_first else owner * groups + index
            return first * size + row
        if group_first:
            second, row = divmod(row, size // 2)
            return index * (4 * size) + second * (2 * size) + (turned if second else owner) * (size // 2) + row
        second, index = divmod(index, groups // 2)
        half = groups // 2 * size
        return second * (4 * half) + (turned if second else owner) * half + index * size + row

    def enc_regions(self, groups):
        return [(self.enc_starts[z], self.enc_ends[z], k, 0) for k, z in enumerate(groups)]

    def dec_regions(self):
        length = self.room // 2
        found = []
        for z in range(self.full):
            low, high = self.dec_starts[z], self.dec_ends[z]
            found += [(low, low + length, 2 * z, 0), (low + length, high, 2 * z + 1, 0)]
        middle = self.rest_start + self.part_out[0]
        found.append((self.rest_start, middle, 1, length - self.part_out[0]))
        found.append((middle, self.rest_end, 3, length - self.part_out[1]))
        return found

    def segments(self):
        count = len(DEC_LAYOUT) + 2
        table = np.zeros((self.ns, self.ng, count, 3), np.int32)
        length = self.room // 2
        for s, layout in enumerate((ENC_LAYOUT, DEC_LAYOUT)):
            flat, used = flat_starts(layout)
            for z in range(self.ng):
                low, high = z * self.chunk, (z + 1) * self.chunk
                found = []
                for name, extent in layout:
                    first, last = max(flat[name], low), min(flat[name] + rows_of(extent), high)
                    while first < last:
                        row, stop = self.kept_row(layout, first), last
                        if s == 0:
                            source = row - self.enc_starts[z]
                        elif z < self.full:
                            source = row - self.dec_starts[z]
                        else:
                            row -= self.rest_start
                            k = int(row >= self.part_out[0])
                            row -= k * self.part_out[0]
                            source = (k + 1) * length - self.part_out[k] + row
                            stop = min(last, first + self.part_out[k] - row)
                        found.append((source, first - low, -(-(stop - first) // 8)))
                        first = stop
                if used < high:
                    found.append((self.room, max(used - low, 0), 1))
                table[s, z, : len(found)] = found
        return table


def widen_block(held, wide, spare, ranges):
    def load(start, count):
        first = start // 16 * 16
        size = up_to(start + count - first, 16)
        return held[first : first + size, :].astype(f32), size, start - first

    if len(ranges) == 1:
        block, size, skip = load(*ranges[0])
        wide[0:size, :] = block
        return skip
    here = 0
    for start, count in ranges:
        block, size, skip = load(start, count)
        spare[0:size, :] = block
        wide[here : here + count, :] = spare[skip : skip + count, :]
        here += count
    return 0


def unpack_kernel(plan, layout, unit, cut, chunks, room, counts, place_ref, *refs):
    sources = refs[: len(counts)]
    refs = refs[len(counts) :]
    matrices = [(n, e) for n, e in layout if len(e) == 2]
    outs, vec = refs[: len(matrices)], refs[len(matrices)]
    held, wide, spare, sems = refs[len(matrices) + 1 :]
    per_chunk = room // unit
    number = 0
    for source, count in zip(sources, counts):
        for k in range(count):
            slot = place_ref[number]
            number += 1
            target = held.at[pl.ds(pl.multiple_of(slot * unit, 16), unit), :]
            pltpu.make_async_copy(source.at[pl.ds(k * unit, unit), :], target, sems.at[slot // per_chunk]).start()
    arrived = set()

    def arrive(ranges):
        for start, count in ranges:
            z = start // room
            if z not in arrived:
                arrived.add(z)
                part = held.at[pl.ds(z * room, room), :]
                pltpu.make_async_copy(part, part, sems.at[z]).wait()

    vec[...] = jnp.zeros_like(vec)
    flat, _ = flat_starts(layout)
    by_name = dict(zip([n for n, _ in matrices], outs))
    for name, extent in layout:
        if len(extent) == 2:
            depth, lanes = extent[0], extent[1] // LANES
            step = depth if name == POS else max(128, 2048 // lanes // 128 * 128)
            out = by_name[name]
            if name == POS:
                out[...] = jnp.zeros_like(out)
            for first in range(0, depth, step):
                size = min(step, depth - first)
                ranges = plan.ranges(flat[name] + first * lanes, size * lanes, cut, chunks, room)
                arrive(ranges)
                skip = widen_block(held, wide, spare, ranges)
                for j in range(lanes):
                    block = wide[pl.ds(skip + j, size, stride=lanes), :].astype(bf16)
                    out[first : first + size, j * LANES : (j + 1) * LANES] = block
        else:
            lanes = extent[0] // LANES
            ranges = plan.ranges(flat[name], lanes, cut, chunks, room)
            arrive(ranges)
            skip = widen_block(held, wide, spare, ranges)
            row, shift = {QB: (2, 0), VB: (2, 2 * extent[0])}.get(name, (VEC.get(name), 0))
            for j in range(lanes):
                vec[row : row + 1, shift + j * LANES : shift + (j + 1) * LANES] = wide[skip + j : skip + j + 1, :]
    for z in range(chunks):
        arrive([(z * room, 1)])


def unpack(plan, layout, unit, cut, chunks, room, place, sources):
    matrices = [(n, e) for n, e in layout if len(e) == 2]
    outs = [
        shape((SLOT_PAD if n == POS else e[0], e[1]), bf16) for n, e in matrices
    ] + [shape((VEC_ROWS, 4 * dict(layout)[PB][0]), f32)]
    operands = list(sources)
    rows = chunks * room
    result = pl.pallas_call(
        partial(unpack_kernel, plan, layout, unit, cut, chunks, room, [s.shape[0] // unit for s in sources]),
        in_specs=[pl.BlockSpec(memory_space=pltpu.SMEM)]
        + [pl.BlockSpec(memory_space=pl.ANY)] * len(operands),
        out_shape=outs,
        scratch_shapes=[
            pltpu.VMEM((rows, LANES), bf16),
            pltpu.VMEM((3200, LANES), f32),
            pltpu.VMEM((3200, LANES), f32),
            pltpu.SemaphoreType.DMA((chunks,)),
        ],
        compiler_params=params_of(),
        cost_estimate=cost(12),
        name="unpack",
    )(place, *operands)
    return dict(zip([n for n, _ in matrices] + [VECS], result))


def pack_kernel(plan, layout, names, regions, size, groups, group_first, place_ref, *refs):
    pairs = {}
    for name in names:
        pairs[name], refs = refs[:2], refs[2:]
    vec, refs = refs[0], refs[1:]
    pos = None
    if POS in names:
        pos, refs = pairs[POS][0], refs
    mine, theirs, wide, stage, small, sems = refs
    kept, _ = kept_starts(layout)
    extents = dict(layout)
    ny = plan.ny

    def send(source, first, rows, sem):
        moved = 0
        for low, high, index, base in regions:
            start, stop = max(first, low), min(first + rows, high)
            while start < stop:
                number, row = divmod(base + start - low, size)
                c, s, y = number // (2 * ny), number // ny % 2, number % ny
                away_x, away_y = lax.rem(s - place_ref[0] + 2, 2), lax.rem(y - place_ref[1] + ny, ny)
                count = min(stop - start, size - row)
                if group_first:
                    count = min(count, size // 2 - row % (size // 2))
                where = plan.packed_row(size, groups, group_first, index, row, away_x, away_y)
                target = pl.ds(pl.multiple_of(where, 16), count)
                block = source.at[pl.ds(start - first, count), :]
                for same, table in ((True, mine), (False, theirs)):

                    @pl.when((place_ref[2] == c) == same)
                    def _():
                        pltpu.make_async_copy(block, table.at[target, :], sem).start()

                moved += count
                start += count
        return moved

    def wait(rows, slot):
        if rows:
            block = stage.at[slot, pl.ds(0, rows), :]
            pltpu.make_async_copy(block, block, sems.at[slot]).wait()

    turn = 0
    pending = [0, 0]
    for name in names:
        if name == POS:
            continue
        left, right = pairs[name]
        depth, width = extents[name]
        lanes = width // LANES
        step = max(k for k in (128, 256, 384, 512) if depth % k == 0 and k * lanes <= 3072)
        rows = step * lanes
        for first in range(0, depth, step):
            start = kept[name] + first * lanes
            if all(start >= high or start + rows <= low for low, high, _, _ in regions):
                continue
            slot = turn % 2
            turn += 1
            columns = flip(left[:, first : first + step])
            part = 256
            for start in range(0, width, part):
                block = dot(columns, right[:, start : start + part])
                for j in range(part // LANES):
                    wide[pl.ds(start // LANES + j, step, stride=lanes), :] = block[:, j * LANES : (j + 1) * LANES]
            wait(pending[slot], slot)
            stage[slot, 0:rows, :] = wide[0:rows, :].astype(bf16)
            pending[slot] = send(stage.at[slot], kept[name] + first * lanes, rows, sems.at[slot])
    here = 0
    total = 0
    for name, extent in layout:
        if name not in names and len(extent) == 2 or name not in kept_names(names):
            continue
        if len(extent) == 2 and name != POS:
            continue
        rows = rows_of(extent)
        room = up_to(rows, 16)
        wide[0:room, :] = jnp.zeros((room, LANES), f32)
        if name == POS:
            lanes = extent[1] // LANES
            for j in range(lanes):
                wide[pl.ds(j, extent[0], stride=lanes), :] = pos[0 : extent[0], j * LANES : (j + 1) * LANES]
        else:
            row, shift = {QB: (2, 0), VB: (2, 2 * extent[0])}.get(name, (VEC.get(name), 0))
            for j in range(rows):
                wide[j : j + 1, :] = vec[row : row + 1, shift + j * LANES : shift + (j + 1) * LANES]
        small[here : here + room, :] = wide[0:room, :].astype(bf16)
        total += send(small.at[pl.ds(here, room), :], kept[name], room, sems.at[2])
        here += room
    wait(pending[0], 0)
    wait(pending[1], 1)
    block = small.at[pl.ds(0, total), :]
    pltpu.make_async_copy(block, block, sems.at[2]).wait()


def pack_enc_kernel(plan, names, regions, size, groups, place_ref, *refs):
    pairs = {}
    for name in names:
        pairs[name], refs = refs[:4], refs[4:]
    vec, vec_other, *tables = refs[: 2 + plan.tables]
    wide, stage, small, sems = refs[2 + plan.tables :]
    kept, _ = kept_starts(ENC_LAYOUT)
    extents = dict(ENC_LAYOUT)
    ny = plan.ny

    def pieces(first, rows, core):
        for low, high, index, base in regions:
            start, stop = max(first, low), min(first + rows, high)
            while start < stop:
                number, row = divmod(base + start - low, size)
                count = min(stop - start, size - row)
                if number // (2 * ny) == core:
                    yield start - first, count, index, row, number // ny % 2, number % ny
                start += count

    def send(source, first, rows, sem, core):
        moved = 0
        for skip, count, index, row, s, y in pieces(first, rows, core):
            away_x, away_y = lax.rem(s - place_ref[0] + 2, 2), lax.rem(y - place_ref[1] + ny, ny)
            if ny == 2 and index >= groups // 2:
                keep, away, other, index = tables[2:], away_y, away_x, index - groups // 2
            else:
                keep, away, other = tables[:2], away_x, away_y
            length = (groups // 2 if ny == 2 else groups) * size
            target = pl.ds(pl.multiple_of(other * length, 16) + index * size + row, count)
            block = source.at[pl.ds(skip, count), :]
            for k in range(2):

                @pl.when(away == k)
                def _():
                    pltpu.make_async_copy(block, keep[k].at[target, :], sem).start()

            moved += count
        return moved

    def wait(rows, slot):
        if rows:
            block = stage.at[slot, pl.ds(0, rows), :]
            pltpu.make_async_copy(block, block, sems.at[slot]).wait()

    def run(core):
        turn = 0
        pending = [0, 0]
        for name in names:
            left, left_other, right, right_other = pairs[name]
            depth, width = extents[name]
            lanes = width // LANES
            step = max(k for k in (128, 256, 384, 512) if depth % k == 0 and k * lanes <= 3072)
            rows = step * lanes
            for first in range(0, depth, step):
                begin = kept[name] + first * lanes
                if not list(pieces(begin, rows, core)):
                    continue
                slot = turn % 2
                turn += 1
                columns = flip(left[:, first : first + step])
                others = flip(left_other[:, first : first + step])
                part = 256
                for start in range(0, width, part):
                    cols = slice(start, start + part)
                    block = dot(columns, right[:, cols]) + dot(others, right_other[:, cols])
                    for j in range(part // LANES):
                        wide[pl.ds(start // LANES + j, step, stride=lanes), :] = block[:, j * LANES : (j + 1) * LANES]
                wait(pending[slot], slot)
                stage[slot, 0:rows, :] = wide[0:rows, :].astype(bf16)
                pending[slot] = send(stage.at[slot], begin, rows, sems.at[slot], core)
        here = 0
        total = 0
        for name, extent in ENC_LAYOUT:
            if name not in kept_names(names):
                continue
            rows = rows_of(extent)
            room = up_to(rows, 16)
            if list(pieces(kept[name], room, core)):
                wide[0:room, :] = jnp.zeros((room, LANES), f32)
                row, shift = {QB: (2, 0), VB: (2, 2 * extent[0])}.get(name, (VEC.get(name), 0))
                for j in range(rows):
                    cols = slice(shift + j * LANES, shift + (j + 1) * LANES)
                    wide[j : j + 1, :] = vec[row : row + 1, cols] + vec_other[row : row + 1, cols]
                small[here : here + room, :] = wide[0:room, :].astype(bf16)
                total += send(small.at[pl.ds(here, room), :], kept[name], room, sems.at[2], core)
            here += room
        wait(pending[0], 0)
        wait(pending[1], 1)
        if total:
            block = small.at[pl.ds(0, total), :]
            pltpu.make_async_copy(block, block, sems.at[2]).wait()

    for core in range(2):

        @pl.when(place_ref[2] == core)
        def _():
            run(core)


def pack_enc(plan, regions, size, groups, place, pairs, vec, vec_other):
    names = list(pairs)
    operands = [a for name in names for a in pairs[name]] + [vec, vec_other]
    extents = dict(ENC_LAYOUT)
    small = sum(up_to(rows_of(extents[n]), 16) for n in kept_names(names))
    rows = 2 * plan.ny * groups * size // plan.tables
    return pl.pallas_call(
        partial(pack_enc_kernel, plan, names, regions, size, groups),
        in_specs=[pl.BlockSpec(memory_space=pltpu.SMEM)]
        + [pl.BlockSpec(memory_space=pltpu.VMEM)] * len(operands),
        out_specs=[pl.BlockSpec(memory_space=pl.ANY)] * plan.tables,
        out_shape=[shape((rows, LANES), bf16)] * plan.tables,
        scratch_shapes=[
            pltpu.VMEM((3072, LANES), f32),
            pltpu.VMEM((2, 3072 + 64, LANES), bf16),
            pltpu.VMEM((small + 64, LANES), bf16),
            pltpu.SemaphoreType.DMA((3,)),
        ],
        compiler_params=params_of(),
        cost_estimate=cost(8),
        name="pack_enc",
    )(place, *operands)


def kept_names(names):
    with_matrix = {
        QKV_W: [N1G, N1B, QB, VB],
        PROJ_W: [PB, N2G, N2B],
        UP_W: [UB],
        DOWN_W: [DB],
        EMBED_W: [EB, MT],
        POS: [POS],
    }
    return [v for n in names for v in with_matrix[n]]


def pack(plan, layout, regions, size, groups, group_first, place, pairs, vec):
    names = list(pairs)
    operands = [a for name in names for a in pairs[name]] + [vec]
    extents = dict(layout)
    small = sum(up_to(rows_of(extents[n]), 16) for n in kept_names(names))
    rows = 2 * plan.ny * groups * size
    return pl.pallas_call(
        partial(pack_kernel, plan, layout, names, regions, size, groups, group_first),
        in_specs=[pl.BlockSpec(memory_space=pltpu.SMEM)]
        + [pl.BlockSpec(memory_space=pltpu.VMEM)] * len(operands),
        out_specs=[pl.BlockSpec(memory_space=pl.ANY)] * 2,
        out_shape=[shape((rows, LANES), bf16)] * 2,
        scratch_shapes=[
            pltpu.VMEM((3072, LANES), f32),
            pltpu.VMEM((2, 3072 + 64, LANES), bf16),
            pltpu.VMEM((small + 64, LANES), bf16),
            pltpu.SemaphoreType.DMA((3,)),
        ],
        compiler_params=params_of(),
        cost_estimate=cost(25 if EMBED_W in names else 12),
        name="pack",
    )(place, *operands)


def finish_kernel(plan, counts, place_ref, seg_ref, *refs):
    sources, result, held, wide, out, sem = refs[: len(counts)], *refs[len(counts) :]
    unit = plan.half
    number = 0
    for source, count in zip(sources, counts):
        for k in range(count):
            target = held.at[pl.ds(pl.multiple_of(place_ref[number] * unit, 16), unit), :]
            number += 1
            pltpu.make_async_copy(source.at[pl.ds(k * unit, unit), :], target, sem.at[0]).start()
    out[...] = jnp.zeros_like(out)
    pltpu.make_async_copy(held, held, sem.at[0]).wait()
    total = plan.room
    wide[total : total + 16, :] = jnp.zeros((16, LANES), f32)
    wide[0:total, :] = held[...].astype(f32)

    def one(k, carry):
        source, first, steps = seg_ref[3 * k], seg_ref[3 * k + 1], seg_ref[3 * k + 2]

        def step(i, carry):
            out[pl.ds(first + 8 * i, 8), :] = wide[pl.ds(source + 8 * i, 8), :]
            return carry

        def steps8(i, carry):
            out[pl.ds(first + 64 * i, 64), :] = wide[pl.ds(source + 64 * i, 64), :]
            return carry

        many = steps // 8
        lax.fori_loop(0, many, steps8, 0)
        return lax.fori_loop(many * 8, steps, step, carry)

    lax.fori_loop(0, seg_ref.shape[0] // 3, one, 0)
    rows = up_to(plan.chunk, 8)
    lines = out.at[pl.ds(0, rows), :].reshape(rows, 1, LANES)
    copy = pltpu.make_async_copy(lines.at[pl.ds(0, plan.chunk)], result, sem.at[0])
    copy.start()
    copy.wait()


def finish(plan, place, segments, sources):
    total = plan.room
    return pl.pallas_call(
        partial(finish_kernel, plan, [s.shape[0] // plan.half for s in sources]),
        in_specs=[pl.BlockSpec(memory_space=pltpu.SMEM)] * 2
        + [pl.BlockSpec(memory_space=pl.ANY)] * len(sources),
        out_specs=pl.BlockSpec(memory_space=pl.ANY),
        out_shape=shape((plan.chunk, 1, LANES), f32),
        scratch_shapes=[
            pltpu.VMEM((total, LANES), bf16),
            pltpu.VMEM((total + 16, LANES), f32),
            pltpu.VMEM((up_to(plan.chunk, 8) + 8, LANES), f32),
            pltpu.SemaphoreType.DMA((1,)),
        ],
        compiler_params=params_of(),
        cost_estimate=cost(8),
        name="finish",
    )(place, segments, *sources)


def completed(pairs, count):
    senders = [k for k in range(count) if k not in [a for a, _ in pairs]]
    receivers = [k for k in range(count) if k not in [b for _, b in pairs]]
    return list(pairs) + list(zip(senders, receivers))


def after(values, *before):
    return lax.optimization_barrier((values, before))[0]


def per_device(plan, enc_input, segments, slots, params, cot):
    ns, ng, nd, ny = plan.ns, plan.ng, plan.nd, plan.ny
    piece, half, room, chunk = plan.piece, plan.half, plan.room, plan.chunk
    sec = lax.axis_index(SEC)
    grp = lax.axis_index(GRP)
    dp = lax.axis_index(DP)
    yy, core = dp // 2, dp % 2
    first_section = sec == 0

    def over_x(block):
        return lax.ppermute(block, SEC, [(0, 1), (1, 0)])

    def over_core(block):
        return lax.ppermute(block, DP, [(d, d ^ 1) for d in range(nd)])

    def over_y(block):
        return lax.ppermute(block, DP, [(d, (d + 2) % nd) for d in range(nd)])

    def over_z(block, senders=None):
        senders = range(ng) if senders is None else senders
        return lax.ppermute(block, GRP, [(g, (g + 1) % ng) for g in senders])

    unit = plan.unit

    def share(start, params):
        cut = lax.dynamic_slice(params, (0, start * LANES), (1, unit * LANES))
        return cut.astype(f32).reshape(unit, LANES).astype(bf16)

    def shares(section, params):
        number = section * nd + dp
        enc_first = jnp.minimum(number * piece, chunk - piece)
        dec_first = [jnp.minimum((h * plan.pieces + number) * unit, chunk - unit) for h in range(2)]
        if plan.parts_in == 1:
            dec_first[0] = jnp.where(grp == plan.full, 0, dec_first[0])
        return (
            share(jnp.where(first_section, enc_first, dec_first[0]), params),
            share(jnp.where(first_section, enc_first + piece - unit, dec_first[1]), params),
        )

    send = shares(1 - sec, params)
    keep = shares(sec, after(params, *send))

    def whole_piece(parts):
        return jnp.concatenate([parts[0][:half], parts[1][unit - half :]])

    routes = [[(z, 2 * z + h) for z in range(plan.full)] for h in range(2)]
    if plan.parts_in == 1:
        routes[0].append((plan.full, 1))
    routes = [completed(route, ng) for route in routes]
    crossed = []
    for h in range(2):
        pairs = [(z, ng + z) for z in range(ng)] + [(ng + a, b) for a, b in routes[h]]
        crossed.append(lax.ppermute(send[h], (SEC, GRP), pairs))
    spread = [lax.ppermute(keep[h], GRP, routes[h]) for h in range(2)]
    enc_piece = jnp.where(first_section, whole_piece(keep), whole_piece(crossed))
    even, odd = (jnp.where(first_section, crossed[h], spread[h]) for h in range(2))
    dec_piece = jnp.where(grp % 2 == 0, even, odd)
    class Gather:
        def __init__(self, here):
            self.here = here
            if ny == 2:
                self.arrays = [here, over_x(here), over_y(here)]
                self.owners = [(sec, yy), (1 - sec, yy), (sec, 1 - yy), (1 - sec, 1 - yy)]
            else:
                column = [here]
                for _ in range(ny - 1):
                    column.append(over_y(column[-1]))
                self.arrays = column
                self.owners = [(s, (yy - k) % ny) for s in (sec, 1 - sec) for k in range(ny)]

        def second(self):
            if ny == 2:
                middle = self.here.shape[0] // 2
                self.corners = [self.arrays[1][:middle], self.arrays[2][middle:]]
            else:
                self.corners = self.arrays
            return tuple(self.corners)

        def third(self):
            if ny == 2:
                self.arrays += [over_y(self.corners[0]), over_x(self.corners[1])]
            else:
                self.arrays = self.arrays + [over_x(block) for block in self.corners]
            return tuple(self.arrays[-2:])

        def fourth(self, joined=True):
            arrays = [jnp.concatenate(self.arrays)] if joined else self.arrays
            return arrays + [over_core(block) for block in arrays]

        def places(self, parts):
            found = []
            for c in (core, 1 - core):
                for s, y in self.owners:
                    for k in parts:
                        number = (grp - k) % ng * plan.pieces + s * nd + y * 2 + c
                        found += [2 * number, 2 * number + 1]
            return found

    last = jnp.logical_and(sec == ns - 1, dp == nd - 1)
    if plan.parts_in == 1:
        dec_piece = jnp.where(jnp.logical_and(last, grp == 1), even, dec_piece)
    else:
        for k in range(plan.parts_in):
            part = share(jnp.minimum(k * unit, chunk - unit), params)
            part = lax.ppermute(part, GRP, [(plan.full, 2 * k + 1)])
            dec_piece = jnp.where(jnp.logical_and(last, grp == 2 * k + 1), part, dec_piece)
    gathers = [Gather(enc_piece)]
    both = jnp.concatenate([enc_piece, dec_piece])
    dec_parts = [dec_piece]
    for k in range(1, ng):
        both = over_z(both)
        if k >= 2:
            both = after(both, *gathers[k - 2].second())
        if k >= 3:
            both = after(both, *gathers[k - 3].third())
        dec_parts.append(both[piece:])
        gathers.append(Gather(both[:piece]))
    gathers[-2].second()
    gathers[-1].second()
    enc_sources, enc_places = [], []
    for k, g in enumerate(gathers):
        if k >= ng - 3:
            g.third()
        enc_sources += g.fourth()
        enc_places += g.places([k])
    enc_places = jnp.stack(enc_places).astype(jnp.int32)
    dec_gather = Gather(after(jnp.concatenate(dec_parts), *gathers[-1].corners))
    dec_places = jnp.stack(dec_gather.places(range(ng))).astype(jnp.int32)

    micro_rows = enc_input.reshape(ROW, WIDTH)
    seg = lax.dynamic_index_in_dim(segments, sec, 0, keepdims=False).reshape(ROW)
    slot = lax.dynamic_index_in_dim(slots, sec, 0, keepdims=False).reshape(ROW)
    cot_rows = jnp.pad(
        cot.reshape(IMAGES_ROW, SLOTS, DEC_WIDTH), ((0, 0), (0, SLOT_PAD - SLOTS), (0, 0))
    ).reshape(IMAGES_ROW * SLOT_PAD, DEC_WIDTH)

    enc_weights = unpack(plan, ENC_LAYOUT, half, piece, ng, room, enc_places, enc_sources)
    dec_gather.arrays[1:] = after(dec_gather.arrays[1:], enc_weights[VECS])
    micro_rows = after(micro_rows, *dec_gather.second())
    saved = dict(
        zip([SENT, H1, QKV, PROBS, ATT, MID, H2, ACT, SLOPE], encode(micro_rows, seg, enc_weights))
    )
    others = {k: over_core(saved[k]) for k in (H1, ATT, H2, ACT)}
    dec_gather.third()
    dec_sources = dec_gather.fourth(False)
    dec_weights = unpack(plan, DEC_LAYOUT, plan.unit // 2, plan.unit, plan.full, plan.dec_room, dec_places, dec_sources)
    dec = dict(
        zip(
            [OUT, H1, QKV_L, ATT, PROJ_L, H2, UP_L, ACT, EMBED_L, GSENT, VECS, GPOS],
            decode(saved[SENT], seg, slot, cot_rows, dec_weights),
        )
    )

    def add(first, *others):
        total = first.astype(f32)
        for other in others:
            total = total + other.astype(f32)
        return total.astype(bf16)

    class Square:
        def __init__(self, tables):
            self.keep, self.sends = tables[0::2], tables[1::2]
            self.m = tables[0].shape[0] // ny

        def second(self, *before):
            m = self.m
            if ny == 2:
                self.ax, self.by = after((over_x(self.sends[0]), over_y(self.sends[1])), *before)
                self.sends = (add(self.keep[0][m:], self.ax[m:]), add(self.keep[1][m:], self.by[m:]))
            else:
                column = add(self.keep[0], after(over_x(self.sends[0]), *before))
                total = column[(ny - 1) * m :]
                for k in range(ny - 2, -1, -1):
                    total = add(column[k * m : (k + 1) * m], over_y(total))
                self.sends = (total,)
            return self.sends

        def third(self, *before):
            m = self.m
            if ny == 2:
                ay, bx = after((over_y(self.sends[0]), over_x(self.sends[1])), *before)
                self.own = (
                    add(self.keep[0][:m], self.ax[:m], ay), add(self.keep[1][:m], self.by[:m], bx),
                )
            else:
                self.own = (self.sends[0][: m // 2], self.sends[0][m // 2 :])
            return self.own

    class Ring:
        def __init__(self, one):
            self.one, self.step = one, 0
            self.total = add(*one(grp - 1))

        def next(self, *before):
            self.total = after(over_z(self.total), *before)
            self.step += 1
            self.total = add(*self.one(grp - 1 - self.step), self.total)
            return self.total

    place = jnp.stack([sec, yy, core]).astype(jnp.int32)
    every = list(range(ng))
    near = ng // 2
    upper, lower = every[near:], every[:near]
    dec_mine, dec_theirs = pack(
        plan, DEC_LAYOUT, plan.dec_regions(), half, ng, True, place,
        {
            EMBED_W: (saved[SENT], dec[EMBED_L]),
            QKV_W: (dec[H1], dec[QKV_L]),
            PROJ_W: (dec[ATT], dec[PROJ_L]),
            UP_W: (dec[H2], dec[UP_L]),
            DOWN_W: (dec[ACT], cot_rows),
            POS: (dec[GPOS], dec[GPOS]),
        },
        dec[VECS],
    )
    dec_core = over_core(dec_theirs)
    grad_sent = after(dec[GSENT], dec_mine)
    grad_other = over_core(grad_sent)
    up_low, proj_low, grad_middle, enc_vec = mlp_back(grad_sent, saved, enc_weights)
    dec_core, grad_other = after((dec_core, grad_other), up_low)

    def dec_block(g):
        rows = 2 * ny * half
        return [lax.dynamic_slice(t, (g % ng * rows, 0), (rows, LANES)) for t in (dec_mine, dec_core)]

    dec_ring = Ring(dec_block)
    up_other, proj_other = over_core(up_low), over_core(proj_low)
    in_grad, qkv_low, enc_vec = attention_back(
        after(grad_middle, dec_ring.total), proj_low, micro_rows, saved, enc_weights, enc_vec
    )
    up_other, proj_other = after((up_other, proj_other), qkv_low)
    qkv_other, vec_other = over_core(qkv_low), over_core(enc_vec)
    others = after(others, enc_vec)
    up_tables = pack_enc(
        plan, plan.enc_regions(upper), piece, len(upper), place,
        {
            DOWN_W: (saved[ACT], others[ACT], grad_sent, grad_other),
            UP_W: (saved[H2], others[H2], up_low, up_other),
        },
        enc_vec, vec_other,
    )
    qkv_other = after(qkv_other, up_tables[0])
    low_tables = pack_enc(
        plan, plan.enc_regions(lower), piece, len(lower), place,
        {
            PROJ_W: (saved[ATT], others[ATT], proj_low, proj_other),
            QKV_W: (saved[H1], others[H1], qkv_low, qkv_other),
            UP_W: (saved[H2], others[H2], up_low, up_other),
        },
        enc_vec, vec_other,
    )
    upper_sum, lower_sum = Square(up_tables), Square(low_tables)
    dec_ring.next(low_tables[0])
    upper_sum.second(low_tables[0], dec_ring.total)
    dec_ring.next(*upper_sum.sends)
    upper_sum.third(dec_ring.total)
    lower_sum.second(*upper_sum.own)
    for _ in range(ng - 3):
        dec_ring.next(*lower_sum.sends)
    m = dec_ring.total.shape[0] // (2 * ny)
    if ny == 2:
        dec_sum = Square([dec_ring.total[k * m : (k + 1) * m] for k in range(4)])
    else:
        dec_sum = Square([dec_ring.total[: ny * m], dec_ring.total[ny * m :]])
    dec_sum.second(*lower_sum.sends)
    lower_sum.third(*dec_sum.sends)
    blocks = list(lower_sum.own) + list(upper_sum.own)

    def enc_block(g):
        g = g % ng
        if ng == 4:
            return [jnp.where(g < 2, jnp.where(g == 0, *blocks[:2]), jnp.where(g == 2, *blocks[2:]))]
        return [lax.dynamic_slice(jnp.concatenate(blocks), (g * piece, 0), (piece, LANES))]

    enc_ring = Ring(enc_block)
    dec_own = jnp.concatenate(dec_sum.third(enc_ring.total))
    back = [[(2 * z + h, z) for z in range(plan.full)] for h in range(2)]
    back[0].append((1, plan.full))
    back.append([(3, plan.full)])
    dec_low, dec_high, dec_rest = (lax.ppermute(dec_own, GRP, completed(pairs, ng)) for pairs in back)
    enc_ring.next()
    dec_own = jnp.concatenate([dec_low, jnp.where(grp == plan.full, dec_rest, dec_high)])
    for _ in range(ng - 2):
        enc_ring.next(dec_own)
    enc_own = enc_ring.total

    own = jnp.where(first_section, enc_own, dec_own)
    other = jnp.where(first_section, dec_own, enc_own)
    if ny == 2:
        from_x, from_y = over_x(other), over_y(own)
        sources = [own, from_x, from_y, over_y(from_x)]
        owners = [(sec, yy), (1 - sec, yy), (sec, 1 - yy), (1 - sec, 1 - yy)]
    else:
        column = [jnp.concatenate([own, over_x(other)])]
        for _ in range(ny - 1):
            column.append(over_y(column[-1]))
        sources = column
        owners = [(s, (yy - k) % ny) for k in range(ny) for s in (sec, 1 - sec)]
    sources = sources + [over_core(block) for block in sources]
    places = []
    for c in (core, 1 - core):
        for s, y in owners:
            number = (c * 2 + s) * ny + y
            places += [
                jnp.where(first_section, 2 * number, number),
                jnp.where(first_section, 2 * number + 1, plan.pieces + number),
            ]
    table = jnp.asarray(plan.segments())[sec, grp].reshape(-1)
    flat = finish(plan, jnp.stack(places).astype(jnp.int32), table, sources)
    param_grad = flat.reshape(1, chunk * LANES)
    dec_out = dec[OUT].reshape(IMAGES_ROW, SLOT_PAD, DEC_WIDTH)[:, :SLOTS]
    return (
        dec_out.reshape(1, 1, IMAGES_ROW * SLOTS, DEC_WIDTH),
        in_grad.reshape(1, 1, ROW, WIDTH),
        param_grad,
    )


def solution(mesh):
    placed = (
        P(SEC, (GRP, DP), None, None),
        P(None, (GRP, DP), None),
        P(None, (GRP, DP), None),
        P(SEC, GRP),
        P(SEC, (GRP, DP), None, None),
    )
    return jax.shard_map(
        partial(per_device, Plan(dict(mesh.shape))),
        mesh=mesh,
        in_specs=placed,
        out_specs=(
            P(SEC, (GRP, DP), None, None),
            P(SEC, (GRP, DP), None, None),
            P(SEC, GRP),
        ),
        check_vma=False,
    )
```

```python
from functools import partial
import math

import jax
import jax.numpy as jnp
import numpy as np
from jax import lax
from jax.experimental import pallas as pl
from jax.experimental.pallas import tpu as pltpu
from jax.sharding import PartitionSpec as P

WIDTH = 768
HEADS = 12
HIDDEN_SIZE = 3072
DEC_WIDTH = 512
DEC_HEADS = 16
DEC_HIDDEN = 2048
SLOTS = 196
IMAGES_ROW = 5
ROW = 256
PARAMS = 7088128
LANES = 128
SEC, GRP, DP = "section", "group", "dp"
(
    N1G, N1B, QKV_W, QB, VB, PROJ_W, PB, N2G,
) = range(0, 8)
(
    N2B, UP_W, UB, DOWN_W, DB, EMBED_W, EB, MT,
) = range(8, 16)
(
    POS, QKV_B, VECS, SENT, H1, QKV, PROBS, ATT,
) = range(16, 24)
(
    MID, H2, ACT, SLOPE, OUT, QKV_L, PROJ_L, UP_L,
) = range(24, 32)
(
    EMBED_L, GSENT, GPOS,
) = range(32, 35)
SLOT_PAD = 208
VMEM_BYTES = 60 * 1024 * 1024

norm_eps = 1e-06
masked_score = -1000000000.0
f32 = jnp.float32
bf16 = jnp.bfloat16


def block_layout(width, hidden):
    return [
        (N1G, (width,)),
        (N1B, (width,)),
        (QKV_W, (width, 3 * width)),
        (QB, (width,)),
        (VB, (width,)),
        (PROJ_W, (width, width)),
        (PB, (width,)),
        (N2G, (width,)),
        (N2B, (width,)),
        (UP_W, (width, hidden)),
        (UB, (hidden,)),
        (DOWN_W, (hidden, width)),
        (DB, (width,)),
    ]


def decoder_layout(enc_width, width, hidden, slot_count):
    return [
        (EMBED_W, (enc_width, width)),
        (EB, (width,)),
        (MT, (width,)),
        (POS, (slot_count, width)),
    ] + block_layout(width, hidden)


ENC_LAYOUT = block_layout(WIDTH, HIDDEN_SIZE)
DEC_LAYOUT = decoder_layout(WIDTH, DEC_WIDTH, DEC_HIDDEN, SLOTS)
VEC = {
    N1G: 0,
    N1B: 1,
    QKV_B: 2,
    PB: 3,
    N2G: 4,
    N2B: 5,
    UB: 6,
    DB: 7,
    EB: 8,
    MT: 9,
}
VEC_ROWS = 16


def dot(a, b):
    return lax.dot_general(a, b, (((1,), (0,)), ((), ())), preferred_element_type=f32)


def dot_nt(a, b):
    return lax.dot_general(a, b, (((1,), (1,)), ((), ())), preferred_element_type=f32)


def dot_tn(a, b):
    return lax.dot_general(a, b, (((0,), (0,)), ((), ())), preferred_element_type=f32)


def normalised(values):
    centered = values - jnp.mean(values, axis=-1, keepdims=True)
    inverse = lax.rsqrt(jnp.mean(centered * centered, axis=-1, keepdims=True) + norm_eps)
    return centered * inverse, inverse


def norm_back(grad, hat, inverse, gain):
    scaled = grad * gain
    first = jnp.mean(scaled, axis=-1, keepdims=True)
    second = jnp.mean(scaled * hat, axis=-1, keepdims=True)
    return inverse * (scaled - first - hat * second)


def col_sum(values):
    return jnp.sum(values, axis=0, keepdims=True)


def gelu_parts(upward):
    half = 0.5 + 0.5 * lax.erf(upward * f32(math.sqrt(0.5)))
    slope = half + upward * (jnp.exp(upward * upward * f32(-0.5)) * f32(1.0 / math.sqrt(2.0 * math.pi)))
    return upward * half, slope


def head_mask(head, head_dim):
    lane = lax.broadcasted_iota(jnp.int32, (1, LANES), 1)
    return jnp.where(lane // head_dim == head, 1.0, 0.0).astype(bf16)


def lane_block(group, start=0):
    if isinstance(group, int):
        return slice(start + group * LANES, start + (group + 1) * LANES)
    return pl.ds(pl.multiple_of(start + group * LANES, LANES), LANES)


def flip(values):
    return values.astype(f32).T.astype(bf16)


def attention_forward(qkv_ref, probs_ref, joined_ref, width, heads, keep):
    head_dim = width // heads
    scale = f32(head_dim ** (-0.5))
    per_group = LANES // head_dim

    def one_group(group):
        queries = qkv_ref[:, lane_block(group)]
        keys = qkv_ref[:, lane_block(group, width)]
        values_t = flip(qkv_ref[:, lane_block(group, 2 * width)])
        subs = range(per_group)
        scores = [dot_nt(keys, queries * head_mask(sub, head_dim)) for sub in subs]
        scores = [keep(s * scale) for s in scores]
        expo = [jnp.exp(s - jnp.max(s, axis=0, keepdims=True)) for s in scores]
        probs = [e * (1.0 / col_sum(e)) for e in expo]
        for sub in subs:
            probs_ref[group * per_group + sub] = probs[sub]
        outs = [
            dot(values_t[sub * head_dim : (sub + 1) * head_dim], probs[sub].astype(bf16)) for sub in subs
        ]
        joined_ref[lane_block(group), :] = jnp.concatenate(outs, axis=0)

    if width == WIDTH:
        lax.fori_loop(0, width // LANES, lambda g, c: (one_group(g), c)[1], 0)
    else:
        for group in range(width // LANES):
            one_group(group)


def attention_backward(qkv_ref, probs_ref, grad_ref, low_ref, width, heads):
    head_dim = width // heads
    scale = f32(head_dim ** (-0.5))
    per_group = LANES // head_dim

    def one_group(group):
        queries = qkv_ref[:, lane_block(group)]
        keys = qkv_ref[:, lane_block(group, width)]
        values = qkv_ref[:, lane_block(group, 2 * width)]
        grads = grad_ref[:, lane_block(group)]
        keys_t = flip(keys)
        subs = range(per_group)
        masks = [head_mask(sub, head_dim) for sub in subs]
        own = [grads * m for m in masks]
        grad_probs = [dot_nt(values, o) for o in own]
        probs = [probs_ref[group * per_group + sub] for sub in subs]
        grad_values = sum(dot(p.astype(bf16), o) for p, o in zip(probs, own))
        low = [
            (p * (g - col_sum(p * g))).astype(bf16) for p, g in zip(probs, grad_probs)
        ]
        grad_keys = sum(dot(l, queries * m) for l, m in zip(low, masks))
        grad_queries = [
            dot(keys_t[sub * head_dim : (sub + 1) * head_dim], low[sub]) for sub in subs
        ]
        low_ref[:, lane_block(group)] = (jnp.concatenate(grad_queries, axis=0).T * scale).astype(bf16)
        low_ref[:, lane_block(group, width)] = (grad_keys * scale).astype(bf16)
        low_ref[:, lane_block(group, 2 * width)] = grad_values.astype(bf16)

    for group in range(width // LANES):
        one_group(group)


class Late:
    def __init__(self, source, target, sem):
        self.copy, self.target, self.shape = pltpu.make_async_copy(source, target, sem), target, target.shape
        self.here = False
        self.copy.start()

    def arrive(self):
        if not self.here:
            self.copy.wait()
            self.here = True

    def __getitem__(self, index):
        self.arrive()
        return self.target[index]


def late_call(kernel, early, late, outs, scratch, **options):
    count, many = len(early), len(late)

    def body(*refs):
        sources, results = refs[count : count + many], refs[count + many : count + many + len(outs)]
        rest = refs[count + many + len(outs) :]
        held, sems = rest[:many], rest[many]
        lates = [Late(sources[k], held[k], sems.at[k]) for k in range(many)]
        kernel(*refs[:count], *lates, *results, *rest[many + 1 :])
        for each in lates:
            each.arrive()

    return pl.pallas_call(
        body,
        in_specs=[pl.BlockSpec(memory_space=m) for _, m in early] + [pl.BlockSpec(memory_space=pl.ANY)] * many,
        out_specs=[pl.BlockSpec(memory_space=m) for _, m in outs],
        out_shape=[o for o, _ in outs],
        scratch_shapes=[pltpu.VMEM(a.shape, a.dtype) for a in late]
        + [pltpu.SemaphoreType.DMA((many,))]
        + list(scratch),
        compiler_params=params_of(),
        **options,
    )(*[a for a, _ in early], *late)


def encode_kernel(plan, counts, place_ref, *refs):
    sources, refs = refs[: len(counts)], refs[len(counts) :]
    x_ref, seg_row_ref, seg_col_ref = refs[:3]
    weight_outs, vec = refs[3:7], refs[7]
    (
        sent_ref, normed1_ref, qkv_ref, probs_ref, attended_ref, middle_ref, normed2_ref, active_ref,
        slope_ref,
    ) = refs[8:17]
    held, wide, spare, sems, out_sems, joined_ref = refs[17:23]
    weights = refs[23:27]
    qkv_w, proj_w, up_w, down_w = weights
    copies = [pltpu.make_async_copy(w, o, out_sems.at[k]) for k, (w, o) in enumerate(zip(weights, weight_outs))]
    unpack_weights(
        plan, ENC_LAYOUT, plan.half, plan.piece, plan.ng, plan.room, place_ref, sources, counts,
        weights, vec, held, wide, spare, sems, copies,
    )
    width, hidden = WIDTH, HIDDEN_SIZE
    inputs = x_ref[...].astype(f32)
    hat, _ = normalised(inputs)
    normed1 = (hat * vec[0:1, :width] + vec[1:2, :width]).astype(bf16)
    normed1_ref[...] = normed1
    qkv_ref[...] = (dot(normed1, qkv_w[...]) + vec[2:3, : 3 * width]).astype(bf16)
    allowed = seg_col_ref[...] == seg_row_ref[...]
    attention_forward(
        qkv_ref, probs_ref, joined_ref, width, HEADS,
        lambda scores: jnp.where(allowed, scores, f32(masked_score)),
    )
    attended = joined_ref[...].T.astype(bf16)
    attended_ref[...] = attended
    middle = inputs + (dot(attended, proj_w[...]) + vec[3:4, :width])
    middle_ref[...] = middle
    hat, _ = normalised(middle)
    normed2_ref[...] = (hat * vec[4:5, :width] + vec[5:6, :width]).astype(bf16)
    joined_ref[...] = jnp.zeros_like(joined_ref)
    total = jnp.zeros((inputs.shape[0], width), f32)
    part = 1536
    for start in range(0, hidden, part):
        cols = slice(start, start + part)
        upward = dot(normed2_ref[...], up_w[:, cols]) + vec[6:7, cols]
        active, slope = gelu_parts(upward)
        active_ref[:, cols] = active.astype(bf16)
        slope_ref[:, cols] = slope.astype(slope_ref.dtype)
        total += dot(active_ref[:, cols], down_w[cols, :])
    sent_ref[...] = (middle + (total + vec[7:8, :width])).astype(bf16)
    for copy in copies:
        copy.wait()


def mlp_back_kernel(
    grad_ref, down_w, slope_ref, up_w, middle_ref, vec,
    up_low_ref, proj_low_ref, grad_middle_ref, vec_grad,
):
    width, hidden = WIDTH, HIDDEN_SIZE
    grad_out = grad_ref[...]
    vec_grad[...] = jnp.zeros_like(vec_grad)
    vec_grad[7:8, :width] = col_sum(grad_out.astype(f32))
    grad_normed2 = jnp.zeros((grad_out.shape[0], width), f32)
    part = 3072
    for start in range(0, hidden, part):
        cols = slice(start, start + part)
        low = (dot_nt(grad_out, down_w[cols, :]) * slope_ref[:, cols]).astype(bf16)
        up_low_ref[:, cols] = low
        vec_grad[6:7, cols] = col_sum(low.astype(f32))
        grad_normed2 += dot_nt(low, up_w[:, cols])
    hat, inverse = normalised(middle_ref[...])
    vec_grad[4:5, :width] = col_sum(grad_normed2 * hat)
    vec_grad[5:6, :width] = col_sum(grad_normed2)
    grad_middle = grad_out.astype(f32) + norm_back(grad_normed2, hat, inverse, vec[4:5, :width])
    grad_middle_ref[...] = grad_middle
    proj_low = grad_middle.astype(bf16)
    proj_low_ref[...] = proj_low
    vec_grad[3:4, :width] = col_sum(proj_low.astype(f32))


def attention_back_kernel(
    proj_low_ref, proj_w, qkv_ref, probs_ref, qkv_w, x_ref, vec_in, vec, grad_middle_ref,
    in_grad_ref, qkv_low_ref, vec_grad, grad_att_ref,
):
    width = WIDTH
    grad_att_ref[...] = dot_nt(proj_low_ref[...], proj_w[...]).astype(bf16)
    attention_backward(qkv_ref, probs_ref, grad_att_ref, qkv_low_ref, width, HEADS)
    qkv_low = qkv_low_ref[...]
    vec_grad[...] = vec_in[...]
    vec_grad[2:3, : 3 * width] = col_sum(qkv_low.astype(f32))
    grad_normed1 = dot_nt(qkv_low, qkv_w[...])
    hat, inverse = normalised(x_ref[...].astype(f32))
    vec_grad[0:1, :width] = col_sum(grad_normed1 * hat)
    vec_grad[1:2, :width] = col_sum(grad_normed1)
    in_grad_ref[...] = grad_middle_ref[...] + norm_back(grad_normed1, hat, inverse, vec[0:1, :width])


def decode_kernel(plan, counts, place_ref, *refs):
    sources, refs = refs[: len(counts)], refs[len(counts) :]
    sent_ref, seg_row, slot_row, seg_col, slot_col, cot_ref = refs[:6]
    (
        out_ref, normed1_ref, qkv_low_ref, attended_ref, proj_low_ref, normed2_ref, up_low_ref,
        active_ref, embed_low_ref, grad_sent_ref, vec_grad, pos_grad,
    ) = refs[6:18]
    embedded_ref, embed_sum, qkv_ref, probs_ref, joined_ref, grad_att_ref = refs[18:24]
    held, wide, spare, sems, vec = refs[24:29]
    weights = refs[29:]
    embed_w, pos_ref, qkv_w, proj_w, up_w, down_w = weights
    width, hidden = DEC_WIDTH, DEC_HIDDEN
    image = pl.program_id(0)
    length = SLOT_PAD

    @pl.when(image == 0)
    def _():
        unpack_weights(
            plan, DEC_LAYOUT, plan.unit // 2, plan.unit, plan.full, plan.dec_room, place_ref, sources, counts,
            weights, vec, held, wide, spare, sems,
        )
        embedded_ref[...] = (dot(sent_ref[...], embed_w[...]) + vec[8:9, :width]).astype(bf16)
        vec_grad[...] = jnp.zeros_like(vec_grad)
        pos_grad[...] = jnp.zeros_like(pos_grad)
        embed_sum[...] = jnp.zeros_like(embed_sum)

    def add_vec(row, values):
        vec_grad[row : row + 1, : values.shape[1]] += values

    place = lax.broadcasted_iota(jnp.int32, (length, ROW), 0)
    match = (seg_row[...] == image) & (slot_row[...] == place)
    onehot = jnp.where(match, 1.0, 0.0)
    free = 1.0 - jnp.sum(onehot, axis=1, keepdims=True)
    x = dot(onehot.astype(bf16), embedded_ref[...]) + free * vec[9:10, :width] + pos_ref[...].astype(f32)
    hat1, inverse1 = normalised(x)
    normed1 = (hat1 * vec[0:1, :width] + vec[1:2, :width]).astype(bf16)
    normed1_ref[...] = normed1
    qkv_ref[...] = (dot(normed1, qkv_w[...]) + vec[2:3, : 3 * width]).astype(bf16)
    key_place = lax.broadcasted_iota(jnp.int32, (length, length), 0)
    attention_forward(
        qkv_ref, probs_ref, joined_ref, width, DEC_HEADS,
        lambda scores: jnp.where(key_place < SLOTS, scores, f32(-1e30)),
    )
    attended = joined_ref[...].T.astype(bf16)
    attended_ref[...] = attended
    middle = x + (dot(attended, proj_w[...]) + vec[3:4, :width])
    hat2, inverse2 = normalised(middle)
    normed2 = (hat2 * vec[4:5, :width] + vec[5:6, :width]).astype(bf16)
    normed2_ref[...] = normed2
    cot = cot_ref[...]
    add_vec(7, col_sum(cot.astype(f32)))
    total = jnp.zeros((length, width), f32)
    grad_normed2 = jnp.zeros((length, width), f32)
    part = 1024
    for start in range(0, hidden, part):
        cols = slice(start, start + part)
        upward = dot(normed2_ref[...], up_w[:, cols]) + vec[6:7, cols]
        active, slope = gelu_parts(upward)
        active = active.astype(bf16)
        active_ref[:, cols] = active
        total += dot(active, down_w[cols, :])
        low = (dot_nt(cot_ref[...], down_w[cols, :]) * slope).astype(bf16)
        up_low_ref[:, cols] = low
        vec_grad[6:7, cols] += col_sum(low.astype(f32))
        grad_normed2 += dot_nt(low, up_w[:, cols])
    out_ref[...] = (middle + (total + vec[7:8, :width])).astype(bf16)

    add_vec(4, col_sum(grad_normed2 * hat2))
    add_vec(5, col_sum(grad_normed2))
    grad_middle = cot.astype(f32) + norm_back(grad_normed2, hat2, inverse2, vec[4:5, :width])
    proj_low = grad_middle.astype(bf16)
    proj_low_ref[...] = proj_low
    add_vec(3, col_sum(proj_low.astype(f32)))
    grad_att_ref[...] = dot_nt(proj_low, proj_w[...]).astype(bf16)
    attention_backward(qkv_ref, probs_ref, grad_att_ref, qkv_low_ref, width, DEC_HEADS)
    qkv_low = qkv_low_ref[...]
    add_vec(2, col_sum(qkv_low.astype(f32)))
    grad_normed1 = dot_nt(qkv_low, qkv_w[...])
    add_vec(0, col_sum(grad_normed1 * hat1))
    add_vec(1, col_sum(grad_normed1))
    grad_in = grad_middle + norm_back(grad_normed1, hat1, inverse1, vec[0:1, :width])
    low_in = grad_in.astype(bf16)
    wide = low_in.astype(f32)
    add_vec(9, col_sum(free * wide))
    pos_grad[...] += wide
    place_t = lax.broadcasted_iota(jnp.int32, (ROW, length), 1)
    match_t = (seg_col[...] == image) & (slot_col[...] == place_t)
    embed_sum[...] += dot(jnp.where(match_t, 1.0, 0.0).astype(bf16), low_in)

    @pl.when(image == IMAGES_ROW - 1)
    def _():
        embed_low = embed_sum[...].astype(bf16)
        embed_low_ref[...] = embed_low
        add_vec(8, col_sum(embed_low.astype(f32)))
        grad_sent_ref[...] = dot_nt(embed_low, embed_w[...]).astype(bf16)


def cost(microseconds):
    return pl.CostEstimate(flops=int(microseconds * 1e11), bytes_accessed=int(microseconds * 3e8), transcendentals=0)


def params_of(**extra):
    return pltpu.CompilerParams(vmem_limit_bytes=VMEM_BYTES, **extra)


def shape(dims, kind):
    return jax.ShapeDtypeStruct(dims, kind)


def unpack_scratch(chunks, room):
    return [
        pltpu.VMEM((chunks * room, LANES), bf16),
        pltpu.VMEM((3200, LANES), f32),
        pltpu.VMEM((3200, LANES), f32),
        pltpu.SemaphoreType.DMA((chunks,)),
    ]


def encode(plan, place, sources, x, seg):
    width, hidden, length = WIDTH, HIDDEN_SIZE, ROW
    weights = [shape(e, bf16) for _, e in ENC_LAYOUT if len(e) == 2]
    kept = [
        shape((VEC_ROWS, hidden), f32),
        shape((length, width), bf16),
        shape((length, width), bf16),
        shape((length, 3 * width), bf16),
        shape((HEADS, length, length), f32),
        shape((length, width), bf16),
        shape((length, width), f32),
        shape((length, width), bf16),
        shape((length, hidden), bf16),
        shape((length, hidden), bf16),
    ]
    result = pl.pallas_call(
        partial(encode_kernel, plan, [s.shape[0] // plan.half for s in sources]),
        in_specs=[pl.BlockSpec(memory_space=pltpu.SMEM)]
        + [pl.BlockSpec(memory_space=pl.ANY)] * len(sources)
        + [pl.BlockSpec(memory_space=pltpu.VMEM)] * 3,
        out_specs=[pl.BlockSpec(memory_space=pl.ANY)] * 4 + [pl.BlockSpec(memory_space=pltpu.VMEM)] * len(kept),
        out_shape=weights + kept,
        scratch_shapes=unpack_scratch(plan.ng, plan.room)
        + [pltpu.SemaphoreType.DMA((4,)), pltpu.VMEM((width, length), f32)]
        + [pltpu.VMEM(w.shape, bf16) for w in weights],
        compiler_params=params_of(),
        cost_estimate=cost(24),
        name="encode",
    )(place, *sources, x, seg.reshape(1, length), seg.reshape(length, 1))
    weights = dict(zip([QKV_W, PROJ_W, UP_W, DOWN_W, VECS], result))
    return weights, dict(zip([SENT, H1, QKV, PROBS, ATT, MID, H2, ACT, SLOPE], result[5:]))


def mlp_back(grad, saved, weights):
    width, hidden, length = WIDTH, HIDDEN_SIZE, ROW
    return late_call(
        mlp_back_kernel,
        [],
        [grad, weights[DOWN_W], saved[SLOPE], weights[UP_W], saved[MID], weights[VECS]],
        [
            (shape((length, hidden), bf16), pltpu.VMEM),
            (shape((length, width), bf16), pltpu.VMEM),
            (shape((length, width), f32), pltpu.VMEM),
            (shape((VEC_ROWS, hidden), f32), pltpu.VMEM),
        ],
        [],
        cost_estimate=cost(9),
        name="mlp_back",
    )


def attention_back(grad_middle, proj_low, x, saved, weights, vec_grad):
    width, hidden, length = WIDTH, HIDDEN_SIZE, ROW
    return late_call(
        attention_back_kernel,
        [],
        [
            proj_low, weights[PROJ_W], saved[QKV], saved[PROBS], weights[QKV_W], x, vec_grad, weights[VECS],
            grad_middle,
        ],
        [
            (shape((length, width), f32), pltpu.VMEM),
            (shape((length, 3 * width), bf16), pltpu.VMEM),
            (shape((VEC_ROWS, hidden), f32), pltpu.VMEM),
        ],
        [pltpu.VMEM((length, width), bf16)],
        cost_estimate=cost(10),
        name="attention_back",
    )


def decode(plan, place, sources, sent, seg, slot, cot):
    width, hidden, length = DEC_WIDTH, DEC_HIDDEN, SLOT_PAD
    held = [sent, seg.reshape(1, ROW), slot.reshape(1, ROW), seg.reshape(ROW, 1), slot.reshape(ROW, 1)]

    def whole(array):
        return pl.BlockSpec(array.shape, lambda i: (0,) * array.ndim, pipeline_mode=pl.Buffered(1))

    def image(cols):
        return pl.BlockSpec((length, cols), lambda i: (i, 0))

    rows = IMAGES_ROW * length
    per_image = [width, width, 3 * width, width, width, width, hidden, hidden]
    kept = [
        shape((ROW, width), bf16),
        shape((ROW, WIDTH), bf16),
        shape((VEC_ROWS, hidden), f32),
        shape((length, width), f32),
    ]
    return pl.pallas_call(
        partial(decode_kernel, plan, [s.shape[0] // (plan.unit // 2) for s in sources]),
        grid=(IMAGES_ROW,),
        in_specs=[pl.BlockSpec(memory_space=pltpu.SMEM)]
        + [pl.BlockSpec(memory_space=pl.ANY)] * len(sources)
        + [whole(a) for a in held]
        + [image(width)],
        out_specs=[image(c) for c in per_image]
        + [pl.BlockSpec(s.shape, lambda i: (0, 0)) for s in kept],
        out_shape=[shape((rows, c), bf16) for c in per_image] + kept,
        scratch_shapes=[
            pltpu.VMEM((ROW, width), bf16),
            pltpu.VMEM((ROW, width), f32),
            pltpu.VMEM((length, 3 * width), bf16),
            pltpu.VMEM((DEC_HEADS, length, length), f32),
            pltpu.VMEM((width, length), f32),
            pltpu.VMEM((length, width), bf16),
        ]
        + unpack_scratch(plan.full, plan.dec_room)
        + [pltpu.VMEM((VEC_ROWS, hidden), f32)]
        + [
            pltpu.VMEM((SLOT_PAD if n == POS else e[0], e[1]), bf16) for n, e in DEC_LAYOUT if len(e) == 2
        ],
        compiler_params=params_of(dimension_semantics=("arbitrary",)),
        cost_estimate=cost(85),
        name="decode",
    )(place, *sources, *held, cot)


def rows_of(extent):
    return math.prod(extent) // LANES


def up_to(value, step):
    return -(-value // step) * step


def flat_starts(layout):
    starts, here = {}, 0
    for name, extent in layout:
        starts[name] = here
        here += rows_of(extent)
    return starts, here


def kept_starts(layout):
    starts, here = {}, 0
    for name, extent in layout:
        starts[name] = here
        here += up_to(rows_of(extent), 16)
    return starts, here


class Plan:
    def __init__(self, mesh_shape):
        self.ns, self.ng, self.nd = (mesh_shape[a] for a in (SEC, GRP, DP))
        self.ny = self.nd // 2
        self.chunk = PARAMS // LANES // self.ng
        self.pieces = self.ns * self.nd
        self.piece = up_to(-(-self.chunk // self.pieces), 64)
        self.half = self.piece // 2
        self.room = self.piece * self.pieces
        self.tables = 4 if self.ny == 2 else 2
        self.units = 2 * self.pieces
        self.full = self.ng // 2
        self.rest = flat_starts(DEC_LAYOUT)[1] - self.full * self.chunk
        assert 0 < self.rest <= self.chunk
        self.unit = up_to(-(-self.chunk // (self.units - 1)), 64)
        self.dec_room = self.unit * self.units
        whole = self.chunk // self.unit * self.unit
        self.part_in = self.unit if whole < self.dec_room - self.unit else 0
        self.parts_in = -(-self.rest // self.part_in)
        assert self.parts_in <= self.full
        self.enc_starts = [self.kept_row(ENC_LAYOUT, z * self.chunk) // 16 * 16 for z in range(self.ng)]
        self.enc_ends = [
            up_to(self.kept_row(ENC_LAYOUT, min((z + 1) * self.chunk, flat_starts(ENC_LAYOUT)[1]) - 1) + 1, 16)
            for z in range(self.ng)
        ]
        self.dec_starts = [self.kept_row(DEC_LAYOUT, z * self.chunk) // 16 * 16 for z in range(self.full)]
        self.dec_ends = [
            up_to(self.kept_row(DEC_LAYOUT, (z + 1) * self.chunk - 1) + 1, 16) for z in range(self.full)
        ]
        assert all(e - s <= self.room for s, e in zip(self.enc_starts, self.enc_ends))
        self.rest_start = self.kept_row(DEC_LAYOUT, self.full * self.chunk) // 16 * 16
        self.rest_end = kept_starts(DEC_LAYOUT)[1]
        self.part_out = [self.room - (self.dec_ends[k] - self.dec_starts[k]) for k in range(2)]
        assert max(self.part_out) <= self.room // 2
        assert self.part_out[0] < self.rest_end - self.rest_start <= sum(self.part_out)

    def kept_row(self, layout, flat_row):
        flat, _ = flat_starts(layout)
        kept, _ = kept_starts(layout)
        for name, extent in layout:
            if flat_row < flat[name] + rows_of(extent):
                return kept[name] + flat_row - flat[name]
        return kept[name] + rows_of(extent)

    def ranges(self, first, count, cut, chunks, chunk_room):
        found = []
        whole = self.chunk // cut * cut
        while count:
            z, row = divmod(first, self.chunk)
            if z >= chunks:
                k, row = divmod(row, self.part_in)
                here, room = (k + 1) * chunk_room - cut + row, self.part_in - row
            elif row < whole:
                here, room = z * chunk_room + row, whole - row
            else:
                here, room = z * chunk_room + row + cut - (self.chunk - whole), self.chunk - row
            take = min(count, room)
            found.append((here, take))
            first, count = first + take, count - take
        return found

    def packed_row(self, size, groups, group_first, index, row, away_x, away_y):
        owner = away_x * self.ny + away_y
        turned = away_y * 2 + away_x
        if self.ny != 2:
            first = index * (2 * self.ny) + owner if group_first else owner * groups + index
            return first * size + row
        if group_first:
            second, row = divmod(row, size // 2)
            return index * (4 * size) + second * (2 * size) + (turned if second else owner) * (size // 2) + row
        second, index = divmod(index, groups // 2)
        half = groups // 2 * size
        return second * (4 * half) + (turned if second else owner) * half + index * size + row

    def enc_regions(self, groups):
        return [(self.enc_starts[z], self.enc_ends[z], k, 0) for k, z in enumerate(groups)]

    def dec_regions(self):
        length = self.room // 2
        found = []
        for z in range(self.full):
            low, high = self.dec_starts[z], self.dec_ends[z]
            found += [(low, low + length, 2 * z, 0), (low + length, high, 2 * z + 1, 0)]
        middle = self.rest_start + self.part_out[0]
        found.append((self.rest_start, middle, 1, length - self.part_out[0]))
        found.append((middle, self.rest_end, 3, length - self.part_out[1]))
        return found

    def segments(self):
        count = len(DEC_LAYOUT) + 2
        table = np.zeros((self.ns, self.ng, count, 3), np.int32)
        length = self.room // 2
        for s, layout in enumerate((ENC_LAYOUT, DEC_LAYOUT)):
            flat, used = flat_starts(layout)
            for z in range(self.ng):
                low, high = z * self.chunk, (z + 1) * self.chunk
                found = []
                for name, extent in layout:
                    first, last = max(flat[name], low), min(flat[name] + rows_of(extent), high)
                    while first < last:
                        row, stop = self.kept_row(layout, first), last
                        if s == 0:
                            source = row - self.enc_starts[z]
                        elif z < self.full:
                            source = row - self.dec_starts[z]
                        else:
                            row -= self.rest_start
                            k = int(row >= self.part_out[0])
                            row -= k * self.part_out[0]
                            source = (k + 1) * length - self.part_out[k] + row
                            stop = min(last, first + self.part_out[k] - row)
                        found.append((source, first - low, -(-(stop - first) // 8)))
                        first = stop
                if used < high:
                    found.append((self.room, max(used - low, 0), 1))
                table[s, z, : len(found)] = found
        return table


def widen_block(held, wide, spare, ranges):
    def load(start, count):
        first = start // 16 * 16
        size = up_to(start + count - first, 16)
        return held[first : first + size, :].astype(f32), size, start - first

    if len(ranges) == 1:
        block, size, skip = load(*ranges[0])
        wide[0:size, :] = block
        return skip
    here = 0
    for start, count in ranges:
        block, size, skip = load(start, count)
        spare[0:size, :] = block
        wide[here : here + count, :] = spare[skip : skip + count, :]
        here += count
    return 0


def unpack_weights(
    plan, layout, unit, cut, chunks, room, place_ref, sources, counts, outs, vec, held, wide, spare, sems, copies=(),
):
    matrices = [n for n, e in layout if len(e) == 2]
    per_chunk = room // unit
    number = 0
    for source, count in zip(sources, counts):
        for k in range(count):
            slot = place_ref[number]
            number += 1
            target = held.at[pl.ds(pl.multiple_of(slot * unit, 16), unit), :]
            pltpu.make_async_copy(source.at[pl.ds(k * unit, unit), :], target, sems.at[slot // per_chunk]).start()
    arrived = set()

    def arrive(ranges):
        for start, count in ranges:
            z = start // room
            if z not in arrived:
                arrived.add(z)
                part = held.at[pl.ds(z * room, room), :]
                pltpu.make_async_copy(part, part, sems.at[z]).wait()

    vec[...] = jnp.zeros_like(vec)
    flat, _ = flat_starts(layout)
    by_name = dict(zip(matrices, outs))
    order = dict(zip(matrices, copies))
    for name, extent in layout:
        if len(extent) == 2:
            depth, lanes = extent[0], extent[1] // LANES
            step = depth if name == POS else max(128, 2048 // lanes // 128 * 128)
            out = by_name[name]
            if name == POS:
                out[...] = jnp.zeros_like(out)
            for first in range(0, depth, step):
                size = min(step, depth - first)
                ranges = plan.ranges(flat[name] + first * lanes, size * lanes, cut, chunks, room)
                arrive(ranges)
                skip = widen_block(held, wide, spare, ranges)
                for j in range(lanes):
                    block = wide[pl.ds(skip + j, size, stride=lanes), :].astype(bf16)
                    out[first : first + size, j * LANES : (j + 1) * LANES] = block
            if name in order:
                order[name].start()
        else:
            lanes = extent[0] // LANES
            ranges = plan.ranges(flat[name], lanes, cut, chunks, room)
            arrive(ranges)
            skip = widen_block(held, wide, spare, ranges)
            row, shift = {QB: (2, 0), VB: (2, 2 * extent[0])}.get(name, (VEC.get(name), 0))
            for j in range(lanes):
                vec[row : row + 1, shift + j * LANES : shift + (j + 1) * LANES] = wide[skip + j : skip + j + 1, :]
    for z in range(chunks):
        arrive([(z * room, 1)])


def pack_kernel(plan, layout, names, regions, size, groups, group_first, place_ref, *refs):
    pairs = {}
    for name in names:
        pairs[name], refs = refs[:2], refs[2:]
    vec, refs = refs[0], refs[1:]
    pos = None
    if POS in names:
        pos, refs = pairs[POS][0], refs
    mine, theirs, wide, stage, small, sems = refs
    kept, _ = kept_starts(layout)
    extents = dict(layout)
    ny = plan.ny

    def send(source, first, rows, sem):
        moved = 0
        for low, high, index, base in regions:
            start, stop = max(first, low), min(first + rows, high)
            while start < stop:
                number, row = divmod(base + start - low, size)
                c, s, y = number // (2 * ny), number // ny % 2, number % ny
                away_x, away_y = lax.rem(s - place_ref[0] + 2, 2), lax.rem(y - place_ref[1] + ny, ny)
                count = min(stop - start, size - row)
                if group_first:
                    count = min(count, size // 2 - row % (size // 2))
                where = plan.packed_row(size, groups, group_first, index, row, away_x, away_y)
                target = pl.ds(pl.multiple_of(where, 16), count)
                block = source.at[pl.ds(start - first, count), :]
                for same, table in ((True, mine), (False, theirs)):

                    @pl.when((place_ref[2] == c) == same)
                    def _():
                        pltpu.make_async_copy(block, table.at[target, :], sem).start()

                moved += count
                start += count
        return moved

    def wait(rows, slot):
        if rows:
            block = stage.at[slot, pl.ds(0, rows), :]
            pltpu.make_async_copy(block, block, sems.at[slot]).wait()

    turn = 0
    pending = [0, 0]
    for name in names:
        if name == POS:
            continue
        left, right = pairs[name]
        depth, width = extents[name]
        lanes = width // LANES
        step = max(k for k in (128, 256, 384, 512) if depth % k == 0 and k * lanes <= 3072)
        rows = step * lanes
        for first in range(0, depth, step):
            start = kept[name] + first * lanes
            if all(start >= high or start + rows <= low for low, high, _, _ in regions):
                continue
            slot = turn % 2
            turn += 1
            columns = flip(left[:, first : first + step])
            part = 256
            for start in range(0, width, part):
                block = dot(columns, right[:, start : start + part])
                for j in range(part // LANES):
                    wide[pl.ds(start // LANES + j, step, stride=lanes), :] = block[:, j * LANES : (j + 1) * LANES]
            wait(pending[slot], slot)
            stage[slot, 0:rows, :] = wide[0:rows, :].astype(bf16)
            pending[slot] = send(stage.at[slot], kept[name] + first * lanes, rows, sems.at[slot])
    here = 0
    total = 0
    for name, extent in layout:
        if name not in names and len(extent) == 2 or name not in kept_names(names):
            continue
        if len(extent) == 2 and name != POS:
            continue
        rows = rows_of(extent)
        room = up_to(rows, 16)
        wide[0:room, :] = jnp.zeros((room, LANES), f32)
        if name == POS:
            lanes = extent[1] // LANES
            for j in range(lanes):
                wide[pl.ds(j, extent[0], stride=lanes), :] = pos[0 : extent[0], j * LANES : (j + 1) * LANES]
        else:
            row, shift = {QB: (2, 0), VB: (2, 2 * extent[0])}.get(name, (VEC.get(name), 0))
            for j in range(rows):
                wide[j : j + 1, :] = vec[row : row + 1, shift + j * LANES : shift + (j + 1) * LANES]
        small[here : here + room, :] = wide[0:room, :].astype(bf16)
        total += send(small.at[pl.ds(here, room), :], kept[name], room, sems.at[2])
        here += room
    wait(pending[0], 0)
    wait(pending[1], 1)
    block = small.at[pl.ds(0, total), :]
    pltpu.make_async_copy(block, block, sems.at[2]).wait()


def pack_enc_kernel(plan, names, regions, size, groups, place_ref, *refs):
    pairs = {}
    for name in names:
        pairs[name], refs = refs[:4], refs[4:]
    vec, vec_other, *tables = refs[: 2 + plan.tables]
    wide, stage, small, sems = refs[2 + plan.tables :]
    lates = [a for four in pairs.values() for a in four] + [vec, vec_other]
    kept, _ = kept_starts(ENC_LAYOUT)
    extents = dict(ENC_LAYOUT)
    ny = plan.ny

    def pieces(first, rows, core):
        for low, high, index, base in regions:
            start, stop = max(first, low), min(first + rows, high)
            while start < stop:
                number, row = divmod(base + start - low, size)
                count = min(stop - start, size - row)
                if number // (2 * ny) == core:
                    yield start - first, count, index, row, number // ny % 2, number % ny
                start += count

    def send(source, first, rows, sem, core):
        moved = 0
        for skip, count, index, row, s, y in pieces(first, rows, core):
            away_x, away_y = lax.rem(s - place_ref[0] + 2, 2), lax.rem(y - place_ref[1] + ny, ny)
            if ny == 2 and index >= groups // 2:
                keep, away, other, index = tables[2:], away_y, away_x, index - groups // 2
            else:
                keep, away, other = tables[:2], away_x, away_y
            length = (groups // 2 if ny == 2 else groups) * size
            target = pl.ds(pl.multiple_of(other * length, 16) + index * size + row, count)
            block = source.at[pl.ds(skip, count), :]
            for k in range(2):

                @pl.when(away == k)
                def _():
                    pltpu.make_async_copy(block, keep[k].at[target, :], sem).start()

            moved += count
        return moved

    def wait(rows, slot):
        if rows:
            block = stage.at[slot, pl.ds(0, rows), :]
            pltpu.make_async_copy(block, block, sems.at[slot]).wait()

    def run(core):
        turn = 0
        pending = [0, 0]
        for name in names:
            left, left_other, right, right_other = pairs[name]
            depth, width = extents[name]
            lanes = width // LANES
            step = max(k for k in (128, 256, 384, 512) if depth % k == 0 and k * lanes <= 3072)
            rows = step * lanes
            for first in range(0, depth, step):
                begin = kept[name] + first * lanes
                if not list(pieces(begin, rows, core)):
                    continue
                slot = turn % 2
                turn += 1
                columns = flip(left[:, first : first + step])
                others = flip(left_other[:, first : first + step])
                part = 256
                for start in range(0, width, part):
                    cols = slice(start, start + part)
                    block = dot(columns, right[:, cols]) + dot(others, right_other[:, cols])
                    for j in range(part // LANES):
                        wide[pl.ds(start // LANES + j, step, stride=lanes), :] = block[:, j * LANES : (j + 1) * LANES]
                wait(pending[slot], slot)
                stage[slot, 0:rows, :] = wide[0:rows, :].astype(bf16)
                pending[slot] = send(stage.at[slot], begin, rows, sems.at[slot], core)
        here = 0
        total = 0
        for name, extent in ENC_LAYOUT:
            if name not in kept_names(names):
                continue
            rows = rows_of(extent)
            room = up_to(rows, 16)
            if list(pieces(kept[name], room, core)):
                wide[0:room, :] = jnp.zeros((room, LANES), f32)
                row, shift = {QB: (2, 0), VB: (2, 2 * extent[0])}.get(name, (VEC.get(name), 0))
                for j in range(rows):
                    cols = slice(shift + j * LANES, shift + (j + 1) * LANES)
                    wide[j : j + 1, :] = vec[row : row + 1, cols] + vec_other[row : row + 1, cols]
                small[here : here + room, :] = wide[0:room, :].astype(bf16)
                total += send(small.at[pl.ds(here, room), :], kept[name], room, sems.at[2], core)
            here += room
        wait(pending[0], 0)
        wait(pending[1], 1)
        if total:
            block = small.at[pl.ds(0, total), :]
            pltpu.make_async_copy(block, block, sems.at[2]).wait()

    for core in range(2):

        @pl.when(place_ref[2] == core)
        def _():
            for each in lates:
                each.here = False
            run(core)
            for each in lates:
                each.arrive()


def pack_enc(plan, regions, size, groups, place, pairs, vec, vec_other):
    names = list(pairs)
    operands = [a for name in names for a in pairs[name]] + [vec, vec_other]
    extents = dict(ENC_LAYOUT)
    small = sum(up_to(rows_of(extents[n]), 16) for n in kept_names(names))
    rows = 2 * plan.ny * groups * size // plan.tables
    return late_call(
        partial(pack_enc_kernel, plan, names, regions, size, groups),
        [(place, pltpu.SMEM)],
        operands,
        [(shape((rows, LANES), bf16), pl.ANY)] * plan.tables,
        [
            pltpu.VMEM((3072, LANES), f32),
            pltpu.VMEM((2, 3072 + 64, LANES), bf16),
            pltpu.VMEM((small + 64, LANES), bf16),
            pltpu.SemaphoreType.DMA((3,)),
        ],
        cost_estimate=cost(8),
        name="pack_enc",
    )


def kept_names(names):
    with_matrix = {
        QKV_W: [N1G, N1B, QB, VB],
        PROJ_W: [PB, N2G, N2B],
        UP_W: [UB],
        DOWN_W: [DB],
        EMBED_W: [EB, MT],
        POS: [POS],
    }
    return [v for n in names for v in with_matrix[n]]


def pack(plan, layout, regions, size, groups, group_first, place, pairs, vec):
    names = list(pairs)
    operands = [a for name in names for a in pairs[name]] + [vec]
    extents = dict(layout)
    small = sum(up_to(rows_of(extents[n]), 16) for n in kept_names(names))
    rows = 2 * plan.ny * groups * size
    return late_call(
        partial(pack_kernel, plan, layout, names, regions, size, groups, group_first),
        [(place, pltpu.SMEM)],
        operands,
        [(shape((rows, LANES), bf16), pl.ANY)] * 2,
        [
            pltpu.VMEM((3072, LANES), f32),
            pltpu.VMEM((2, 3072 + 64, LANES), bf16),
            pltpu.VMEM((small + 64, LANES), bf16),
            pltpu.SemaphoreType.DMA((3,)),
        ],
        cost_estimate=cost(19),
        name="pack",
    )


def finish_kernel(plan, counts, place_ref, seg_ref, *refs):
    sources, result, held, wide, out, sem = refs[: len(counts)], *refs[len(counts) :]
    unit = plan.half
    number = 0
    for source, count in zip(sources, counts):
        for k in range(count):
            target = held.at[pl.ds(pl.multiple_of(place_ref[number] * unit, 16), unit), :]
            number += 1
            pltpu.make_async_copy(source.at[pl.ds(k * unit, unit), :], target, sem.at[0]).start()
    out[...] = jnp.zeros_like(out)
    pltpu.make_async_copy(held, held, sem.at[0]).wait()
    total = plan.room
    wide[total : total + 16, :] = jnp.zeros((16, LANES), f32)
    wide[0:total, :] = held[...].astype(f32)

    def one(k, carry):
        source, first, steps = seg_ref[3 * k], seg_ref[3 * k + 1], seg_ref[3 * k + 2]

        def step(i, carry):
            out[pl.ds(first + 8 * i, 8), :] = wide[pl.ds(source + 8 * i, 8), :]
            return carry

        def steps8(i, carry):
            out[pl.ds(first + 64 * i, 64), :] = wide[pl.ds(source + 64 * i, 64), :]
            return carry

        many = steps // 8
        lax.fori_loop(0, many, steps8, 0)
        return lax.fori_loop(many * 8, steps, step, carry)

    lax.fori_loop(0, seg_ref.shape[0] // 3, one, 0)
    rows = up_to(plan.chunk, 8)
    lines = out.at[pl.ds(0, rows), :].reshape(rows, 1, LANES)
    copy = pltpu.make_async_copy(lines.at[pl.ds(0, plan.chunk)], result, sem.at[0])
    copy.start()
    copy.wait()


def finish(plan, place, segments, sources):
    total = plan.room
    return pl.pallas_call(
        partial(finish_kernel, plan, [s.shape[0] // plan.half for s in sources]),
        in_specs=[pl.BlockSpec(memory_space=pltpu.SMEM)] * 2
        + [pl.BlockSpec(memory_space=pl.ANY)] * len(sources),
        out_specs=pl.BlockSpec(memory_space=pl.ANY),
        out_shape=shape((plan.chunk, 1, LANES), f32),
        scratch_shapes=[
            pltpu.VMEM((total, LANES), bf16),
            pltpu.VMEM((total + 16, LANES), f32),
            pltpu.VMEM((up_to(plan.chunk, 8) + 8, LANES), f32),
            pltpu.SemaphoreType.DMA((1,)),
        ],
        compiler_params=params_of(),
        cost_estimate=cost(8),
        name="finish",
    )(place, segments, *sources)


def completed(pairs, count):
    senders = [k for k in range(count) if k not in [a for a, _ in pairs]]
    receivers = [k for k in range(count) if k not in [b for _, b in pairs]]
    return list(pairs) + list(zip(senders, receivers))


def after(values, *before):
    return lax.optimization_barrier((values, before))[0]


def per_device(plan, enc_input, segments, slots, params, cot):
    ns, ng, nd, ny = plan.ns, plan.ng, plan.nd, plan.ny
    piece, half, room, chunk = plan.piece, plan.half, plan.room, plan.chunk
    sec = lax.axis_index(SEC)
    grp = lax.axis_index(GRP)
    dp = lax.axis_index(DP)
    yy, core = dp // 2, dp % 2
    first_section = sec == 0

    def over_x(block):
        return lax.ppermute(block, SEC, [(0, 1), (1, 0)])

    def over_core(block):
        return lax.ppermute(block, DP, [(d, d ^ 1) for d in range(nd)])

    def over_y(block):
        return lax.ppermute(block, DP, [(d, (d + 2) % nd) for d in range(nd)])

    def over_z(block, senders=None):
        senders = range(ng) if senders is None else senders
        return lax.ppermute(block, GRP, [(g, (g + 1) % ng) for g in senders])

    unit = plan.unit

    def share(start, params):
        cut = lax.dynamic_slice(params, (0, start * LANES), (1, unit * LANES))
        return cut.astype(f32).reshape(unit, LANES).astype(bf16)

    def shares(section, params):
        number = section * nd + dp
        enc_first = jnp.minimum(number * piece, chunk - piece)
        dec_first = [jnp.minimum((h * plan.pieces + number) * unit, chunk - unit) for h in range(2)]
        if plan.parts_in == 1:
            dec_first[0] = jnp.where(grp == plan.full, 0, dec_first[0])
        return (
            share(jnp.where(first_section, enc_first, dec_first[0]), params),
            share(jnp.where(first_section, enc_first + piece - unit, dec_first[1]), params),
        )

    send = shares(1 - sec, params)
    keep = shares(sec, after(params, *send))

    def whole_piece(parts):
        return jnp.concatenate([parts[0][:half], parts[1][unit - half :]])

    routes = [[(z, 2 * z + h) for z in range(plan.full)] for h in range(2)]
    if plan.parts_in == 1:
        routes[0].append((plan.full, 1))
    routes = [completed(route, ng) for route in routes]
    crossed = []
    for h in range(2):
        pairs = [(z, ng + z) for z in range(ng)] + [(ng + a, b) for a, b in routes[h]]
        crossed.append(lax.ppermute(send[h], (SEC, GRP), pairs))
    spread = [lax.ppermute(keep[h], GRP, routes[h]) for h in range(2)]
    enc_piece = jnp.where(first_section, whole_piece(keep), whole_piece(crossed))
    even, odd = (jnp.where(first_section, crossed[h], spread[h]) for h in range(2))
    dec_piece = jnp.where(grp % 2 == 0, even, odd)
    class Gather:
        def __init__(self, here):
            self.here = here
            if ny == 2:
                self.arrays = [here, over_x(here), over_y(here)]
                self.owners = [(sec, yy), (1 - sec, yy), (sec, 1 - yy), (1 - sec, 1 - yy)]
            else:
                column = [here]
                for _ in range(ny - 1):
                    column.append(over_y(column[-1]))
                self.arrays = column
                self.owners = [(s, (yy - k) % ny) for s in (sec, 1 - sec) for k in range(ny)]

        def second(self):
            if ny == 2:
                middle = self.here.shape[0] // 2
                self.corners = [self.arrays[1][:middle], self.arrays[2][middle:]]
            else:
                self.corners = self.arrays
            return tuple(self.corners)

        def third(self):
            if ny == 2:
                self.arrays += [over_y(self.corners[0]), over_x(self.corners[1])]
            else:
                self.arrays = self.arrays + [over_x(block) for block in self.corners]
            return tuple(self.arrays[-2:])

        def fourth(self, joined=True):
            arrays = [jnp.concatenate(self.arrays)] if joined else self.arrays
            return arrays + [over_core(block) for block in arrays]

        def places(self, parts):
            found = []
            for c in (core, 1 - core):
                for s, y in self.owners:
                    for k in parts:
                        number = (grp - k) % ng * plan.pieces + s * nd + y * 2 + c
                        found += [2 * number, 2 * number + 1]
            return found

    last = jnp.logical_and(sec == ns - 1, dp == nd - 1)
    if plan.parts_in == 1:
        dec_piece = jnp.where(jnp.logical_and(last, grp == 1), even, dec_piece)
    else:
        for k in range(plan.parts_in):
            part = share(jnp.minimum(k * unit, chunk - unit), params)
            part = lax.ppermute(part, GRP, [(plan.full, 2 * k + 1)])
            dec_piece = jnp.where(jnp.logical_and(last, grp == 2 * k + 1), part, dec_piece)
    here = enc_piece
    gathers = [Gather(here)]
    for k in range(1, ng):
        here = over_z(here)
        if k >= 2:
            here = after(here, *gathers[k - 2].second())
        if k >= 3:
            here = after(here, *gathers[k - 3].third())
        gathers.append(Gather(here))
    gathers[-2].second()
    dec_parts = [after(dec_piece, here)]
    for _ in range(ng - 1):
        dec_parts.append(over_z(dec_parts[-1]))
    gathers[-1].arrays[1:] = after(gathers[-1].arrays[1:], *dec_parts[1:-1])
    gathers[-1].second()
    enc_sources, enc_places = [], []
    for k, g in enumerate(gathers):
        if k >= ng - 3:
            g.third()
        if k == ng - 1:
            g.arrays = after(g.arrays, dec_parts[-1])
        enc_sources += g.fourth()
        enc_places += g.places([k])
    enc_places = jnp.stack(enc_places).astype(jnp.int32)
    dec_gather = Gather(after(jnp.concatenate(dec_parts), *gathers[-1].corners))
    dec_places = jnp.stack(dec_gather.places(range(ng))).astype(jnp.int32)

    micro_rows = enc_input.reshape(ROW, WIDTH)
    seg = lax.dynamic_index_in_dim(segments, sec, 0, keepdims=False).reshape(ROW)
    slot = lax.dynamic_index_in_dim(slots, sec, 0, keepdims=False).reshape(ROW)
    cot_rows = jnp.pad(
        cot.reshape(IMAGES_ROW, SLOTS, DEC_WIDTH), ((0, 0), (0, SLOT_PAD - SLOTS), (0, 0))
    ).reshape(IMAGES_ROW * SLOT_PAD, DEC_WIDTH)

    enc_weights, saved = encode(plan, enc_places, enc_sources, micro_rows, seg)
    dec_gather.arrays[1:] = after(dec_gather.arrays[1:], saved[SENT])
    dec_gather.second()
    others = {k: over_core(saved[k]) for k in (H1, ATT, H2, ACT)}
    dec_gather.third()
    dec_sources = dec_gather.fourth(False)
    dec = dict(
        zip(
            [OUT, H1, QKV_L, ATT, PROJ_L, H2, UP_L, ACT, EMBED_L, GSENT, VECS, GPOS],
            decode(plan, dec_places, dec_sources, saved[SENT], seg, slot, cot_rows),
        )
    )

    def add(first, *others):
        total = first.astype(f32)
        for other in others:
            total = total + other.astype(f32)
        return total.astype(bf16)

    class Square:
        def __init__(self, tables):
            self.keep, self.sends = tables[0::2], tables[1::2]
            self.m = tables[0].shape[0] // ny

        def first(self):
            self.got = (over_x(self.sends[0]), over_y(self.sends[1])) if ny == 2 else (over_x(self.sends[0]),)
            return self.got

        def second(self, *got):
            m = self.m
            self.got = got
            if ny == 2:
                self.sends = (add(self.keep[0][m:], got[0][m:]), add(self.keep[1][m:], got[1][m:]))
            else:
                column = add(self.keep[0], got[0])
                total = column[(ny - 1) * m :]
                for k in range(ny - 2, -1, -1):
                    total = add(column[k * m : (k + 1) * m], over_y(total))
                self.sends = (total,)
            return self.sends

        def third(self, *before):
            m = self.m
            if ny == 2:
                ay, bx = after((over_y(self.sends[0]), over_x(self.sends[1])), *before)
                self.own = (
                    add(self.keep[0][:m], self.got[0][:m], ay), add(self.keep[1][:m], self.got[1][:m], bx),
                )
            else:
                self.own = (self.sends[0][: m // 2], self.sends[0][m // 2 :])
            return self.own

    class Ring:
        def __init__(self, one):
            self.one, self.step = one, 0
            self.total = add(*one((grp - 1) % ng))

        def next(self, *before):
            got = after(over_z(self.total), *before)
            self.step += 1
            self.total = add(*self.one((grp - 1 - self.step) % ng), got)
            return self.total

    place = jnp.stack([sec, yy, core]).astype(jnp.int32)
    every = list(range(ng))
    near = ng // 2
    upper, lower = every[near:], every[:near]
    dec_mine, dec_theirs = pack(
        plan, DEC_LAYOUT, plan.dec_regions(), half, ng, True, place,
        {
            EMBED_W: (saved[SENT], dec[EMBED_L]),
            QKV_W: (dec[H1], dec[QKV_L]),
            PROJ_W: (dec[ATT], dec[PROJ_L]),
            UP_W: (dec[H2], dec[UP_L]),
            DOWN_W: (dec[ACT], cot_rows),
            POS: (dec[GPOS], dec[GPOS]),
        },
        dec[VECS],
    )
    dec_core = over_core(dec_theirs)
    grad_sent, others = after((dec[GSENT], others), dec_mine)
    grad_sent = after(grad_sent, *others.values())
    grad_other = over_core(grad_sent)
    up_low, proj_low, grad_middle, mlp_vec = mlp_back(grad_sent, saved, enc_weights)
    dec_core, grad_other = after((dec_core, grad_other), up_low)

    def dec_block(g):
        rows = 2 * ny * half
        return [lax.dynamic_slice(t, (g * rows, 0), (rows, LANES)) for t in (dec_mine, dec_core)]

    dec_ring = Ring(dec_block)
    up_other, proj_other, mlp_vec_other = over_core(up_low), over_core(proj_low), over_core(mlp_vec)
    in_grad, qkv_low, enc_vec = attention_back(
        after(grad_middle, dec_ring.total), proj_low, micro_rows, saved, enc_weights, mlp_vec
    )
    up_other, proj_other, mlp_vec_other = after((up_other, proj_other, mlp_vec_other), qkv_low)
    up_tables = pack_enc(
        plan, plan.enc_regions(upper), piece, len(upper), place,
        {
            DOWN_W: (saved[ACT], others[ACT], grad_sent, grad_other),
            UP_W: (saved[H2], others[H2], after(up_low, qkv_low), up_other),
        },
        mlp_vec, mlp_vec_other,
    )
    qkv_other, vec_other = after((over_core(qkv_low), over_core(enc_vec)), up_tables[0])
    dec_ring.next(up_tables[0])
    low_tables = pack_enc(
        plan, plan.enc_regions(lower), piece, len(lower), place,
        {
            PROJ_W: (saved[ATT], others[ATT], proj_low, proj_other),
            QKV_W: (saved[H1], others[H1], qkv_low, qkv_other),
            UP_W: (saved[H2], others[H2], after(up_low, dec_ring.total), up_other),
        },
        enc_vec, vec_other,
    )
    upper_sum, lower_sum = Square(up_tables), Square(low_tables)
    upper_first, lower_first = upper_sum.first(), lower_sum.first()
    upper_sum.second(*after(upper_first, low_tables[0]))
    dec_ring.next(*upper_sum.sends)
    lower_sum.second(*after(lower_first, dec_ring.total))
    for _ in range(ng - 3):
        dec_ring.next(*lower_sum.sends)
    count = plan.tables
    rows = dec_ring.total.shape[0] // count
    dec_sum = Square([dec_ring.total[k * rows : (k + 1) * rows] for k in range(count)])
    dec_first = dec_sum.first()
    upper_sum.third(*dec_sum.sends)
    lower_sum.third(*upper_sum.own)
    blocks = list(lower_sum.own) + list(upper_sum.own)

    def enc_block(g):
        if len(blocks) == 4 == ng:
            return [jnp.where(g < 2, jnp.where(g == 0, *blocks[:2]), jnp.where(g == 2, *blocks[2:]))]
        return [lax.dynamic_slice(jnp.concatenate(blocks), (g * piece, 0), (piece, LANES))]

    enc_ring = Ring(enc_block)
    dec_sum.second(*after(dec_first, enc_ring.total))
    dec_own = jnp.concatenate(dec_sum.third())
    back = [[(2 * z + h, z) for z in range(plan.full)] for h in range(2)]
    back[0].append((1, plan.full))
    back.append([(3, plan.full)])
    dec_back = [lax.ppermute(dec_own, GRP, completed(pairs, ng)) for pairs in back]
    enc_ring.next()
    dec_low, dec_high, dec_rest = after(dec_back, enc_ring.total)
    dec_own = jnp.concatenate([dec_low, jnp.where(grp == plan.full, dec_rest, dec_high)])
    for _ in range(ng - 2):
        enc_ring.next(dec_own)
    enc_own = enc_ring.total

    own = jnp.where(first_section, enc_own, dec_own)
    other = jnp.where(first_section, dec_own, enc_own)
    if ny == 2:
        from_x, from_y = over_x(other), over_y(own)
        sources = [own, from_x, from_y, over_y(from_x)]
        owners = [(sec, yy), (1 - sec, yy), (sec, 1 - yy), (1 - sec, 1 - yy)]
    else:
        column = [jnp.concatenate([own, over_x(other)])]
        for _ in range(ny - 1):
            column.append(over_y(column[-1]))
        sources = column
        owners = [(s, (yy - k) % ny) for k in range(ny) for s in (sec, 1 - sec)]
    sources = sources + [over_core(block) for block in sources]
    places = []
    for c in (core, 1 - core):
        for s, y in owners:
            number = (c * 2 + s) * ny + y
            places += [
                jnp.where(first_section, 2 * number, number),
                jnp.where(first_section, 2 * number + 1, plan.pieces + number),
            ]
    table = jnp.asarray(plan.segments())[sec, grp].reshape(-1)
    flat = finish(plan, jnp.stack(places).astype(jnp.int32), table, sources)
    param_grad = flat.reshape(1, chunk * LANES)
    dec_out = dec[OUT].reshape(IMAGES_ROW, SLOT_PAD, DEC_WIDTH)[:, :SLOTS]
    return (
        dec_out.reshape(1, 1, IMAGES_ROW * SLOTS, DEC_WIDTH),
        in_grad.reshape(1, 1, ROW, WIDTH),
        param_grad,
    )


def solution(mesh):
    placed = (
        P(SEC, (GRP, DP), None, None),
        P(None, (GRP, DP), None),
        P(None, (GRP, DP), None),
        P(SEC, GRP),
        P(SEC, (GRP, DP), None, None),
    )
    return jax.shard_map(
        partial(per_device, Plan(dict(mesh.shape))),
        mesh=mesh,
        in_specs=placed,
        out_specs=(
            P(SEC, (GRP, DP), None, None),
            P(SEC, (GRP, DP), None, None),
            P(SEC, GRP),
        ),
        check_vma=False,
    )
```

```python
from functools import partial
import math

import jax
import jax.numpy as jnp
import numpy as np
from jax import lax
from jax.experimental import pallas as pl
from jax.experimental.pallas import tpu as pltpu
from jax.sharding import PartitionSpec as P

WIDTH = 768
HEADS = 12
HIDDEN_SIZE = 3072
DEC_WIDTH = 512
DEC_HEADS = 16
DEC_HIDDEN = 2048
SLOTS = 196
IMAGES_ROW = 5
ROW = 256
PARAMS = 7088128
LANES = 128
SEC, GRP, DP = "section", "group", "dp"
(
    N1G, N1B, QKV_W, QB, VB, PROJ_W, PB, N2G,
) = range(0, 8)
(
    N2B, UP_W, UB, DOWN_W, DB, EMBED_W, EB, MT,
) = range(8, 16)
(
    POS, QKV_B, VECS, SENT, H1, QKV, PROBS, ATT,
) = range(16, 24)
(
    MID, H2, ACT, SLOPE, OUT, QKV_L, PROJ_L, UP_L,
) = range(24, 32)
(
    EMBED_L, GSENT, GPOS,
) = range(32, 35)
SLOT_PAD = 208
VMEM_BYTES = 60 * 1024 * 1024

norm_eps = 1e-06
masked_score = -1000000000.0
f32 = jnp.float32
bf16 = jnp.bfloat16


def block_layout(width, hidden):
    return [
        (N1G, (width,)),
        (N1B, (width,)),
        (QKV_W, (width, 3 * width)),
        (QB, (width,)),
        (VB, (width,)),
        (PROJ_W, (width, width)),
        (PB, (width,)),
        (N2G, (width,)),
        (N2B, (width,)),
        (UP_W, (width, hidden)),
        (UB, (hidden,)),
        (DOWN_W, (hidden, width)),
        (DB, (width,)),
    ]


def decoder_layout(enc_width, width, hidden, slot_count):
    return [
        (EMBED_W, (enc_width, width)),
        (EB, (width,)),
        (MT, (width,)),
        (POS, (slot_count, width)),
    ] + block_layout(width, hidden)


ENC_LAYOUT = block_layout(WIDTH, HIDDEN_SIZE)
DEC_LAYOUT = decoder_layout(WIDTH, DEC_WIDTH, DEC_HIDDEN, SLOTS)
VEC = {
    N1G: 0,
    N1B: 1,
    QKV_B: 2,
    PB: 3,
    N2G: 4,
    N2B: 5,
    UB: 6,
    DB: 7,
    EB: 8,
    MT: 9,
}
VEC_ROWS = 16


def dot(a, b):
    return lax.dot_general(a, b, (((1,), (0,)), ((), ())), preferred_element_type=f32)


def dot_nt(a, b):
    return lax.dot_general(a, b, (((1,), (1,)), ((), ())), preferred_element_type=f32)


def dot_tn(a, b):
    return lax.dot_general(a, b, (((0,), (0,)), ((), ())), preferred_element_type=f32)


def normalised(values):
    centered = values - jnp.mean(values, axis=-1, keepdims=True)
    inverse = lax.rsqrt(jnp.mean(centered * centered, axis=-1, keepdims=True) + norm_eps)
    return centered * inverse, inverse


def norm_back(grad, hat, inverse, gain):
    scaled = grad * gain
    first = jnp.mean(scaled, axis=-1, keepdims=True)
    second = jnp.mean(scaled * hat, axis=-1, keepdims=True)
    return inverse * (scaled - first - hat * second)


def col_sum(values):
    return jnp.sum(values, axis=0, keepdims=True)


def gelu_parts(upward):
    half = 0.5 + 0.5 * lax.erf(upward * f32(math.sqrt(0.5)))
    slope = half + upward * (jnp.exp(upward * upward * f32(-0.5)) * f32(1.0 / math.sqrt(2.0 * math.pi)))
    return upward * half, slope


def head_mask(head, head_dim):
    lane = lax.broadcasted_iota(jnp.int32, (1, LANES), 1)
    return jnp.where(lane // head_dim == head, 1.0, 0.0).astype(bf16)


def lane_block(group, start=0):
    if isinstance(group, int):
        return slice(start + group * LANES, start + (group + 1) * LANES)
    return pl.ds(pl.multiple_of(start + group * LANES, LANES), LANES)


def flip(values):
    return values.astype(f32).T.astype(bf16)


def attention_forward(qkv_ref, probs_ref, joined_ref, width, heads, keep):
    head_dim = width // heads
    scale = f32(head_dim ** (-0.5))
    per_group = LANES // head_dim

    def one_group(group):
        queries = qkv_ref[:, lane_block(group)]
        keys = qkv_ref[:, lane_block(group, width)]
        values_t = flip(qkv_ref[:, lane_block(group, 2 * width)])
        subs = range(per_group)
        scores = [dot_nt(keys, queries * head_mask(sub, head_dim)) for sub in subs]
        scores = [keep(s * scale) for s in scores]
        expo = [jnp.exp(s - jnp.max(s, axis=0, keepdims=True)) for s in scores]
        probs = [e * (1.0 / col_sum(e)) for e in expo]
        for sub in subs:
            probs_ref[group * per_group + sub] = probs[sub]
        outs = [
            dot(values_t[sub * head_dim : (sub + 1) * head_dim], probs[sub].astype(bf16)) for sub in subs
        ]
        joined_ref[lane_block(group), :] = jnp.concatenate(outs, axis=0)

    for group in range(width // LANES):
        one_group(group)


def attention_backward(qkv_ref, probs_ref, grad_ref, low_ref, width, heads):
    head_dim = width // heads
    scale = f32(head_dim ** (-0.5))
    per_group = LANES // head_dim
    for each in (qkv_ref, probs_ref):
        if isinstance(each, Late):
            each.arrive()

    def one_group(group):
        queries = qkv_ref[:, lane_block(group)]
        keys = qkv_ref[:, lane_block(group, width)]
        values = qkv_ref[:, lane_block(group, 2 * width)]
        grads = grad_ref[:, lane_block(group)]
        keys_t = flip(keys)
        subs = range(per_group)
        masks = [head_mask(sub, head_dim) for sub in subs]
        own = [grads * m for m in masks]
        grad_probs = [dot_nt(values, o) for o in own]
        probs = [probs_ref[group * per_group + sub] for sub in subs]
        grad_values = sum(dot(p.astype(bf16), o) for p, o in zip(probs, own))
        low = [
            (p * (g - col_sum(p * g))).astype(bf16) for p, g in zip(probs, grad_probs)
        ]
        grad_keys = sum(dot(l, queries * m) for l, m in zip(low, masks))
        grad_queries = [
            dot(keys_t[sub * head_dim : (sub + 1) * head_dim], low[sub]) for sub in subs
        ]
        low_ref[:, lane_block(group)] = (jnp.concatenate(grad_queries, axis=0).T * scale).astype(bf16)
        low_ref[:, lane_block(group, width)] = (grad_keys * scale).astype(bf16)
        low_ref[:, lane_block(group, 2 * width)] = grad_values.astype(bf16)

    for group in range(width // LANES):
        one_group(group)


class Late:
    def __init__(self, source, target, sem):
        self.copy, self.target, self.shape = pltpu.make_async_copy(source, target, sem), target, target.shape
        self.here = False
        self.copy.start()

    def arrive(self):
        if not self.here:
            self.copy.wait()
            self.here = True

    def __getitem__(self, index):
        self.arrive()
        return self.target[index]


def late_call(kernel, early, late, outs, scratch, **options):
    count, many = len(early), len(late)

    def body(*refs):
        sources, results = refs[count : count + many], refs[count + many : count + many + len(outs)]
        rest = refs[count + many + len(outs) :]
        held, sems = rest[:many], rest[many]
        lates = [Late(sources[k], held[k], sems.at[k]) for k in range(many)]
        kernel(*refs[:count], *lates, *results, *rest[many + 1 :])
        for each in lates:
            each.arrive()

    return pl.pallas_call(
        body,
        in_specs=[pl.BlockSpec(memory_space=m) for _, m in early] + [pl.BlockSpec(memory_space=pl.ANY)] * many,
        out_specs=[pl.BlockSpec(memory_space=m) for _, m in outs],
        out_shape=[o for o, _ in outs],
        scratch_shapes=[pltpu.VMEM(a.shape, a.dtype) for a in late]
        + [pltpu.SemaphoreType.DMA((many,))]
        + list(scratch),
        compiler_params=params_of(),
        **options,
    )(*[a for a, _ in early], *late)


def encode_kernel(plan, counts, place_ref, *refs):
    sources, refs = refs[: len(counts)], refs[len(counts) :]
    x_ref, seg_row_ref, seg_col_ref = refs[:3]
    weight_outs, vec = refs[3:7], refs[7]
    normed1_ref, qkv_ref, probs_ref, attended_ref, middle_ref, normed2_ref = refs[8:14]
    held, wide, spare, sems, out_sems, joined_ref = refs[14:20]
    weights = refs[20:24]
    qkv_w, proj_w = weights[:2]
    copies = [pltpu.make_async_copy(w, o, out_sems.at[k]) for k, (w, o) in enumerate(zip(weights, weight_outs))]
    unpack_weights(
        plan, ENC_LAYOUT, plan.half, plan.piece, plan.ng, plan.room, place_ref, sources, counts,
        weights, vec, held, wide, spare, sems, copies,
    )
    width, hidden = WIDTH, HIDDEN_SIZE
    inputs = x_ref[...].astype(f32)
    hat, _ = normalised(inputs)
    normed1 = (hat * vec[0:1, :width] + vec[1:2, :width]).astype(bf16)
    normed1_ref[...] = normed1
    qkv_ref[...] = (dot(normed1, qkv_w[...]) + vec[2:3, : 3 * width]).astype(bf16)
    allowed = seg_col_ref[...] == seg_row_ref[...]
    attention_forward(
        qkv_ref, probs_ref, joined_ref, width, HEADS,
        lambda scores: jnp.where(allowed, scores, f32(masked_score)),
    )
    attended = joined_ref[...].T.astype(bf16)
    attended_ref[...] = attended
    middle = inputs + (dot(attended, proj_w[...]) + vec[3:4, :width])
    middle_ref[...] = middle
    hat, _ = normalised(middle)
    normed2_ref[...] = (hat * vec[4:5, :width] + vec[5:6, :width]).astype(bf16)
    for copy in copies:
        copy.wait()


def encode_mlp_kernel(normed2_ref, up_w, vec, down_w, middle_ref, sent_ref, active_ref, slope_ref):
    width, hidden = WIDTH, HIDDEN_SIZE
    total = jnp.zeros((ROW, width), f32)
    part = 1536
    for start in range(0, hidden, part):
        cols = slice(start, start + part)
        upward = dot(normed2_ref[...], up_w[:, cols]) + vec[6:7, cols]
        active, slope = gelu_parts(upward)
        active_ref[:, cols] = active.astype(bf16)
        slope_ref[:, cols] = slope.astype(slope_ref.dtype)
        total += dot(active_ref[:, cols], down_w[cols, :])
    sent_ref[...] = (middle_ref[...] + (total + vec[7:8, :width])).astype(bf16)


def mlp_back_kernel(
    grad_ref, down_w, slope_ref, up_w, middle_ref, vec,
    up_low_ref, proj_low_ref, grad_middle_ref, vec_grad,
):
    width, hidden = WIDTH, HIDDEN_SIZE
    grad_out = grad_ref[...]
    vec_grad[...] = jnp.zeros_like(vec_grad)
    vec_grad[7:8, :width] = col_sum(grad_out.astype(f32))
    grad_normed2 = jnp.zeros((grad_out.shape[0], width), f32)
    part = 3072
    for start in range(0, hidden, part):
        cols = slice(start, start + part)
        low = (dot_nt(grad_out, down_w[cols, :]) * slope_ref[:, cols]).astype(bf16)
        up_low_ref[:, cols] = low
        vec_grad[6:7, cols] = col_sum(low.astype(f32))
        grad_normed2 += dot_nt(low, up_w[:, cols])
    hat, inverse = normalised(middle_ref[...])
    vec_grad[4:5, :width] = col_sum(grad_normed2 * hat)
    vec_grad[5:6, :width] = col_sum(grad_normed2)
    grad_middle = grad_out.astype(f32) + norm_back(grad_normed2, hat, inverse, vec[4:5, :width])
    grad_middle_ref[...] = grad_middle
    proj_low = grad_middle.astype(bf16)
    proj_low_ref[...] = proj_low
    vec_grad[3:4, :width] = col_sum(proj_low.astype(f32))


def attention_back_kernel(
    proj_low_ref, proj_w, qkv_ref, probs_ref, qkv_w, x_ref, vec_in, vec, grad_middle_ref,
    in_grad_ref, qkv_low_ref, vec_grad, grad_att_ref,
):
    width = WIDTH
    grad_att_ref[...] = dot_nt(proj_low_ref[...], proj_w[...]).astype(bf16)
    attention_backward(qkv_ref, probs_ref, grad_att_ref, qkv_low_ref, width, HEADS)
    qkv_low = qkv_low_ref[...]
    vec_grad[...] = vec_in[...]
    vec_grad[2:3, : 3 * width] = col_sum(qkv_low.astype(f32))
    grad_normed1 = dot_nt(qkv_low, qkv_w[...])
    hat, inverse = normalised(x_ref[...].astype(f32))
    vec_grad[0:1, :width] = col_sum(grad_normed1 * hat)
    vec_grad[1:2, :width] = col_sum(grad_normed1)
    in_grad_ref[...] = grad_middle_ref[...] + norm_back(grad_normed1, hat, inverse, vec[0:1, :width])


def decode_kernel(plan, counts, place_ref, *refs):
    sources, refs = refs[: len(counts)], refs[len(counts) :]
    sent_ref, seg_row, slot_row, seg_col, slot_col, cot_ref = refs[:6]
    (
        out_ref, normed1_ref, qkv_low_ref, attended_ref, proj_low_ref, normed2_ref, up_low_ref,
        active_ref, embed_low_ref, grad_sent_ref, vec_grad, pos_grad,
    ) = refs[6:18]
    embedded_ref, embed_sum, qkv_ref, probs_ref, joined_ref, grad_att_ref = refs[18:24]
    held, wide, spare, sems, vec = refs[24:29]
    weights = refs[29:]
    embed_w, pos_ref, qkv_w, proj_w, up_w, down_w = weights
    width, hidden = DEC_WIDTH, DEC_HIDDEN
    image = pl.program_id(0)
    length = SLOT_PAD

    @pl.when(image == 0)
    def _():
        unpack_weights(
            plan, DEC_LAYOUT, plan.unit // 2, plan.unit, plan.full, plan.dec_room, place_ref, sources, counts,
            weights, vec, held, wide, spare, sems,
        )
        embedded_ref[...] = (dot(sent_ref[...], embed_w[...]) + vec[8:9, :width]).astype(bf16)
        vec_grad[...] = jnp.zeros_like(vec_grad)
        pos_grad[...] = jnp.zeros_like(pos_grad)
        embed_sum[...] = jnp.zeros_like(embed_sum)

    def add_vec(row, values):
        vec_grad[row : row + 1, : values.shape[1]] += values

    place = lax.broadcasted_iota(jnp.int32, (length, ROW), 0)
    match = (seg_row[...] == image) & (slot_row[...] == place)
    onehot = jnp.where(match, 1.0, 0.0)
    free = 1.0 - jnp.sum(onehot, axis=1, keepdims=True)
    x = dot(onehot.astype(bf16), embedded_ref[...]) + free * vec[9:10, :width] + pos_ref[...].astype(f32)
    hat1, inverse1 = normalised(x)
    normed1 = (hat1 * vec[0:1, :width] + vec[1:2, :width]).astype(bf16)
    normed1_ref[...] = normed1
    qkv_ref[...] = (dot(normed1, qkv_w[...]) + vec[2:3, : 3 * width]).astype(bf16)
    key_place = lax.broadcasted_iota(jnp.int32, (length, length), 0)
    attention_forward(
        qkv_ref, probs_ref, joined_ref, width, DEC_HEADS,
        lambda scores: jnp.where(key_place < SLOTS, scores, f32(-1e30)),
    )
    attended = joined_ref[...].T.astype(bf16)
    attended_ref[...] = attended
    middle = x + (dot(attended, proj_w[...]) + vec[3:4, :width])
    hat2, inverse2 = normalised(middle)
    normed2 = (hat2 * vec[4:5, :width] + vec[5:6, :width]).astype(bf16)
    normed2_ref[...] = normed2
    cot = cot_ref[...]
    add_vec(7, col_sum(cot.astype(f32)))
    total = jnp.zeros((length, width), f32)
    grad_normed2 = jnp.zeros((length, width), f32)
    part = 1024
    for start in range(0, hidden, part):
        cols = slice(start, start + part)
        upward = dot(normed2_ref[...], up_w[:, cols]) + vec[6:7, cols]
        active, slope = gelu_parts(upward)
        active = active.astype(bf16)
        active_ref[:, cols] = active
        total += dot(active, down_w[cols, :])
        low = (dot_nt(cot_ref[...], down_w[cols, :]) * slope).astype(bf16)
        up_low_ref[:, cols] = low
        vec_grad[6:7, cols] += col_sum(low.astype(f32))
        grad_normed2 += dot_nt(low, up_w[:, cols])
    out_ref[...] = (middle + (total + vec[7:8, :width])).astype(bf16)

    add_vec(4, col_sum(grad_normed2 * hat2))
    add_vec(5, col_sum(grad_normed2))
    grad_middle = cot.astype(f32) + norm_back(grad_normed2, hat2, inverse2, vec[4:5, :width])
    proj_low = grad_middle.astype(bf16)
    proj_low_ref[...] = proj_low
    add_vec(3, col_sum(proj_low.astype(f32)))
    grad_att_ref[...] = dot_nt(proj_low, proj_w[...]).astype(bf16)
    attention_backward(qkv_ref, probs_ref, grad_att_ref, qkv_low_ref, width, DEC_HEADS)
    qkv_low = qkv_low_ref[...]
    add_vec(2, col_sum(qkv_low.astype(f32)))
    grad_normed1 = dot_nt(qkv_low, qkv_w[...])
    add_vec(0, col_sum(grad_normed1 * hat1))
    add_vec(1, col_sum(grad_normed1))
    grad_in = grad_middle + norm_back(grad_normed1, hat1, inverse1, vec[0:1, :width])
    low_in = grad_in.astype(bf16)
    wide = low_in.astype(f32)
    add_vec(9, col_sum(free * wide))
    pos_grad[...] += wide
    place_t = lax.broadcasted_iota(jnp.int32, (ROW, length), 1)
    match_t = (seg_col[...] == image) & (slot_col[...] == place_t)
    embed_sum[...] += dot(jnp.where(match_t, 1.0, 0.0).astype(bf16), low_in)

    @pl.when(image == IMAGES_ROW - 1)
    def _():
        embed_low = embed_sum[...].astype(bf16)
        embed_low_ref[...] = embed_low
        add_vec(8, col_sum(embed_low.astype(f32)))
        grad_sent_ref[...] = dot_nt(embed_low, embed_w[...]).astype(bf16)


def cost(microseconds):
    return pl.CostEstimate(flops=int(microseconds * 1e11), bytes_accessed=int(microseconds * 3e8), transcendentals=0)


def params_of(**extra):
    return pltpu.CompilerParams(vmem_limit_bytes=VMEM_BYTES, **extra)


def shape(dims, kind):
    return jax.ShapeDtypeStruct(dims, kind)


def unpack_scratch(chunks, room):
    return [
        pltpu.VMEM((chunks * room, LANES), bf16),
        pltpu.VMEM((3200, LANES), f32),
        pltpu.VMEM((3200, LANES), f32),
        pltpu.SemaphoreType.DMA((chunks,)),
    ]


def encode(plan, place, sources, x, seg, seg_column):
    width, hidden, length = WIDTH, HIDDEN_SIZE, ROW
    weights = [shape(e, bf16) for _, e in ENC_LAYOUT if len(e) == 2]
    kept = [
        shape((VEC_ROWS, hidden), f32),
        shape((length, width), bf16),
        shape((length, 3 * width), bf16),
        shape((HEADS, length, length), f32),
        shape((length, width), bf16),
        shape((length, width), f32),
        shape((length, width), bf16),
    ]
    result = pl.pallas_call(
        partial(encode_kernel, plan, [s.shape[0] // plan.half for s in sources]),
        in_specs=[pl.BlockSpec(memory_space=pltpu.SMEM)]
        + [pl.BlockSpec(memory_space=pl.ANY)] * len(sources)
        + [pl.BlockSpec(memory_space=pltpu.VMEM)] * 3,
        out_specs=[pl.BlockSpec(memory_space=pl.ANY)] * 4 + [pl.BlockSpec(memory_space=pltpu.VMEM)] * len(kept),
        out_shape=weights + kept,
        scratch_shapes=unpack_scratch(plan.ng, plan.room)
        + [pltpu.SemaphoreType.DMA((4,)), pltpu.VMEM((width, length), f32)]
        + [pltpu.VMEM(w.shape, bf16) for w in weights],
        compiler_params=params_of(),
        cost_estimate=cost(24),
        name="encode",
    )(place, *sources, x, seg.reshape(1, length), seg_column)
    weights = dict(zip([QKV_W, PROJ_W, UP_W, DOWN_W, VECS], result))
    return weights, dict(zip([H1, QKV, PROBS, ATT, MID, H2], result[5:]))


def encode_mlp(saved, weights):
    width, hidden, length = WIDTH, HIDDEN_SIZE, ROW
    result = late_call(
        encode_mlp_kernel,
        [],
        [saved[H2], weights[UP_W], weights[VECS], weights[DOWN_W], saved[MID]],
        [
            (shape((length, width), bf16), pltpu.VMEM),
            (shape((length, hidden), bf16), pltpu.VMEM),
            (shape((length, hidden), bf16), pltpu.VMEM),
        ],
        [],
        cost_estimate=cost(8),
        name="encode_mlp",
    )
    return dict(zip([SENT, ACT, SLOPE], result))


def mlp_back(grad, saved, weights):
    width, hidden, length = WIDTH, HIDDEN_SIZE, ROW
    return late_call(
        mlp_back_kernel,
        [],
        [grad, weights[DOWN_W], saved[SLOPE], weights[UP_W], saved[MID], weights[VECS]],
        [
            (shape((length, hidden), bf16), pltpu.VMEM),
            (shape((length, width), bf16), pltpu.VMEM),
            (shape((length, width), f32), pltpu.VMEM),
            (shape((VEC_ROWS, hidden), f32), pltpu.VMEM),
        ],
        [],
        cost_estimate=cost(9),
        name="mlp_back",
    )


def attention_back(grad_middle, proj_low, x, saved, weights, vec_grad):
    width, hidden, length = WIDTH, HIDDEN_SIZE, ROW
    return late_call(
        attention_back_kernel,
        [],
        [
            proj_low, weights[PROJ_W], saved[QKV], saved[PROBS], weights[QKV_W], x, vec_grad, weights[VECS],
            grad_middle,
        ],
        [
            (shape((length, width), f32), pltpu.VMEM),
            (shape((length, 3 * width), bf16), pltpu.VMEM),
            (shape((VEC_ROWS, hidden), f32), pltpu.VMEM),
        ],
        [pltpu.VMEM((length, width), bf16)],
        cost_estimate=cost(10),
        name="attention_back",
    )


def decode(plan, place, sources, sent, seg, slot, columns, cot):
    width, hidden, length = DEC_WIDTH, DEC_HIDDEN, SLOT_PAD
    held = [sent, seg.reshape(1, ROW), slot.reshape(1, ROW), *columns]

    def whole(array):
        return pl.BlockSpec(array.shape, lambda i: (0,) * array.ndim, pipeline_mode=pl.Buffered(1))

    def image(cols):
        return pl.BlockSpec((length, cols), lambda i: (i, 0))

    rows = IMAGES_ROW * length
    per_image = [width, width, 3 * width, width, width, width, hidden, hidden]
    kept = [
        shape((ROW, width), bf16),
        shape((ROW, WIDTH), bf16),
        shape((VEC_ROWS, hidden), f32),
        shape((length, width), f32),
    ]
    return pl.pallas_call(
        partial(decode_kernel, plan, [s.shape[0] // (plan.unit // 2) for s in sources]),
        grid=(IMAGES_ROW,),
        in_specs=[pl.BlockSpec(memory_space=pltpu.SMEM)]
        + [pl.BlockSpec(memory_space=pl.ANY)] * len(sources)
        + [whole(a) for a in held]
        + [image(width)],
        out_specs=[image(c) for c in per_image]
        + [pl.BlockSpec(s.shape, lambda i: (0, 0)) for s in kept],
        out_shape=[shape((rows, c), bf16) for c in per_image] + kept,
        scratch_shapes=[
            pltpu.VMEM((ROW, width), bf16),
            pltpu.VMEM((ROW, width), f32),
            pltpu.VMEM((length, 3 * width), bf16),
            pltpu.VMEM((DEC_HEADS, length, length), f32),
            pltpu.VMEM((width, length), f32),
            pltpu.VMEM((length, width), bf16),
        ]
        + unpack_scratch(plan.full, plan.dec_room)
        + [pltpu.VMEM((VEC_ROWS, hidden), f32)]
        + [
            pltpu.VMEM((SLOT_PAD if n == POS else e[0], e[1]), bf16) for n, e in DEC_LAYOUT if len(e) == 2
        ],
        compiler_params=params_of(dimension_semantics=("arbitrary",)),
        cost_estimate=cost(85),
        name="decode",
    )(place, *sources, *held, cot)


def rows_of(extent):
    return math.prod(extent) // LANES


def up_to(value, step):
    return -(-value // step) * step


def flat_starts(layout):
    starts, here = {}, 0
    for name, extent in layout:
        starts[name] = here
        here += rows_of(extent)
    return starts, here


def kept_starts(layout):
    starts, here = {}, 0
    for name, extent in layout:
        starts[name] = here
        here += up_to(rows_of(extent), 16)
    return starts, here


class Plan:
    def __init__(self, mesh_shape):
        self.ns, self.ng, self.nd = (mesh_shape[a] for a in (SEC, GRP, DP))
        self.ny = self.nd // 2
        self.chunk = PARAMS // LANES // self.ng
        self.pieces = self.ns * self.nd
        self.piece = up_to(-(-self.chunk // self.pieces), 64)
        self.half = self.piece // 2
        self.room = self.piece * self.pieces
        self.tables = 4 if self.ny == 2 else 2
        self.units = 2 * self.pieces
        self.full = self.ng // 2
        self.rest = flat_starts(DEC_LAYOUT)[1] - self.full * self.chunk
        assert 0 < self.rest <= self.chunk
        self.unit = up_to(-(-self.chunk // (self.units - 1)), 64)
        self.dec_room = self.unit * self.units
        whole = self.chunk // self.unit * self.unit
        self.part_in = self.unit if whole < self.dec_room - self.unit else 0
        self.parts_in = -(-self.rest // self.part_in)
        assert self.parts_in <= self.full
        self.enc_starts = [self.kept_row(ENC_LAYOUT, z * self.chunk) // 16 * 16 for z in range(self.ng)]
        self.enc_ends = [
            up_to(self.kept_row(ENC_LAYOUT, min((z + 1) * self.chunk, flat_starts(ENC_LAYOUT)[1]) - 1) + 1, 16)
            for z in range(self.ng)
        ]
        self.dec_starts = [self.kept_row(DEC_LAYOUT, z * self.chunk) // 16 * 16 for z in range(self.full)]
        self.dec_ends = [
            up_to(self.kept_row(DEC_LAYOUT, (z + 1) * self.chunk - 1) + 1, 16) for z in range(self.full)
        ]
        assert all(e - s <= self.room for s, e in zip(self.enc_starts, self.enc_ends))
        self.rest_start = self.kept_row(DEC_LAYOUT, self.full * self.chunk) // 16 * 16
        self.rest_end = kept_starts(DEC_LAYOUT)[1]
        self.part_out = [self.room - (self.dec_ends[k] - self.dec_starts[k]) for k in range(2)]
        assert max(self.part_out) <= self.room // 2
        assert self.part_out[0] < self.rest_end - self.rest_start <= sum(self.part_out)

    def kept_row(self, layout, flat_row):
        flat, _ = flat_starts(layout)
        kept, _ = kept_starts(layout)
        for name, extent in layout:
            if flat_row < flat[name] + rows_of(extent):
                return kept[name] + flat_row - flat[name]
        return kept[name] + rows_of(extent)

    def ranges(self, first, count, cut, chunks, chunk_room):
        found = []
        whole = self.chunk // cut * cut
        while count:
            z, row = divmod(first, self.chunk)
            if z >= chunks:
                k, row = divmod(row, self.part_in)
                here, room = (k + 1) * chunk_room - cut + row, self.part_in - row
            elif row < whole:
                here, room = z * chunk_room + row, whole - row
            else:
                here, room = z * chunk_room + row + cut - (self.chunk - whole), self.chunk - row
            take = min(count, room)
            found.append((here, take))
            first, count = first + take, count - take
        return found

    def packed_row(self, size, groups, index, row, away_x, away_y):
        owner, turned = away_x * self.ny + away_y, away_y * 2 + away_x
        if self.ny != 2:
            return (owner * groups + index) * size + row, size - row
        part = size // 2
        late, row = divmod(row, part)
        if not late:
            second, index = divmod(index, groups // 2)
            block = groups // 2 * part
            return second * (4 * block) + (turned if second else owner) * block + index * part + row, part - row
        fine = part // 2
        second, row = divmod(row, fine)
        start = groups * 4 * part + index * (4 * part) + second * (4 * fine)
        return start + (turned if second else owner) * fine + row, fine - row

    def enc_regions(self, groups):
        return [(self.enc_starts[z], self.enc_ends[z], k, 0) for k, z in enumerate(groups)]

    def dec_regions(self):
        length = self.room // 2
        found = []
        for z in range(self.full):
            low, high = self.dec_starts[z], self.dec_ends[z]
            found += [(low, low + length, 2 * z, 0), (low + length, high, 2 * z + 1, 0)]
        middle = self.rest_start + self.part_out[0]
        found.append((self.rest_start, middle, 1, length - self.part_out[0]))
        found.append((middle, self.rest_end, 3, length - self.part_out[1]))
        return found

    def segments(self):
        count = len(DEC_LAYOUT) + 2
        table = np.zeros((self.ns, self.ng, count, 3), np.int32)
        length = self.room // 2
        for s, layout in enumerate((ENC_LAYOUT, DEC_LAYOUT)):
            flat, used = flat_starts(layout)
            for z in range(self.ng):
                low, high = z * self.chunk, (z + 1) * self.chunk
                found = []
                for name, extent in layout:
                    first, last = max(flat[name], low), min(flat[name] + rows_of(extent), high)
                    while first < last:
                        row, stop = self.kept_row(layout, first), last
                        if s == 0:
                            source = row - self.enc_starts[z]
                        elif z < self.full:
                            source = row - self.dec_starts[z]
                        else:
                            row -= self.rest_start
                            k = int(row >= self.part_out[0])
                            row -= k * self.part_out[0]
                            source = (k + 1) * length - self.part_out[k] + row
                            stop = min(last, first + self.part_out[k] - row)
                        found.append((source, first - low, -(-(stop - first) // 8)))
                        first = stop
                if used < high:
                    found.append((self.room, max(used - low, 0), 1))
                table[s, z, : len(found)] = found
        return table


def widen_block(held, wide, spare, ranges, rows):
    def load(start, count, further=0):
        first = start // 16 * 16
        size = up_to(start + count - first, 16)
        if isinstance(further, int):
            return held[first : first + size, :].astype(f32), size, start - first
        return held[pl.ds(pl.multiple_of(first + further, 16), size), :].astype(f32), size, start - first

    if isinstance(ranges, tuple):
        block, size, skip = load(ranges[0], rows, ranges[1])
        wide[0:size, :] = block
        return skip
    if len(ranges) == 1:
        block, size, skip = load(*ranges[0])
        wide[0:size, :] = block
        return skip
    here = 0
    for start, count in ranges:
        block, size, skip = load(start, count)
        spare[0:size, :] = block
        wide[here : here + count, :] = spare[skip : skip + count, :]
        here += count
    return 0


def unpack_weights(
    plan, layout, unit, cut, chunks, room, place_ref, sources, counts, outs, vec, held, wide, spare, sems, copies=(),
):
    matrices = [n for n, e in layout if len(e) == 2]
    per_chunk = room // unit
    number = 0
    for source, count in zip(sources, counts):
        for k in range(count):
            slot = place_ref[number]
            number += 1
            target = held.at[pl.ds(pl.multiple_of(slot * unit, 16), unit), :]
            pltpu.make_async_copy(source.at[pl.ds(k * unit, unit), :], target, sems.at[slot // per_chunk]).start()
    arrived = set()

    def arrive(ranges):
        for start, count in ranges:
            z = start // room
            if z not in arrived:
                arrived.add(z)
                part = held.at[pl.ds(z * room, room), :]
                pltpu.make_async_copy(part, part, sems.at[z]).wait()

    vec[...] = jnp.zeros_like(vec)
    flat, _ = flat_starts(layout)
    by_name = dict(zip(matrices, outs))
    order = dict(zip(matrices, copies))
    for name, extent in layout:
        if len(extent) == 2:
            depth, lanes = extent[0], extent[1] // LANES
            step = depth if name == POS else max(128, 2048 // lanes // 128 * 128)
            out = by_name[name]
            if name == POS:
                out[...] = jnp.zeros_like(out)
            found = [
                plan.ranges(flat[name] + first * lanes, min(step, depth - first) * lanes, cut, chunks, room)
                for first in range(0, depth, step)
            ]
            for ranges in found:
                arrive(ranges)

            def move(number, start, size, lanes=lanes, step=step, out=out):
                skip = widen_block(held, wide, spare, start, size * lanes)
                rows = pl.ds(number * step if isinstance(number, int) else pl.multiple_of(number * step, step), size)
                for j in range(lanes):
                    out[rows, j * LANES : (j + 1) * LANES] = wide[pl.ds(skip + j, size, stride=lanes), :].astype(bf16)

            k = 0
            while k < len(found):
                size = min(step, depth - k * step)
                run = 1
                if len(found[k]) == 1 and size == step and step * lanes % 16 == 0:
                    begin = found[k][0][0]
                    while k + run < len(found) and found[k + run] == [(begin + run * step * lanes, step * lanes)]:
                        run += 1
                if run > 1:

                    def turn(i, carry, k=k, begin=begin, lanes=lanes, step=step, move=move):
                        move(k + i, (begin, i * step * lanes), step)
                        return carry

                    lax.fori_loop(0, run, turn, 0)
                else:
                    move(k, found[k], size)
                k += run
            if name in order:
                order[name].start()
        else:
            lanes = extent[0] // LANES
            ranges = plan.ranges(flat[name], lanes, cut, chunks, room)
            arrive(ranges)
            skip = widen_block(held, wide, spare, ranges, lanes)
            row, shift = {QB: (2, 0), VB: (2, 2 * extent[0])}.get(name, (VEC.get(name), 0))
            for j in range(lanes):
                vec[row : row + 1, shift + j * LANES : shift + (j + 1) * LANES] = wide[skip + j : skip + j + 1, :]
    for z in range(chunks):
        arrive([(z * room, 1)])


def pack_kernel(plan, layout, names, regions, size, groups, place_ref, *refs):
    pairs = {}
    for name in names:
        pairs[name], refs = refs[:2], refs[2:]
    vec, refs = refs[0], refs[1:]
    pos = None
    if POS in names:
        pos, refs = pairs[POS][0], refs
    mine, theirs, wide, stage, small, sems = refs
    kept, _ = kept_starts(layout)
    extents = dict(layout)
    ny = plan.ny

    def send(source, first, rows, sem):
        moved = 0
        for low, high, index, base in regions:
            start, stop = max(first, low), min(first + rows, high)
            while start < stop:
                number, row = divmod(base + start - low, size)
                c, s, y = number // (2 * ny), number // ny % 2, number % ny
                away_x, away_y = lax.rem(s - place_ref[0] + 2, 2), lax.rem(y - place_ref[1] + ny, ny)
                where, room = plan.packed_row(size, groups, index, row, away_x, away_y)
                count = min(stop - start, room)
                target = pl.ds(pl.multiple_of(where, 16), count)
                block = source.at[pl.ds(start - first, count), :]
                for same, table in ((True, mine), (False, theirs)):

                    @pl.when((place_ref[2] == c) == same)
                    def _():
                        pltpu.make_async_copy(block, table.at[target, :], sem).start()

                moved += count
                start += count
        return moved

    def wait(rows, slot):
        if rows:
            block = stage.at[slot, pl.ds(0, rows), :]
            pltpu.make_async_copy(block, block, sems.at[slot]).wait()

    turn = 0
    pending = [0, 0]
    for name in names:
        if name == POS:
            continue
        left, right = pairs[name]
        depth, width = extents[name]
        lanes = width // LANES
        step = max(k for k in (128, 256, 384, 512) if depth % k == 0 and k * lanes <= 3072)
        rows = step * lanes
        for first in range(0, depth, step):
            start = kept[name] + first * lanes
            if all(start >= high or start + rows <= low for low, high, _, _ in regions):
                continue
            slot = turn % 2
            turn += 1
            columns = flip(left[:, first : first + step])
            part = 256
            for start in range(0, width, part):
                block = dot(columns, right[:, start : start + part])
                for j in range(part // LANES):
                    wide[pl.ds(start // LANES + j, step, stride=lanes), :] = block[:, j * LANES : (j + 1) * LANES]
            wait(pending[slot], slot)
            stage[slot, 0:rows, :] = wide[0:rows, :].astype(bf16)
            pending[slot] = send(stage.at[slot], kept[name] + first * lanes, rows, sems.at[slot])
    here = 0
    total = 0
    for name, extent in layout:
        if name not in names and len(extent) == 2 or name not in kept_names(names):
            continue
        if len(extent) == 2 and name != POS:
            continue
        rows = rows_of(extent)
        room = up_to(rows, 16)
        wide[0:room, :] = jnp.zeros((room, LANES), f32)
        if name == POS:
            lanes = extent[1] // LANES
            for j in range(lanes):
                wide[pl.ds(j, extent[0], stride=lanes), :] = pos[0 : extent[0], j * LANES : (j + 1) * LANES]
        else:
            row, shift = {QB: (2, 0), VB: (2, 2 * extent[0])}.get(name, (VEC.get(name), 0))
            for j in range(rows):
                wide[j : j + 1, :] = vec[row : row + 1, shift + j * LANES : shift + (j + 1) * LANES]
        small[here : here + room, :] = wide[0:room, :].astype(bf16)
        total += send(small.at[pl.ds(here, room), :], kept[name], room, sems.at[2])
        here += room
    wait(pending[0], 0)
    wait(pending[1], 1)
    block = small.at[pl.ds(0, total), :]
    pltpu.make_async_copy(block, block, sems.at[2]).wait()


def pack_enc_kernel(plan, names, regions, size, groups, place_ref, *refs):
    pairs = {}
    for name in names:
        pairs[name], refs = refs[:4], refs[4:]
    vec, vec_other, *tables = refs[: 2 + plan.tables]
    wide, stage, small, sems = refs[2 + plan.tables :]
    lates = [a for four in pairs.values() for a in four] + [vec, vec_other]
    kept, _ = kept_starts(ENC_LAYOUT)
    extents = dict(ENC_LAYOUT)
    ny = plan.ny

    def pieces(first, rows, core):
        for low, high, index, base in regions:
            start, stop = max(first, low), min(first + rows, high)
            while start < stop:
                number, row = divmod(base + start - low, size)
                count = min(stop - start, size - row)
                if number // (2 * ny) == core:
                    yield start - first, count, index, row, number // ny % 2, number % ny
                start += count

    def send(source, first, rows, sem, core):
        moved = 0
        for skip, count, index, row, s, y in pieces(first, rows, core):
            away_x, away_y = lax.rem(s - place_ref[0] + 2, 2), lax.rem(y - place_ref[1] + ny, ny)
            if ny == 2 and index >= groups // 2:
                keep, away, other, index = tables[2:], away_y, away_x, index - groups // 2
            else:
                keep, away, other = tables[:2], away_x, away_y
            length = (groups // 2 if ny == 2 else groups) * size
            target = pl.ds(pl.multiple_of(other * length, 16) + index * size + row, count)
            block = source.at[pl.ds(skip, count), :]
            for k in range(2):

                @pl.when(away == k)
                def _():
                    pltpu.make_async_copy(block, keep[k].at[target, :], sem).start()

            moved += count
        return moved

    def wait(rows, slot):
        if rows:
            block = stage.at[slot, pl.ds(0, rows), :]
            pltpu.make_async_copy(block, block, sems.at[slot]).wait()

    def run(core):
        turn = 0
        pending = [0, 0]
        for name in names:
            left, left_other, right, right_other = pairs[name]
            depth, width = extents[name]
            lanes = width // LANES
            step = max(k for k in (128, 256, 384, 512) if depth % k == 0 and k * lanes <= 3072)
            rows = step * lanes
            for first in range(0, depth, step):
                begin = kept[name] + first * lanes
                if not list(pieces(begin, rows, core)):
                    continue
                slot = turn % 2
                turn += 1
                columns = flip(left[:, first : first + step])
                others = flip(left_other[:, first : first + step])
                part = 256
                for start in range(0, width, part):
                    cols = slice(start, start + part)
                    block = dot(columns, right[:, cols]) + dot(others, right_other[:, cols])
                    for j in range(part // LANES):
                        wide[pl.ds(start // LANES + j, step, stride=lanes), :] = block[:, j * LANES : (j + 1) * LANES]
                wait(pending[slot], slot)
                stage[slot, 0:rows, :] = wide[0:rows, :].astype(bf16)
                pending[slot] = send(stage.at[slot], begin, rows, sems.at[slot], core)
        here = 0
        total = 0
        for name, extent in ENC_LAYOUT:
            if name not in kept_names(names):
                continue
            rows = rows_of(extent)
            room = up_to(rows, 16)
            if list(pieces(kept[name], room, core)):
                wide[0:room, :] = jnp.zeros((room, LANES), f32)
                row, shift = {QB: (2, 0), VB: (2, 2 * extent[0])}.get(name, (VEC.get(name), 0))
                for j in range(rows):
                    cols = slice(shift + j * LANES, shift + (j + 1) * LANES)
                    wide[j : j + 1, :] = vec[row : row + 1, cols] + vec_other[row : row + 1, cols]
                small[here : here + room, :] = wide[0:room, :].astype(bf16)
                total += send(small.at[pl.ds(here, room), :], kept[name], room, sems.at[2], core)
            here += room
        wait(pending[0], 0)
        wait(pending[1], 1)
        if total:
            block = small.at[pl.ds(0, total), :]
            pltpu.make_async_copy(block, block, sems.at[2]).wait()

    for core in range(2):

        @pl.when(place_ref[2] == core)
        def _():
            for each in lates:
                each.here = False
            run(core)
            for each in lates:
                each.arrive()


def pack_enc(plan, regions, size, groups, place, pairs, vec, vec_other):
    names = list(pairs)
    operands = [a for name in names for a in pairs[name]] + [vec, vec_other]
    extents = dict(ENC_LAYOUT)
    small = sum(up_to(rows_of(extents[n]), 16) for n in kept_names(names))
    rows = 2 * plan.ny * groups * size // plan.tables
    return late_call(
        partial(pack_enc_kernel, plan, names, regions, size, groups),
        [(place, pltpu.SMEM)],
        operands,
        [(shape((rows, LANES), bf16), pl.ANY)] * plan.tables,
        [
            pltpu.VMEM((3072, LANES), f32),
            pltpu.VMEM((2, 3072 + 64, LANES), bf16),
            pltpu.VMEM((small + 64, LANES), bf16),
            pltpu.SemaphoreType.DMA((3,)),
        ],
        cost_estimate=cost(8),
        name="pack_enc",
    )


def kept_names(names):
    with_matrix = {
        QKV_W: [N1G, N1B, QB, VB],
        PROJ_W: [PB, N2G, N2B],
        UP_W: [UB],
        DOWN_W: [DB],
        EMBED_W: [EB, MT],
        POS: [POS],
    }
    return [v for n in names for v in with_matrix[n]]


def pack(plan, layout, regions, size, groups, place, pairs, vec):
    names = list(pairs)
    operands = [a for name in names for a in pairs[name]] + [vec]
    extents = dict(layout)
    small = sum(up_to(rows_of(extents[n]), 16) for n in kept_names(names))
    rows = 2 * plan.ny * groups * size
    return late_call(
        partial(pack_kernel, plan, layout, names, regions, size, groups),
        [(place, pltpu.SMEM)],
        operands,
        [(shape((rows, LANES), bf16), pl.ANY)] * 2,
        [
            pltpu.VMEM((3072, LANES), f32),
            pltpu.VMEM((2, 3072 + 64, LANES), bf16),
            pltpu.VMEM((small + 64, LANES), bf16),
            pltpu.SemaphoreType.DMA((3,)),
        ],
        cost_estimate=cost(19),
        name="pack",
    )


def finish_kernel(plan, counts, place_ref, seg_ref, *refs):
    sources, result, held, wide, out, sem = refs[: len(counts)], *refs[len(counts) :]
    unit = plan.half
    number = 0
    for source, count in zip(sources, counts):
        for k in range(count):
            target = held.at[pl.ds(pl.multiple_of(place_ref[number] * unit, 16), unit), :]
            number += 1
            pltpu.make_async_copy(source.at[pl.ds(k * unit, unit), :], target, sem.at[0]).start()
    out[...] = jnp.zeros_like(out)
    pltpu.make_async_copy(held, held, sem.at[0]).wait()
    total = plan.room
    wide[total : total + 16, :] = jnp.zeros((16, LANES), f32)
    wide[0:total, :] = held[...].astype(f32)

    def one(k, carry):
        source, first, steps = seg_ref[3 * k], seg_ref[3 * k + 1], seg_ref[3 * k + 2]

        def step(i, carry):
            out[pl.ds(first + 8 * i, 8), :] = wide[pl.ds(source + 8 * i, 8), :]
            return carry

        def steps8(i, carry):
            out[pl.ds(first + 64 * i, 64), :] = wide[pl.ds(source + 64 * i, 64), :]
            return carry

        many = steps // 8
        lax.fori_loop(0, many, steps8, 0)
        return lax.fori_loop(many * 8, steps, step, carry)

    lax.fori_loop(0, seg_ref.shape[0] // 3, one, 0)
    rows = up_to(plan.chunk, 8)
    lines = out.at[pl.ds(0, rows), :].reshape(rows, 1, LANES)
    copy = pltpu.make_async_copy(lines.at[pl.ds(0, plan.chunk)], result, sem.at[0])
    copy.start()
    copy.wait()


def finish(plan, place, segments, sources):
    total = plan.room
    return pl.pallas_call(
        partial(finish_kernel, plan, [s.shape[0] // plan.half for s in sources]),
        in_specs=[pl.BlockSpec(memory_space=pltpu.SMEM)] * 2
        + [pl.BlockSpec(memory_space=pl.ANY)] * len(sources),
        out_specs=pl.BlockSpec(memory_space=pl.ANY),
        out_shape=shape((plan.chunk, 1, LANES), f32),
        scratch_shapes=[
            pltpu.VMEM((total, LANES), bf16),
            pltpu.VMEM((total + 16, LANES), f32),
            pltpu.VMEM((up_to(plan.chunk, 8) + 8, LANES), f32),
            pltpu.SemaphoreType.DMA((1,)),
        ],
        compiler_params=params_of(),
        cost_estimate=cost(8),
        name="finish",
    )(place, segments, *sources)


def completed(pairs, count):
    senders = [k for k in range(count) if k not in [a for a, _ in pairs]]
    receivers = [k for k in range(count) if k not in [b for _, b in pairs]]
    return list(pairs) + list(zip(senders, receivers))


def after(values, *before):
    return lax.optimization_barrier((values, before))[0]


def per_device(plan, enc_input, segments, slots, params, cot):
    ns, ng, nd, ny = plan.ns, plan.ng, plan.nd, plan.ny
    piece, half, room, chunk = plan.piece, plan.half, plan.room, plan.chunk
    sec = lax.axis_index(SEC)
    grp = lax.axis_index(GRP)
    dp = lax.axis_index(DP)
    yy, core = dp // 2, dp % 2
    first_section = sec == 0

    def over_x(block):
        return lax.ppermute(block, SEC, [(0, 1), (1, 0)])

    def over_core(block):
        return lax.ppermute(block, DP, [(d, d ^ 1) for d in range(nd)])

    def over_y(block):
        return lax.ppermute(block, DP, [(d, (d + 2) % nd) for d in range(nd)])

    def over_z(block, senders=None):
        senders = range(ng) if senders is None else senders
        return lax.ppermute(block, GRP, [(g, (g + 1) % ng) for g in senders])

    def final_places():
        if ny == 2:
            owners = [(sec, yy), (1 - sec, yy), (sec, 1 - yy), (1 - sec, 1 - yy)]
        else:
            owners = [(s, (yy - k) % ny) for k in range(ny) for s in (sec, 1 - sec)]
        found = []
        for c in (core, 1 - core):
            for s, y in owners:
                number = (c * 2 + s) * ny + y
                found += [
                    jnp.where(first_section, 2 * number, number),
                    jnp.where(first_section, 2 * number + 1, plan.pieces + number),
                ]
        return found

    unit = plan.unit

    def share(start, params):
        cut = lax.dynamic_slice(params, (0, start * LANES), (1, unit * LANES))
        return cut.astype(f32).reshape(unit, LANES).astype(bf16)

    def shares(section, params):
        number = section * nd + dp
        enc_first = jnp.minimum(number * piece, chunk - piece)
        dec_first = [jnp.minimum((h * plan.pieces + number) * unit, chunk - unit) for h in range(2)]
        if plan.parts_in == 1:
            dec_first[0] = jnp.where(grp == plan.full, 0, dec_first[0])
        return (
            share(jnp.where(first_section, enc_first, dec_first[0]), params),
            share(jnp.where(first_section, enc_first + piece - unit, dec_first[1]), params),
        )

    send = shares(1 - sec, params)
    keep = shares(sec, after(params, *send))

    def whole_piece(parts):
        return jnp.concatenate([parts[0][:half], parts[1][unit - half :]])

    routes = [[(z, 2 * z + h) for z in range(plan.full)] for h in range(2)]
    if plan.parts_in == 1:
        routes[0].append((plan.full, 1))
    routes = [completed(route, ng) for route in routes]
    crossed = []
    for h in range(2):
        pairs = [(z, ng + z) for z in range(ng)] + [(ng + a, b) for a, b in routes[h]]
        crossed.append(lax.ppermute(send[h], (SEC, GRP), pairs))
    spread = [lax.ppermute(keep[h], GRP, routes[h]) for h in range(2)]
    enc_piece = jnp.where(first_section, whole_piece(keep), whole_piece(crossed))
    even, odd = (jnp.where(first_section, crossed[h], spread[h]) for h in range(2))
    dec_piece = jnp.where(grp % 2 == 0, even, odd)
    class Gather:
        def __init__(self, here):
            self.here = here
            if ny == 2:
                self.arrays = [here, over_x(here), over_y(here)]
                self.owners = [(sec, yy), (1 - sec, yy), (sec, 1 - yy), (1 - sec, 1 - yy)]
            else:
                column = [here]
                for _ in range(ny - 1):
                    column.append(over_y(column[-1]))
                self.arrays = column
                self.owners = [(s, (yy - k) % ny) for s in (sec, 1 - sec) for k in range(ny)]

        def second(self):
            if ny == 2:
                middle = self.here.shape[0] // 2
                self.corners = [self.arrays[1][:middle], self.arrays[2][middle:]]
            else:
                self.corners = self.arrays
            return tuple(self.corners)

        def third(self):
            if ny == 2:
                self.arrays += [over_y(self.corners[0]), over_x(self.corners[1])]
            else:
                self.arrays = self.arrays + [over_x(block) for block in self.corners]
            return tuple(self.arrays[-2:])

        def fourth(self, joined=True):
            arrays = [jnp.concatenate(self.arrays)] if joined else self.arrays
            return arrays + [over_core(block) for block in arrays]

        def places(self, parts):
            found = []
            for c in (core, 1 - core):
                for s, y in self.owners:
                    for k in parts:
                        number = (grp - k) % ng * plan.pieces + s * nd + y * 2 + c
                        found += [2 * number, 2 * number + 1]
            return found

    last = jnp.logical_and(sec == ns - 1, dp == nd - 1)
    if plan.parts_in == 1:
        dec_piece = jnp.where(jnp.logical_and(last, grp == 1), even, dec_piece)
    else:
        for k in range(plan.parts_in):
            part = share(jnp.minimum(k * unit, chunk - unit), params)
            part = lax.ppermute(part, GRP, [(plan.full, 2 * k + 1)])
            dec_piece = jnp.where(jnp.logical_and(last, grp == 2 * k + 1), part, dec_piece)
    here = enc_piece
    gathers = [Gather(here)]
    micro_rows = enc_input.reshape(ROW, WIDTH)
    seg = lax.dynamic_index_in_dim(segments, sec, 0, keepdims=False).reshape(ROW)
    slot = lax.dynamic_index_in_dim(slots, sec, 0, keepdims=False).reshape(ROW)
    cot_rows = jnp.pad(
        cot.reshape(IMAGES_ROW, SLOTS, DEC_WIDTH), ((0, 0), (0, SLOT_PAD - SLOTS), (0, 0))
    ).reshape(IMAGES_ROW * SLOT_PAD, DEC_WIDTH)

    columns = (seg.reshape(ROW, 1), slot.reshape(ROW, 1))
    table = jnp.asarray(plan.segments())[sec, grp].reshape(-1)
    place = jnp.stack([sec, yy, core]).astype(jnp.int32)
    finish_places = jnp.stack(final_places()).astype(jnp.int32)
    enc_places = jnp.stack([p for k in range(ng) for p in gathers[0].places([k])]).astype(jnp.int32)
    dec_places = jnp.stack(gathers[0].places(range(ng))).astype(jnp.int32)
    small = (columns, table, place, finish_places, enc_places, dec_places, cot_rows)
    for k in range(1, ng):
        here = over_z(here)
        if k == 1:
            here, small = after((here, small), enc_piece)
            here = after(here, *small)
        if k >= 2:
            here = after(here, *gathers[k - 2].second())
        if k >= 3:
            here = after(here, *gathers[k - 3].third())
        gathers.append(Gather(here))
    gathers[-2].second()
    dec_parts = [after(dec_piece, here)]
    for _ in range(ng - 1):
        dec_parts.append(over_z(dec_parts[-1]))
    gathers[-1].arrays[1:] = after(gathers[-1].arrays[1:], *dec_parts[1:-1])
    gathers[-1].second()
    columns, table, place, finish_places, enc_places, dec_places, cot_rows = small
    enc_sources = []
    for k, g in enumerate(gathers):
        if k >= ng - 3:
            g.third()
        if k == ng - 1:
            g.arrays = after(g.arrays, dec_parts[-1])
        enc_sources += g.fourth()
    dec_gather = Gather(after(jnp.concatenate(dec_parts), *gathers[-1].corners))

    enc_weights, saved = encode(plan, enc_places, enc_sources, micro_rows, seg, columns[0])
    dec_gather.arrays[1:] = after(dec_gather.arrays[1:], saved[H2])
    saved[H2] = after(saved[H2], *dec_gather.second())
    saved.update(encode_mlp(saved, enc_weights))
    others = {k: over_core(saved[k]) for k in (H1, ATT, H2, ACT)}
    dec_gather.third()
    dec_gather.arrays[-2:] = after(dec_gather.arrays[-2:], saved[SENT])
    dec_sources = dec_gather.fourth(False)
    dec = dict(
        zip(
            [OUT, H1, QKV_L, ATT, PROJ_L, H2, UP_L, ACT, EMBED_L, GSENT, VECS, GPOS],
            decode(plan, dec_places, dec_sources, saved[SENT], seg, slot, columns, cot_rows),
        )
    )

    def add(first, *others):
        total = first.astype(f32)
        for other in others:
            total = total + other.astype(f32)
        return total.astype(bf16)

    class Square:
        def __init__(self, keeps, sends):
            self.keeps, self.sends = keeps, [add(*parts) if len(parts) > 1 else parts[0] for parts in sends]
            self.m = keeps[0][0].shape[0] // ny

        def kept(self, half, low, high, *others):
            return add(*[part[low:high] for part in self.keeps[half]], *others)

        def first(self):
            return (over_x(self.sends[0]), over_y(self.sends[1])) if ny == 2 else (over_x(self.sends[0]),)

        def second(self, *got):
            m = self.m
            self.got = got
            if ny == 2:
                self.sends = tuple(self.kept(k, m, 2 * m, got[k][m:]) for k in range(2))
            else:
                column = self.kept(0, 0, ny * m, got[0])
                total = column[(ny - 1) * m :]
                for k in range(ny - 2, -1, -1):
                    total = add(column[k * m : (k + 1) * m], over_y(total))
                self.sends = (total,)
            return self.sends

        def third(self, *before):
            m = self.m
            if ny == 2:
                late = after((over_y(self.sends[0]), over_x(self.sends[1])), *before)
                self.own = tuple(self.kept(k, 0, m, self.got[k][:m], late[k]) for k in range(2))
            else:
                self.own = (self.sends[0][: m // 2], self.sends[0][m // 2 :])
            return self.own

    class Ring:
        def __init__(self, one):
            self.one, self.step = one, 0
            self.total = add(*one((grp - 1) % ng))

        def next(self, *before):
            got = after(over_z(self.total), *before)
            self.step += 1
            self.total = add(*self.one((grp - 1 - self.step) % ng), got)
            return self.total

    def pick(blocks, g):
        if len(blocks) == 4 == ng:
            return jnp.where(g < 2, jnp.where(g == 0, *blocks[:2]), jnp.where(g == 2, *blocks[2:]))
        rows = jnp.concatenate(blocks)
        size = rows.shape[0] // ng
        return lax.dynamic_slice(rows, (g * size, 0), (size, LANES))

    def halves(block):
        return [block[: block.shape[0] // 2], block[block.shape[0] // 2 :]]

    every = list(range(ng))
    near = ng // 2
    upper, lower = every[near:], every[:near]
    grad_sent, others = after((dec[GSENT], others), dec[VECS])
    grad_sent = after(grad_sent, *others.values())
    grad_other = over_core(grad_sent)
    up_low, proj_low, grad_middle, mlp_vec = mlp_back(grad_sent, saved, enc_weights)
    grad_other = after(grad_other, up_low)
    up_other, proj_other, mlp_vec_other = over_core(up_low), over_core(proj_low), over_core(mlp_vec)
    in_grad, qkv_low, enc_vec = attention_back(grad_middle, proj_low, micro_rows, saved, enc_weights, mlp_vec)
    up_other, proj_other, mlp_vec_other = after((up_other, proj_other, mlp_vec_other), qkv_low)
    up_tables = pack_enc(
        plan, plan.enc_regions(upper), piece, len(upper), place,
        {
            DOWN_W: (saved[ACT], others[ACT], grad_sent, grad_other),
            UP_W: (saved[H2], others[H2], after(up_low, qkv_low), up_other),
        },
        mlp_vec, mlp_vec_other,
    )
    qkv_other, vec_other = after((over_core(qkv_low), over_core(enc_vec)), up_tables[0])
    dec_mine, dec_theirs = pack(
        plan, DEC_LAYOUT, plan.dec_regions(), half, ng, place,
        {
            EMBED_W: (saved[SENT], dec[EMBED_L]),
            QKV_W: (dec[H1], dec[QKV_L]),
            PROJ_W: (dec[ATT], dec[PROJ_L]),
            UP_W: (dec[H2], dec[UP_L]),
            DOWN_W: (dec[ACT], cot_rows),
            POS: (dec[GPOS], dec[GPOS]),
        },
        after(dec[VECS], up_tables[0]),
    )
    qkv_other, vec_other = after((qkv_other, vec_other), dec_mine)

    def table_square(tables):
        return Square([[t] for t in tables[0::2]], [[t] for t in tables[1::2]])

    upper_sum = table_square(up_tables)
    upper_sum.second(*after(upper_sum.first(), dec_mine))
    low_tables = pack_enc(
        plan, plan.enc_regions(lower), piece, len(lower), place,
        {
            PROJ_W: (saved[ATT], others[ATT], proj_low, proj_other),
            QKV_W: (saved[H1], others[H1], qkv_low, qkv_other),
            UP_W: (saved[H2], others[H2], after(up_low, *upper_sum.sends), up_other),
        },
        enc_vec, vec_other,
    )
    lower_sum = table_square(low_tables)
    lower_first = lower_sum.first()
    dec_parts = (dec_mine, after(over_core(dec_theirs), low_tables[0]))

    def dec_rows(low, high):
        return [part[low:high] for part in dec_parts]

    if ny == 2:
        rows = dec_mine.shape[0] // 2
        size = rows // ng

        def dec_late(g):
            return [lax.dynamic_slice(part, (rows + g * size, 0), (size, LANES)) for part in dec_parts]

        late_ring = Ring(dec_late)
        quarter = rows // 4
        cuts = [dec_rows(k * quarter, (k + 1) * quarter) for k in range(4)]
        upper_sum.third(late_ring.total)
        lower_sum.second(*after(lower_first, *upper_sum.own))
        early = Square(cuts[0::2], cuts[1::2])
        early.sends = after(early.sends, *lower_sum.sends)
        early_first = early.first()
        late_ring.next(*early.sends)
        lower_sum.third(late_ring.total)
        enc_ring = Ring(lambda g: [pick(list(lower_sum.own) + list(upper_sum.own), g)])
        early.second(*after(early_first, enc_ring.total))
        for _ in range(ng - 3):
            late_ring.next(*early.sends)
        early_own = [b for o in early.third(late_ring.total) for b in halves(o)]
        early_ring = Ring(lambda g: [pick(early_own, g)])
        enc_ring.next(early_ring.total)
        late_ring.next(enc_ring.total)
        quarter = size // 4
        cuts = [[late_ring.total[k * quarter : (k + 1) * quarter]] for k in range(4)]
        late = Square(cuts[0::2], cuts[1::2])
        late_first = late.first()
        early_ring.next(*late.sends)
        late.second(*after(late_first, early_ring.total))
        early_ring.next(*late.sends)
        late_own = late.third(early_ring.total)
        for _ in range(ng - 3):
            early_ring.next(*late_own)
        dec_own = jnp.concatenate([early_ring.total, *late_own])
    else:
        lower_sum.second(*lower_first)
        rows = dec_mine.shape[0] // 2
        whole = Square([dec_rows(0, rows)], [dec_rows(rows, 2 * rows)])
        whole.second(*whole.first())
        dec_ring = Ring(lambda g: [pick(list(whole.third()), g)])
        for _ in range(ng - 1):
            dec_ring.next()
        dec_own = dec_ring.total
        upper_sum.third()
        lower_sum.third()
        enc_ring = Ring(lambda g: [pick(list(lower_sum.own) + list(upper_sum.own), g)])
        enc_ring.next()
    back = [[(2 * z + h, z) for z in range(plan.full)] for h in range(2)]
    back[0].append((1, plan.full))
    back.append([(3, plan.full)])
    dec_back = [lax.ppermute(dec_own, GRP, completed(pairs, ng)) for pairs in back]
    enc_ring.next(dec_own)
    dec_low, dec_high, dec_rest = after(dec_back, enc_ring.total)
    dec_own = jnp.concatenate([dec_low, jnp.where(grp == plan.full, dec_rest, dec_high)])
    for _ in range(ng - 3):
        enc_ring.next(dec_own)
    enc_own = enc_ring.total

    own = jnp.where(first_section, enc_own, dec_own)
    other = jnp.where(first_section, dec_own, enc_own)
    if ny == 2:
        from_x, from_y = over_x(other), over_y(own)
        sources = [own, from_x, from_y, over_y(from_x)]
    else:
        column = [jnp.concatenate([own, over_x(other)])]
        for _ in range(ny - 1):
            column.append(over_y(column[-1]))
        sources = column
    sources = sources + [over_core(block) for block in sources]
    flat = finish(plan, finish_places, table, sources)
    param_grad = flat.reshape(1, chunk * LANES)
    dec_out = dec[OUT].reshape(IMAGES_ROW, SLOT_PAD, DEC_WIDTH)[:, :SLOTS]
    return (
        dec_out.reshape(1, 1, IMAGES_ROW * SLOTS, DEC_WIDTH),
        in_grad.reshape(1, 1, ROW, WIDTH),
        param_grad,
    )


def solution(mesh):
    placed = (
        P(SEC, (GRP, DP), None, None),
        P(None, (GRP, DP), None),
        P(None, (GRP, DP), None),
        P(SEC, GRP),
        P(SEC, (GRP, DP), None, None),
    )
    return jax.shard_map(
        partial(per_device, Plan(dict(mesh.shape))),
        mesh=mesh,
        in_specs=placed,
        out_specs=(
            P(SEC, (GRP, DP), None, None),
            P(SEC, (GRP, DP), None, None),
            P(SEC, GRP),
        ),
        check_vma=False,
    )
```

```python
from functools import partial
import math

import jax
import jax.numpy as jnp
import numpy as np
from jax import lax
from jax.experimental import pallas as pl
from jax.experimental.pallas import tpu as pltpu
from jax.sharding import PartitionSpec as P

WIDTH = 768
HEADS = 12
HIDDEN_SIZE = 3072
DEC_WIDTH = 512
DEC_HEADS = 16
DEC_HIDDEN = 2048
SLOTS = 196
IMAGES_ROW = 5
ROW = 256
PARAMS = 7088128
LANES = 128
SEC, GRP, DP = "section", "group", "dp"
(
    N1G, N1B, QKV_W, QB, VB, PROJ_W, PB, N2G,
) = range(0, 8)
(
    N2B, UP_W, UB, DOWN_W, DB, EMBED_W, EB, MT,
) = range(8, 16)
(
    POS, QKV_B, VECS, SENT, H1, QKV, PROBS, ATT,
) = range(16, 24)
(
    MID, H2, ACT, SLOPE, OUT, QKV_L, PROJ_L, UP_L,
) = range(24, 32)
(
    EMBED_L, GSENT, GPOS,
) = range(32, 35)
SLOT_PAD = 208
VMEM_BYTES = 60 * 1024 * 1024

norm_eps = 1e-06
masked_score = -1000000000.0
f32 = jnp.float32
bf16 = jnp.bfloat16


def block_layout(width, hidden):
    return [
        (N1G, (width,)),
        (N1B, (width,)),
        (QKV_W, (width, 3 * width)),
        (QB, (width,)),
        (VB, (width,)),
        (PROJ_W, (width, width)),
        (PB, (width,)),
        (N2G, (width,)),
        (N2B, (width,)),
        (UP_W, (width, hidden)),
        (UB, (hidden,)),
        (DOWN_W, (hidden, width)),
        (DB, (width,)),
    ]


def decoder_layout(enc_width, width, hidden, slot_count):
    return [
        (EMBED_W, (enc_width, width)),
        (EB, (width,)),
        (MT, (width,)),
        (POS, (slot_count, width)),
    ] + block_layout(width, hidden)


ENC_LAYOUT = block_layout(WIDTH, HIDDEN_SIZE)
DEC_LAYOUT = decoder_layout(WIDTH, DEC_WIDTH, DEC_HIDDEN, SLOTS)
VEC = {
    N1G: 0,
    N1B: 1,
    QKV_B: 2,
    PB: 3,
    N2G: 4,
    N2B: 5,
    UB: 6,
    DB: 7,
    EB: 8,
    MT: 9,
}
VEC_ROWS = 16


def dot(a, b):
    return lax.dot_general(a, b, (((1,), (0,)), ((), ())), preferred_element_type=f32)


def dot_nt(a, b):
    return lax.dot_general(a, b, (((1,), (1,)), ((), ())), preferred_element_type=f32)


def dot_tn(a, b):
    return lax.dot_general(a, b, (((0,), (0,)), ((), ())), preferred_element_type=f32)


def normalised(values):
    centered = values - jnp.mean(values, axis=-1, keepdims=True)
    inverse = lax.rsqrt(jnp.mean(centered * centered, axis=-1, keepdims=True) + norm_eps)
    return centered * inverse, inverse


def norm_back(grad, hat, inverse, gain):
    scaled = grad * gain
    first = jnp.mean(scaled, axis=-1, keepdims=True)
    second = jnp.mean(scaled * hat, axis=-1, keepdims=True)
    return inverse * (scaled - first - hat * second)


def col_sum(values):
    return jnp.sum(values, axis=0, keepdims=True)


def gelu_parts(upward):
    half = 0.5 + 0.5 * lax.erf(upward * f32(math.sqrt(0.5)))
    slope = half + upward * (jnp.exp(upward * upward * f32(-0.5)) * f32(1.0 / math.sqrt(2.0 * math.pi)))
    return upward * half, slope


def head_mask(head, head_dim):
    lane = lax.broadcasted_iota(jnp.int32, (1, LANES), 1)
    return jnp.where(lane // head_dim == head, 1.0, 0.0).astype(bf16)


def lane_block(group, start=0):
    if isinstance(group, int):
        return slice(start + group * LANES, start + (group + 1) * LANES)
    return pl.ds(pl.multiple_of(start + group * LANES, LANES), LANES)


def flip(values):
    return values.astype(f32).T.astype(bf16)


def attention_forward(qkv_ref, probs_ref, joined_ref, width, heads, keep):
    head_dim = width // heads
    factor = f32(head_dim ** (-0.5) * math.log2(math.e))
    per_group = LANES // head_dim

    def one_group(group):
        queries = qkv_ref[:, lane_block(group)]
        keys = qkv_ref[:, lane_block(group, width)]
        values_t = flip(qkv_ref[:, lane_block(group, 2 * width)])
        subs = range(per_group)
        scores = [dot_nt(keys, queries * head_mask(sub, head_dim)) for sub in subs]
        scores = [keep(s) for s in scores]
        expo = [jnp.exp2((s - jnp.max(s, axis=0, keepdims=True)) * factor) for s in scores]
        probs = [e * (1.0 / col_sum(e)) for e in expo]
        for sub in subs:
            probs_ref[group * per_group + sub] = probs[sub]
        outs = [
            dot(values_t[sub * head_dim : (sub + 1) * head_dim], probs[sub].astype(bf16)) for sub in subs
        ]
        joined_ref[lane_block(group), :] = jnp.concatenate(outs, axis=0)

    for group in range(width // LANES):
        one_group(group)


def attention_backward(qkv_ref, probs_ref, grad_ref, low_ref, width, heads):
    head_dim = width // heads
    scale = f32(head_dim ** (-0.5))
    per_group = LANES // head_dim
    for each in (qkv_ref, probs_ref):
        if isinstance(each, Late):
            each.arrive()

    def one_group(group):
        queries = qkv_ref[:, lane_block(group)]
        keys = qkv_ref[:, lane_block(group, width)]
        values = qkv_ref[:, lane_block(group, 2 * width)]
        grads = grad_ref[:, lane_block(group)]
        keys_t = flip(keys)
        subs = range(per_group)
        masks = [head_mask(sub, head_dim) for sub in subs]
        own = [grads * m for m in masks]
        grad_probs = [dot_nt(values, o) for o in own]
        probs = [probs_ref[group * per_group + sub] for sub in subs]
        grad_values = sum(dot(p.astype(bf16), o) for p, o in zip(probs, own))
        low = [
            (p * (g - col_sum(p * g))).astype(bf16) for p, g in zip(probs, grad_probs)
        ]
        grad_keys = sum(dot(l, queries * m) for l, m in zip(low, masks))
        grad_queries = [
            dot(keys_t[sub * head_dim : (sub + 1) * head_dim], low[sub]) for sub in subs
        ]
        low_ref[:, lane_block(group)] = (jnp.concatenate(grad_queries, axis=0).T * scale).astype(bf16)
        low_ref[:, lane_block(group, width)] = (grad_keys * scale).astype(bf16)
        low_ref[:, lane_block(group, 2 * width)] = grad_values.astype(bf16)

    for group in range(width // LANES):
        one_group(group)


class Late:
    def __init__(self, source, target, sem):
        self.copy, self.target, self.shape = pltpu.make_async_copy(source, target, sem), target, target.shape
        self.here = False
        self.copy.start()

    def arrive(self):
        if not self.here:
            self.copy.wait()
            self.here = True

    def __getitem__(self, index):
        self.arrive()
        return self.target[index]


def late_call(kernel, early, late, outs, scratch, **options):
    count, many = len(early), len(late)

    def body(*refs):
        sources, results = refs[count : count + many], refs[count + many : count + many + len(outs)]
        rest = refs[count + many + len(outs) :]
        held, sems = rest[:many], rest[many]
        lates = [Late(sources[k], held[k], sems.at[k]) for k in range(many)]
        kernel(*refs[:count], *lates, *results, *rest[many + 1 :])
        for each in lates:
            each.arrive()

    return pl.pallas_call(
        body,
        in_specs=[pl.BlockSpec(memory_space=m) for _, m in early] + [pl.BlockSpec(memory_space=pl.ANY)] * many,
        out_specs=[pl.BlockSpec(memory_space=m) for _, m in outs],
        out_shape=[o for o, _ in outs],
        scratch_shapes=[pltpu.VMEM(a.shape, a.dtype) for a in late]
        + [pltpu.SemaphoreType.DMA((many,))]
        + list(scratch),
        compiler_params=params_of(),
        **options,
    )(*[a for a, _ in early], *late)


def encode_kernel(plan, counts, place_ref, *refs):
    sources, refs = refs[: len(counts)], refs[len(counts) :]
    x_ref, seg_row_ref, seg_col_ref = refs[:3]
    weight_outs, vec = refs[3:7], refs[7]
    normed1_ref, qkv_ref, probs_ref, attended_ref, middle_ref, normed2_ref = refs[8:14]
    held, wide, spare, sems, out_sems, joined_ref = refs[14:20]
    weights = refs[20:24]
    qkv_w, proj_w = weights[:2]
    copies = [pltpu.make_async_copy(w, o, out_sems.at[k]) for k, (w, o) in enumerate(zip(weights, weight_outs))]
    unpack_weights(
        plan, ENC_LAYOUT, plan.half, plan.piece, plan.ng, plan.room, place_ref, sources, counts,
        weights, vec, held, wide, spare, sems, copies,
    )
    width, hidden = WIDTH, HIDDEN_SIZE
    inputs = x_ref[...].astype(f32)
    hat, _ = normalised(inputs)
    normed1 = (hat * vec[0:1, :width] + vec[1:2, :width]).astype(bf16)
    normed1_ref[...] = normed1
    qkv_ref[...] = (dot(normed1, qkv_w[...]) + vec[2:3, : 3 * width]).astype(bf16)
    allowed = seg_col_ref[...] == seg_row_ref[...]
    attention_forward(
        qkv_ref, probs_ref, joined_ref, width, HEADS,
        lambda scores: jnp.where(allowed, scores, f32(masked_score * (width // HEADS) ** 0.5)),
    )
    attended = joined_ref[...].T.astype(bf16)
    attended_ref[...] = attended
    middle = inputs + (dot(attended, proj_w[...]) + vec[3:4, :width])
    middle_ref[...] = middle
    hat, _ = normalised(middle)
    normed2_ref[...] = (hat * vec[4:5, :width] + vec[5:6, :width]).astype(bf16)
    for copy in copies:
        copy.wait()


def encode_mlp_kernel(normed2_ref, up_w, vec, down_w, middle_ref, sent_ref, active_ref, slope_ref):
    width, hidden = WIDTH, HIDDEN_SIZE
    total = jnp.zeros((ROW, width), f32)
    part = 1536
    for start in range(0, hidden, part):
        cols = slice(start, start + part)
        upward = dot(normed2_ref[...], up_w[:, cols]) + vec[6:7, cols]
        active, slope = gelu_parts(upward)
        active_ref[:, cols] = active.astype(bf16)
        slope_ref[:, cols] = slope.astype(slope_ref.dtype)
        total += dot(active_ref[:, cols], down_w[cols, :])
    sent_ref[...] = (middle_ref[...] + (total + vec[7:8, :width])).astype(bf16)


def mlp_back_kernel(
    grad_ref, down_w, slope_ref, up_w, middle_ref, vec,
    up_low_ref, proj_low_ref, grad_middle_ref, vec_grad,
):
    width, hidden = WIDTH, HIDDEN_SIZE
    grad_out = grad_ref[...]
    vec_grad[...] = jnp.zeros_like(vec_grad)
    vec_grad[7:8, :width] = col_sum(grad_out.astype(f32))
    grad_normed2 = jnp.zeros((grad_out.shape[0], width), f32)
    part = 3072
    for start in range(0, hidden, part):
        cols = slice(start, start + part)
        low = (dot_nt(grad_out, down_w[cols, :]) * slope_ref[:, cols]).astype(bf16)
        up_low_ref[:, cols] = low
        vec_grad[6:7, cols] = col_sum(low.astype(f32))
        grad_normed2 += dot_nt(low, up_w[:, cols])
    hat, inverse = normalised(middle_ref[...])
    vec_grad[4:5, :width] = col_sum(grad_normed2 * hat)
    vec_grad[5:6, :width] = col_sum(grad_normed2)
    grad_middle = grad_out.astype(f32) + norm_back(grad_normed2, hat, inverse, vec[4:5, :width])
    grad_middle_ref[...] = grad_middle
    proj_low = grad_middle.astype(bf16)
    proj_low_ref[...] = proj_low
    vec_grad[3:4, :width] = col_sum(proj_low.astype(f32))


def attention_back_kernel(
    proj_low_ref, proj_w, qkv_ref, probs_ref, qkv_w, x_ref, vec_in, vec, grad_middle_ref,
    in_grad_ref, qkv_low_ref, vec_grad, grad_att_ref,
):
    width = WIDTH
    grad_att_ref[...] = dot_nt(proj_low_ref[...], proj_w[...]).astype(bf16)
    attention_backward(qkv_ref, probs_ref, grad_att_ref, qkv_low_ref, width, HEADS)
    qkv_low = qkv_low_ref[...]
    vec_grad[...] = vec_in[...]
    vec_grad[2:3, : 3 * width] = col_sum(qkv_low.astype(f32))
    grad_normed1 = dot_nt(qkv_low, qkv_w[...])
    hat, inverse = normalised(x_ref[...].astype(f32))
    vec_grad[0:1, :width] = col_sum(grad_normed1 * hat)
    vec_grad[1:2, :width] = col_sum(grad_normed1)
    in_grad_ref[...] = grad_middle_ref[...] + norm_back(grad_normed1, hat, inverse, vec[0:1, :width])


def decode_kernel(plan, counts, place_ref, *refs):
    sources, refs = refs[: len(counts)], refs[len(counts) :]
    sent_ref, seg_row, slot_row, seg_col, slot_col, cot_ref = refs[:6]
    (
        out_ref, normed1_ref, qkv_low_ref, attended_ref, proj_low_ref, normed2_ref, up_low_ref,
        active_ref, embed_low_ref, grad_sent_ref, vec_grad, pos_grad,
    ) = refs[6:18]
    embedded_ref, embed_sum, qkv_ref, probs_ref, joined_ref, grad_att_ref = refs[18:24]
    held, wide, spare, sems, vec = refs[24:29]
    weights = refs[29:]
    embed_w, pos_ref, qkv_w, proj_w, up_w, down_w = weights
    width, hidden = DEC_WIDTH, DEC_HIDDEN
    image = pl.program_id(0)
    length = SLOT_PAD

    @pl.when(image == 0)
    def _():
        unpack_weights(
            plan, DEC_LAYOUT, plan.unit // 2, plan.unit, plan.full, plan.dec_room, place_ref, sources, counts,
            weights, vec, held, wide, spare, sems,
        )
        embedded_ref[...] = (dot(sent_ref[...], embed_w[...]) + vec[8:9, :width]).astype(bf16)
        vec_grad[...] = jnp.zeros_like(vec_grad)
        pos_grad[...] = jnp.zeros_like(pos_grad)
        embed_sum[...] = jnp.zeros_like(embed_sum)

    def add_vec(row, values):
        vec_grad[row : row + 1, : values.shape[1]] += values

    place = lax.broadcasted_iota(jnp.int32, (length, ROW), 0)
    match = (seg_row[...] == image) & (slot_row[...] == place)
    onehot = jnp.where(match, 1.0, 0.0)
    free = 1.0 - jnp.sum(onehot, axis=1, keepdims=True)
    x = dot(onehot.astype(bf16), embedded_ref[...]) + free * vec[9:10, :width] + pos_ref[...].astype(f32)
    hat1, inverse1 = normalised(x)
    normed1 = (hat1 * vec[0:1, :width] + vec[1:2, :width]).astype(bf16)
    normed1_ref[...] = normed1
    qkv_ref[...] = (dot(normed1, qkv_w[...]) + vec[2:3, : 3 * width]).astype(bf16)
    whole = SLOTS // 16 * 16
    tail_place = lax.broadcasted_iota(jnp.int32, (length - whole, length), 0)

    def without_padding(scores):
        tail = jnp.where(tail_place < SLOTS - whole, scores[whole:], f32(-1e30))
        return jnp.concatenate([scores[:whole], tail], axis=0)

    attention_forward(qkv_ref, probs_ref, joined_ref, width, DEC_HEADS, without_padding)
    attended = joined_ref[...].T.astype(bf16)
    attended_ref[...] = attended
    middle = x + (dot(attended, proj_w[...]) + vec[3:4, :width])
    hat2, inverse2 = normalised(middle)
    normed2 = (hat2 * vec[4:5, :width] + vec[5:6, :width]).astype(bf16)
    normed2_ref[...] = normed2
    cot = cot_ref[...]
    add_vec(7, col_sum(cot.astype(f32)))
    total = jnp.zeros((length, width), f32)
    grad_normed2 = jnp.zeros((length, width), f32)
    part = 1024
    for start in range(0, hidden, part):
        cols = slice(start, start + part)
        upward = dot(normed2_ref[...], up_w[:, cols]) + vec[6:7, cols]
        active, slope = gelu_parts(upward)
        active = active.astype(bf16)
        active_ref[:, cols] = active
        total += dot(active, down_w[cols, :])
        low = (dot_nt(cot_ref[...], down_w[cols, :]) * slope).astype(bf16)
        up_low_ref[:, cols] = low
        vec_grad[6:7, cols] += col_sum(low.astype(f32))
        grad_normed2 += dot_nt(low, up_w[:, cols])
    out_ref[...] = (middle + (total + vec[7:8, :width])).astype(bf16)

    add_vec(4, col_sum(grad_normed2 * hat2))
    add_vec(5, col_sum(grad_normed2))
    grad_middle = cot.astype(f32) + norm_back(grad_normed2, hat2, inverse2, vec[4:5, :width])
    proj_low = grad_middle.astype(bf16)
    proj_low_ref[...] = proj_low
    add_vec(3, col_sum(proj_low.astype(f32)))
    grad_att_ref[...] = dot_nt(proj_low, proj_w[...]).astype(bf16)
    attention_backward(qkv_ref, probs_ref, grad_att_ref, qkv_low_ref, width, DEC_HEADS)
    qkv_low = qkv_low_ref[...]
    add_vec(2, col_sum(qkv_low.astype(f32)))
    grad_normed1 = dot_nt(qkv_low, qkv_w[...])
    add_vec(0, col_sum(grad_normed1 * hat1))
    add_vec(1, col_sum(grad_normed1))
    grad_in = grad_middle + norm_back(grad_normed1, hat1, inverse1, vec[0:1, :width])
    low_in = grad_in.astype(bf16)
    wide = low_in.astype(f32)
    add_vec(9, col_sum(free * wide))
    pos_grad[...] += wide
    place_t = lax.broadcasted_iota(jnp.int32, (ROW, length), 1)
    match_t = (seg_col[...] == image) & (slot_col[...] == place_t)
    embed_sum[...] += dot(jnp.where(match_t, 1.0, 0.0).astype(bf16), low_in)

    @pl.when(image == IMAGES_ROW - 1)
    def _():
        embed_low = embed_sum[...].astype(bf16)
        embed_low_ref[...] = embed_low
        add_vec(8, col_sum(embed_low.astype(f32)))
        grad_sent_ref[...] = dot_nt(embed_low, embed_w[...]).astype(bf16)


def cost(microseconds):
    return pl.CostEstimate(flops=int(microseconds * 1e11), bytes_accessed=int(microseconds * 3e8), transcendentals=0)


def params_of(**extra):
    return pltpu.CompilerParams(vmem_limit_bytes=VMEM_BYTES, **extra)


def shape(dims, kind):
    return jax.ShapeDtypeStruct(dims, kind)


def unpack_scratch(chunks, room):
    return [
        pltpu.VMEM((chunks * room, LANES), bf16),
        pltpu.VMEM((3200, LANES), f32),
        pltpu.VMEM((3200, LANES), f32),
        pltpu.SemaphoreType.DMA((chunks,)),
    ]


def encode(plan, place, sources, x, seg, seg_column):
    width, hidden, length = WIDTH, HIDDEN_SIZE, ROW
    weights = [shape(e, bf16) for _, e in ENC_LAYOUT if len(e) == 2]
    kept = [
        shape((VEC_ROWS, hidden), f32),
        shape((length, width), bf16),
        shape((length, 3 * width), bf16),
        shape((HEADS, length, length), f32),
        shape((length, width), bf16),
        shape((length, width), f32),
        shape((length, width), bf16),
    ]
    result = pl.pallas_call(
        partial(encode_kernel, plan, [s.shape[0] // plan.half for s in sources]),
        in_specs=[pl.BlockSpec(memory_space=pltpu.SMEM)]
        + [pl.BlockSpec(memory_space=pl.ANY)] * len(sources)
        + [pl.BlockSpec(memory_space=pltpu.VMEM)] * 3,
        out_specs=[pl.BlockSpec(memory_space=pl.ANY)] * 4 + [pl.BlockSpec(memory_space=pltpu.VMEM)] * len(kept),
        out_shape=weights + kept,
        scratch_shapes=unpack_scratch(plan.ng, plan.room)
        + [pltpu.SemaphoreType.DMA((4,)), pltpu.VMEM((width, length), f32)]
        + [pltpu.VMEM(w.shape, bf16) for w in weights],
        compiler_params=params_of(),
        cost_estimate=cost(24),
        name="encode",
    )(place, *sources, x, seg.reshape(1, length), seg_column)
    weights = dict(zip([QKV_W, PROJ_W, UP_W, DOWN_W, VECS], result))
    return weights, dict(zip([H1, QKV, PROBS, ATT, MID, H2], result[5:]))


def encode_mlp(saved, weights):
    width, hidden, length = WIDTH, HIDDEN_SIZE, ROW
    result = late_call(
        encode_mlp_kernel,
        [],
        [saved[H2], weights[UP_W], weights[VECS], weights[DOWN_W], saved[MID]],
        [
            (shape((length, width), bf16), pltpu.VMEM),
            (shape((length, hidden), bf16), pltpu.VMEM),
            (shape((length, hidden), bf16), pltpu.VMEM),
        ],
        [],
        cost_estimate=cost(8),
        name="encode_mlp",
    )
    return dict(zip([SENT, ACT, SLOPE], result))


def mlp_back(grad, saved, weights):
    width, hidden, length = WIDTH, HIDDEN_SIZE, ROW
    return late_call(
        mlp_back_kernel,
        [],
        [grad, weights[DOWN_W], saved[SLOPE], weights[UP_W], saved[MID], weights[VECS]],
        [
            (shape((length, hidden), bf16), pltpu.VMEM),
            (shape((length, width), bf16), pltpu.VMEM),
            (shape((length, width), f32), pltpu.VMEM),
            (shape((VEC_ROWS, hidden), f32), pltpu.VMEM),
        ],
        [],
        cost_estimate=cost(9),
        name="mlp_back",
    )


def attention_back(grad_middle, proj_low, x, saved, weights, vec_grad):
    width, hidden, length = WIDTH, HIDDEN_SIZE, ROW
    return late_call(
        attention_back_kernel,
        [],
        [
            proj_low, weights[PROJ_W], saved[QKV], saved[PROBS], weights[QKV_W], x, vec_grad, weights[VECS],
            grad_middle,
        ],
        [
            (shape((length, width), f32), pltpu.VMEM),
            (shape((length, 3 * width), bf16), pltpu.VMEM),
            (shape((VEC_ROWS, hidden), f32), pltpu.VMEM),
        ],
        [pltpu.VMEM((length, width), bf16)],
        cost_estimate=cost(10),
        name="attention_back",
    )


def decode(plan, place, sources, sent, seg, slot, columns, cot):
    width, hidden, length = DEC_WIDTH, DEC_HIDDEN, SLOT_PAD
    held = [sent, seg.reshape(1, ROW), slot.reshape(1, ROW), *columns]

    def whole(array):
        return pl.BlockSpec(array.shape, lambda i: (0,) * array.ndim, pipeline_mode=pl.Buffered(1))

    def image(cols):
        return pl.BlockSpec((length, cols), lambda i: (i, 0))

    rows = IMAGES_ROW * length
    per_image = [width, width, 3 * width, width, width, width, hidden, hidden]
    kept = [
        shape((ROW, width), bf16),
        shape((ROW, WIDTH), bf16),
        shape((VEC_ROWS, hidden), f32),
        shape((length, width), f32),
    ]
    return pl.pallas_call(
        partial(decode_kernel, plan, [s.shape[0] // (plan.unit // 2) for s in sources]),
        grid=(IMAGES_ROW,),
        in_specs=[pl.BlockSpec(memory_space=pltpu.SMEM)]
        + [pl.BlockSpec(memory_space=pl.ANY)] * len(sources)
        + [whole(a) for a in held]
        + [image(width)],
        out_specs=[image(c) for c in per_image]
        + [pl.BlockSpec(s.shape, lambda i: (0, 0)) for s in kept],
        out_shape=[shape((rows, c), bf16) for c in per_image] + kept,
        scratch_shapes=[
            pltpu.VMEM((ROW, width), bf16),
            pltpu.VMEM((ROW, width), f32),
            pltpu.VMEM((length, 3 * width), bf16),
            pltpu.VMEM((DEC_HEADS, length, length), f32),
            pltpu.VMEM((width, length), f32),
            pltpu.VMEM((length, width), bf16),
        ]
        + unpack_scratch(plan.full, plan.dec_room)
        + [pltpu.VMEM((VEC_ROWS, hidden), f32)]
        + [
            pltpu.VMEM((SLOT_PAD if n == POS else e[0], e[1]), bf16) for n, e in DEC_LAYOUT if len(e) == 2
        ],
        compiler_params=params_of(dimension_semantics=("arbitrary",)),
        cost_estimate=cost(85),
        name="decode",
    )(place, *sources, *held, cot)


def rows_of(extent):
    return math.prod(extent) // LANES


def up_to(value, step):
    return -(-value // step) * step


def flat_starts(layout):
    starts, here = {}, 0
    for name, extent in layout:
        starts[name] = here
        here += rows_of(extent)
    return starts, here


def kept_starts(layout):
    starts, here = {}, 0
    for name, extent in layout:
        starts[name] = here
        here += up_to(rows_of(extent), 16)
    return starts, here


class Plan:
    def __init__(self, mesh_shape):
        self.ns, self.ng, self.nd = (mesh_shape[a] for a in (SEC, GRP, DP))
        self.ny = self.nd // 2
        self.chunk = PARAMS // LANES // self.ng
        self.pieces = self.ns * self.nd
        self.piece = up_to(-(-self.chunk // self.pieces), 64)
        self.half = self.piece // 2
        self.room = self.piece * self.pieces
        self.tables = 4 if self.ny == 2 else 2
        self.units = 2 * self.pieces
        self.full = self.ng // 2
        self.rest = flat_starts(DEC_LAYOUT)[1] - self.full * self.chunk
        assert 0 < self.rest <= self.chunk
        self.unit = up_to(-(-self.chunk // (self.units - 1)), 64)
        self.dec_room = self.unit * self.units
        whole = self.chunk // self.unit * self.unit
        self.part_in = self.unit if whole < self.dec_room - self.unit else 0
        self.parts_in = -(-self.rest // self.part_in)
        assert self.parts_in <= self.full
        self.enc_starts = [self.kept_row(ENC_LAYOUT, z * self.chunk) // 16 * 16 for z in range(self.ng)]
        self.enc_ends = [
            up_to(self.kept_row(ENC_LAYOUT, min((z + 1) * self.chunk, flat_starts(ENC_LAYOUT)[1]) - 1) + 1, 16)
            for z in range(self.ng)
        ]
        self.dec_starts = [self.kept_row(DEC_LAYOUT, z * self.chunk) // 16 * 16 for z in range(self.full)]
        self.dec_ends = [
            up_to(self.kept_row(DEC_LAYOUT, (z + 1) * self.chunk - 1) + 1, 16) for z in range(self.full)
        ]
        assert all(e - s <= self.room for s, e in zip(self.enc_starts, self.enc_ends))
        self.rest_start = self.kept_row(DEC_LAYOUT, self.full * self.chunk) // 16 * 16
        self.rest_end = kept_starts(DEC_LAYOUT)[1]
        self.part_out = [self.room - (self.dec_ends[k] - self.dec_starts[k]) for k in range(2)]
        assert max(self.part_out) <= self.room // 2
        assert self.part_out[0] < self.rest_end - self.rest_start <= sum(self.part_out)

    def kept_row(self, layout, flat_row):
        flat, _ = flat_starts(layout)
        kept, _ = kept_starts(layout)
        for name, extent in layout:
            if flat_row < flat[name] + rows_of(extent):
                return kept[name] + flat_row - flat[name]
        return kept[name] + rows_of(extent)

    def ranges(self, first, count, cut, chunks, chunk_room):
        found = []
        whole = self.chunk // cut * cut
        while count:
            z, row = divmod(first, self.chunk)
            if z >= chunks:
                k, row = divmod(row, self.part_in)
                here, room = (k + 1) * chunk_room - cut + row, self.part_in - row
            elif row < whole:
                here, room = z * chunk_room + row, whole - row
            else:
                here, room = z * chunk_room + row + cut - (self.chunk - whole), self.chunk - row
            take = min(count, room)
            found.append((here, take))
            first, count = first + take, count - take
        return found

    def packed_row(self, size, groups, index, row, away_x, away_y):
        owner, turned = away_x * self.ny + away_y, away_y * 2 + away_x
        if self.ny != 2:
            return (owner * groups + index) * size + row, size - row
        part = size // 2
        late, row = divmod(row, part)
        if not late:
            second, index = divmod(index, groups // 2)
            block = groups // 2 * part
            return second * (4 * block) + (turned if second else owner) * block + index * part + row, part - row
        fine = part // 2
        second, row = divmod(row, fine)
        start = groups * 4 * part + index * (4 * part) + second * (4 * fine)
        return start + (turned if second else owner) * fine + row, fine - row

    def enc_regions(self, groups):
        return [(self.enc_starts[z], self.enc_ends[z], k, 0) for k, z in enumerate(groups)]

    def dec_regions(self):
        length = self.room // 2
        found = []
        for z in range(self.full):
            low, high = self.dec_starts[z], self.dec_ends[z]
            found += [(low, low + length, 2 * z, 0), (low + length, high, 2 * z + 1, 0)]
        middle = self.rest_start + self.part_out[0]
        found.append((self.rest_start, middle, 1, length - self.part_out[0]))
        found.append((middle, self.rest_end, 3, length - self.part_out[1]))
        return found

    def segments(self):
        length = self.room // 2
        self.block = up_to(-(-self.chunk // 4), 8)
        rows = {}
        for s, layout in enumerate((ENC_LAYOUT, DEC_LAYOUT)):
            flat, used = flat_starts(layout)
            for z in range(self.ng):
                low, high = z * self.chunk, (z + 1) * self.chunk
                found = [[] for _ in range(4)]

                def put(source, first, stop):
                    while first < stop:
                        block = first // self.block
                        end = min(stop, (block + 1) * self.block)
                        found[block].append((source, first, -(-(end - first) // 8)))
                        source, first = source + end - first, end

                for name, extent in layout:
                    first, last = max(flat[name], low), min(flat[name] + rows_of(extent), high)
                    while first < last:
                        row, stop = self.kept_row(layout, first), last
                        if s == 0:
                            source = row - self.enc_starts[z]
                        elif z < self.full:
                            source = row - self.dec_starts[z]
                        else:
                            row -= self.rest_start
                            k = int(row >= self.part_out[0])
                            row -= k * self.part_out[0]
                            source = (k + 1) * length - self.part_out[k] + row
                            stop = min(last, first + self.part_out[k] - row)
                        put(source, first - low, stop - low)
                        first = stop
                free = max(used, low) - low
                if free < self.chunk:
                    put(self.room, free, min(free + 8, self.chunk))
                rows[s, z] = found, int(free + 8 < self.chunk)
        count = max(len(block) for found, _ in rows.values() for block in found)
        table = np.zeros((self.ns, self.ng, 12 * count + 1), np.int32)
        for (s, z), (found, left) in rows.items():
            for k, block in enumerate(found):
                for j, entry in enumerate(block):
                    table[s, z, 3 * (k * count + j) : 3 * (k * count + j) + 3] = entry
            table[s, z, -1] = left
        return table


def widen_block(held, wide, spare, ranges, rows):
    def load(start, count, further=0):
        first = start // 16 * 16
        size = up_to(start + count - first, 16)
        if isinstance(further, int):
            return held[first : first + size, :].astype(f32), size, start - first
        return held[pl.ds(pl.multiple_of(first + further, 16), size), :].astype(f32), size, start - first

    if isinstance(ranges, tuple):
        block, size, skip = load(ranges[0], rows, ranges[1])
        wide[0:size, :] = block
        return skip
    if len(ranges) == 1:
        block, size, skip = load(*ranges[0])
        wide[0:size, :] = block
        return skip
    here = 0
    for start, count in ranges:
        block, size, skip = load(start, count)
        spare[0:size, :] = block
        wide[here : here + count, :] = spare[skip : skip + count, :]
        here += count
    return 0


def unpack_weights(
    plan, layout, unit, cut, chunks, room, place_ref, sources, counts, outs, vec, held, wide, spare, sems, copies=(),
):
    matrices = [n for n, e in layout if len(e) == 2]
    per_chunk = room // unit
    number = 0
    for source, count in zip(sources, counts):
        for k in range(count):
            slot = place_ref[number]
            number += 1
            target = held.at[pl.ds(pl.multiple_of(slot * unit, 16), unit), :]
            pltpu.make_async_copy(source.at[pl.ds(k * unit, unit), :], target, sems.at[slot // per_chunk]).start()
    arrived = set()

    def arrive(ranges):
        for start, count in ranges:
            z = start // room
            if z not in arrived:
                arrived.add(z)
                part = held.at[pl.ds(z * room, room), :]
                pltpu.make_async_copy(part, part, sems.at[z]).wait()

    vec[...] = jnp.zeros_like(vec)
    flat, _ = flat_starts(layout)
    by_name = dict(zip(matrices, outs))
    order = dict(zip(matrices, copies))
    for name, extent in layout:
        if len(extent) == 2:
            depth, lanes = extent[0], extent[1] // LANES
            step = depth if name == POS else max(128, 2048 // lanes // 128 * 128)
            out = by_name[name]
            if name == POS:
                out[...] = jnp.zeros_like(out)
            found = [
                plan.ranges(flat[name] + first * lanes, min(step, depth - first) * lanes, cut, chunks, room)
                for first in range(0, depth, step)
            ]
            for ranges in found:
                arrive(ranges)

            def move(number, start, size, lanes=lanes, step=step, out=out):
                skip = widen_block(held, wide, spare, start, size * lanes)
                rows = pl.ds(number * step if isinstance(number, int) else pl.multiple_of(number * step, step), size)
                for j in range(lanes):
                    out[rows, j * LANES : (j + 1) * LANES] = wide[pl.ds(skip + j, size, stride=lanes), :].astype(bf16)

            k = 0
            while k < len(found):
                size = min(step, depth - k * step)
                run = 1
                if len(found[k]) == 1 and size == step and step * lanes % 16 == 0:
                    begin = found[k][0][0]
                    while k + run < len(found) and found[k + run] == [(begin + run * step * lanes, step * lanes)]:
                        run += 1
                if run > 1:

                    def turn(i, carry, k=k, begin=begin, lanes=lanes, step=step, move=move):
                        move(k + i, (begin, i * step * lanes), step)
                        return carry

                    lax.fori_loop(0, run, turn, 0)
                else:
                    move(k, found[k], size)
                k += run
            if name in order:
                order[name].start()
        else:
            lanes = extent[0] // LANES
            ranges = plan.ranges(flat[name], lanes, cut, chunks, room)
            arrive(ranges)
            skip = widen_block(held, wide, spare, ranges, lanes)
            row, shift = {QB: (2, 0), VB: (2, 2 * extent[0])}.get(name, (VEC.get(name), 0))
            for j in range(lanes):
                vec[row : row + 1, shift + j * LANES : shift + (j + 1) * LANES] = wide[skip + j : skip + j + 1, :]
    for z in range(chunks):
        arrive([(z * room, 1)])


def pack_kernel(plan, layout, names, regions, size, groups, place_ref, *refs):
    pairs = {}
    for name in names:
        pairs[name], refs = refs[:2], refs[2:]
    vec, refs = refs[0], refs[1:]
    pos = None
    if POS in names:
        pos, refs = pairs[POS][0], refs
    mine, theirs, wide, stage, small, sems = refs
    kept, _ = kept_starts(layout)
    extents = dict(layout)
    ny = plan.ny

    def send(source, first, rows, sem):
        moved = 0
        for low, high, index, base in regions:
            start, stop = max(first, low), min(first + rows, high)
            while start < stop:
                number, row = divmod(base + start - low, size)
                c, s, y = number // (2 * ny), number // ny % 2, number % ny
                away_x, away_y = lax.rem(s - place_ref[0] + 2, 2), lax.rem(y - place_ref[1] + ny, ny)
                where, room = plan.packed_row(size, groups, index, row, away_x, away_y)
                count = min(stop - start, room)
                target = pl.ds(pl.multiple_of(where, 16), count)
                block = source.at[pl.ds(start - first, count), :]
                for same, table in ((True, mine), (False, theirs)):

                    @pl.when((place_ref[2] == c) == same)
                    def _():
                        pltpu.make_async_copy(block, table.at[target, :], sem).start()

                moved += count
                start += count
        return moved

    def wait(rows, slot):
        if rows:
            block = stage.at[slot, pl.ds(0, rows), :]
            pltpu.make_async_copy(block, block, sems.at[slot]).wait()

    turn = 0
    pending = [0, 0]
    for name in names:
        if name == POS:
            continue
        left, right = pairs[name]
        depth, width = extents[name]
        lanes = width // LANES
        step = max(k for k in (128, 256, 384, 512) if depth % k == 0 and k * lanes <= 3072)
        rows = step * lanes
        for first in range(0, depth, step):
            start = kept[name] + first * lanes
            if all(start >= high or start + rows <= low for low, high, _, _ in regions):
                continue
            slot = turn % 2
            turn += 1
            columns = flip(left[:, first : first + step])
            part = 256
            for start in range(0, width, part):
                block = dot(columns, right[:, start : start + part])
                for j in range(part // LANES):
                    wide[pl.ds(start // LANES + j, step, stride=lanes), :] = block[:, j * LANES : (j + 1) * LANES]
            wait(pending[slot], slot)
            stage[slot, 0:rows, :] = wide[0:rows, :].astype(bf16)
            pending[slot] = send(stage.at[slot], kept[name] + first * lanes, rows, sems.at[slot])
    here = 0
    total = 0
    for name, extent in layout:
        if name not in names and len(extent) == 2 or name not in kept_names(names):
            continue
        if len(extent) == 2 and name != POS:
            continue
        rows = rows_of(extent)
        room = up_to(rows, 16)
        wide[0:room, :] = jnp.zeros((room, LANES), f32)
        if name == POS:
            lanes = extent[1] // LANES
            for j in range(lanes):
                wide[pl.ds(j, extent[0], stride=lanes), :] = pos[0 : extent[0], j * LANES : (j + 1) * LANES]
        else:
            row, shift = {QB: (2, 0), VB: (2, 2 * extent[0])}.get(name, (VEC.get(name), 0))
            for j in range(rows):
                wide[j : j + 1, :] = vec[row : row + 1, shift + j * LANES : shift + (j + 1) * LANES]
        small[here : here + room, :] = wide[0:room, :].astype(bf16)
        total += send(small.at[pl.ds(here, room), :], kept[name], room, sems.at[2])
        here += room
    wait(pending[0], 0)
    wait(pending[1], 1)
    block = small.at[pl.ds(0, total), :]
    pltpu.make_async_copy(block, block, sems.at[2]).wait()


def pack_enc_kernel(plan, names, regions, size, groups, place_ref, *refs):
    pairs = {}
    for name in names:
        pairs[name], refs = refs[:4], refs[4:]
    vec, vec_other, *tables = refs[: 2 + plan.tables]
    wide, stage, small, sems = refs[2 + plan.tables :]
    lates = [a for four in pairs.values() for a in four] + [vec, vec_other]
    kept, _ = kept_starts(ENC_LAYOUT)
    extents = dict(ENC_LAYOUT)
    ny = plan.ny

    def pieces(first, rows, core):
        for low, high, index, base in regions:
            start, stop = max(first, low), min(first + rows, high)
            while start < stop:
                number, row = divmod(base + start - low, size)
                count = min(stop - start, size - row)
                if number // (2 * ny) == core:
                    yield start - first, count, index, row, number // ny % 2, number % ny
                start += count

    def send(source, first, rows, sem, core):
        moved = 0
        for skip, count, index, row, s, y in pieces(first, rows, core):
            away_x, away_y = lax.rem(s - place_ref[0] + 2, 2), lax.rem(y - place_ref[1] + ny, ny)
            if ny == 2 and index >= groups // 2:
                keep, away, other, index = tables[2:], away_y, away_x, index - groups // 2
            else:
                keep, away, other = tables[:2], away_x, away_y
            length = (groups // 2 if ny == 2 else groups) * size
            target = pl.ds(pl.multiple_of(other * length, 16) + index * size + row, count)
            block = source.at[pl.ds(skip, count), :]
            for k in range(2):

                @pl.when(away == k)
                def _():
                    pltpu.make_async_copy(block, keep[k].at[target, :], sem).start()

            moved += count
        return moved

    def wait(rows, slot):
        if rows:
            block = stage.at[slot, pl.ds(0, rows), :]
            pltpu.make_async_copy(block, block, sems.at[slot]).wait()

    def run(core):
        turn = 0
        pending = [0, 0]
        for name in names:
            left, left_other, right, right_other = pairs[name]
            depth, width = extents[name]
            lanes = width // LANES
            step = max(k for k in (128, 256, 384, 512) if depth % k == 0 and k * lanes <= 3072)
            rows = step * lanes
            for first in range(0, depth, step):
                begin = kept[name] + first * lanes
                if not list(pieces(begin, rows, core)):
                    continue
                slot = turn % 2
                turn += 1
                columns = flip(left[:, first : first + step])
                others = flip(left_other[:, first : first + step])
                part = 256
                for start in range(0, width, part):
                    cols = slice(start, start + part)
                    block = dot(columns, right[:, cols]) + dot(others, right_other[:, cols])
                    for j in range(part // LANES):
                        wide[pl.ds(start // LANES + j, step, stride=lanes), :] = block[:, j * LANES : (j + 1) * LANES]
                wait(pending[slot], slot)
                stage[slot, 0:rows, :] = wide[0:rows, :].astype(bf16)
                pending[slot] = send(stage.at[slot], begin, rows, sems.at[slot], core)
        here = 0
        total = 0
        for name, extent in ENC_LAYOUT:
            if name not in kept_names(names):
                continue
            rows = rows_of(extent)
            room = up_to(rows, 16)
            if list(pieces(kept[name], room, core)):
                wide[0:room, :] = jnp.zeros((room, LANES), f32)
                row, shift = {QB: (2, 0), VB: (2, 2 * extent[0])}.get(name, (VEC.get(name), 0))
                for j in range(rows):
                    cols = slice(shift + j * LANES, shift + (j + 1) * LANES)
                    wide[j : j + 1, :] = vec[row : row + 1, cols] + vec_other[row : row + 1, cols]
                small[here : here + room, :] = wide[0:room, :].astype(bf16)
                total += send(small.at[pl.ds(here, room), :], kept[name], room, sems.at[2], core)
            here += room
        wait(pending[0], 0)
        wait(pending[1], 1)
        if total:
            block = small.at[pl.ds(0, total), :]
            pltpu.make_async_copy(block, block, sems.at[2]).wait()

    for core in range(2):

        @pl.when(place_ref[2] == core)
        def _():
            for each in lates:
                each.here = False
            run(core)
            for each in lates:
                each.arrive()


def pack_enc(plan, regions, size, groups, place, pairs, vec, vec_other):
    names = list(pairs)
    operands = [a for name in names for a in pairs[name]] + [vec, vec_other]
    extents = dict(ENC_LAYOUT)
    small = sum(up_to(rows_of(extents[n]), 16) for n in kept_names(names))
    rows = 2 * plan.ny * groups * size // plan.tables
    return late_call(
        partial(pack_enc_kernel, plan, names, regions, size, groups),
        [(place, pltpu.SMEM)],
        operands,
        [(shape((rows, LANES), bf16), pl.ANY)] * plan.tables,
        [
            pltpu.VMEM((3072, LANES), f32),
            pltpu.VMEM((2, 3072 + 64, LANES), bf16),
            pltpu.VMEM((small + 64, LANES), bf16),
            pltpu.SemaphoreType.DMA((3,)),
        ],
        cost_estimate=cost(8),
        name="pack_enc",
    )


def kept_names(names):
    with_matrix = {
        QKV_W: [N1G, N1B, QB, VB],
        PROJ_W: [PB, N2G, N2B],
        UP_W: [UB],
        DOWN_W: [DB],
        EMBED_W: [EB, MT],
        POS: [POS],
    }
    return [v for n in names for v in with_matrix[n]]


def pack(plan, layout, regions, size, groups, place, pairs, vec):
    names = list(pairs)
    operands = [a for name in names for a in pairs[name]] + [vec]
    extents = dict(layout)
    small = sum(up_to(rows_of(extents[n]), 16) for n in kept_names(names))
    rows = 2 * plan.ny * groups * size
    return late_call(
        partial(pack_kernel, plan, layout, names, regions, size, groups),
        [(place, pltpu.SMEM)],
        operands,
        [(shape((rows, LANES), bf16), pl.ANY)] * 2,
        [
            pltpu.VMEM((3072, LANES), f32),
            pltpu.VMEM((2, 3072 + 64, LANES), bf16),
            pltpu.VMEM((small + 64, LANES), bf16),
            pltpu.SemaphoreType.DMA((3,)),
        ],
        cost_estimate=cost(19),
        name="pack",
    )


def finish_kernel(plan, counts, place_ref, seg_ref, *refs):
    sources, result, held, wide, out, sem, out_sems = refs[: len(counts)], *refs[len(counts) :]
    unit = plan.half
    number = 0
    for source, count in zip(sources, counts):
        for k in range(count):
            target = held.at[pl.ds(pl.multiple_of(place_ref[number] * unit, 16), unit), :]
            number += 1
            pltpu.make_async_copy(source.at[pl.ds(k * unit, unit), :], target, sem.at[0]).start()
    count = seg_ref.shape[0] // 12

    @pl.when(seg_ref[12 * count] != 0)
    def _():
        out[...] = jnp.zeros_like(out)

    pltpu.make_async_copy(held, held, sem.at[0]).wait()
    total = plan.room
    wide[total : total + 16, :] = jnp.zeros((16, LANES), f32)
    wide[0:total, :] = held[...].astype(f32)

    def one(k, carry):
        source, first, steps = seg_ref[3 * k], seg_ref[3 * k + 1], seg_ref[3 * k + 2]

        def step(i, carry):
            out[pl.ds(first + 8 * i, 8), :] = wide[pl.ds(source + 8 * i, 8), :]
            return carry

        def steps16(i, carry):
            out[pl.ds(first + 128 * i, 128), :] = wide[pl.ds(source + 128 * i, 128), :]
            return carry

        many = steps // 16
        lax.fori_loop(0, many, steps16, 0)
        return lax.fori_loop(many * 16, steps, step, carry)

    rows = up_to(plan.chunk, 8)
    lines = out.at[pl.ds(0, rows), :].reshape(rows, 1, LANES)
    copies = []
    for block in range(4):
        lax.fori_loop(block * count, (block + 1) * count, one, 0)
        first = block * plan.block
        part = pl.ds(first, min(plan.block, plan.chunk - first))
        copies.append(pltpu.make_async_copy(lines.at[part], result.at[part], out_sems.at[block]))
        copies[-1].start()
    for copy in copies:
        copy.wait()


def finish(plan, place, segments, sources):
    total = plan.room
    return pl.pallas_call(
        partial(finish_kernel, plan, [s.shape[0] // plan.half for s in sources]),
        in_specs=[pl.BlockSpec(memory_space=pltpu.SMEM)] * 2
        + [pl.BlockSpec(memory_space=pl.ANY)] * len(sources),
        out_specs=pl.BlockSpec(memory_space=pl.ANY),
        out_shape=shape((plan.chunk, 1, LANES), f32),
        scratch_shapes=[
            pltpu.VMEM((total, LANES), bf16),
            pltpu.VMEM((total + 16, LANES), f32),
            pltpu.VMEM((up_to(plan.chunk, 8) + 8, LANES), f32),
            pltpu.SemaphoreType.DMA((1,)),
            pltpu.SemaphoreType.DMA((4,)),
        ],
        compiler_params=params_of(),
        cost_estimate=cost(8),
        name="finish",
    )(place, segments, *sources)


def completed(pairs, count):
    senders = [k for k in range(count) if k not in [a for a, _ in pairs]]
    receivers = [k for k in range(count) if k not in [b for _, b in pairs]]
    return list(pairs) + list(zip(senders, receivers))


def after(values, *before):
    return lax.optimization_barrier((values, before))[0]


def per_device(plan, enc_input, segments, slots, params, cot):
    ns, ng, nd, ny = plan.ns, plan.ng, plan.nd, plan.ny
    piece, half, room, chunk = plan.piece, plan.half, plan.room, plan.chunk
    sec = lax.axis_index(SEC)
    grp = lax.axis_index(GRP)
    dp = lax.axis_index(DP)
    yy, core = dp // 2, dp % 2
    first_section = sec == 0

    def over_x(block):
        return lax.ppermute(block, SEC, [(0, 1), (1, 0)])

    def over_core(block):
        return lax.ppermute(block, DP, [(d, d ^ 1) for d in range(nd)])

    def over_y(block):
        return lax.ppermute(block, DP, [(d, (d + 2) % nd) for d in range(nd)])

    def over_z(block, senders=None):
        senders = range(ng) if senders is None else senders
        return lax.ppermute(block, GRP, [(g, (g + 1) % ng) for g in senders])

    def final_places():
        if ny == 2:
            owners = [(sec, yy), (1 - sec, yy), (sec, 1 - yy), (1 - sec, 1 - yy)]
        else:
            owners = [(s, (yy - k) % ny) for k in range(ny) for s in (sec, 1 - sec)]
        found = []
        for c in (core, 1 - core):
            for s, y in owners:
                number = (c * 2 + s) * ny + y
                found += [
                    jnp.where(first_section, 2 * number, number),
                    jnp.where(first_section, 2 * number + 1, plan.pieces + number),
                ]
        return found

    unit = plan.unit

    def share(start, params):
        cut = lax.dynamic_slice(params, (0, start * LANES), (1, unit * LANES))
        return cut.astype(f32).reshape(unit, LANES).astype(bf16)

    def shares(section, params):
        number = section * nd + dp
        enc_first = jnp.minimum(number * piece, chunk - piece)
        dec_first = [jnp.minimum((h * plan.pieces + number) * unit, chunk - unit) for h in range(2)]
        if plan.parts_in == 1:
            dec_first[0] = jnp.where(grp == plan.full, 0, dec_first[0])
        return (
            share(jnp.where(first_section, enc_first, dec_first[0]), params),
            share(jnp.where(first_section, enc_first + piece - unit, dec_first[1]), params),
        )

    send = shares(1 - sec, params)
    keep = shares(sec, after(params, *send))

    def whole_piece(parts):
        return jnp.concatenate([parts[0][:half], parts[1][unit - half :]])

    routes = [[(z, 2 * z + h) for z in range(plan.full)] for h in range(2)]
    if plan.parts_in == 1:
        routes[0].append((plan.full, 1))
    routes = [completed(route, ng) for route in routes]
    crossed = []
    for h in range(2):
        pairs = [(z, ng + z) for z in range(ng)] + [(ng + a, b) for a, b in routes[h]]
        crossed.append(lax.ppermute(send[h], (SEC, GRP), pairs))
    spread = [lax.ppermute(keep[h], GRP, routes[h]) for h in range(2)]
    enc_piece = jnp.where(first_section, whole_piece(keep), whole_piece(crossed))
    even, odd = (jnp.where(first_section, crossed[h], spread[h]) for h in range(2))
    dec_piece = jnp.where(grp % 2 == 0, even, odd)
    class Gather:
        def __init__(self, here):
            self.here = here
            if ny == 2:
                self.arrays = [here, over_x(here), over_y(here)]
                self.owners = [(sec, yy), (1 - sec, yy), (sec, 1 - yy), (1 - sec, 1 - yy)]
            else:
                column = [here]
                for _ in range(ny - 1):
                    column.append(over_y(column[-1]))
                self.arrays = column
                self.owners = [(s, (yy - k) % ny) for s in (sec, 1 - sec) for k in range(ny)]

        def second(self):
            if ny == 2:
                middle = self.here.shape[0] // 2
                self.corners = [self.arrays[1][:middle], self.arrays[2][middle:]]
            else:
                self.corners = self.arrays
            return tuple(self.corners)

        def third(self):
            if ny == 2:
                self.arrays += [over_y(self.corners[0]), over_x(self.corners[1])]
            else:
                self.arrays = self.arrays + [over_x(block) for block in self.corners]
            return tuple(self.arrays[-2:])

        def fourth(self, joined=True):
            arrays = [jnp.concatenate(self.arrays)] if joined else self.arrays
            return arrays + [over_core(block) for block in arrays]

        def places(self, parts):
            found = []
            for c in (core, 1 - core):
                for s, y in self.owners:
                    for k in parts:
                        number = (grp - k) % ng * plan.pieces + s * nd + y * 2 + c
                        found += [2 * number, 2 * number + 1]
            return found

    last = jnp.logical_and(sec == ns - 1, dp == nd - 1)
    if plan.parts_in == 1:
        dec_piece = jnp.where(jnp.logical_and(last, grp == 1), even, dec_piece)
    else:
        for k in range(plan.parts_in):
            part = share(jnp.minimum(k * unit, chunk - unit), params)
            part = lax.ppermute(part, GRP, [(plan.full, 2 * k + 1)])
            dec_piece = jnp.where(jnp.logical_and(last, grp == 2 * k + 1), part, dec_piece)
    here = enc_piece
    gathers = [Gather(here)]
    micro_rows = enc_input.reshape(ROW, WIDTH)
    seg = lax.dynamic_index_in_dim(segments, sec, 0, keepdims=False).reshape(ROW)
    slot = lax.dynamic_index_in_dim(slots, sec, 0, keepdims=False).reshape(ROW)
    cot_rows = jnp.pad(
        cot.reshape(IMAGES_ROW, SLOTS, DEC_WIDTH), ((0, 0), (0, SLOT_PAD - SLOTS), (0, 0))
    ).reshape(IMAGES_ROW * SLOT_PAD, DEC_WIDTH)

    columns = (seg.reshape(ROW, 1), slot.reshape(ROW, 1))
    table = jnp.asarray(plan.segments())[sec, grp].reshape(-1)
    place = jnp.stack([sec, yy, core]).astype(jnp.int32)
    finish_places = jnp.stack(final_places()).astype(jnp.int32)
    enc_places = jnp.stack([p for k in range(ng) for p in gathers[0].places([k])]).astype(jnp.int32)
    dec_places = jnp.stack(gathers[0].places(range(ng))).astype(jnp.int32)
    small = (columns, table, place, finish_places, enc_places, dec_places, cot_rows)
    for k in range(1, ng):
        here = over_z(here)
        if k == 1:
            here, small = after((here, small), enc_piece)
            here = after(here, *small)
        if k >= 2:
            here = after(here, *gathers[k - 2].second())
        if k >= 3:
            here = after(here, *gathers[k - 3].third())
        gathers.append(Gather(here))
    gathers[-2].second()
    dec_parts = [after(dec_piece, here)]
    for _ in range(ng - 1):
        dec_parts.append(over_z(dec_parts[-1]))
    gathers[-1].arrays[1:] = after(gathers[-1].arrays[1:], *dec_parts[1:-1])
    gathers[-1].second()
    columns, table, place, finish_places, enc_places, dec_places, cot_rows = small
    enc_sources = []
    for k, g in enumerate(gathers):
        if k >= ng - 3:
            g.third()
        if k == ng - 1:
            g.arrays = after(g.arrays, dec_parts[-1])
        enc_sources += g.fourth()
    dec_gather = Gather(after(jnp.concatenate(dec_parts), *gathers[-1].corners))

    enc_weights, saved = encode(plan, enc_places, enc_sources, micro_rows, seg, columns[0])
    dec_gather.arrays[1:] = after(dec_gather.arrays[1:], saved[H2])
    saved[H2] = after(saved[H2], *dec_gather.second())
    saved.update(encode_mlp(saved, enc_weights))
    others = {k: over_core(saved[k]) for k in (H1, ATT, H2, ACT)}
    dec_gather.third()
    dec_gather.arrays[-2:] = after(dec_gather.arrays[-2:], saved[SENT])
    dec_sources = dec_gather.fourth(False)
    dec = dict(
        zip(
            [OUT, H1, QKV_L, ATT, PROJ_L, H2, UP_L, ACT, EMBED_L, GSENT, VECS, GPOS],
            decode(plan, dec_places, dec_sources, saved[SENT], seg, slot, columns, cot_rows),
        )
    )

    def add(first, *others):
        total = first.astype(f32)
        for other in others:
            total = total + other.astype(f32)
        return total.astype(bf16)

    class Square:
        def __init__(self, keeps, sends):
            self.keeps, self.sends = keeps, [add(*parts) if len(parts) > 1 else parts[0] for parts in sends]
            self.m = keeps[0][0].shape[0] // ny

        def kept(self, half, low, high, *others):
            return add(*[part[low:high] for part in self.keeps[half]], *others)

        def first(self):
            return (over_x(self.sends[0]), over_y(self.sends[1])) if ny == 2 else (over_x(self.sends[0]),)

        def second(self, *got):
            m = self.m
            self.got = got
            if ny == 2:
                self.sends = tuple(self.kept(k, m, 2 * m, got[k][m:]) for k in range(2))
            else:
                column = self.kept(0, 0, ny * m, got[0])
                total = column[(ny - 1) * m :]
                for k in range(ny - 2, -1, -1):
                    total = add(column[k * m : (k + 1) * m], over_y(total))
                self.sends = (total,)
            return self.sends

        def third(self, *before):
            m = self.m
            if ny == 2:
                late = after((over_y(self.sends[0]), over_x(self.sends[1])), *before)
                self.own = tuple(self.kept(k, 0, m, self.got[k][:m], late[k]) for k in range(2))
            else:
                self.own = (self.sends[0][: m // 2], self.sends[0][m // 2 :])
            return self.own

    class Ring:
        def __init__(self, one):
            self.one, self.step = one, 0
            self.total = add(*one((grp - 1) % ng))

        def next(self, *before):
            got = after(over_z(self.total), *before)
            self.step += 1
            self.total = add(*self.one((grp - 1 - self.step) % ng), got)
            return self.total

    def pick(blocks, g):
        if len(blocks) == 4 == ng:
            return jnp.where(g < 2, jnp.where(g == 0, *blocks[:2]), jnp.where(g == 2, *blocks[2:]))
        rows = jnp.concatenate(blocks)
        size = rows.shape[0] // ng
        return lax.dynamic_slice(rows, (g * size, 0), (size, LANES))

    def halves(block):
        return [block[: block.shape[0] // 2], block[block.shape[0] // 2 :]]

    every = list(range(ng))
    near = ng // 2
    upper, lower = every[near:], every[:near]
    grad_sent, others = after((dec[GSENT], others), dec[VECS])
    grad_sent = after(grad_sent, *others.values())
    grad_other = over_core(grad_sent)
    up_low, proj_low, grad_middle, mlp_vec = mlp_back(grad_sent, saved, enc_weights)
    grad_other = after(grad_other, up_low)
    up_other, proj_other, mlp_vec_other = over_core(up_low), over_core(proj_low), over_core(mlp_vec)
    in_grad, qkv_low, enc_vec = attention_back(grad_middle, proj_low, micro_rows, saved, enc_weights, mlp_vec)
    up_other, proj_other, mlp_vec_other = after((up_other, proj_other, mlp_vec_other), qkv_low)
    up_tables = pack_enc(
        plan, plan.enc_regions(upper), piece, len(upper), place,
        {
            DOWN_W: (saved[ACT], others[ACT], grad_sent, grad_other),
            UP_W: (saved[H2], others[H2], after(up_low, qkv_low), up_other),
        },
        mlp_vec, mlp_vec_other,
    )
    qkv_other, vec_other = after((over_core(qkv_low), over_core(enc_vec)), up_tables[0])
    dec_mine, dec_theirs = pack(
        plan, DEC_LAYOUT, plan.dec_regions(), half, ng, place,
        {
            EMBED_W: (saved[SENT], dec[EMBED_L]),
            QKV_W: (dec[H1], dec[QKV_L]),
            PROJ_W: (dec[ATT], dec[PROJ_L]),
            UP_W: (dec[H2], dec[UP_L]),
            DOWN_W: (dec[ACT], cot_rows),
            POS: (dec[GPOS], dec[GPOS]),
        },
        after(dec[VECS], up_tables[0]),
    )
    qkv_other, vec_other = after((qkv_other, vec_other), dec_mine)

    def table_square(tables):
        return Square([[t] for t in tables[0::2]], [[t] for t in tables[1::2]])

    upper_sum = table_square(up_tables)
    upper_sum.second(*after(upper_sum.first(), dec_mine))
    low_tables = pack_enc(
        plan, plan.enc_regions(lower), piece, len(lower), place,
        {
            PROJ_W: (saved[ATT], others[ATT], proj_low, proj_other),
            QKV_W: (saved[H1], others[H1], qkv_low, qkv_other),
            UP_W: (saved[H2], others[H2], after(up_low, *upper_sum.sends), up_other),
        },
        enc_vec, vec_other,
    )
    lower_sum = table_square(low_tables)
    lower_first = lower_sum.first()
    dec_parts = (dec_mine, after(over_core(dec_theirs), low_tables[0]))

    def dec_rows(low, high):
        return [part[low:high] for part in dec_parts]

    if ny == 2:
        rows = dec_mine.shape[0] // 2
        size = rows // ng

        def dec_late(g):
            return [lax.dynamic_slice(part, (rows + g * size, 0), (size, LANES)) for part in dec_parts]

        late_ring = Ring(dec_late)
        quarter = rows // 4
        cuts = [dec_rows(k * quarter, (k + 1) * quarter) for k in range(4)]
        upper_sum.third(late_ring.total)
        lower_sum.second(*after(lower_first, *upper_sum.own))
        early = Square(cuts[0::2], cuts[1::2])
        early.sends = after(early.sends, *lower_sum.sends)
        early_first = early.first()
        late_ring.next(*early.sends)
        lower_sum.third(late_ring.total)
        enc_ring = Ring(lambda g: [pick(list(lower_sum.own) + list(upper_sum.own), g)])
        early.second(*after(early_first, enc_ring.total))
        for _ in range(ng - 3):
            late_ring.next(*early.sends)
        early_own = [b for o in early.third(late_ring.total) for b in halves(o)]
        early_ring = Ring(lambda g: [pick(early_own, g)])
        enc_ring.next(early_ring.total)
        late_ring.next(enc_ring.total)
        quarter = size // 4
        cuts = [[late_ring.total[k * quarter : (k + 1) * quarter]] for k in range(4)]
        late = Square(cuts[0::2], cuts[1::2])
        late_first = late.first()
        early_ring.next(*late.sends)
        late.second(*after(late_first, early_ring.total))
        early_ring.next(*late.sends)
        late_own = late.third(early_ring.total)
        for _ in range(ng - 3):
            early_ring.next(*late_own)
        dec_own = jnp.concatenate([early_ring.total, *late_own])
    else:
        lower_sum.second(*lower_first)
        rows = dec_mine.shape[0] // 2
        whole = Square([dec_rows(0, rows)], [dec_rows(rows, 2 * rows)])
        whole.second(*whole.first())
        dec_ring = Ring(lambda g: [pick(list(whole.third()), g)])
        for _ in range(ng - 1):
            dec_ring.next()
        dec_own = dec_ring.total
        upper_sum.third()
        lower_sum.third()
        enc_ring = Ring(lambda g: [pick(list(lower_sum.own) + list(upper_sum.own), g)])
        enc_ring.next()
    back = [[(2 * z + h, z) for z in range(plan.full)] for h in range(2)]
    back[0].append((1, plan.full))
    back.append([(3, plan.full)])
    dec_back = [lax.ppermute(dec_own, GRP, completed(pairs, ng)) for pairs in back]
    enc_ring.next(dec_own)
    dec_low, dec_high, dec_rest = after(dec_back, enc_ring.total)
    dec_own = jnp.concatenate([dec_low, jnp.where(grp == plan.full, dec_rest, dec_high)])
    for _ in range(ng - 3):
        enc_ring.next(dec_own)
    enc_own = enc_ring.total

    own = jnp.where(first_section, enc_own, dec_own)
    other = jnp.where(first_section, dec_own, enc_own)
    if ny == 2:
        from_x, from_y = over_x(other), over_y(own)
        sources = [own, from_x, from_y, over_y(from_x)]
    else:
        column = [jnp.concatenate([own, over_x(other)])]
        for _ in range(ny - 1):
            column.append(over_y(column[-1]))
        sources = column
    sources = sources + [over_core(block) for block in sources]
    flat = finish(plan, finish_places, table, sources)
    param_grad = flat.reshape(1, chunk * LANES)
    dec_out = dec[OUT].reshape(IMAGES_ROW, SLOT_PAD, DEC_WIDTH)[:, :SLOTS]
    return (
        dec_out.reshape(1, 1, IMAGES_ROW * SLOTS, DEC_WIDTH),
        in_grad.reshape(1, 1, ROW, WIDTH),
        param_grad,
    )


def solution(mesh):
    placed = (
        P(SEC, (GRP, DP), None, None),
        P(None, (GRP, DP), None),
        P(None, (GRP, DP), None),
        P(SEC, GRP),
        P(SEC, (GRP, DP), None, None),
    )
    return jax.shard_map(
        partial(per_device, Plan(dict(mesh.shape))),
        mesh=mesh,
        in_specs=placed,
        out_specs=(
            P(SEC, (GRP, DP), None, None),
            P(SEC, (GRP, DP), None, None),
            P(SEC, GRP),
        ),
        check_vma=False,
    )
```

```python
from functools import partial
import math

import jax
import jax.numpy as jnp
import numpy as np
from jax import lax
from jax.experimental import pallas as pl
from jax.experimental.pallas import tpu as pltpu
from jax.sharding import PartitionSpec as P

WIDTH = 768
HEADS = 12
HIDDEN_SIZE = 3072
DEC_WIDTH = 512
DEC_HEADS = 16
DEC_HIDDEN = 2048
SLOTS = 196
IMAGES_ROW = 5
ROW = 256
PARAMS = 7088128
LANES = 128
SEC, GRP, DP = "section", "group", "dp"
(
    N1G, N1B, QKV_W, QB, VB, PROJ_W, PB, N2G,
) = range(0, 8)
(
    N2B, UP_W, UB, DOWN_W, DB, EMBED_W, EB, MT,
) = range(8, 16)
(
    POS, QKV_B, VECS, SENT, H1, QKV, PROBS, ATT,
) = range(16, 24)
(
    MID, H2, ACT, SLOPE, OUT, QKV_L, PROJ_L, UP_L,
) = range(24, 32)
(
    EMBED_L, GSENT, GPOS,
) = range(32, 35)
SLOT_PAD = 208
VMEM_BYTES = 60 * 1024 * 1024

norm_eps = 1e-06
masked_score = -1000000000.0
f32 = jnp.float32
bf16 = jnp.bfloat16


def block_layout(width, hidden):
    return [
        (N1G, (width,)),
        (N1B, (width,)),
        (QKV_W, (width, 3 * width)),
        (QB, (width,)),
        (VB, (width,)),
        (PROJ_W, (width, width)),
        (PB, (width,)),
        (N2G, (width,)),
        (N2B, (width,)),
        (UP_W, (width, hidden)),
        (UB, (hidden,)),
        (DOWN_W, (hidden, width)),
        (DB, (width,)),
    ]


def decoder_layout(enc_width, width, hidden, slot_count):
    return [
        (EMBED_W, (enc_width, width)),
        (EB, (width,)),
        (MT, (width,)),
        (POS, (slot_count, width)),
    ] + block_layout(width, hidden)


ENC_LAYOUT = block_layout(WIDTH, HIDDEN_SIZE)
DEC_LAYOUT = decoder_layout(WIDTH, DEC_WIDTH, DEC_HIDDEN, SLOTS)
VEC = {
    N1G: 0,
    N1B: 1,
    QKV_B: 2,
    PB: 3,
    N2G: 4,
    N2B: 5,
    UB: 6,
    DB: 7,
    EB: 8,
    MT: 9,
}
VEC_ROWS = 16


def dot(a, b):
    return lax.dot_general(a, b, (((1,), (0,)), ((), ())), preferred_element_type=f32)


def dot_nt(a, b):
    return lax.dot_general(a, b, (((1,), (1,)), ((), ())), preferred_element_type=f32)


def dot_tn(a, b):
    return lax.dot_general(a, b, (((0,), (0,)), ((), ())), preferred_element_type=f32)


def normalised(values):
    centered = values - jnp.mean(values, axis=-1, keepdims=True)
    inverse = lax.rsqrt(jnp.mean(centered * centered, axis=-1, keepdims=True) + norm_eps)
    return centered * inverse, inverse


def norm_back(grad, hat, inverse, gain):
    scaled = grad * gain
    first = jnp.mean(scaled, axis=-1, keepdims=True)
    second = jnp.mean(scaled * hat, axis=-1, keepdims=True)
    return inverse * (scaled - first - hat * second)


def col_sum(values):
    return jnp.sum(values, axis=0, keepdims=True)


def gelu_parts(upward):
    half = 0.5 + 0.5 * lax.erf(upward * f32(math.sqrt(0.5)))
    slope = half + upward * (jnp.exp(upward * upward * f32(-0.5)) * f32(1.0 / math.sqrt(2.0 * math.pi)))
    return upward * half, slope


def head_mask(head, head_dim):
    lane = lax.broadcasted_iota(jnp.int32, (1, LANES), 1)
    return jnp.where(lane // head_dim == head, 1.0, 0.0).astype(bf16)


def lane_block(group, start=0):
    if isinstance(group, int):
        return slice(start + group * LANES, start + (group + 1) * LANES)
    return pl.ds(pl.multiple_of(start + group * LANES, LANES), LANES)


def flip(values):
    return values.astype(f32).T.astype(bf16)


def attention_forward(qkv_ref, probs_ref, joined_ref, width, heads, keep):
    head_dim = width // heads
    factor = f32(head_dim ** (-0.5) * math.log2(math.e))
    per_group = LANES // head_dim

    def some_groups(groups):
        heads_here = [(group, sub) for group in groups for sub in range(per_group)]
        queries = {g: qkv_ref[:, lane_block(g)] for g in groups}
        keys = {g: qkv_ref[:, lane_block(g, width)] for g in groups}
        values_t = {g: flip(qkv_ref[:, lane_block(g, 2 * width)]) for g in groups}
        scores = [dot_nt(keys[g], queries[g] * head_mask(sub, head_dim)) for g, sub in heads_here]
        scores = [keep(s) for s in scores]
        expo = [jnp.exp2((s - jnp.max(s, axis=0, keepdims=True)) * factor) for s in scores]
        probs = [e * (1.0 / col_sum(e)) for e in expo]
        for (g, sub), p in zip(heads_here, probs):
            probs_ref[g * per_group + sub] = p
        outs = [
            dot(values_t[g][sub * head_dim : (sub + 1) * head_dim], p.astype(bf16))
            for (g, sub), p in zip(heads_here, probs)
        ]
        joined_ref[groups[0] * LANES : (groups[-1] + 1) * LANES, :] = jnp.concatenate(outs, axis=0)

    some_groups(range(width // LANES))


def attention_backward(qkv_ref, probs_ref, grad_ref, low_ref, width, heads):
    head_dim = width // heads
    scale = f32(head_dim ** (-0.5))
    per_group = LANES // head_dim
    for each in (qkv_ref, probs_ref):
        if isinstance(each, Late):
            each.arrive()

    def some_groups(groups):
        heads_here = [(group, sub) for group in groups for sub in range(per_group)]
        masks = [head_mask(sub, head_dim) for sub in range(per_group)]
        queries = {g: qkv_ref[:, lane_block(g)] for g in groups}
        keys = {g: qkv_ref[:, lane_block(g, width)] for g in groups}
        values = {g: qkv_ref[:, lane_block(g, 2 * width)] for g in groups}
        grads = {g: grad_ref[:, lane_block(g)] for g in groups}
        keys_t = {g: flip(keys[g]) for g in groups}
        own = [grads[g] * masks[sub] for g, sub in heads_here]
        grad_probs = [dot_nt(values[g], o) for (g, sub), o in zip(heads_here, own)]
        probs = [probs_ref[g * per_group + sub] for g, sub in heads_here]
        grad_values = [dot(p.astype(bf16), o) for p, o in zip(probs, own)]
        low = [(p * (g - col_sum(p * g))).astype(bf16) for p, g in zip(probs, grad_probs)]
        grad_keys = [dot(l, queries[g] * masks[sub]) for (g, sub), l in zip(heads_here, low)]
        grad_queries = [
            dot(keys_t[g][sub * head_dim : (sub + 1) * head_dim], l) for (g, sub), l in zip(heads_here, low)
        ]
        for k, g in enumerate(groups):
            mine = slice(k * per_group, (k + 1) * per_group)
            low_ref[:, lane_block(g)] = (jnp.concatenate(grad_queries[mine], axis=0).T * scale).astype(bf16)
            low_ref[:, lane_block(g, width)] = (sum(grad_keys[mine]) * scale).astype(bf16)
            low_ref[:, lane_block(g, 2 * width)] = sum(grad_values[mine]).astype(bf16)

    some_groups(range(width // LANES))


class Late:
    def __init__(self, source, target, sem):
        self.copy, self.target, self.shape = pltpu.make_async_copy(source, target, sem), target, target.shape
        self.here = False
        self.copy.start()

    def arrive(self):
        if not self.here:
            self.copy.wait()
            self.here = True

    def __getitem__(self, index):
        self.arrive()
        return self.target[index]


def late_call(kernel, early, late, outs, scratch, **options):
    count, many = len(early), len(late)

    def body(*refs):
        sources, results = refs[count : count + many], refs[count + many : count + many + len(outs)]
        rest = refs[count + many + len(outs) :]
        held, sems = rest[:many], rest[many]
        lates = [Late(sources[k], held[k], sems.at[k]) for k in range(many)]
        kernel(*refs[:count], *lates, *results, *rest[many + 1 :])
        for each in lates:
            each.arrive()

    return pl.pallas_call(
        body,
        in_specs=[pl.BlockSpec(memory_space=m) for _, m in early] + [pl.BlockSpec(memory_space=pl.ANY)] * many,
        out_specs=[pl.BlockSpec(memory_space=m) for _, m in outs],
        out_shape=[o for o, _ in outs],
        scratch_shapes=[pltpu.VMEM(a.shape, a.dtype) for a in late]
        + [pltpu.SemaphoreType.DMA((many,))]
        + list(scratch),
        compiler_params=params_of(),
        **options,
    )(*[a for a, _ in early], *late)


def encode_kernel(plan, counts, place_ref, *refs):
    sources, refs = refs[: len(counts)], refs[len(counts) :]
    x_ref, seg_row_ref, seg_col_ref = refs[:3]
    weight_outs, vec = refs[3:7], refs[7]
    normed1_ref, qkv_ref, probs_ref, attended_ref, middle_ref, normed2_ref = refs[8:14]
    held, wide, spare, sems, out_sems, joined_ref = refs[14:20]
    weights = refs[20:24]
    qkv_w, proj_w = weights[:2]
    copies = [pltpu.make_async_copy(w, o, out_sems.at[k]) for k, (w, o) in enumerate(zip(weights, weight_outs))]
    unpack_weights(
        plan, ENC_LAYOUT, plan.half, plan.piece, plan.ng, plan.room, place_ref, sources, counts,
        weights, vec, held, wide, spare, sems, copies,
    )
    width, hidden = WIDTH, HIDDEN_SIZE
    inputs = x_ref[...].astype(f32)
    hat, _ = normalised(inputs)
    normed1 = (hat * vec[0:1, :width] + vec[1:2, :width]).astype(bf16)
    normed1_ref[...] = normed1
    qkv_ref[...] = (dot(normed1, qkv_w[...]) + vec[2:3, : 3 * width]).astype(bf16)
    allowed = seg_col_ref[...] == seg_row_ref[...]
    attention_forward(
        qkv_ref, probs_ref, joined_ref, width, HEADS,
        lambda scores: jnp.where(allowed, scores, f32(masked_score * (width // HEADS) ** 0.5)),
    )
    attended = joined_ref[...].T.astype(bf16)
    attended_ref[...] = attended
    middle = inputs + (dot(attended, proj_w[...]) + vec[3:4, :width])
    middle_ref[...] = middle
    hat, _ = normalised(middle)
    normed2_ref[...] = (hat * vec[4:5, :width] + vec[5:6, :width]).astype(bf16)
    for copy in copies:
        copy.wait()


def encode_mlp_kernel(normed2_ref, up_w, vec, down_w, middle_ref, sent_ref, active_ref, slope_ref):
    width, hidden = WIDTH, HIDDEN_SIZE
    total = jnp.zeros((ROW, width), f32)
    part = 1536
    for start in range(0, hidden, part):
        cols = slice(start, start + part)
        upward = dot(normed2_ref[...], up_w[:, cols]) + vec[6:7, cols]
        active, slope = gelu_parts(upward)
        active_ref[:, cols] = active.astype(bf16)
        slope_ref[:, cols] = slope.astype(slope_ref.dtype)
        total += dot(active_ref[:, cols], down_w[cols, :])
    sent_ref[...] = (middle_ref[...] + (total + vec[7:8, :width])).astype(bf16)


def mlp_back_kernel(
    grad_ref, down_w, slope_ref, up_w, middle_ref, vec,
    up_low_ref, proj_low_ref, grad_middle_ref, vec_grad,
):
    width, hidden = WIDTH, HIDDEN_SIZE
    grad_out = grad_ref[...]
    vec_grad[...] = jnp.zeros_like(vec_grad)
    vec_grad[7:8, :width] = col_sum(grad_out.astype(f32))
    grad_normed2 = jnp.zeros((grad_out.shape[0], width), f32)
    part = 3072
    for start in range(0, hidden, part):
        cols = slice(start, start + part)
        low = (dot_nt(grad_out, down_w[cols, :]) * slope_ref[:, cols]).astype(bf16)
        up_low_ref[:, cols] = low
        vec_grad[6:7, cols] = col_sum(low.astype(f32))
        grad_normed2 += dot_nt(low, up_w[:, cols])
    hat, inverse = normalised(middle_ref[...])
    vec_grad[4:5, :width] = col_sum(grad_normed2 * hat)
    vec_grad[5:6, :width] = col_sum(grad_normed2)
    grad_middle = grad_out.astype(f32) + norm_back(grad_normed2, hat, inverse, vec[4:5, :width])
    grad_middle_ref[...] = grad_middle
    proj_low = grad_middle.astype(bf16)
    proj_low_ref[...] = proj_low
    vec_grad[3:4, :width] = col_sum(proj_low.astype(f32))


def attention_back_kernel(
    proj_low_ref, proj_w, qkv_ref, probs_ref, qkv_w, x_ref, vec_in, vec, grad_middle_ref,
    in_grad_ref, qkv_low_ref, vec_grad, grad_att_ref,
):
    width = WIDTH
    grad_att_ref[...] = dot_nt(proj_low_ref[...], proj_w[...]).astype(bf16)
    attention_backward(qkv_ref, probs_ref, grad_att_ref, qkv_low_ref, width, HEADS)
    qkv_low = qkv_low_ref[...]
    vec_grad[...] = vec_in[...]
    vec_grad[2:3, : 3 * width] = col_sum(qkv_low.astype(f32))
    grad_normed1 = dot_nt(qkv_low, qkv_w[...])
    hat, inverse = normalised(x_ref[...].astype(f32))
    vec_grad[0:1, :width] = col_sum(grad_normed1 * hat)
    vec_grad[1:2, :width] = col_sum(grad_normed1)
    in_grad_ref[...] = grad_middle_ref[...] + norm_back(grad_normed1, hat, inverse, vec[0:1, :width])


def decode_kernel(plan, counts, place_ref, *refs):
    sources, refs = refs[: len(counts)], refs[len(counts) :]
    sent_ref, seg_row, slot_row, seg_col, slot_col, cot_ref = refs[:6]
    (
        out_ref, normed1_ref, qkv_low_ref, attended_ref, proj_low_ref, normed2_ref, up_low_ref,
        active_ref, embed_low_ref, grad_sent_ref, vec_grad, pos_grad,
    ) = refs[6:18]
    embedded_ref, embed_sum, qkv_ref, probs_ref, joined_ref, grad_att_ref = refs[18:24]
    held, wide, spare, sems, vec = refs[24:29]
    weights = refs[29:]
    embed_w, pos_ref, qkv_w, proj_w, up_w, down_w = weights
    width, hidden = DEC_WIDTH, DEC_HIDDEN
    image = pl.program_id(0)
    length = SLOT_PAD

    @pl.when(image == 0)
    def _():
        unpack_weights(
            plan, DEC_LAYOUT, plan.unit // 2, plan.unit, plan.full, plan.dec_room, place_ref, sources, counts,
            weights, vec, held, wide, spare, sems,
        )
        embedded_ref[...] = (dot(sent_ref[...], embed_w[...]) + vec[8:9, :width]).astype(bf16)
        vec_grad[...] = jnp.zeros_like(vec_grad)
        pos_grad[...] = jnp.zeros_like(pos_grad)
        embed_sum[...] = jnp.zeros_like(embed_sum)

    def add_vec(row, values):
        vec_grad[row : row + 1, : values.shape[1]] += values

    place = lax.broadcasted_iota(jnp.int32, (length, ROW), 0)
    match = (seg_row[...] == image) & (slot_row[...] == place)
    onehot = jnp.where(match, 1.0, 0.0)
    free = 1.0 - jnp.sum(onehot, axis=1, keepdims=True)
    x = dot(onehot.astype(bf16), embedded_ref[...]) + free * vec[9:10, :width] + pos_ref[...].astype(f32)
    hat1, inverse1 = normalised(x)
    normed1 = (hat1 * vec[0:1, :width] + vec[1:2, :width]).astype(bf16)
    normed1_ref[...] = normed1
    qkv_ref[...] = (dot(normed1, qkv_w[...]) + vec[2:3, : 3 * width]).astype(bf16)
    whole = SLOTS // 16 * 16
    tail_place = lax.broadcasted_iota(jnp.int32, (length - whole, length), 0)

    def without_padding(scores):
        tail = jnp.where(tail_place < SLOTS - whole, scores[whole:], f32(-1e30))
        return jnp.concatenate([scores[:whole], tail], axis=0)

    attention_forward(qkv_ref, probs_ref, joined_ref, width, DEC_HEADS, without_padding)
    attended = joined_ref[...].T.astype(bf16)
    attended_ref[...] = attended
    middle = x + (dot(attended, proj_w[...]) + vec[3:4, :width])
    hat2, inverse2 = normalised(middle)
    normed2 = (hat2 * vec[4:5, :width] + vec[5:6, :width]).astype(bf16)
    normed2_ref[...] = normed2
    cot = cot_ref[...]
    add_vec(7, col_sum(cot.astype(f32)))
    total = jnp.zeros((length, width), f32)
    grad_normed2 = jnp.zeros((length, width), f32)
    part = 1024
    for start in range(0, hidden, part):
        cols = slice(start, start + part)
        upward = dot(normed2_ref[...], up_w[:, cols]) + vec[6:7, cols]
        active, slope = gelu_parts(upward)
        active = active.astype(bf16)
        active_ref[:, cols] = active
        total += dot(active, down_w[cols, :])
        low = (dot_nt(cot_ref[...], down_w[cols, :]) * slope).astype(bf16)
        up_low_ref[:, cols] = low
        vec_grad[6:7, cols] += col_sum(low.astype(f32))
        grad_normed2 += dot_nt(low, up_w[:, cols])
    out_ref[...] = (middle + (total + vec[7:8, :width])).astype(bf16)

    add_vec(4, col_sum(grad_normed2 * hat2))
    add_vec(5, col_sum(grad_normed2))
    grad_middle = cot.astype(f32) + norm_back(grad_normed2, hat2, inverse2, vec[4:5, :width])
    proj_low = grad_middle.astype(bf16)
    proj_low_ref[...] = proj_low
    add_vec(3, col_sum(proj_low.astype(f32)))
    grad_att_ref[...] = dot_nt(proj_low, proj_w[...]).astype(bf16)
    attention_backward(qkv_ref, probs_ref, grad_att_ref, qkv_low_ref, width, DEC_HEADS)
    qkv_low = qkv_low_ref[...]
    add_vec(2, col_sum(qkv_low.astype(f32)))
    grad_normed1 = dot_nt(qkv_low, qkv_w[...])
    add_vec(0, col_sum(grad_normed1 * hat1))
    add_vec(1, col_sum(grad_normed1))
    grad_in = grad_middle + norm_back(grad_normed1, hat1, inverse1, vec[0:1, :width])
    low_in = grad_in.astype(bf16)
    wide = low_in.astype(f32)
    add_vec(9, col_sum(free * wide))
    pos_grad[...] += wide
    place_t = lax.broadcasted_iota(jnp.int32, (ROW, length), 1)
    match_t = (seg_col[...] == image) & (slot_col[...] == place_t)
    embed_sum[...] += dot(jnp.where(match_t, 1.0, 0.0).astype(bf16), low_in)

    @pl.when(image == IMAGES_ROW - 1)
    def _():
        embed_low = embed_sum[...].astype(bf16)
        embed_low_ref[...] = embed_low
        add_vec(8, col_sum(embed_low.astype(f32)))
        grad_sent_ref[...] = dot_nt(embed_low, embed_w[...]).astype(bf16)


def cost(microseconds):
    return pl.CostEstimate(flops=int(microseconds * 1e11), bytes_accessed=int(microseconds * 3e8), transcendentals=0)


def params_of(**extra):
    return pltpu.CompilerParams(vmem_limit_bytes=VMEM_BYTES, **extra)


def shape(dims, kind):
    return jax.ShapeDtypeStruct(dims, kind)


def unpack_scratch(chunks, room):
    return [
        pltpu.VMEM((chunks * room, LANES), bf16),
        pltpu.VMEM((3200, LANES), f32),
        pltpu.VMEM((3200, LANES), f32),
        pltpu.SemaphoreType.DMA((chunks,)),
    ]


def encode(plan, place, sources, x, seg, seg_column):
    width, hidden, length = WIDTH, HIDDEN_SIZE, ROW
    weights = [shape(e, bf16) for _, e in ENC_LAYOUT if len(e) == 2]
    kept = [
        shape((VEC_ROWS, hidden), f32),
        shape((length, width), bf16),
        shape((length, 3 * width), bf16),
        shape((HEADS, length, length), f32),
        shape((length, width), bf16),
        shape((length, width), f32),
        shape((length, width), bf16),
    ]
    result = pl.pallas_call(
        partial(encode_kernel, plan, [s.shape[0] // plan.half for s in sources]),
        in_specs=[pl.BlockSpec(memory_space=pltpu.SMEM)]
        + [pl.BlockSpec(memory_space=pl.ANY)] * len(sources)
        + [pl.BlockSpec(memory_space=pltpu.VMEM)] * 3,
        out_specs=[pl.BlockSpec(memory_space=pl.ANY)] * 4 + [pl.BlockSpec(memory_space=pltpu.VMEM)] * len(kept),
        out_shape=weights + kept,
        scratch_shapes=unpack_scratch(plan.ng, plan.room)
        + [pltpu.SemaphoreType.DMA((4,)), pltpu.VMEM((width, length), f32)]
        + [pltpu.VMEM(w.shape, bf16) for w in weights],
        compiler_params=params_of(),
        cost_estimate=cost(24),
        name="encode",
    )(place, *sources, x, seg.reshape(1, length), seg_column)
    weights = dict(zip([QKV_W, PROJ_W, UP_W, DOWN_W, VECS], result))
    return weights, dict(zip([H1, QKV, PROBS, ATT, MID, H2], result[5:]))


def encode_mlp(saved, weights):
    width, hidden, length = WIDTH, HIDDEN_SIZE, ROW
    result = late_call(
        encode_mlp_kernel,
        [],
        [saved[H2], weights[UP_W], weights[VECS], weights[DOWN_W], saved[MID]],
        [
            (shape((length, width), bf16), pltpu.VMEM),
            (shape((length, hidden), bf16), pltpu.VMEM),
            (shape((length, hidden), bf16), pltpu.VMEM),
        ],
        [],
        cost_estimate=cost(8),
        name="encode_mlp",
    )
    return dict(zip([SENT, ACT, SLOPE], result))


def mlp_back(grad, saved, weights):
    width, hidden, length = WIDTH, HIDDEN_SIZE, ROW
    return late_call(
        mlp_back_kernel,
        [],
        [grad, weights[DOWN_W], saved[SLOPE], weights[UP_W], saved[MID], weights[VECS]],
        [
            (shape((length, hidden), bf16), pltpu.VMEM),
            (shape((length, width), bf16), pltpu.VMEM),
            (shape((length, width), f32), pltpu.VMEM),
            (shape((VEC_ROWS, hidden), f32), pltpu.VMEM),
        ],
        [],
        cost_estimate=cost(9),
        name="mlp_back",
    )


def attention_back(grad_middle, proj_low, x, saved, weights, vec_grad):
    width, hidden, length = WIDTH, HIDDEN_SIZE, ROW
    return late_call(
        attention_back_kernel,
        [],
        [
            proj_low, weights[PROJ_W], saved[QKV], saved[PROBS], weights[QKV_W], x, vec_grad, weights[VECS],
            grad_middle,
        ],
        [
            (shape((length, width), f32), pltpu.VMEM),
            (shape((length, 3 * width), bf16), pltpu.VMEM),
            (shape((VEC_ROWS, hidden), f32), pltpu.VMEM),
        ],
        [pltpu.VMEM((length, width), bf16)],
        cost_estimate=cost(10),
        name="attention_back",
    )


def decode(plan, place, sources, sent, seg, slot, columns, cot):
    width, hidden, length = DEC_WIDTH, DEC_HIDDEN, SLOT_PAD
    held = [sent, seg.reshape(1, ROW), slot.reshape(1, ROW), *columns]

    def whole(array):
        return pl.BlockSpec(array.shape, lambda i: (0,) * array.ndim, pipeline_mode=pl.Buffered(1))

    def image(cols):
        return pl.BlockSpec((length, cols), lambda i: (i, 0))

    rows = IMAGES_ROW * length
    per_image = [width, width, 3 * width, width, width, width, hidden, hidden]
    kept = [
        shape((ROW, width), bf16),
        shape((ROW, WIDTH), bf16),
        shape((VEC_ROWS, hidden), f32),
        shape((length, width), f32),
    ]
    return pl.pallas_call(
        partial(decode_kernel, plan, [s.shape[0] // (plan.unit // 2) for s in sources]),
        grid=(IMAGES_ROW,),
        in_specs=[pl.BlockSpec(memory_space=pltpu.SMEM)]
        + [pl.BlockSpec(memory_space=pl.ANY)] * len(sources)
        + [whole(a) for a in held]
        + [image(width)],
        out_specs=[image(c) for c in per_image]
        + [pl.BlockSpec(s.shape, lambda i: (0, 0)) for s in kept],
        out_shape=[shape((rows, c), bf16) for c in per_image] + kept,
        scratch_shapes=[
            pltpu.VMEM((ROW, width), bf16),
            pltpu.VMEM((ROW, width), f32),
            pltpu.VMEM((length, 3 * width), bf16),
            pltpu.VMEM((DEC_HEADS, length, length), f32),
            pltpu.VMEM((width, length), f32),
            pltpu.VMEM((length, width), bf16),
        ]
        + unpack_scratch(plan.full, plan.dec_room)
        + [pltpu.VMEM((VEC_ROWS, hidden), f32)]
        + [
            pltpu.VMEM((SLOT_PAD if n == POS else e[0], e[1]), bf16) for n, e in DEC_LAYOUT if len(e) == 2
        ],
        compiler_params=params_of(dimension_semantics=("arbitrary",)),
        cost_estimate=cost(85),
        name="decode",
    )(place, *sources, *held, cot)


def rows_of(extent):
    return math.prod(extent) // LANES


def up_to(value, step):
    return -(-value // step) * step


def flat_starts(layout):
    starts, here = {}, 0
    for name, extent in layout:
        starts[name] = here
        here += rows_of(extent)
    return starts, here


def kept_starts(layout):
    starts, here = {}, 0
    for name, extent in layout:
        starts[name] = here
        here += up_to(rows_of(extent), 16)
    return starts, here


class Plan:
    def __init__(self, mesh_shape):
        self.ns, self.ng, self.nd = (mesh_shape[a] for a in (SEC, GRP, DP))
        self.ny = self.nd // 2
        self.chunk = PARAMS // LANES // self.ng
        self.pieces = self.ns * self.nd
        self.piece = up_to(-(-self.chunk // self.pieces), 64)
        self.half = self.piece // 2
        self.room = self.piece * self.pieces
        self.tables = 4 if self.ny == 2 else 2
        self.units = 2 * self.pieces
        self.full = self.ng // 2
        self.rest = flat_starts(DEC_LAYOUT)[1] - self.full * self.chunk
        assert 0 < self.rest <= self.chunk
        self.unit = up_to(-(-self.chunk // (self.units - 1)), 64)
        self.dec_room = self.unit * self.units
        whole = self.chunk // self.unit * self.unit
        self.part_in = self.unit if whole < self.dec_room - self.unit else 0
        self.parts_in = -(-self.rest // self.part_in)
        assert self.parts_in <= self.full
        self.enc_starts = [self.kept_row(ENC_LAYOUT, z * self.chunk) // 16 * 16 for z in range(self.ng)]
        self.enc_ends = [
            up_to(self.kept_row(ENC_LAYOUT, min((z + 1) * self.chunk, flat_starts(ENC_LAYOUT)[1]) - 1) + 1, 16)
            for z in range(self.ng)
        ]
        self.dec_starts = [self.kept_row(DEC_LAYOUT, z * self.chunk) // 16 * 16 for z in range(self.full)]
        self.dec_ends = [
            up_to(self.kept_row(DEC_LAYOUT, (z + 1) * self.chunk - 1) + 1, 16) for z in range(self.full)
        ]
        assert all(e - s <= self.room for s, e in zip(self.enc_starts, self.enc_ends))
        self.rest_start = self.kept_row(DEC_LAYOUT, self.full * self.chunk) // 16 * 16
        self.rest_end = kept_starts(DEC_LAYOUT)[1]
        self.part_out = [self.room - (self.dec_ends[k] - self.dec_starts[k]) for k in range(2)]
        assert max(self.part_out) <= self.room // 2
        assert self.part_out[0] < self.rest_end - self.rest_start <= sum(self.part_out)

    def kept_row(self, layout, flat_row):
        flat, _ = flat_starts(layout)
        kept, _ = kept_starts(layout)
        for name, extent in layout:
            if flat_row < flat[name] + rows_of(extent):
                return kept[name] + flat_row - flat[name]
        return kept[name] + rows_of(extent)

    def ranges(self, first, count, cut, chunks, chunk_room):
        found = []
        whole = self.chunk // cut * cut
        while count:
            z, row = divmod(first, self.chunk)
            if z >= chunks:
                k, row = divmod(row, self.part_in)
                here, room = (k + 1) * chunk_room - cut + row, self.part_in - row
            elif row < whole:
                here, room = z * chunk_room + row, whole - row
            else:
                here, room = z * chunk_room + row + cut - (self.chunk - whole), self.chunk - row
            take = min(count, room)
            found.append((here, take))
            first, count = first + take, count - take
        return found

    def packed_row(self, size, groups, index, row, away_x, away_y):
        owner, turned = away_x * self.ny + away_y, away_y * 2 + away_x
        if self.ny != 2:
            return (owner * groups + index) * size + row, size - row
        part = size // 2
        late, row = divmod(row, part)
        if not late:
            second, index = divmod(index, groups // 2)
            block = groups // 2 * part
            return second * (4 * block) + (turned if second else owner) * block + index * part + row, part - row
        fine = part // 2
        second, row = divmod(row, fine)
        start = groups * 4 * part + index * (4 * part) + second * (4 * fine)
        return start + (turned if second else owner) * fine + row, fine - row

    def enc_regions(self, groups):
        return [(self.enc_starts[z], self.enc_ends[z], k, 0) for k, z in enumerate(groups)]

    def dec_regions(self):
        length = self.room // 2
        found = []
        for z in range(self.full):
            low, high = self.dec_starts[z], self.dec_ends[z]
            found += [(low, low + length, 2 * z, 0), (low + length, high, 2 * z + 1, 0)]
        middle = self.rest_start + self.part_out[0]
        found.append((self.rest_start, middle, 1, length - self.part_out[0]))
        found.append((middle, self.rest_end, 3, length - self.part_out[1]))
        return found

    def segments(self):
        length = self.room // 2
        self.block = up_to(-(-self.chunk // 4), 8)
        rows = {}
        for s, layout in enumerate((ENC_LAYOUT, DEC_LAYOUT)):
            flat, used = flat_starts(layout)
            for z in range(self.ng):
                low, high = z * self.chunk, (z + 1) * self.chunk
                found = [[] for _ in range(4)]

                def put(source, first, stop):
                    while first < stop:
                        block = first // self.block
                        end = min(stop, (block + 1) * self.block)
                        found[block].append((source, first, -(-(end - first) // 8)))
                        source, first = source + end - first, end

                for name, extent in layout:
                    first, last = max(flat[name], low), min(flat[name] + rows_of(extent), high)
                    while first < last:
                        row, stop = self.kept_row(layout, first), last
                        if s == 0:
                            source = row - self.enc_starts[z]
                        elif z < self.full:
                            source = row - self.dec_starts[z]
                        else:
                            row -= self.rest_start
                            k = int(row >= self.part_out[0])
                            row -= k * self.part_out[0]
                            source = (k + 1) * length - self.part_out[k] + row
                            stop = min(last, first + self.part_out[k] - row)
                        put(source, first - low, stop - low)
                        first = stop
                free = max(used, low) - low
                if free < self.chunk:
                    put(self.room, free, min(free + 8, self.chunk))
                rows[s, z] = found, int(free + 8 < self.chunk)
        count = max(len(block) for found, _ in rows.values() for block in found)
        table = np.zeros((self.ns, self.ng, 12 * count + 1), np.int32)
        for (s, z), (found, left) in rows.items():
            for k, block in enumerate(found):
                for j, entry in enumerate(block):
                    table[s, z, 3 * (k * count + j) : 3 * (k * count + j) + 3] = entry
            table[s, z, -1] = left
        return table


def widen_block(held, wide, spare, ranges, rows):
    def load(start, count, further=0):
        first = start // 16 * 16
        size = up_to(start + count - first, 16)
        if isinstance(further, int):
            return held[first : first + size, :].astype(f32), size, start - first
        return held[pl.ds(pl.multiple_of(first + further, 16), size), :].astype(f32), size, start - first

    if isinstance(ranges, tuple):
        block, size, skip = load(ranges[0], rows, ranges[1])
        wide[0:size, :] = block
        return skip
    if len(ranges) == 1:
        block, size, skip = load(*ranges[0])
        wide[0:size, :] = block
        return skip
    here = 0
    for start, count in ranges:
        block, size, skip = load(start, count)
        spare[0:size, :] = block
        wide[here : here + count, :] = spare[skip : skip + count, :]
        here += count
    return 0


def unpack_weights(
    plan, layout, unit, cut, chunks, room, place_ref, sources, counts, outs, vec, held, wide, spare, sems, copies=(),
):
    matrices = [n for n, e in layout if len(e) == 2]
    per_chunk = room // unit
    number = 0
    for source, count in zip(sources, counts):
        for k in range(count):
            slot = place_ref[number]
            number += 1
            target = held.at[pl.ds(pl.multiple_of(slot * unit, 16), unit), :]
            pltpu.make_async_copy(source.at[pl.ds(k * unit, unit), :], target, sems.at[slot // per_chunk]).start()
    arrived = set()

    def arrive(ranges):
        for start, count in ranges:
            z = start // room
            if z not in arrived:
                arrived.add(z)
                part = held.at[pl.ds(z * room, room), :]
                pltpu.make_async_copy(part, part, sems.at[z]).wait()

    vec[...] = jnp.zeros_like(vec)
    flat, _ = flat_starts(layout)
    by_name = dict(zip(matrices, outs))
    order = dict(zip(matrices, copies))
    for name, extent in layout:
        if len(extent) == 2:
            depth, lanes = extent[0], extent[1] // LANES
            step = depth if name == POS else max(128, 2048 // lanes // 128 * 128)
            out = by_name[name]
            if name == POS:
                out[...] = jnp.zeros_like(out)
            found = [
                plan.ranges(flat[name] + first * lanes, min(step, depth - first) * lanes, cut, chunks, room)
                for first in range(0, depth, step)
            ]
            for ranges in found:
                arrive(ranges)

            def move(number, start, size, lanes=lanes, step=step, out=out):
                skip = widen_block(held, wide, spare, start, size * lanes)
                rows = pl.ds(number * step if isinstance(number, int) else pl.multiple_of(number * step, step), size)
                for j in range(lanes):
                    out[rows, j * LANES : (j + 1) * LANES] = wide[pl.ds(skip + j, size, stride=lanes), :].astype(bf16)

            k = 0
            while k < len(found):
                size = min(step, depth - k * step)
                run = 1
                if len(found[k]) == 1 and size == step and step * lanes % 16 == 0:
                    begin = found[k][0][0]
                    while k + run < len(found) and found[k + run] == [(begin + run * step * lanes, step * lanes)]:
                        run += 1
                if run > 1:

                    def turn(i, carry, k=k, begin=begin, lanes=lanes, step=step, move=move):
                        move(k + i, (begin, i * step * lanes), step)
                        return carry

                    lax.fori_loop(0, run, turn, 0)
                else:
                    move(k, found[k], size)
                k += run
            if name in order:
                order[name].start()
        else:
            lanes = extent[0] // LANES
            ranges = plan.ranges(flat[name], lanes, cut, chunks, room)
            arrive(ranges)
            skip = widen_block(held, wide, spare, ranges, lanes)
            row, shift = {QB: (2, 0), VB: (2, 2 * extent[0])}.get(name, (VEC.get(name), 0))
            for j in range(lanes):
                vec[row : row + 1, shift + j * LANES : shift + (j + 1) * LANES] = wide[skip + j : skip + j + 1, :]
    for z in range(chunks):
        arrive([(z * room, 1)])


def pack_kernel(plan, layout, names, regions, size, groups, place_ref, *refs):
    pairs = {}
    for name in names:
        pairs[name], refs = refs[:2], refs[2:]
    vec, refs = refs[0], refs[1:]
    pos = None
    if POS in names:
        pos, refs = pairs[POS][0], refs
    mine, theirs, wide, stage, small, sems = refs
    kept, _ = kept_starts(layout)
    extents = dict(layout)
    ny = plan.ny

    def send(source, first, rows, sem):
        moved = 0
        for low, high, index, base in regions:
            start, stop = max(first, low), min(first + rows, high)
            while start < stop:
                number, row = divmod(base + start - low, size)
                c, s, y = number // (2 * ny), number // ny % 2, number % ny
                away_x, away_y = lax.rem(s - place_ref[0] + 2, 2), lax.rem(y - place_ref[1] + ny, ny)
                where, room = plan.packed_row(size, groups, index, row, away_x, away_y)
                count = min(stop - start, room)
                target = pl.ds(pl.multiple_of(where, 16), count)
                block = source.at[pl.ds(start - first, count), :]
                for same, table in ((True, mine), (False, theirs)):

                    @pl.when((place_ref[2] == c) == same)
                    def _():
                        pltpu.make_async_copy(block, table.at[target, :], sem).start()

                moved += count
                start += count
        return moved

    def wait(rows, slot):
        if rows:
            block = stage.at[slot, pl.ds(0, rows), :]
            pltpu.make_async_copy(block, block, sems.at[slot]).wait()

    turn = 0
    pending = [0, 0]
    for name in names:
        if name == POS:
            continue
        left, right = pairs[name]
        depth, width = extents[name]
        lanes = width // LANES
        step = max(k for k in (128, 256, 384, 512) if depth % k == 0 and k * lanes <= 3072)
        rows = step * lanes
        for first in range(0, depth, step):
            start = kept[name] + first * lanes
            if all(start >= high or start + rows <= low for low, high, _, _ in regions):
                continue
            slot = turn % 2
            turn += 1
            columns = flip(left[:, first : first + step])
            part = 256
            for start in range(0, width, part):
                block = dot(columns, right[:, start : start + part])
                for j in range(part // LANES):
                    wide[pl.ds(start // LANES + j, step, stride=lanes), :] = block[:, j * LANES : (j + 1) * LANES]
            wait(pending[slot], slot)
            stage[slot, 0:rows, :] = wide[0:rows, :].astype(bf16)
            pending[slot] = send(stage.at[slot], kept[name] + first * lanes, rows, sems.at[slot])
    here = 0
    total = 0
    for name, extent in layout:
        if name not in names and len(extent) == 2 or name not in kept_names(names):
            continue
        if len(extent) == 2 and name != POS:
            continue
        rows = rows_of(extent)
        room = up_to(rows, 16)
        wide[0:room, :] = jnp.zeros((room, LANES), f32)
        if name == POS:
            lanes = extent[1] // LANES
            for j in range(lanes):
                wide[pl.ds(j, extent[0], stride=lanes), :] = pos[0 : extent[0], j * LANES : (j + 1) * LANES]
        else:
            row, shift = {QB: (2, 0), VB: (2, 2 * extent[0])}.get(name, (VEC.get(name), 0))
            for j in range(rows):
                wide[j : j + 1, :] = vec[row : row + 1, shift + j * LANES : shift + (j + 1) * LANES]
        small[here : here + room, :] = wide[0:room, :].astype(bf16)
        total += send(small.at[pl.ds(here, room), :], kept[name], room, sems.at[2])
        here += room
    wait(pending[0], 0)
    wait(pending[1], 1)
    block = small.at[pl.ds(0, total), :]
    pltpu.make_async_copy(block, block, sems.at[2]).wait()


def pack_enc_kernel(plan, names, regions, size, groups, place_ref, *refs):
    pairs = {}
    for name in names:
        pairs[name], refs = refs[:4], refs[4:]
    vec, vec_other, *tables = refs[: 2 + plan.tables]
    wide, stage, small, sems = refs[2 + plan.tables :]
    lates = [a for four in pairs.values() for a in four] + [vec, vec_other]
    kept, _ = kept_starts(ENC_LAYOUT)
    extents = dict(ENC_LAYOUT)
    ny = plan.ny

    def pieces(first, rows, core):
        for low, high, index, base in regions:
            start, stop = max(first, low), min(first + rows, high)
            while start < stop:
                number, row = divmod(base + start - low, size)
                count = min(stop - start, size - row)
                if number // (2 * ny) == core:
                    yield start - first, count, index, row, number // ny % 2, number % ny
                start += count

    def send(source, first, rows, sem, core):
        moved = 0
        for skip, count, index, row, s, y in pieces(first, rows, core):
            away_x, away_y = lax.rem(s - place_ref[0] + 2, 2), lax.rem(y - place_ref[1] + ny, ny)
            if ny == 2 and index >= groups // 2:
                keep, away, other, index = tables[2:], away_y, away_x, index - groups // 2
            else:
                keep, away, other = tables[:2], away_x, away_y
            length = (groups // 2 if ny == 2 else groups) * size
            target = pl.ds(pl.multiple_of(other * length, 16) + index * size + row, count)
            block = source.at[pl.ds(skip, count), :]
            for k in range(2):

                @pl.when(away == k)
                def _():
                    pltpu.make_async_copy(block, keep[k].at[target, :], sem).start()

            moved += count
        return moved

    def wait(rows, slot):
        if rows:
            block = stage.at[slot, pl.ds(0, rows), :]
            pltpu.make_async_copy(block, block, sems.at[slot]).wait()

    def run(core):
        turn = 0
        pending = [0, 0]
        for name in names:
            left, left_other, right, right_other = pairs[name]
            depth, width = extents[name]
            lanes = width // LANES
            step = max(k for k in (128, 256, 384, 512) if depth % k == 0 and k * lanes <= 3072)
            rows = step * lanes
            for first in range(0, depth, step):
                begin = kept[name] + first * lanes
                if not list(pieces(begin, rows, core)):
                    continue
                slot = turn % 2
                turn += 1
                columns = flip(left[:, first : first + step])
                others = flip(left_other[:, first : first + step])
                part = 256
                for start in range(0, width, part):
                    cols = slice(start, start + part)
                    block = dot(columns, right[:, cols]) + dot(others, right_other[:, cols])
                    for j in range(part // LANES):
                        wide[pl.ds(start // LANES + j, step, stride=lanes), :] = block[:, j * LANES : (j + 1) * LANES]
                wait(pending[slot], slot)
                stage[slot, 0:rows, :] = wide[0:rows, :].astype(bf16)
                pending[slot] = send(stage.at[slot], begin, rows, sems.at[slot], core)
        here = 0
        total = 0
        for name, extent in ENC_LAYOUT:
            if name not in kept_names(names):
                continue
            rows = rows_of(extent)
            room = up_to(rows, 16)
            if list(pieces(kept[name], room, core)):
                wide[0:room, :] = jnp.zeros((room, LANES), f32)
                row, shift = {QB: (2, 0), VB: (2, 2 * extent[0])}.get(name, (VEC.get(name), 0))
                for j in range(rows):
                    cols = slice(shift + j * LANES, shift + (j + 1) * LANES)
                    wide[j : j + 1, :] = vec[row : row + 1, cols] + vec_other[row : row + 1, cols]
                small[here : here + room, :] = wide[0:room, :].astype(bf16)
                total += send(small.at[pl.ds(here, room), :], kept[name], room, sems.at[2], core)
            here += room
        wait(pending[0], 0)
        wait(pending[1], 1)
        if total:
            block = small.at[pl.ds(0, total), :]
            pltpu.make_async_copy(block, block, sems.at[2]).wait()

    for core in range(2):

        @pl.when(place_ref[2] == core)
        def _():
            for each in lates:
                each.here = False
            run(core)
            for each in lates:
                each.arrive()


def pack_enc(plan, regions, size, groups, place, pairs, vec, vec_other):
    names = list(pairs)
    operands = [a for name in names for a in pairs[name]] + [vec, vec_other]
    extents = dict(ENC_LAYOUT)
    small = sum(up_to(rows_of(extents[n]), 16) for n in kept_names(names))
    rows = 2 * plan.ny * groups * size // plan.tables
    return late_call(
        partial(pack_enc_kernel, plan, names, regions, size, groups),
        [(place, pltpu.SMEM)],
        operands,
        [(shape((rows, LANES), bf16), pl.ANY)] * plan.tables,
        [
            pltpu.VMEM((3072, LANES), f32),
            pltpu.VMEM((2, 3072 + 64, LANES), bf16),
            pltpu.VMEM((small + 64, LANES), bf16),
            pltpu.SemaphoreType.DMA((3,)),
        ],
        cost_estimate=cost(8),
        name="pack_enc",
    )


def kept_names(names):
    with_matrix = {
        QKV_W: [N1G, N1B, QB, VB],
        PROJ_W: [PB, N2G, N2B],
        UP_W: [UB],
        DOWN_W: [DB],
        EMBED_W: [EB, MT],
        POS: [POS],
    }
    return [v for n in names for v in with_matrix[n]]


def pack(plan, layout, regions, size, groups, place, pairs, vec):
    names = list(pairs)
    operands = [a for name in names for a in pairs[name]] + [vec]
    extents = dict(layout)
    small = sum(up_to(rows_of(extents[n]), 16) for n in kept_names(names))
    rows = 2 * plan.ny * groups * size
    return late_call(
        partial(pack_kernel, plan, layout, names, regions, size, groups),
        [(place, pltpu.SMEM)],
        operands,
        [(shape((rows, LANES), bf16), pl.ANY)] * 2,
        [
            pltpu.VMEM((3072, LANES), f32),
            pltpu.VMEM((2, 3072 + 64, LANES), bf16),
            pltpu.VMEM((small + 64, LANES), bf16),
            pltpu.SemaphoreType.DMA((3,)),
        ],
        cost_estimate=cost(19),
        name="pack",
    )


def finish_kernel(plan, counts, place_ref, seg_ref, *refs):
    sources, result, held, wide, out, sem, out_sems = refs[: len(counts)], *refs[len(counts) :]
    unit = plan.half
    number = 0
    for source, count in zip(sources, counts):
        for k in range(count):
            target = held.at[pl.ds(pl.multiple_of(place_ref[number] * unit, 16), unit), :]
            number += 1
            pltpu.make_async_copy(source.at[pl.ds(k * unit, unit), :], target, sem.at[0]).start()
    count = seg_ref.shape[0] // 12

    @pl.when(seg_ref[12 * count] != 0)
    def _():
        out[...] = jnp.zeros_like(out)

    pltpu.make_async_copy(held, held, sem.at[0]).wait()
    total = plan.room
    wide[total : total + 16, :] = jnp.zeros((16, LANES), f32)
    wide[0:total, :] = held[...].astype(f32)

    def one(k, carry):
        source, first, steps = seg_ref[3 * k], seg_ref[3 * k + 1], seg_ref[3 * k + 2]

        def step(i, carry):
            out[pl.ds(first + 8 * i, 8), :] = wide[pl.ds(source + 8 * i, 8), :]
            return carry

        def steps16(i, carry):
            out[pl.ds(first + 128 * i, 128), :] = wide[pl.ds(source + 128 * i, 128), :]
            return carry

        many = steps // 16
        lax.fori_loop(0, many, steps16, 0)
        return lax.fori_loop(many * 16, steps, step, carry)

    rows = up_to(plan.chunk, 8)
    lines = out.at[pl.ds(0, rows), :].reshape(rows, 1, LANES)
    copies = []
    for block in range(4):
        lax.fori_loop(block * count, (block + 1) * count, one, 0)
        first = block * plan.block
        part = pl.ds(first, min(plan.block, plan.chunk - first))
        copies.append(pltpu.make_async_copy(lines.at[part], result.at[part], out_sems.at[block]))
        copies[-1].start()
    for copy in copies:
        copy.wait()


def finish(plan, place, segments, sources):
    total = plan.room
    return pl.pallas_call(
        partial(finish_kernel, plan, [s.shape[0] // plan.half for s in sources]),
        in_specs=[pl.BlockSpec(memory_space=pltpu.SMEM)] * 2
        + [pl.BlockSpec(memory_space=pl.ANY)] * len(sources),
        out_specs=pl.BlockSpec(memory_space=pl.ANY),
        out_shape=shape((plan.chunk, 1, LANES), f32),
        scratch_shapes=[
            pltpu.VMEM((total, LANES), bf16),
            pltpu.VMEM((total + 16, LANES), f32),
            pltpu.VMEM((up_to(plan.chunk, 8) + 8, LANES), f32),
            pltpu.SemaphoreType.DMA((1,)),
            pltpu.SemaphoreType.DMA((4,)),
        ],
        compiler_params=params_of(),
        cost_estimate=cost(8),
        name="finish",
    )(place, segments, *sources)


def completed(pairs, count):
    senders = [k for k in range(count) if k not in [a for a, _ in pairs]]
    receivers = [k for k in range(count) if k not in [b for _, b in pairs]]
    return list(pairs) + list(zip(senders, receivers))


def after(values, *before):
    return lax.optimization_barrier((values, before))[0]


def per_device(plan, enc_input, segments, slots, params, cot):
    ns, ng, nd, ny = plan.ns, plan.ng, plan.nd, plan.ny
    piece, half, room, chunk = plan.piece, plan.half, plan.room, plan.chunk
    sec = lax.axis_index(SEC)
    grp = lax.axis_index(GRP)
    dp = lax.axis_index(DP)
    yy, core = dp // 2, dp % 2
    first_section = sec == 0

    def over_x(block):
        return lax.ppermute(block, SEC, [(0, 1), (1, 0)])

    def over_core(block):
        return lax.ppermute(block, DP, [(d, d ^ 1) for d in range(nd)])

    def over_y(block):
        return lax.ppermute(block, DP, [(d, (d + 2) % nd) for d in range(nd)])

    def over_z(block, senders=None):
        senders = range(ng) if senders is None else senders
        return lax.ppermute(block, GRP, [(g, (g + 1) % ng) for g in senders])

    def final_places():
        if ny == 2:
            owners = [(sec, yy), (1 - sec, yy), (sec, 1 - yy), (1 - sec, 1 - yy)]
        else:
            owners = [(s, (yy - k) % ny) for k in range(ny) for s in (sec, 1 - sec)]
        found = []
        for c in (core, 1 - core):
            for s, y in owners:
                number = (c * 2 + s) * ny + y
                found += [
                    jnp.where(first_section, 2 * number, number),
                    jnp.where(first_section, 2 * number + 1, plan.pieces + number),
                ]
        return found

    unit = plan.unit

    def share(start, params):
        cut = lax.dynamic_slice(params, (0, start * LANES), (1, unit * LANES))
        return cut.astype(f32).reshape(unit, LANES).astype(bf16)

    def shares(section, params):
        number = section * nd + dp
        enc_first = jnp.minimum(number * piece, chunk - piece)
        dec_first = [jnp.minimum((h * plan.pieces + number) * unit, chunk - unit) for h in range(2)]
        if plan.parts_in == 1:
            dec_first[0] = jnp.where(grp == plan.full, 0, dec_first[0])
        return (
            share(jnp.where(first_section, enc_first, dec_first[0]), params),
            share(jnp.where(first_section, enc_first + piece - unit, dec_first[1]), params),
        )

    send = shares(1 - sec, params)
    keep = shares(sec, after(params, *send))

    def whole_piece(parts):
        return jnp.concatenate([parts[0][:half], parts[1][unit - half :]])

    routes = [[(z, 2 * z + h) for z in range(plan.full)] for h in range(2)]
    if plan.parts_in == 1:
        routes[0].append((plan.full, 1))
    routes = [completed(route, ng) for route in routes]
    crossed = []
    for h in range(2):
        pairs = [(z, ng + z) for z in range(ng)] + [(ng + a, b) for a, b in routes[h]]
        crossed.append(lax.ppermute(send[h], (SEC, GRP), pairs))
    spread = [lax.ppermute(keep[h], GRP, routes[h]) for h in range(2)]
    enc_piece = jnp.where(first_section, whole_piece(keep), whole_piece(crossed))
    even, odd = (jnp.where(first_section, crossed[h], spread[h]) for h in range(2))
    dec_piece = jnp.where(grp % 2 == 0, even, odd)
    class Gather:
        def __init__(self, here):
            self.here = here
            if ny == 2:
                self.arrays = [here, over_x(here), over_y(here)]
                self.owners = [(sec, yy), (1 - sec, yy), (sec, 1 - yy), (1 - sec, 1 - yy)]
            else:
                column = [here]
                for _ in range(ny - 1):
                    column.append(over_y(column[-1]))
                self.arrays = column
                self.owners = [(s, (yy - k) % ny) for s in (sec, 1 - sec) for k in range(ny)]

        def second(self):
            if ny == 2:
                middle = self.here.shape[0] // 2
                self.corners = [self.arrays[1][:middle], self.arrays[2][middle:]]
            else:
                self.corners = self.arrays
            return tuple(self.corners)

        def third(self):
            if ny == 2:
                self.arrays += [over_y(self.corners[0]), over_x(self.corners[1])]
            else:
                self.arrays = self.arrays + [over_x(block) for block in self.corners]
            return tuple(self.arrays[-2:])

        def fourth(self, joined=True):
            arrays = [jnp.concatenate(self.arrays)] if joined else self.arrays
            return arrays + [over_core(block) for block in arrays]

        def places(self, parts):
            found = []
            for c in (core, 1 - core):
                for s, y in self.owners:
                    for k in parts:
                        number = (grp - k) % ng * plan.pieces + s * nd + y * 2 + c
                        found += [2 * number, 2 * number + 1]
            return found

    last = jnp.logical_and(sec == ns - 1, dp == nd - 1)
    if plan.parts_in == 1:
        dec_piece = jnp.where(jnp.logical_and(last, grp == 1), even, dec_piece)
    else:
        for k in range(plan.parts_in):
            part = share(jnp.minimum(k * unit, chunk - unit), params)
            part = lax.ppermute(part, GRP, [(plan.full, 2 * k + 1)])
            dec_piece = jnp.where(jnp.logical_and(last, grp == 2 * k + 1), part, dec_piece)
    here = enc_piece
    gathers = [Gather(here)]
    micro_rows = enc_input.reshape(ROW, WIDTH)
    seg = lax.dynamic_index_in_dim(segments, sec, 0, keepdims=False).reshape(ROW)
    slot = lax.dynamic_index_in_dim(slots, sec, 0, keepdims=False).reshape(ROW)
    cot_rows = jnp.pad(
        cot.reshape(IMAGES_ROW, SLOTS, DEC_WIDTH), ((0, 0), (0, SLOT_PAD - SLOTS), (0, 0))
    ).reshape(IMAGES_ROW * SLOT_PAD, DEC_WIDTH)

    columns = (seg.reshape(ROW, 1), slot.reshape(ROW, 1))
    table = jnp.asarray(plan.segments())[sec, grp].reshape(-1)
    place = jnp.stack([sec, yy, core]).astype(jnp.int32)
    finish_places = jnp.stack(final_places()).astype(jnp.int32)
    enc_places = jnp.stack([p for k in range(ng) for p in gathers[0].places([k])]).astype(jnp.int32)
    dec_places = jnp.stack(gathers[0].places(range(ng))).astype(jnp.int32)
    small = (columns, table, place, finish_places, enc_places, dec_places, cot_rows)
    for k in range(1, ng):
        here = over_z(here)
        if k == 1:
            here, small = after((here, small), enc_piece)
            here = after(here, *small)
        if k >= 2:
            here = after(here, *gathers[k - 2].second())
        if k >= 3:
            here = after(here, *gathers[k - 3].third())
        gathers.append(Gather(here))
    gathers[-2].second()
    dec_parts = [after(dec_piece, here)]
    for _ in range(ng - 1):
        dec_parts.append(over_z(dec_parts[-1]))
    gathers[-1].arrays[1:] = after(gathers[-1].arrays[1:], *dec_parts[1:-1])
    gathers[-1].second()
    columns, table, place, finish_places, enc_places, dec_places, cot_rows = small
    enc_sources = []
    for k, g in enumerate(gathers):
        if k >= ng - 3:
            g.third()
        if k == ng - 1:
            g.arrays = after(g.arrays, dec_parts[-1])
        enc_sources += g.fourth()
    dec_gather = Gather(after(jnp.concatenate(dec_parts), *gathers[-1].corners))

    enc_weights, saved = encode(plan, enc_places, enc_sources, micro_rows, seg, columns[0])
    dec_gather.arrays[1:] = after(dec_gather.arrays[1:], saved[H2])
    saved[H2] = after(saved[H2], *dec_gather.second())
    saved.update(encode_mlp(saved, enc_weights))
    others = {k: over_core(saved[k]) for k in (H1, ATT, H2, ACT)}
    dec_gather.third()
    dec_gather.arrays[-2:] = after(dec_gather.arrays[-2:], saved[SENT])
    dec_sources = dec_gather.fourth(False)
    dec = dict(
        zip(
            [OUT, H1, QKV_L, ATT, PROJ_L, H2, UP_L, ACT, EMBED_L, GSENT, VECS, GPOS],
            decode(plan, dec_places, dec_sources, saved[SENT], seg, slot, columns, cot_rows),
        )
    )

    def add(first, *others):
        total = first.astype(f32)
        for other in others:
            total = total + other.astype(f32)
        return total.astype(bf16)

    class Square:
        def __init__(self, keeps, sends):
            self.keeps, self.sends = keeps, [add(*parts) if len(parts) > 1 else parts[0] for parts in sends]
            self.m = keeps[0][0].shape[0] // ny

        def kept(self, half, low, high, *others):
            return add(*[part[low:high] for part in self.keeps[half]], *others)

        def first(self):
            return (over_x(self.sends[0]), over_y(self.sends[1])) if ny == 2 else (over_x(self.sends[0]),)

        def second(self, *got):
            m = self.m
            self.got = got
            if ny == 2:
                self.sends = tuple(self.kept(k, m, 2 * m, got[k][m:]) for k in range(2))
            else:
                column = self.kept(0, 0, ny * m, got[0])
                total = column[(ny - 1) * m :]
                for k in range(ny - 2, -1, -1):
                    total = add(column[k * m : (k + 1) * m], over_y(total))
                self.sends = (total,)
            return self.sends

        def third(self, *before):
            m = self.m
            if ny == 2:
                late = after((over_y(self.sends[0]), over_x(self.sends[1])), *before)
                self.own = tuple(self.kept(k, 0, m, self.got[k][:m], late[k]) for k in range(2))
            else:
                self.own = (self.sends[0][: m // 2], self.sends[0][m // 2 :])
            return self.own

    class Ring:
        def __init__(self, one):
            self.one, self.step = one, 0
            self.total = add(*one((grp - 1) % ng))

        def next(self, *before):
            got = after(over_z(self.total), *before)
            self.step += 1
            self.total = add(*self.one((grp - 1 - self.step) % ng), got)
            return self.total

    def pick(blocks, g):
        if len(blocks) == 4 == ng:
            return jnp.where(g < 2, jnp.where(g == 0, *blocks[:2]), jnp.where(g == 2, *blocks[2:]))
        rows = jnp.concatenate(blocks)
        size = rows.shape[0] // ng
        return lax.dynamic_slice(rows, (g * size, 0), (size, LANES))

    def halves(block):
        return [block[: block.shape[0] // 2], block[block.shape[0] // 2 :]]

    every = list(range(ng))
    near = ng // 2
    upper, lower = every[near:], every[:near]
    grad_sent, others = after((dec[GSENT], others), dec[VECS])
    grad_sent = after(grad_sent, *others.values())
    grad_other = over_core(grad_sent)
    up_low, proj_low, grad_middle, mlp_vec = mlp_back(grad_sent, saved, enc_weights)
    grad_other = after(grad_other, up_low)
    up_other, proj_other, mlp_vec_other = over_core(up_low), over_core(proj_low), over_core(mlp_vec)
    in_grad, qkv_low, enc_vec = attention_back(grad_middle, proj_low, micro_rows, saved, enc_weights, mlp_vec)
    up_other, proj_other, mlp_vec_other = after((up_other, proj_other, mlp_vec_other), qkv_low)
    up_tables = pack_enc(
        plan, plan.enc_regions(upper), piece, len(upper), place,
        {
            DOWN_W: (saved[ACT], others[ACT], grad_sent, grad_other),
            UP_W: (saved[H2], others[H2], after(up_low, qkv_low), up_other),
        },
        mlp_vec, mlp_vec_other,
    )
    qkv_other, vec_other = after((over_core(qkv_low), over_core(enc_vec)), up_tables[0])
    dec_mine, dec_theirs = pack(
        plan, DEC_LAYOUT, plan.dec_regions(), half, ng, place,
        {
            EMBED_W: (saved[SENT], dec[EMBED_L]),
            QKV_W: (dec[H1], dec[QKV_L]),
            PROJ_W: (dec[ATT], dec[PROJ_L]),
            UP_W: (dec[H2], dec[UP_L]),
            DOWN_W: (dec[ACT], cot_rows),
            POS: (dec[GPOS], dec[GPOS]),
        },
        after(dec[VECS], up_tables[0]),
    )
    qkv_other, vec_other = after((qkv_other, vec_other), dec_mine)

    def table_square(tables):
        return Square([[t] for t in tables[0::2]], [[t] for t in tables[1::2]])

    upper_sum = table_square(up_tables)
    upper_sum.second(*after(upper_sum.first(), dec_mine))
    low_tables = pack_enc(
        plan, plan.enc_regions(lower), piece, len(lower), place,
        {
            PROJ_W: (saved[ATT], others[ATT], proj_low, proj_other),
            QKV_W: (saved[H1], others[H1], qkv_low, qkv_other),
            UP_W: (saved[H2], others[H2], after(up_low, *upper_sum.sends), up_other),
        },
        enc_vec, vec_other,
    )
    lower_sum = table_square(low_tables)
    lower_first = lower_sum.first()
    dec_parts = (dec_mine, after(over_core(dec_theirs), low_tables[0]))

    def dec_rows(low, high):
        return [part[low:high] for part in dec_parts]

    if ny == 2:
        rows = dec_mine.shape[0] // 2
        size = rows // ng

        def dec_late(g):
            return [lax.dynamic_slice(part, (rows + g * size, 0), (size, LANES)) for part in dec_parts]

        late_ring = Ring(dec_late)
        quarter = rows // 4
        cuts = [dec_rows(k * quarter, (k + 1) * quarter) for k in range(4)]
        upper_sum.third(late_ring.total)
        lower_sum.second(*after(lower_first, *upper_sum.own))
        early = Square(cuts[0::2], cuts[1::2])
        early.sends = after(early.sends, *lower_sum.sends)
        early_first = early.first()
        late_ring.next(*early.sends)
        lower_sum.third(late_ring.total)
        enc_ring = Ring(lambda g: [pick(list(lower_sum.own) + list(upper_sum.own), g)])
        early.second(*after(early_first, enc_ring.total))
        for _ in range(ng - 3):
            late_ring.next(*early.sends)
        early_own = [b for o in early.third(late_ring.total) for b in halves(o)]
        early_ring = Ring(lambda g: [pick(early_own, g)])
        enc_ring.next(early_ring.total)
        late_ring.next(enc_ring.total)
        quarter = size // 4
        cuts = [[late_ring.total[k * quarter : (k + 1) * quarter]] for k in range(4)]
        late = Square(cuts[0::2], cuts[1::2])
        late_first = late.first()
        early_ring.next(*late.sends)
        late.second(*after(late_first, early_ring.total))
        early_ring.next(*late.sends)
        late_own = late.third(early_ring.total)
        for _ in range(ng - 3):
            early_ring.next(*late_own)
        dec_own = jnp.concatenate([early_ring.total, *late_own])
    else:
        lower_sum.second(*lower_first)
        rows = dec_mine.shape[0] // 2
        whole = Square([dec_rows(0, rows)], [dec_rows(rows, 2 * rows)])
        whole.second(*whole.first())
        dec_ring = Ring(lambda g: [pick(list(whole.third()), g)])
        for _ in range(ng - 1):
            dec_ring.next()
        dec_own = dec_ring.total
        upper_sum.third()
        lower_sum.third()
        enc_ring = Ring(lambda g: [pick(list(lower_sum.own) + list(upper_sum.own), g)])
        enc_ring.next()
    back = [[(2 * z + h, z) for z in range(plan.full)] for h in range(2)]
    back[0].append((1, plan.full))
    back.append([(3, plan.full)])
    dec_back = [lax.ppermute(dec_own, GRP, completed(pairs, ng)) for pairs in back]
    enc_ring.next(dec_own)
    dec_low, dec_high, dec_rest = after(dec_back, enc_ring.total)
    dec_own = jnp.concatenate([dec_low, jnp.where(grp == plan.full, dec_rest, dec_high)])
    for _ in range(ng - 3):
        enc_ring.next(dec_own)
    enc_own = enc_ring.total

    own = jnp.where(first_section, enc_own, dec_own)
    other = jnp.where(first_section, dec_own, enc_own)
    if ny == 2:
        from_x, from_y = over_x(other), over_y(own)
        sources = [own, from_x, from_y, over_y(from_x)]
    else:
        column = [jnp.concatenate([own, over_x(other)])]
        for _ in range(ny - 1):
            column.append(over_y(column[-1]))
        sources = column
    sources = sources + [over_core(block) for block in sources]
    flat = finish(plan, finish_places, table, sources)
    param_grad = flat.reshape(1, chunk * LANES)
    dec_out = dec[OUT].reshape(IMAGES_ROW, SLOT_PAD, DEC_WIDTH)[:, :SLOTS]
    return (
        dec_out.reshape(1, 1, IMAGES_ROW * SLOTS, DEC_WIDTH),
        in_grad.reshape(1, 1, ROW, WIDTH),
        param_grad,
    )


def solution(mesh):
    placed = (
        P(SEC, (GRP, DP), None, None),
        P(None, (GRP, DP), None),
        P(None, (GRP, DP), None),
        P(SEC, GRP),
        P(SEC, (GRP, DP), None, None),
    )
    return jax.shard_map(
        partial(per_device, Plan(dict(mesh.shape))),
        mesh=mesh,
        in_specs=placed,
        out_specs=(
            P(SEC, (GRP, DP), None, None),
            P(SEC, (GRP, DP), None, None),
            P(SEC, GRP),
        ),
        check_vma=False,
    )
```

```python
from functools import partial
import math

import jax
import jax.numpy as jnp
import numpy as np
from jax import lax
from jax.experimental import pallas as pl
from jax.experimental.pallas import tpu as pltpu
from jax.sharding import PartitionSpec as P

WIDTH = 768
HEADS = 12
HIDDEN_SIZE = 3072
DEC_WIDTH = 512
DEC_HEADS = 16
DEC_HIDDEN = 2048
SLOTS = 196
IMAGES_ROW = 5
ROW = 256
PARAMS = 7088128
LANES = 128
SEC, GRP, DP = "section", "group", "dp"
(
    N1G, N1B, QKV_W, QB, VB, PROJ_W, PB, N2G,
) = range(0, 8)
(
    N2B, UP_W, UB, DOWN_W, DB, EMBED_W, EB, MT,
) = range(8, 16)
(
    POS, QKV_B, VECS, SENT, H1, QKV, PROBS, ATT,
) = range(16, 24)
(
    MID, H2, ACT, SLOPE, OUT, QKV_L, PROJ_L, UP_L,
) = range(24, 32)
(
    EMBED_L, GSENT, GPOS,
) = range(32, 35)
SLOT_PAD = 208
VMEM_BYTES = 60 * 1024 * 1024

norm_eps = 1e-06
masked_score = -1000000000.0
f32 = jnp.float32
bf16 = jnp.bfloat16


def block_layout(width, hidden):
    return [
        (N1G, (width,)),
        (N1B, (width,)),
        (QKV_W, (width, 3 * width)),
        (QB, (width,)),
        (VB, (width,)),
        (PROJ_W, (width, width)),
        (PB, (width,)),
        (N2G, (width,)),
        (N2B, (width,)),
        (UP_W, (width, hidden)),
        (UB, (hidden,)),
        (DOWN_W, (hidden, width)),
        (DB, (width,)),
    ]


def decoder_layout(enc_width, width, hidden, slot_count):
    return [
        (EMBED_W, (enc_width, width)),
        (EB, (width,)),
        (MT, (width,)),
        (POS, (slot_count, width)),
    ] + block_layout(width, hidden)


ENC_LAYOUT = block_layout(WIDTH, HIDDEN_SIZE)
DEC_LAYOUT = decoder_layout(WIDTH, DEC_WIDTH, DEC_HIDDEN, SLOTS)
VEC = {
    N1G: 0,
    N1B: 1,
    QKV_B: 2,
    PB: 3,
    N2G: 4,
    N2B: 5,
    UB: 6,
    DB: 7,
    EB: 8,
    MT: 9,
}
VEC_ROWS = 16


def dot(a, b):
    return lax.dot_general(a, b, (((1,), (0,)), ((), ())), preferred_element_type=f32)


def dot_nt(a, b):
    return lax.dot_general(a, b, (((1,), (1,)), ((), ())), preferred_element_type=f32)


def dot_tn(a, b):
    return lax.dot_general(a, b, (((0,), (0,)), ((), ())), preferred_element_type=f32)


def normalised(values):
    centered = values - jnp.mean(values, axis=-1, keepdims=True)
    inverse = lax.rsqrt(jnp.mean(centered * centered, axis=-1, keepdims=True) + norm_eps)
    return centered * inverse, inverse


def norm_back(grad, hat, inverse, gain):
    scaled = grad * gain
    first = jnp.mean(scaled, axis=-1, keepdims=True)
    second = jnp.mean(scaled * hat, axis=-1, keepdims=True)
    return inverse * (scaled - first - hat * second)


def col_sum(values):
    return jnp.sum(values, axis=0, keepdims=True)


def gelu_parts(upward):
    half = 0.5 + 0.5 * lax.erf(upward * f32(math.sqrt(0.5)))
    slope = half + upward * (jnp.exp(upward * upward * f32(-0.5)) * f32(1.0 / math.sqrt(2.0 * math.pi)))
    return upward * half, slope


def head_mask(head, head_dim):
    lane = lax.broadcasted_iota(jnp.int32, (1, LANES), 1)
    return jnp.where(lane // head_dim == head, 1.0, 0.0).astype(bf16)


def lane_block(group, start=0):
    if isinstance(group, int):
        return slice(start + group * LANES, start + (group + 1) * LANES)
    return pl.ds(pl.multiple_of(start + group * LANES, LANES), LANES)


def flip(values):
    return values.astype(f32).T.astype(bf16)


def attention_forward(qkv_ref, probs_ref, joined_ref, width, heads, keep):
    head_dim = width // heads
    factor = f32(head_dim ** (-0.5) * math.log2(math.e))
    per_group = LANES // head_dim

    def some_groups(groups):
        heads_here = [(group, sub) for group in groups for sub in range(per_group)]
        queries = {g: qkv_ref[:, lane_block(g)] for g in groups}
        keys = {g: qkv_ref[:, lane_block(g, width)] for g in groups}
        values_t = {g: flip(qkv_ref[:, lane_block(g, 2 * width)]) for g in groups}
        scores = [dot_nt(keys[g], queries[g] * head_mask(sub, head_dim)) for g, sub in heads_here]
        scores = [keep(s) for s in scores]
        expo = [jnp.exp2((s - jnp.max(s, axis=0, keepdims=True)) * factor) for s in scores]
        probs = [e * (1.0 / col_sum(e)) for e in expo]
        for (g, sub), p in zip(heads_here, probs):
            probs_ref[g * per_group + sub] = p
        outs = [
            dot(values_t[g][sub * head_dim : (sub + 1) * head_dim], p.astype(bf16))
            for (g, sub), p in zip(heads_here, probs)
        ]
        joined_ref[groups[0] * LANES : (groups[-1] + 1) * LANES, :] = jnp.concatenate(outs, axis=0)

    some_groups(range(width // LANES))


def attention_backward(qkv_ref, probs_ref, grad_ref, low_ref, width, heads):
    head_dim = width // heads
    scale = f32(head_dim ** (-0.5))
    per_group = LANES // head_dim
    for each in (qkv_ref, probs_ref):
        if isinstance(each, Late):
            each.arrive()

    def some_groups(groups):
        heads_here = [(group, sub) for group in groups for sub in range(per_group)]
        masks = [head_mask(sub, head_dim) for sub in range(per_group)]
        queries = {g: qkv_ref[:, lane_block(g)] for g in groups}
        keys = {g: qkv_ref[:, lane_block(g, width)] for g in groups}
        values = {g: qkv_ref[:, lane_block(g, 2 * width)] for g in groups}
        grads = {g: grad_ref[:, lane_block(g)] for g in groups}
        keys_t = {g: flip(keys[g]) for g in groups}
        own = [grads[g] * masks[sub] for g, sub in heads_here]
        grad_probs = [dot_nt(values[g], o) for (g, sub), o in zip(heads_here, own)]
        probs = [probs_ref[g * per_group + sub] for g, sub in heads_here]
        grad_values = [dot(p.astype(bf16), o) for p, o in zip(probs, own)]
        low = [(p * (g - col_sum(p * g))).astype(bf16) for p, g in zip(probs, grad_probs)]
        grad_keys = [dot(l, queries[g] * masks[sub]) for (g, sub), l in zip(heads_here, low)]
        grad_queries = [
            dot(keys_t[g][sub * head_dim : (sub + 1) * head_dim], l) for (g, sub), l in zip(heads_here, low)
        ]
        for k, g in enumerate(groups):
            mine = slice(k * per_group, (k + 1) * per_group)
            low_ref[:, lane_block(g)] = (jnp.concatenate(grad_queries[mine], axis=0).T * scale).astype(bf16)
            low_ref[:, lane_block(g, width)] = (sum(grad_keys[mine]) * scale).astype(bf16)
            low_ref[:, lane_block(g, 2 * width)] = sum(grad_values[mine]).astype(bf16)

    some_groups(range(width // LANES))


class Late:
    def __init__(self, source, target, sem):
        self.copy, self.target, self.shape = pltpu.make_async_copy(source, target, sem), target, target.shape
        self.here = False
        self.copy.start()

    def arrive(self):
        if not self.here:
            self.copy.wait()
            self.here = True

    def __getitem__(self, index):
        self.arrive()
        return self.target[index]


def late_call(kernel, early, late, outs, scratch, **options):
    count, many = len(early), len(late)

    def body(*refs):
        sources, results = refs[count : count + many], refs[count + many : count + many + len(outs)]
        rest = refs[count + many + len(outs) :]
        held, sems = rest[:many], rest[many]
        lates = [Late(sources[k], held[k], sems.at[k]) for k in range(many)]
        kernel(*refs[:count], *lates, *results, *rest[many + 1 :])
        for each in lates:
            each.arrive()

    return pl.pallas_call(
        body,
        in_specs=[pl.BlockSpec(memory_space=m) for _, m in early] + [pl.BlockSpec(memory_space=pl.ANY)] * many,
        out_specs=[pl.BlockSpec(memory_space=m) for _, m in outs],
        out_shape=[o for o, _ in outs],
        scratch_shapes=[pltpu.VMEM(a.shape, a.dtype) for a in late]
        + [pltpu.SemaphoreType.DMA((many,))]
        + list(scratch),
        compiler_params=params_of(),
        **options,
    )(*[a for a, _ in early], *late)


def encode_kernel(plan, counts, place_ref, *refs):
    sources, refs = refs[: len(counts)], refs[len(counts) :]
    x_ref, seg_row_ref, seg_col_ref = refs[:3]
    weight_outs, vec = refs[3:7], refs[7]
    normed1_ref, qkv_ref, probs_ref, attended_ref, middle_ref, normed2_ref = refs[8:14]
    held, wide, spare, sems, out_sems, joined_ref = refs[14:20]
    weights = refs[20:24]
    qkv_w, proj_w = weights[:2]
    copies = [pltpu.make_async_copy(w, o, out_sems.at[k]) for k, (w, o) in enumerate(zip(weights, weight_outs))]
    unpack_weights(
        plan, ENC_LAYOUT, plan.half, plan.piece, plan.ng, plan.room, place_ref, sources, counts,
        weights, vec, held, wide, spare, sems, copies,
    )
    width, hidden = WIDTH, HIDDEN_SIZE
    inputs = x_ref[...].astype(f32)
    hat, _ = normalised(inputs)
    normed1 = (hat * vec[0:1, :width] + vec[1:2, :width]).astype(bf16)
    normed1_ref[...] = normed1
    qkv_ref[...] = (dot(normed1, qkv_w[...]) + vec[2:3, : 3 * width]).astype(bf16)
    allowed = seg_col_ref[...] == seg_row_ref[...]
    attention_forward(
        qkv_ref, probs_ref, joined_ref, width, HEADS,
        lambda scores: jnp.where(allowed, scores, f32(masked_score * (width // HEADS) ** 0.5)),
    )
    attended = joined_ref[...].T.astype(bf16)
    attended_ref[...] = attended
    middle = inputs + (dot(attended, proj_w[...]) + vec[3:4, :width])
    middle_ref[...] = middle
    hat, _ = normalised(middle)
    normed2_ref[...] = (hat * vec[4:5, :width] + vec[5:6, :width]).astype(bf16)
    for copy in copies:
        copy.wait()


def encode_mlp_kernel(normed2_ref, up_w, vec, down_w, middle_ref, sent_ref, active_ref, slope_ref):
    width, hidden = WIDTH, HIDDEN_SIZE
    total = jnp.zeros((ROW, width), f32)
    part = 1536
    for start in range(0, hidden, part):
        cols = slice(start, start + part)
        upward = dot(normed2_ref[...], up_w[:, cols]) + vec[6:7, cols]
        active, slope = gelu_parts(upward)
        active_ref[:, cols] = active.astype(bf16)
        slope_ref[:, cols] = slope.astype(slope_ref.dtype)
        total += dot(active_ref[:, cols], down_w[cols, :])
    sent_ref[...] = (middle_ref[...] + (total + vec[7:8, :width])).astype(bf16)


def mlp_back_kernel(
    grad_ref, down_w, slope_ref, up_w, middle_ref, vec,
    up_low_ref, proj_low_ref, grad_middle_ref, vec_grad,
):
    width, hidden = WIDTH, HIDDEN_SIZE
    grad_out = grad_ref[...]
    vec_grad[...] = jnp.zeros_like(vec_grad)
    vec_grad[7:8, :width] = col_sum(grad_out.astype(f32))
    grad_normed2 = jnp.zeros((grad_out.shape[0], width), f32)
    part = 3072
    for start in range(0, hidden, part):
        cols = slice(start, start + part)
        low = (dot_nt(grad_out, down_w[cols, :]) * slope_ref[:, cols]).astype(bf16)
        up_low_ref[:, cols] = low
        vec_grad[6:7, cols] = col_sum(low.astype(f32))
        grad_normed2 += dot_nt(low, up_w[:, cols])
    hat, inverse = normalised(middle_ref[...])
    vec_grad[4:5, :width] = col_sum(grad_normed2 * hat)
    vec_grad[5:6, :width] = col_sum(grad_normed2)
    grad_middle = grad_out.astype(f32) + norm_back(grad_normed2, hat, inverse, vec[4:5, :width])
    grad_middle_ref[...] = grad_middle
    proj_low = grad_middle.astype(bf16)
    proj_low_ref[...] = proj_low
    vec_grad[3:4, :width] = col_sum(proj_low.astype(f32))


def attention_back_kernel(
    proj_low_ref, proj_w, qkv_ref, probs_ref, qkv_w, x_ref, vec_in, vec, grad_middle_ref,
    in_grad_ref, qkv_low_ref, vec_grad, grad_att_ref,
):
    width = WIDTH
    grad_att_ref[...] = dot_nt(proj_low_ref[...], proj_w[...]).astype(bf16)
    attention_backward(qkv_ref, probs_ref, grad_att_ref, qkv_low_ref, width, HEADS)
    qkv_low = qkv_low_ref[...]
    vec_grad[...] = vec_in[...]
    vec_grad[2:3, : 3 * width] = col_sum(qkv_low.astype(f32))
    grad_normed1 = dot_nt(qkv_low, qkv_w[...])
    hat, inverse = normalised(x_ref[...].astype(f32))
    vec_grad[0:1, :width] = col_sum(grad_normed1 * hat)
    vec_grad[1:2, :width] = col_sum(grad_normed1)
    in_grad_ref[...] = grad_middle_ref[...] + norm_back(grad_normed1, hat, inverse, vec[0:1, :width])


def decode_kernel(plan, counts, place_ref, *refs):
    sources, refs = refs[: len(counts)], refs[len(counts) :]
    sent_ref, seg_row, slot_row, seg_col, slot_col, cot_ref = refs[:6]
    (
        out_ref, normed1_ref, qkv_low_ref, attended_ref, proj_low_ref, normed2_ref, up_low_ref,
        active_ref, embed_low_ref, grad_sent_ref, vec_grad, pos_grad,
    ) = refs[6:18]
    embedded_ref, embed_sum, qkv_ref, probs_ref, joined_ref, grad_att_ref = refs[18:24]
    held, wide, spare, sems, vec = refs[24:29]
    weights = refs[29:]
    embed_w, pos_ref, qkv_w, proj_w, up_w, down_w = weights
    width, hidden = DEC_WIDTH, DEC_HIDDEN
    image = pl.program_id(0)
    length = SLOT_PAD

    @pl.when(image == 0)
    def _():
        unpack_weights(
            plan, DEC_LAYOUT, plan.unit // 2, plan.unit, plan.full, plan.dec_room, place_ref, sources, counts,
            weights, vec, held, wide, spare, sems,
        )
        embedded_ref[...] = (dot(sent_ref[...], embed_w[...]) + vec[8:9, :width]).astype(bf16)
        vec_grad[...] = jnp.zeros_like(vec_grad)
        pos_grad[...] = jnp.zeros_like(pos_grad)
        embed_sum[...] = jnp.zeros_like(embed_sum)

    def add_vec(row, values):
        vec_grad[row : row + 1, : values.shape[1]] += values

    place = lax.broadcasted_iota(jnp.int32, (length, ROW), 0)
    match = (seg_row[...] == image) & (slot_row[...] == place)
    onehot = jnp.where(match, 1.0, 0.0)
    free = 1.0 - jnp.sum(onehot, axis=1, keepdims=True)
    x = dot(onehot.astype(bf16), embedded_ref[...]) + free * vec[9:10, :width] + pos_ref[...].astype(f32)
    hat1, inverse1 = normalised(x)
    normed1 = (hat1 * vec[0:1, :width] + vec[1:2, :width]).astype(bf16)
    normed1_ref[...] = normed1
    qkv_ref[...] = (dot(normed1, qkv_w[...]) + vec[2:3, : 3 * width]).astype(bf16)
    whole = SLOTS // 16 * 16
    tail_place = lax.broadcasted_iota(jnp.int32, (length - whole, length), 0)

    def without_padding(scores):
        tail = jnp.where(tail_place < SLOTS - whole, scores[whole:], f32(-1e30))
        return jnp.concatenate([scores[:whole], tail], axis=0)

    attention_forward(qkv_ref, probs_ref, joined_ref, width, DEC_HEADS, without_padding)
    attended = joined_ref[...].T.astype(bf16)
    attended_ref[...] = attended
    middle = x + (dot(attended, proj_w[...]) + vec[3:4, :width])
    hat2, inverse2 = normalised(middle)
    normed2 = (hat2 * vec[4:5, :width] + vec[5:6, :width]).astype(bf16)
    normed2_ref[...] = normed2
    cot = cot_ref[...]
    add_vec(7, col_sum(cot.astype(f32)))
    total = jnp.zeros((length, width), f32)
    grad_normed2 = jnp.zeros((length, width), f32)
    part = 1024
    for start in range(0, hidden, part):
        cols = slice(start, start + part)
        upward = dot(normed2_ref[...], up_w[:, cols]) + vec[6:7, cols]
        active, slope = gelu_parts(upward)
        active = active.astype(bf16)
        active_ref[:, cols] = active
        total += dot(active, down_w[cols, :])
        low = (dot_nt(cot_ref[...], down_w[cols, :]) * slope).astype(bf16)
        up_low_ref[:, cols] = low
        vec_grad[6:7, cols] += col_sum(low.astype(f32))
        grad_normed2 += dot_nt(low, up_w[:, cols])
    out_ref[...] = (middle + (total + vec[7:8, :width])).astype(bf16)

    add_vec(4, col_sum(grad_normed2 * hat2))
    add_vec(5, col_sum(grad_normed2))
    grad_middle = cot.astype(f32) + norm_back(grad_normed2, hat2, inverse2, vec[4:5, :width])
    proj_low = grad_middle.astype(bf16)
    proj_low_ref[...] = proj_low
    add_vec(3, col_sum(proj_low.astype(f32)))
    grad_att_ref[...] = dot_nt(proj_low, proj_w[...]).astype(bf16)
    attention_backward(qkv_ref, probs_ref, grad_att_ref, qkv_low_ref, width, DEC_HEADS)
    qkv_low = qkv_low_ref[...]
    add_vec(2, col_sum(qkv_low.astype(f32)))
    grad_normed1 = dot_nt(qkv_low, qkv_w[...])
    add_vec(0, col_sum(grad_normed1 * hat1))
    add_vec(1, col_sum(grad_normed1))
    grad_in = grad_middle + norm_back(grad_normed1, hat1, inverse1, vec[0:1, :width])
    low_in = grad_in.astype(bf16)
    wide = low_in.astype(f32)
    add_vec(9, col_sum(free * wide))
    pos_grad[...] += wide
    place_t = lax.broadcasted_iota(jnp.int32, (ROW, length), 1)
    match_t = (seg_col[...] == image) & (slot_col[...] == place_t)
    embed_sum[...] += dot(jnp.where(match_t, 1.0, 0.0).astype(bf16), low_in)

    @pl.when(image == IMAGES_ROW - 1)
    def _():
        embed_low = embed_sum[...].astype(bf16)
        embed_low_ref[...] = embed_low
        add_vec(8, col_sum(embed_low.astype(f32)))
        grad_sent_ref[...] = dot_nt(embed_low, embed_w[...]).astype(bf16)


def cost(microseconds):
    return pl.CostEstimate(flops=int(microseconds * 1e11), bytes_accessed=int(microseconds * 3e8), transcendentals=0)


def params_of(**extra):
    return pltpu.CompilerParams(vmem_limit_bytes=VMEM_BYTES, **extra)


def shape(dims, kind):
    return jax.ShapeDtypeStruct(dims, kind)


def unpack_scratch(chunks, room):
    return [
        pltpu.VMEM((chunks * room, LANES), bf16),
        pltpu.VMEM((3200, LANES), f32),
        pltpu.VMEM((3200, LANES), f32),
        pltpu.SemaphoreType.DMA((chunks,)),
    ]


def encode(plan, place, sources, x, seg, seg_column):
    width, hidden, length = WIDTH, HIDDEN_SIZE, ROW
    weights = [shape(e, bf16) for _, e in ENC_LAYOUT if len(e) == 2]
    kept = [
        shape((VEC_ROWS, hidden), f32),
        shape((length, width), bf16),
        shape((length, 3 * width), bf16),
        shape((HEADS, length, length), f32),
        shape((length, width), bf16),
        shape((length, width), f32),
        shape((length, width), bf16),
    ]
    result = pl.pallas_call(
        partial(encode_kernel, plan, [s.shape[0] // plan.half for s in sources]),
        in_specs=[pl.BlockSpec(memory_space=pltpu.SMEM)]
        + [pl.BlockSpec(memory_space=pl.ANY)] * len(sources)
        + [pl.BlockSpec(memory_space=pltpu.VMEM)] * 3,
        out_specs=[pl.BlockSpec(memory_space=pl.ANY)] * 4 + [pl.BlockSpec(memory_space=pltpu.VMEM)] * len(kept),
        out_shape=weights + kept,
        scratch_shapes=unpack_scratch(plan.ng, plan.room)
        + [pltpu.SemaphoreType.DMA((4,)), pltpu.VMEM((width, length), f32)]
        + [pltpu.VMEM(w.shape, bf16) for w in weights],
        compiler_params=params_of(),
        cost_estimate=cost(24),
        name="encode",
    )(place, *sources, x, seg.reshape(1, length), seg_column)
    weights = dict(zip([QKV_W, PROJ_W, UP_W, DOWN_W, VECS], result))
    return weights, dict(zip([H1, QKV, PROBS, ATT, MID, H2], result[5:]))


def encode_mlp(saved, weights):
    width, hidden, length = WIDTH, HIDDEN_SIZE, ROW
    result = late_call(
        encode_mlp_kernel,
        [],
        [saved[H2], weights[UP_W], weights[VECS], weights[DOWN_W], saved[MID]],
        [
            (shape((length, width), bf16), pltpu.VMEM),
            (shape((length, hidden), bf16), pltpu.VMEM),
            (shape((length, hidden), bf16), pltpu.VMEM),
        ],
        [],
        cost_estimate=cost(8),
        name="encode_mlp",
    )
    return dict(zip([SENT, ACT, SLOPE], result))


def mlp_back(grad, saved, weights):
    width, hidden, length = WIDTH, HIDDEN_SIZE, ROW
    return late_call(
        mlp_back_kernel,
        [],
        [grad, weights[DOWN_W], saved[SLOPE], weights[UP_W], saved[MID], weights[VECS]],
        [
            (shape((length, hidden), bf16), pltpu.VMEM),
            (shape((length, width), bf16), pltpu.VMEM),
            (shape((length, width), f32), pltpu.VMEM),
            (shape((VEC_ROWS, hidden), f32), pltpu.VMEM),
        ],
        [],
        cost_estimate=cost(9),
        name="mlp_back",
    )


def attention_back(grad_middle, proj_low, x, saved, weights, vec_grad):
    width, hidden, length = WIDTH, HIDDEN_SIZE, ROW
    return late_call(
        attention_back_kernel,
        [],
        [
            proj_low, weights[PROJ_W], saved[QKV], saved[PROBS], weights[QKV_W], x, vec_grad, weights[VECS],
            grad_middle,
        ],
        [
            (shape((length, width), f32), pltpu.VMEM),
            (shape((length, 3 * width), bf16), pltpu.VMEM),
            (shape((VEC_ROWS, hidden), f32), pltpu.VMEM),
        ],
        [pltpu.VMEM((length, width), bf16)],
        cost_estimate=cost(10),
        name="attention_back",
    )


def decode(plan, place, sources, sent, seg, slot, columns, cot):
    width, hidden, length = DEC_WIDTH, DEC_HIDDEN, SLOT_PAD
    held = [sent, seg.reshape(1, ROW), slot.reshape(1, ROW), *columns]

    def whole(array):
        return pl.BlockSpec(array.shape, lambda i: (0,) * array.ndim, pipeline_mode=pl.Buffered(1))

    def image(cols):
        return pl.BlockSpec((length, cols), lambda i: (i, 0))

    rows = IMAGES_ROW * length
    per_image = [width, width, 3 * width, width, width, width, hidden, hidden]
    kept = [
        shape((ROW, width), bf16),
        shape((ROW, WIDTH), bf16),
        shape((VEC_ROWS, hidden), f32),
        shape((length, width), f32),
    ]
    return pl.pallas_call(
        partial(decode_kernel, plan, [s.shape[0] // (plan.unit // 2) for s in sources]),
        grid=(IMAGES_ROW,),
        in_specs=[pl.BlockSpec(memory_space=pltpu.SMEM)]
        + [pl.BlockSpec(memory_space=pl.ANY)] * len(sources)
        + [whole(a) for a in held]
        + [image(width)],
        out_specs=[image(c) for c in per_image]
        + [pl.BlockSpec(s.shape, lambda i: (0, 0)) for s in kept],
        out_shape=[shape((rows, c), bf16) for c in per_image] + kept,
        scratch_shapes=[
            pltpu.VMEM((ROW, width), bf16),
            pltpu.VMEM((ROW, width), f32),
            pltpu.VMEM((length, 3 * width), bf16),
            pltpu.VMEM((DEC_HEADS, length, length), f32),
            pltpu.VMEM((width, length), f32),
            pltpu.VMEM((length, width), bf16),
        ]
        + unpack_scratch(plan.full, plan.dec_room)
        + [pltpu.VMEM((VEC_ROWS, hidden), f32)]
        + [
            pltpu.VMEM((SLOT_PAD if n == POS else e[0], e[1]), bf16) for n, e in DEC_LAYOUT if len(e) == 2
        ],
        compiler_params=params_of(dimension_semantics=("arbitrary",)),
        cost_estimate=cost(85),
        name="decode",
    )(place, *sources, *held, cot)


def rows_of(extent):
    return math.prod(extent) // LANES


def up_to(value, step):
    return -(-value // step) * step


def flat_starts(layout):
    starts, here = {}, 0
    for name, extent in layout:
        starts[name] = here
        here += rows_of(extent)
    return starts, here


def kept_starts(layout):
    starts, here = {}, 0
    for name, extent in layout:
        starts[name] = here
        here += up_to(rows_of(extent), 16)
    return starts, here


class Plan:
    def __init__(self, mesh_shape):
        self.ns, self.ng, self.nd = (mesh_shape[a] for a in (SEC, GRP, DP))
        self.ny = self.nd // 2
        self.chunk = PARAMS // LANES // self.ng
        self.pieces = self.ns * self.nd
        self.piece = up_to(-(-self.chunk // self.pieces), 64)
        self.half = self.piece // 2
        self.room = self.piece * self.pieces
        self.tables = 4 if self.ny == 2 else 2
        self.units = 2 * self.pieces
        self.full = self.ng // 2
        self.rest = flat_starts(DEC_LAYOUT)[1] - self.full * self.chunk
        assert 0 < self.rest <= self.chunk
        self.unit = up_to(-(-self.chunk // (self.units - 1)), 64)
        self.dec_room = self.unit * self.units
        whole = self.chunk // self.unit * self.unit
        self.part_in = self.unit if whole < self.dec_room - self.unit else 0
        self.parts_in = -(-self.rest // self.part_in)
        assert self.parts_in <= self.full
        self.enc_starts = [self.kept_row(ENC_LAYOUT, z * self.chunk) // 16 * 16 for z in range(self.ng)]
        self.enc_ends = [
            up_to(self.kept_row(ENC_LAYOUT, min((z + 1) * self.chunk, flat_starts(ENC_LAYOUT)[1]) - 1) + 1, 16)
            for z in range(self.ng)
        ]
        self.dec_starts = [self.kept_row(DEC_LAYOUT, z * self.chunk) // 16 * 16 for z in range(self.full)]
        self.dec_ends = [
            up_to(self.kept_row(DEC_LAYOUT, (z + 1) * self.chunk - 1) + 1, 16) for z in range(self.full)
        ]
        assert all(e - s <= self.room for s, e in zip(self.enc_starts, self.enc_ends))
        self.rest_start = self.kept_row(DEC_LAYOUT, self.full * self.chunk) // 16 * 16
        self.rest_end = kept_starts(DEC_LAYOUT)[1]
        self.part_out = [self.room - (self.dec_ends[k] - self.dec_starts[k]) for k in range(2)]
        assert max(self.part_out) <= self.room // 2
        assert self.part_out[0] < self.rest_end - self.rest_start <= sum(self.part_out)

    def kept_row(self, layout, flat_row):
        flat, _ = flat_starts(layout)
        kept, _ = kept_starts(layout)
        for name, extent in layout:
            if flat_row < flat[name] + rows_of(extent):
                return kept[name] + flat_row - flat[name]
        return kept[name] + rows_of(extent)

    def ranges(self, first, count, cut, chunks, chunk_room):
        found = []
        whole = self.chunk // cut * cut
        while count:
            z, row = divmod(first, self.chunk)
            if z >= chunks:
                k, row = divmod(row, self.part_in)
                here, room = (k + 1) * chunk_room - cut + row, self.part_in - row
            elif row < whole:
                here, room = z * chunk_room + row, whole - row
            else:
                here, room = z * chunk_room + row + cut - (self.chunk - whole), self.chunk - row
            take = min(count, room)
            found.append((here, take))
            first, count = first + take, count - take
        return found

    def packed_row(self, size, groups, index, row, away_x, away_y):
        owner, turned = away_x * self.ny + away_y, away_y * 2 + away_x
        if self.ny != 2:
            return (owner * groups + index) * size + row, size - row
        part = size // 2
        late, row = divmod(row, part)
        if not late:
            second, index = divmod(index, groups // 2)
            block = groups // 2 * part
            return second * (4 * block) + (turned if second else owner) * block + index * part + row, part - row
        fine = part // 2
        second, row = divmod(row, fine)
        start = groups * 4 * part + index * (4 * part) + second * (4 * fine)
        return start + (turned if second else owner) * fine + row, fine - row

    def enc_regions(self, groups):
        return [(self.enc_starts[z], self.enc_ends[z], k, 0) for k, z in enumerate(groups)]

    def dec_regions(self):
        length = self.room // 2
        found = []
        for z in range(self.full):
            low, high = self.dec_starts[z], self.dec_ends[z]
            found += [(low, low + length, 2 * z, 0), (low + length, high, 2 * z + 1, 0)]
        middle = self.rest_start + self.part_out[0]
        found.append((self.rest_start, middle, 1, length - self.part_out[0]))
        found.append((middle, self.rest_end, 3, length - self.part_out[1]))
        return found

    def segments(self):
        length = self.room // 2
        self.block = up_to(-(-self.chunk // 4), 8)
        rows = {}
        for s, layout in enumerate((ENC_LAYOUT, DEC_LAYOUT)):
            flat, used = flat_starts(layout)
            for z in range(self.ng):
                low, high = z * self.chunk, (z + 1) * self.chunk
                found = [[] for _ in range(4)]

                def put(source, first, stop):
                    while first < stop:
                        block = first // self.block
                        end = min(stop, (block + 1) * self.block)
                        found[block].append((source, first, -(-(end - first) // 8)))
                        source, first = source + end - first, end

                for name, extent in layout:
                    first, last = max(flat[name], low), min(flat[name] + rows_of(extent), high)
                    while first < last:
                        row, stop = self.kept_row(layout, first), last
                        if s == 0:
                            source = row - self.enc_starts[z]
                        elif z < self.full:
                            source = row - self.dec_starts[z]
                        else:
                            row -= self.rest_start
                            k = int(row >= self.part_out[0])
                            row -= k * self.part_out[0]
                            source = (k + 1) * length - self.part_out[k] + row
                            stop = min(last, first + self.part_out[k] - row)
                        put(source, first - low, stop - low)
                        first = stop
                free = max(used, low) - low
                if free < self.chunk:
                    put(self.room, free, min(free + 8, self.chunk))
                rows[s, z] = found, int(free + 8 < self.chunk)
        count = max(len(block) for found, _ in rows.values() for block in found)
        table = np.zeros((self.ns, self.ng, 12 * count + 1), np.int32)
        for (s, z), (found, left) in rows.items():
            for k, block in enumerate(found):
                for j, entry in enumerate(block):
                    table[s, z, 3 * (k * count + j) : 3 * (k * count + j) + 3] = entry
            table[s, z, -1] = left
        return table


def widen_block(held, wide, spare, ranges, rows):
    def load(start, count, further=0):
        first = start // 16 * 16
        size = up_to(start + count - first, 16)
        if isinstance(further, int):
            return held[first : first + size, :].astype(f32), size, start - first
        return held[pl.ds(pl.multiple_of(first + further, 16), size), :].astype(f32), size, start - first

    if isinstance(ranges, tuple):
        block, size, skip = load(ranges[0], rows, ranges[1])
        wide[0:size, :] = block
        return skip
    if len(ranges) == 1:
        block, size, skip = load(*ranges[0])
        wide[0:size, :] = block
        return skip
    here = 0
    for start, count in ranges:
        block, size, skip = load(start, count)
        spare[0:size, :] = block
        wide[here : here + count, :] = spare[skip : skip + count, :]
        here += count
    return 0


def unpack_weights(
    plan, layout, unit, cut, chunks, room, place_ref, sources, counts, outs, vec, held, wide, spare, sems, copies=(),
):
    matrices = [n for n, e in layout if len(e) == 2]
    per_chunk = room // unit
    number = 0
    for source, count in zip(sources, counts):
        for k in range(count):
            slot = place_ref[number]
            number += 1
            target = held.at[pl.ds(pl.multiple_of(slot * unit, 16), unit), :]
            pltpu.make_async_copy(source.at[pl.ds(k * unit, unit), :], target, sems.at[slot // per_chunk]).start()
    arrived = set()

    def arrive(ranges):
        for start, count in ranges:
            z = start // room
            if z not in arrived:
                arrived.add(z)
                part = held.at[pl.ds(z * room, room), :]
                pltpu.make_async_copy(part, part, sems.at[z]).wait()

    vec[...] = jnp.zeros_like(vec)
    flat, _ = flat_starts(layout)
    by_name = dict(zip(matrices, outs))
    order = dict(zip(matrices, copies))
    for name, extent in layout:
        if len(extent) == 2:
            depth, lanes = extent[0], extent[1] // LANES
            step = depth if name == POS else max(128, 2048 // lanes // 128 * 128)
            out = by_name[name]
            if name == POS:
                out[...] = jnp.zeros_like(out)
            found = [
                plan.ranges(flat[name] + first * lanes, min(step, depth - first) * lanes, cut, chunks, room)
                for first in range(0, depth, step)
            ]
            for ranges in found:
                arrive(ranges)

            def move(number, start, size, lanes=lanes, step=step, out=out):
                skip = widen_block(held, wide, spare, start, size * lanes)
                rows = pl.ds(number * step if isinstance(number, int) else pl.multiple_of(number * step, step), size)
                for j in range(lanes):
                    out[rows, j * LANES : (j + 1) * LANES] = wide[pl.ds(skip + j, size, stride=lanes), :].astype(bf16)

            k = 0
            while k < len(found):
                size = min(step, depth - k * step)
                run = 1
                if len(found[k]) == 1 and size == step and step * lanes % 16 == 0:
                    begin = found[k][0][0]
                    while k + run < len(found) and found[k + run] == [(begin + run * step * lanes, step * lanes)]:
                        run += 1
                if run > 1:

                    def turn(i, carry, k=k, begin=begin, lanes=lanes, step=step, move=move):
                        move(k + i, (begin, i * step * lanes), step)
                        return carry

                    lax.fori_loop(0, run, turn, 0)
                else:
                    move(k, found[k], size)
                k += run
            if name in order:
                order[name].start()
        else:
            lanes = extent[0] // LANES
            ranges = plan.ranges(flat[name], lanes, cut, chunks, room)
            arrive(ranges)
            skip = widen_block(held, wide, spare, ranges, lanes)
            row, shift = {QB: (2, 0), VB: (2, 2 * extent[0])}.get(name, (VEC.get(name), 0))
            for j in range(lanes):
                vec[row : row + 1, shift + j * LANES : shift + (j + 1) * LANES] = wide[skip + j : skip + j + 1, :]
    for z in range(chunks):
        arrive([(z * room, 1)])


def pack_kernel(plan, layout, names, regions, size, groups, place_ref, *refs):
    pairs = {}
    for name in names:
        pairs[name], refs = refs[:2], refs[2:]
    vec, refs = refs[0], refs[1:]
    pos = None
    if POS in names:
        pos, refs = pairs[POS][0], refs
    mine, theirs, wide, stage, small, sems = refs
    kept, _ = kept_starts(layout)
    extents = dict(layout)
    ny = plan.ny

    def send(source, first, rows, sem):
        moved = 0
        for low, high, index, base in regions:
            start, stop = max(first, low), min(first + rows, high)
            while start < stop:
                number, row = divmod(base + start - low, size)
                c, s, y = number // (2 * ny), number // ny % 2, number % ny
                away_x, away_y = lax.rem(s - place_ref[0] + 2, 2), lax.rem(y - place_ref[1] + ny, ny)
                where, room = plan.packed_row(size, groups, index, row, away_x, away_y)
                count = min(stop - start, room)
                target = pl.ds(pl.multiple_of(where, 16), count)
                block = source.at[pl.ds(start - first, count), :]
                for same, table in ((True, mine), (False, theirs)):

                    @pl.when((place_ref[2] == c) == same)
                    def _():
                        pltpu.make_async_copy(block, table.at[target, :], sem).start()

                moved += count
                start += count
        return moved

    def wait(rows, slot):
        if rows:
            block = stage.at[slot, pl.ds(0, rows), :]
            pltpu.make_async_copy(block, block, sems.at[slot]).wait()

    turn = 0
    pending = [0, 0]
    for name in names:
        if name == POS:
            continue
        left, right = pairs[name]
        depth, width = extents[name]
        lanes = width // LANES
        step = max(k for k in (128, 256, 384, 512) if depth % k == 0 and k * lanes <= 3072)
        rows = step * lanes
        for first in range(0, depth, step):
            start = kept[name] + first * lanes
            if all(start >= high or start + rows <= low for low, high, _, _ in regions):
                continue
            slot = turn % 2
            turn += 1
            columns = flip(left[:, first : first + step])
            part = 256
            for start in range(0, width, part):
                block = dot(columns, right[:, start : start + part])
                for j in range(part // LANES):
                    wide[pl.ds(start // LANES + j, step, stride=lanes), :] = block[:, j * LANES : (j + 1) * LANES]
            wait(pending[slot], slot)
            stage[slot, 0:rows, :] = wide[0:rows, :].astype(bf16)
            pending[slot] = send(stage.at[slot], kept[name] + first * lanes, rows, sems.at[slot])
    here = 0
    total = 0
    for name, extent in layout:
        if name not in names and len(extent) == 2 or name not in kept_names(names):
            continue
        if len(extent) == 2 and name != POS:
            continue
        rows = rows_of(extent)
        room = up_to(rows, 16)
        wide[0:room, :] = jnp.zeros((room, LANES), f32)
        if name == POS:
            lanes = extent[1] // LANES
            for j in range(lanes):
                wide[pl.ds(j, extent[0], stride=lanes), :] = pos[0 : extent[0], j * LANES : (j + 1) * LANES]
        else:
            row, shift = {QB: (2, 0), VB: (2, 2 * extent[0])}.get(name, (VEC.get(name), 0))
            for j in range(rows):
                wide[j : j + 1, :] = vec[row : row + 1, shift + j * LANES : shift + (j + 1) * LANES]
        small[here : here + room, :] = wide[0:room, :].astype(bf16)
        total += send(small.at[pl.ds(here, room), :], kept[name], room, sems.at[2])
        here += room
    wait(pending[0], 0)
    wait(pending[1], 1)
    block = small.at[pl.ds(0, total), :]
    pltpu.make_async_copy(block, block, sems.at[2]).wait()


def pack_enc_kernel(plan, names, regions, size, groups, place_ref, *refs):
    pairs = {}
    for name in names:
        pairs[name], refs = refs[:4], refs[4:]
    vec, vec_other, *tables = refs[: 2 + plan.tables]
    wide, stage, small, sems = refs[2 + plan.tables :]
    lates = [a for four in pairs.values() for a in four] + [vec, vec_other]
    kept, _ = kept_starts(ENC_LAYOUT)
    extents = dict(ENC_LAYOUT)
    ny = plan.ny

    def pieces(first, rows, core):
        for low, high, index, base in regions:
            start, stop = max(first, low), min(first + rows, high)
            while start < stop:
                number, row = divmod(base + start - low, size)
                count = min(stop - start, size - row)
                if number // (2 * ny) == core:
                    yield start - first, count, index, row, number // ny % 2, number % ny
                start += count

    def send(source, first, rows, sem, core):
        moved = 0
        for skip, count, index, row, s, y in pieces(first, rows, core):
            away_x, away_y = lax.rem(s - place_ref[0] + 2, 2), lax.rem(y - place_ref[1] + ny, ny)
            if ny == 2 and index >= groups // 2:
                keep, away, other, index = tables[2:], away_y, away_x, index - groups // 2
            else:
                keep, away, other = tables[:2], away_x, away_y
            length = (groups // 2 if ny == 2 else groups) * size
            target = pl.ds(pl.multiple_of(other * length, 16) + index * size + row, count)
            block = source.at[pl.ds(skip, count), :]
            for k in range(2):

                @pl.when(away == k)
                def _():
                    pltpu.make_async_copy(block, keep[k].at[target, :], sem).start()

            moved += count
        return moved

    def wait(rows, slot):
        if rows:
            block = stage.at[slot, pl.ds(0, rows), :]
            pltpu.make_async_copy(block, block, sems.at[slot]).wait()

    def run(core):
        turn = 0
        pending = [0, 0]
        for name in names:
            left, left_other, right, right_other = pairs[name]
            depth, width = extents[name]
            lanes = width // LANES
            step = max(k for k in (128, 256, 384, 512) if depth % k == 0 and k * lanes <= 3072)
            rows = step * lanes
            for first in range(0, depth, step):
                begin = kept[name] + first * lanes
                if not list(pieces(begin, rows, core)):
                    continue
                slot = turn % 2
                turn += 1
                cut = slice(first, first + step)
                columns = jnp.concatenate([flip(left[:, cut]), flip(left_other[:, cut])], axis=1)
                part = 256
                for start in range(0, width, part):
                    cols = slice(start, start + part)
                    block = dot(columns, jnp.concatenate([right[:, cols], right_other[:, cols]], axis=0))
                    for j in range(part // LANES):
                        wide[pl.ds(start // LANES + j, step, stride=lanes), :] = block[:, j * LANES : (j + 1) * LANES]
                wait(pending[slot], slot)
                stage[slot, 0:rows, :] = wide[0:rows, :].astype(bf16)
                pending[slot] = send(stage.at[slot], begin, rows, sems.at[slot], core)
        here = 0
        total = 0
        for name, extent in ENC_LAYOUT:
            if name not in kept_names(names):
                continue
            rows = rows_of(extent)
            room = up_to(rows, 16)
            if list(pieces(kept[name], room, core)):
                wide[0:room, :] = jnp.zeros((room, LANES), f32)
                row, shift = {QB: (2, 0), VB: (2, 2 * extent[0])}.get(name, (VEC.get(name), 0))
                for j in range(rows):
                    cols = slice(shift + j * LANES, shift + (j + 1) * LANES)
                    wide[j : j + 1, :] = vec[row : row + 1, cols] + vec_other[row : row + 1, cols]
                small[here : here + room, :] = wide[0:room, :].astype(bf16)
                total += send(small.at[pl.ds(here, room), :], kept[name], room, sems.at[2], core)
            here += room
        wait(pending[0], 0)
        wait(pending[1], 1)
        if total:
            block = small.at[pl.ds(0, total), :]
            pltpu.make_async_copy(block, block, sems.at[2]).wait()

    for core in range(2):

        @pl.when(place_ref[2] == core)
        def _():
            for each in lates:
                each.here = False
            run(core)
            for each in lates:
                each.arrive()


def pack_enc(plan, regions, size, groups, place, pairs, vec, vec_other):
    names = list(pairs)
    operands = [a for name in names for a in pairs[name]] + [vec, vec_other]
    extents = dict(ENC_LAYOUT)
    small = sum(up_to(rows_of(extents[n]), 16) for n in kept_names(names))
    rows = 2 * plan.ny * groups * size // plan.tables
    return late_call(
        partial(pack_enc_kernel, plan, names, regions, size, groups),
        [(place, pltpu.SMEM)],
        operands,
        [(shape((rows, LANES), bf16), pl.ANY)] * plan.tables,
        [
            pltpu.VMEM((3072, LANES), f32),
            pltpu.VMEM((2, 3072 + 64, LANES), bf16),
            pltpu.VMEM((small + 64, LANES), bf16),
            pltpu.SemaphoreType.DMA((3,)),
        ],
        cost_estimate=cost(8),
        name="pack_enc",
    )


def kept_names(names):
    with_matrix = {
        QKV_W: [N1G, N1B, QB, VB],
        PROJ_W: [PB, N2G, N2B],
        UP_W: [UB],
        DOWN_W: [DB],
        EMBED_W: [EB, MT],
        POS: [POS],
    }
    return [v for n in names for v in with_matrix[n]]


def pack(plan, layout, regions, size, groups, place, pairs, vec):
    names = list(pairs)
    operands = [a for name in names for a in pairs[name]] + [vec]
    extents = dict(layout)
    small = sum(up_to(rows_of(extents[n]), 16) for n in kept_names(names))
    rows = 2 * plan.ny * groups * size
    return late_call(
        partial(pack_kernel, plan, layout, names, regions, size, groups),
        [(place, pltpu.SMEM)],
        operands,
        [(shape((rows, LANES), bf16), pl.ANY)] * 2,
        [
            pltpu.VMEM((3072, LANES), f32),
            pltpu.VMEM((2, 3072 + 64, LANES), bf16),
            pltpu.VMEM((small + 64, LANES), bf16),
            pltpu.SemaphoreType.DMA((3,)),
        ],
        cost_estimate=cost(19),
        name="pack",
    )


def finish_kernel(plan, counts, place_ref, seg_ref, *refs):
    sources, result, held, wide, out, sem, out_sems = refs[: len(counts)], *refs[len(counts) :]
    unit = plan.half
    number = 0
    for source, count in zip(sources, counts):
        for k in range(count):
            target = held.at[pl.ds(pl.multiple_of(place_ref[number] * unit, 16), unit), :]
            number += 1
            pltpu.make_async_copy(source.at[pl.ds(k * unit, unit), :], target, sem.at[0]).start()
    count = seg_ref.shape[0] // 12

    @pl.when(seg_ref[12 * count] != 0)
    def _():
        out[...] = jnp.zeros_like(out)

    pltpu.make_async_copy(held, held, sem.at[0]).wait()
    total = plan.room
    wide[total : total + 16, :] = jnp.zeros((16, LANES), f32)
    wide[0:total, :] = held[...].astype(f32)

    def one(k, carry):
        source, first, steps = seg_ref[3 * k], seg_ref[3 * k + 1], seg_ref[3 * k + 2]

        def step(i, carry):
            out[pl.ds(first + 8 * i, 8), :] = wide[pl.ds(source + 8 * i, 8), :]
            return carry

        def steps16(i, carry):
            out[pl.ds(first + 128 * i, 128), :] = wide[pl.ds(source + 128 * i, 128), :]
            return carry

        many = steps // 16
        lax.fori_loop(0, many, steps16, 0)
        return lax.fori_loop(many * 16, steps, step, carry)

    rows = up_to(plan.chunk, 8)
    lines = out.at[pl.ds(0, rows), :].reshape(rows, 1, LANES)
    copies = []
    for block in range(4):
        lax.fori_loop(block * count, (block + 1) * count, one, 0)
        first = block * plan.block
        part = pl.ds(first, min(plan.block, plan.chunk - first))
        copies.append(pltpu.make_async_copy(lines.at[part], result.at[part], out_sems.at[block]))
        copies[-1].start()
    for copy in copies:
        copy.wait()


def finish(plan, place, segments, sources):
    total = plan.room
    return pl.pallas_call(
        partial(finish_kernel, plan, [s.shape[0] // plan.half for s in sources]),
        in_specs=[pl.BlockSpec(memory_space=pltpu.SMEM)] * 2
        + [pl.BlockSpec(memory_space=pl.ANY)] * len(sources),
        out_specs=pl.BlockSpec(memory_space=pl.ANY),
        out_shape=shape((plan.chunk, 1, LANES), f32),
        scratch_shapes=[
            pltpu.VMEM((total, LANES), bf16),
            pltpu.VMEM((total + 16, LANES), f32),
            pltpu.VMEM((up_to(plan.chunk, 8) + 8, LANES), f32),
            pltpu.SemaphoreType.DMA((1,)),
            pltpu.SemaphoreType.DMA((4,)),
        ],
        compiler_params=params_of(),
        cost_estimate=cost(8),
        name="finish",
    )(place, segments, *sources)


def completed(pairs, count):
    senders = [k for k in range(count) if k not in [a for a, _ in pairs]]
    receivers = [k for k in range(count) if k not in [b for _, b in pairs]]
    return list(pairs) + list(zip(senders, receivers))


def after(values, *before):
    return lax.optimization_barrier((values, before))[0]


def per_device(plan, enc_input, segments, slots, params, cot):
    ns, ng, nd, ny = plan.ns, plan.ng, plan.nd, plan.ny
    piece, half, room, chunk = plan.piece, plan.half, plan.room, plan.chunk
    sec = lax.axis_index(SEC)
    grp = lax.axis_index(GRP)
    dp = lax.axis_index(DP)
    yy, core = dp // 2, dp % 2
    first_section = sec == 0

    def over_x(block):
        return lax.ppermute(block, SEC, [(0, 1), (1, 0)])

    def over_core(block):
        return lax.ppermute(block, DP, [(d, d ^ 1) for d in range(nd)])

    def over_y(block):
        return lax.ppermute(block, DP, [(d, (d + 2) % nd) for d in range(nd)])

    def over_z(block, senders=None):
        senders = range(ng) if senders is None else senders
        return lax.ppermute(block, GRP, [(g, (g + 1) % ng) for g in senders])

    def final_places():
        if ny == 2:
            owners = [(sec, yy), (1 - sec, yy), (sec, 1 - yy), (1 - sec, 1 - yy)]
        else:
            owners = [(s, (yy - k) % ny) for k in range(ny) for s in (sec, 1 - sec)]
        found = []
        for c in (core, 1 - core):
            for s, y in owners:
                number = (c * 2 + s) * ny + y
                found += [
                    jnp.where(first_section, 2 * number, number),
                    jnp.where(first_section, 2 * number + 1, plan.pieces + number),
                ]
        return found

    unit = plan.unit

    def share(start, params):
        cut = lax.dynamic_slice(params, (0, start * LANES), (1, unit * LANES))
        return cut.astype(f32).reshape(unit, LANES).astype(bf16)

    def shares(section, params):
        number = section * nd + dp
        enc_first = jnp.minimum(number * piece, chunk - piece)
        dec_first = [jnp.minimum((h * plan.pieces + number) * unit, chunk - unit) for h in range(2)]
        if plan.parts_in == 1:
            dec_first[0] = jnp.where(grp == plan.full, 0, dec_first[0])
        return (
            share(jnp.where(first_section, enc_first, dec_first[0]), params),
            share(jnp.where(first_section, enc_first + piece - unit, dec_first[1]), params),
        )

    send = shares(1 - sec, params)
    keep = shares(sec, after(params, *send))

    def whole_piece(parts):
        return jnp.concatenate([parts[0][:half], parts[1][unit - half :]])

    routes = [[(z, 2 * z + h) for z in range(plan.full)] for h in range(2)]
    if plan.parts_in == 1:
        routes[0].append((plan.full, 1))
    routes = [completed(route, ng) for route in routes]
    crossed = []
    for h in range(2):
        pairs = [(z, ng + z) for z in range(ng)] + [(ng + a, b) for a, b in routes[h]]
        crossed.append(lax.ppermute(send[h], (SEC, GRP), pairs))
    spread = [lax.ppermute(keep[h], GRP, routes[h]) for h in range(2)]
    enc_piece = jnp.where(first_section, whole_piece(keep), whole_piece(crossed))
    even, odd = (jnp.where(first_section, crossed[h], spread[h]) for h in range(2))
    dec_piece = jnp.where(grp % 2 == 0, even, odd)
    class Gather:
        def __init__(self, here):
            self.here = here
            if ny == 2:
                self.arrays = [here, over_x(here), over_y(here)]
                self.owners = [(sec, yy), (1 - sec, yy), (sec, 1 - yy), (1 - sec, 1 - yy)]
            else:
                column = [here]
                for _ in range(ny - 1):
                    column.append(over_y(column[-1]))
                self.arrays = column
                self.owners = [(s, (yy - k) % ny) for s in (sec, 1 - sec) for k in range(ny)]

        def second(self):
            if ny == 2:
                middle = self.here.shape[0] // 2
                self.corners = [self.arrays[1][:middle], self.arrays[2][middle:]]
            else:
                self.corners = self.arrays
            return tuple(self.corners)

        def third(self):
            if ny == 2:
                self.arrays += [over_y(self.corners[0]), over_x(self.corners[1])]
            else:
                self.arrays = self.arrays + [over_x(block) for block in self.corners]
            return tuple(self.arrays[-2:])

        def fourth(self, joined=True):
            arrays = [jnp.concatenate(self.arrays)] if joined else self.arrays
            return arrays + [over_core(block) for block in arrays]

        def places(self, parts):
            found = []
            for c in (core, 1 - core):
                for s, y in self.owners:
                    for k in parts:
                        number = (grp - k) % ng * plan.pieces + s * nd + y * 2 + c
                        found += [2 * number, 2 * number + 1]
            return found

    last = jnp.logical_and(sec == ns - 1, dp == nd - 1)
    if plan.parts_in == 1:
        dec_piece = jnp.where(jnp.logical_and(last, grp == 1), even, dec_piece)
    else:
        for k in range(plan.parts_in):
            part = share(jnp.minimum(k * unit, chunk - unit), params)
            part = lax.ppermute(part, GRP, [(plan.full, 2 * k + 1)])
            dec_piece = jnp.where(jnp.logical_and(last, grp == 2 * k + 1), part, dec_piece)
    here = enc_piece
    gathers = [Gather(here)]
    micro_rows = enc_input.reshape(ROW, WIDTH)
    seg = lax.dynamic_index_in_dim(segments, sec, 0, keepdims=False).reshape(ROW)
    slot = lax.dynamic_index_in_dim(slots, sec, 0, keepdims=False).reshape(ROW)
    cot_rows = jnp.pad(
        cot.reshape(IMAGES_ROW, SLOTS, DEC_WIDTH), ((0, 0), (0, SLOT_PAD - SLOTS), (0, 0))
    ).reshape(IMAGES_ROW * SLOT_PAD, DEC_WIDTH)

    columns = (seg.reshape(ROW, 1), slot.reshape(ROW, 1))
    table = jnp.asarray(plan.segments())[sec, grp].reshape(-1)
    place = jnp.stack([sec, yy, core]).astype(jnp.int32)
    finish_places = jnp.stack(final_places()).astype(jnp.int32)
    enc_places = jnp.stack([p for k in range(ng) for p in gathers[0].places([k])]).astype(jnp.int32)
    dec_places = jnp.stack(gathers[0].places(range(ng))).astype(jnp.int32)
    small = (columns, table, place, finish_places, enc_places, dec_places, cot_rows)
    for k in range(1, ng):
        here = over_z(here)
        if k == 1:
            here, small = after((here, small), enc_piece)
            here = after(here, *small)
        if k >= 2:
            here = after(here, *gathers[k - 2].second())
        if k >= 3:
            here = after(here, *gathers[k - 3].third())
        gathers.append(Gather(here))
    gathers[-2].second()
    dec_parts = [after(dec_piece, here)]
    for _ in range(ng - 1):
        dec_parts.append(over_z(dec_parts[-1]))
    gathers[-1].arrays[1:] = after(gathers[-1].arrays[1:], *dec_parts[1:-1])
    gathers[-1].second()
    columns, table, place, finish_places, enc_places, dec_places, cot_rows = small
    enc_sources = []
    for k, g in enumerate(gathers):
        if k >= ng - 3:
            g.third()
        if k == ng - 1:
            g.arrays = after(g.arrays, dec_parts[-1])
        enc_sources += g.fourth()
    dec_gather = Gather(after(jnp.concatenate(dec_parts), *gathers[-1].corners))

    enc_weights, saved = encode(plan, enc_places, enc_sources, micro_rows, seg, columns[0])
    dec_gather.arrays[1:] = after(dec_gather.arrays[1:], saved[H2])
    saved[H2] = after(saved[H2], *dec_gather.second())
    saved.update(encode_mlp(saved, enc_weights))
    others = {k: over_core(saved[k]) for k in (H1, ATT, H2, ACT)}
    dec_gather.third()
    dec_gather.arrays[-2:] = after(dec_gather.arrays[-2:], saved[SENT])
    dec_sources = dec_gather.fourth(False)
    dec = dict(
        zip(
            [OUT, H1, QKV_L, ATT, PROJ_L, H2, UP_L, ACT, EMBED_L, GSENT, VECS, GPOS],
            decode(plan, dec_places, dec_sources, saved[SENT], seg, slot, columns, cot_rows),
        )
    )

    def add(first, *others):
        total = first.astype(f32)
        for other in others:
            total = total + other.astype(f32)
        return total.astype(bf16)

    class Square:
        def __init__(self, keeps, sends):
            self.keeps, self.sends = keeps, [add(*parts) if len(parts) > 1 else parts[0] for parts in sends]
            self.m = keeps[0][0].shape[0] // ny

        def kept(self, half, low, high, *others):
            return add(*[part[low:high] for part in self.keeps[half]], *others)

        def first(self):
            return (over_x(self.sends[0]), over_y(self.sends[1])) if ny == 2 else (over_x(self.sends[0]),)

        def second(self, *got):
            m = self.m
            self.got = got
            if ny == 2:
                self.sends = tuple(self.kept(k, m, 2 * m, got[k][m:]) for k in range(2))
            else:
                column = self.kept(0, 0, ny * m, got[0])
                total = column[(ny - 1) * m :]
                for k in range(ny - 2, -1, -1):
                    total = add(column[k * m : (k + 1) * m], over_y(total))
                self.sends = (total,)
            return self.sends

        def third(self, *before):
            m = self.m
            if ny == 2:
                late = after((over_y(self.sends[0]), over_x(self.sends[1])), *before)
                self.own = tuple(self.kept(k, 0, m, self.got[k][:m], late[k]) for k in range(2))
            else:
                self.own = (self.sends[0][: m // 2], self.sends[0][m // 2 :])
            return self.own

    class Ring:
        def __init__(self, one):
            self.one, self.step = one, 0
            self.total = add(*one((grp - 1) % ng))

        def next(self, *before):
            got = after(over_z(self.total), *before)
            self.step += 1
            self.total = add(*self.one((grp - 1 - self.step) % ng), got)
            return self.total

    def pick(blocks, g):
        if len(blocks) == 4 == ng:
            return jnp.where(g < 2, jnp.where(g == 0, *blocks[:2]), jnp.where(g == 2, *blocks[2:]))
        rows = jnp.concatenate(blocks)
        size = rows.shape[0] // ng
        return lax.dynamic_slice(rows, (g * size, 0), (size, LANES))

    def halves(block):
        return [block[: block.shape[0] // 2], block[block.shape[0] // 2 :]]

    every = list(range(ng))
    near = ng // 2
    upper, lower = every[near:], every[:near]
    grad_sent, others = after((dec[GSENT], others), dec[VECS])
    grad_sent = after(grad_sent, *others.values())
    grad_other = over_core(grad_sent)
    up_low, proj_low, grad_middle, mlp_vec = mlp_back(grad_sent, saved, enc_weights)
    grad_other = after(grad_other, up_low)
    up_other, proj_other, mlp_vec_other = over_core(up_low), over_core(proj_low), over_core(mlp_vec)
    in_grad, qkv_low, enc_vec = attention_back(grad_middle, proj_low, micro_rows, saved, enc_weights, mlp_vec)
    up_other, proj_other, mlp_vec_other = after((up_other, proj_other, mlp_vec_other), qkv_low)
    up_tables = pack_enc(
        plan, plan.enc_regions(upper), piece, len(upper), place,
        {
            DOWN_W: (saved[ACT], others[ACT], grad_sent, grad_other),
            UP_W: (saved[H2], others[H2], after(up_low, qkv_low), up_other),
        },
        mlp_vec, mlp_vec_other,
    )
    qkv_other, vec_other = after((over_core(qkv_low), over_core(enc_vec)), up_tables[0])
    dec_mine, dec_theirs = pack(
        plan, DEC_LAYOUT, plan.dec_regions(), half, ng, place,
        {
            EMBED_W: (saved[SENT], dec[EMBED_L]),
            QKV_W: (dec[H1], dec[QKV_L]),
            PROJ_W: (dec[ATT], dec[PROJ_L]),
            UP_W: (dec[H2], dec[UP_L]),
            DOWN_W: (dec[ACT], cot_rows),
            POS: (dec[GPOS], dec[GPOS]),
        },
        after(dec[VECS], up_tables[0]),
    )
    qkv_other, vec_other = after((qkv_other, vec_other), dec_mine)

    def table_square(tables):
        return Square([[t] for t in tables[0::2]], [[t] for t in tables[1::2]])

    upper_sum = table_square(up_tables)
    upper_sum.second(*after(upper_sum.first(), dec_mine))
    low_tables = pack_enc(
        plan, plan.enc_regions(lower), piece, len(lower), place,
        {
            PROJ_W: (saved[ATT], others[ATT], proj_low, proj_other),
            QKV_W: (saved[H1], others[H1], qkv_low, qkv_other),
            UP_W: (saved[H2], others[H2], after(up_low, *upper_sum.sends), up_other),
        },
        enc_vec, vec_other,
    )
    lower_sum = table_square(low_tables)
    lower_first = lower_sum.first()
    dec_parts = (dec_mine, after(over_core(dec_theirs), low_tables[0]))

    def dec_rows(low, high):
        return [part[low:high] for part in dec_parts]

    if ny == 2:
        rows = dec_mine.shape[0] // 2
        size = rows // ng

        def dec_late(g):
            return [lax.dynamic_slice(part, (rows + g * size, 0), (size, LANES)) for part in dec_parts]

        late_ring = Ring(dec_late)
        quarter = rows // 4
        cuts = [dec_rows(k * quarter, (k + 1) * quarter) for k in range(4)]
        upper_sum.third(late_ring.total)
        lower_sum.second(*after(lower_first, *upper_sum.own))
        early = Square(cuts[0::2], cuts[1::2])
        early.sends = after(early.sends, *lower_sum.sends)
        early_first = early.first()
        late_ring.next(*early.sends)
        lower_sum.third(late_ring.total)
        enc_ring = Ring(lambda g: [pick(list(lower_sum.own) + list(upper_sum.own), g)])
        early.second(*after(early_first, enc_ring.total))
        for _ in range(ng - 3):
            late_ring.next(*early.sends)
        early_own = [b for o in early.third(late_ring.total) for b in halves(o)]
        early_ring = Ring(lambda g: [pick(early_own, g)])
        enc_ring.next(early_ring.total)
        late_ring.next(enc_ring.total)
        quarter = size // 4
        cuts = [[late_ring.total[k * quarter : (k + 1) * quarter]] for k in range(4)]
        late = Square(cuts[0::2], cuts[1::2])
        late_first = late.first()
        early_ring.next(*late.sends)
        late.second(*after(late_first, early_ring.total))
        early_ring.next(*late.sends)
        late_own = late.third(early_ring.total)
        for _ in range(ng - 3):
            early_ring.next(*late_own)
        dec_own = jnp.concatenate([early_ring.total, *late_own])
    else:
        lower_sum.second(*lower_first)
        rows = dec_mine.shape[0] // 2
        whole = Square([dec_rows(0, rows)], [dec_rows(rows, 2 * rows)])
        whole.second(*whole.first())
        dec_ring = Ring(lambda g: [pick(list(whole.third()), g)])
        for _ in range(ng - 1):
            dec_ring.next()
        dec_own = dec_ring.total
        upper_sum.third()
        lower_sum.third()
        enc_ring = Ring(lambda g: [pick(list(lower_sum.own) + list(upper_sum.own), g)])
        enc_ring.next()
    back = [[(2 * z + h, z) for z in range(plan.full)] for h in range(2)]
    back[0].append((1, plan.full))
    back.append([(3, plan.full)])
    dec_back = [lax.ppermute(dec_own, GRP, completed(pairs, ng)) for pairs in back]
    enc_ring.next(dec_own)
    dec_low, dec_high, dec_rest = after(dec_back, enc_ring.total)
    dec_own = jnp.concatenate([dec_low, jnp.where(grp == plan.full, dec_rest, dec_high)])
    for _ in range(ng - 3):
        enc_ring.next(dec_own)
    enc_own = enc_ring.total

    own = jnp.where(first_section, enc_own, dec_own)
    other = jnp.where(first_section, dec_own, enc_own)
    if ny == 2:
        from_x, from_y = over_x(other), over_y(own)
        sources = [own, from_x, from_y, over_y(from_x)]
    else:
        column = [jnp.concatenate([own, over_x(other)])]
        for _ in range(ny - 1):
            column.append(over_y(column[-1]))
        sources = column
    sources = sources + [over_core(block) for block in sources]
    flat = finish(plan, finish_places, table, sources)
    param_grad = flat.reshape(1, chunk * LANES)
    dec_out = dec[OUT].reshape(IMAGES_ROW, SLOT_PAD, DEC_WIDTH)[:, :SLOTS]
    return (
        dec_out.reshape(1, 1, IMAGES_ROW * SLOTS, DEC_WIDTH),
        in_grad.reshape(1, 1, ROW, WIDTH),
        param_grad,
    )


def solution(mesh):
    placed = (
        P(SEC, (GRP, DP), None, None),
        P(None, (GRP, DP), None),
        P(None, (GRP, DP), None),
        P(SEC, GRP),
        P(SEC, (GRP, DP), None, None),
    )
    return jax.shard_map(
        partial(per_device, Plan(dict(mesh.shape))),
        mesh=mesh,
        in_specs=placed,
        out_specs=(
            P(SEC, (GRP, DP), None, None),
            P(SEC, (GRP, DP), None, None),
            P(SEC, GRP),
        ),
        check_vma=False,
    )
```
